32 devices in a mesh: dp: 8 (over z, x), seq: 2 (over core), mp: 2 (over y).
Axes of the slice: x: 2, y: 2, z: 4, core: 2. Of those that a mesh axis runs over, the one named last changes fastest.
Arguments:
- mel_input: bfloat16 [8, 80, 4096], P('dp', None, 'seq'), may hold values from -6 to 6
- conv1_weight: bfloat16 [3, 80, 512], replicated, may hold values from -0.375 to 0.375
- conv1_bias: bfloat16 [512], replicated, may hold values from -2 to 2
- conv2_weight: bfloat16 [3, 512, 512], replicated, may hold values from -0.15625 to 0.15625
- conv2_bias: bfloat16 [512], replicated, may hold values from -2 to 2
- norm1_gain: bfloat16 [512], replicated, may hold values from 0.099609375 to 1.8984375
- norm1_bias: bfloat16 [512], replicated, may hold values from -2 to 2
- qkv_weight: bfloat16 [3, 512, 512], P(None, None, 'mp'), may hold values from -0.375 to 0.375
- qkv_bias: bfloat16 [2, 512], P(None, 'mp'), may hold values from -2 to 2
- out_weight: bfloat16 [512, 512], P('mp'), may hold values from -1 to 1
- out_bias: bfloat16 [512], replicated, may hold values from -2 to 2
- norm2_gain: bfloat16 [512], replicated, may hold values from 0.099609375 to 1.8984375
- norm2_bias: bfloat16 [512], replicated, may hold values from -2 to 2
- up_weight: bfloat16 [512, 2048], P(None, 'mp'), may hold values from -0.25 to 0.25
- up_bias: bfloat16 [2048], P('mp'), may hold values from -2.5 to 2.5
- down_weight: bfloat16 [2048, 512], P('mp'), may hold values from -0.25 to 0.25
- down_bias: bfloat16 [512], replicated, may hold values from -2 to 2
- cotangent: bfloat16 [8, 2048, 512], P('dp', 'seq'), may hold values from -6 to 6
- speech_mask: int32 [8, 2048], P('dp', 'seq'), may hold values 0 or 1
Outputs:
- encoded: bfloat16 [8, 2048, 512], P('dp', 'seq')
- mel_grad: float32 [8, 80, 4096], P('dp', None, 'seq')
- conv1_weight_grad: float32 [3, 80, 512], replicated
- conv1_bias_grad: float32 [512], replicated
- conv2_weight_grad: float32 [3, 512, 512], replicated
- conv2_bias_grad: float32 [512], replicated
- norm1_gain_grad: float32 [512], replicated
- norm1_bias_grad: float32 [512], replicated
- qkv_weight_grad: float32 [3, 512, 512], P(None, None, 'mp')
- qkv_bias_grad: float32 [2, 512], P(None, 'mp')
- out_weight_grad: float32 [512, 512], P('mp')
- out_bias_grad: float32 [512], replicated
- norm2_gain_grad: float32 [512], replicated
- norm2_bias_grad: float32 [512], replicated
- up_weight_grad: float32 [512, 2048], P(None, 'mp')
- up_bias_grad: float32 [2048], P('mp')
- down_weight_grad: float32 [2048, 512], P('mp')
- down_bias_grad: float32 [512], replicated
The draws below stay inside these ranges and needn't reach their ends.
Inputs may be any that keep to these rules, and one draw needn't show every extreme that they name: `speech_mask`: 1 keeps the gradient of a frame, 0 marks a non-speech frame.
All inputs are finite; a program needn't handle non-finite values. No bound on the sum of `speech_mask` on one device may be relied on, other than what follows from the above.
Results may differ from the reference program's by a relative error of at most 0.02.
The reference program's roundings to bfloat16 on the way count: a program that leaves them out, or rounds other values in their place, can miss the bound.
Values may be sent and summed in bfloat16 or wider, within the bound.
A program may use at most 256 MiB of HBM per device.

```python
import math
import jax
import jax.numpy as jnp
from jax import lax

N_MELS = 80
D = 512
HEADS = 8
FF = 2048
FRAMES = 2048
MEL_FRAMES = 4096
CLIPS = 8


def set_ends(array, key, smallest, largest):
    dims = array.shape
    place = [jax.random.randint(jax.random.fold_in(key, axis), (), 0, dims[axis]) for axis in range(len(dims))]
    array = array.at[tuple(place)].set(smallest)
    longest = dims.index(max(dims))
    place[longest] = (place[longest] + 1) % dims[longest]
    return array.at[tuple(place)].set(largest)


def steps_of(own_key, dims, shards, smallest, high):
    loudness, own = 1.0, jax.random.fold_in(own_key, 6)
    for dim, shards_of in shards:
        draws = jnp.exp(jax.random.uniform(jax.random.fold_in(own, dim), (shards_of,), jnp.float32, smallest / len(shards), high / len(shards)))
        loudness = loudness * jnp.repeat(draws, dims[dim] // shards_of).reshape([-1 if axis == dim else 1 for axis in range(len(dims))])
    return loudness


def bell_draw(rng, shape, deviation, reach, shards=(), kind=jnp.bfloat16):
    entries = deviation * jax.random.normal(rng, shape, jnp.float32)
    if shards:
        entries = entries * steps_of(rng, shape, shards, -0.22, 0.18)
    return jnp.clip(entries, -reach, reach).astype(kind)


def setup_inputs(seed: int = 0) -> dict:
    key_list = jax.random.split(jax.random.key(seed), 20)
    mel_input = bell_draw(key_list[0], (CLIPS, N_MELS, MEL_FRAMES), 1.0, 6.0, ((0, 8), (2, 2)))
    conv1_weight = bell_draw(key_list[1], (3, N_MELS, D), (3 * N_MELS) ** -0.5, 0.375)
    conv1_bias = bell_draw(key_list[2], (D,), 0.4, 2.0)
    conv2_weight = bell_draw(key_list[3], (3, D, D), (3 * D) ** -0.5, 0.15625)
    conv2_bias = bell_draw(key_list[4], (D,), 0.4, 2.0)
    norm1_gain = jnp.clip(1.0 + 0.18 * jax.random.normal(key_list[5], (D,), jnp.float32), 0.099609375, 1.8984375).astype(jnp.bfloat16)
    norm1_bias = bell_draw(key_list[6], (D,), 0.4, 2.0)
    qkv_weight = bell_draw(key_list[7], (3, D, D), (D // 2) ** -0.5, 0.375, ((2, 2),))
    qkv_bias = bell_draw(key_list[8], (2, D), 0.4, 2.0, ((1, 2),))
    out_weight = bell_draw(key_list[9], (D, D), (D // 16) ** -0.5, 1.0, ((0, 2),))
    out_bias = bell_draw(key_list[10], (D,), 0.4, 2.0)
    norm2_gain = jnp.clip(1.0 + 0.18 * jax.random.normal(key_list[11], (D,), jnp.float32), 0.099609375, 1.8984375).astype(jnp.bfloat16)
    norm2_bias = bell_draw(key_list[12], (D,), 0.4, 2.0)
    up_weight = bell_draw(key_list[13], (D, FF), D ** -0.5, 0.25, ((1, 2),))
    up_bias = bell_draw(key_list[14], (FF,), 0.5, 2.5, ((0, 2),))
    down_weight = bell_draw(key_list[15], (FF, D), (FF // 4) ** -0.5, 0.25, ((0, 2),))
    down_bias = bell_draw(key_list[16], (D,), 0.4, 2.0)
    cotangent = bell_draw(key_list[17], (CLIPS, FRAMES, D), 1.0, 6.0, ((0, 8), (1, 2)))
    speech_mask = set_ends((jax.random.randint(key_list[18], (CLIPS, FRAMES), 0, 4) < 3).astype(jnp.int32), jax.random.fold_in(key_list[18], 1), 0, 1)
    return {"mel_input": mel_input, "conv1_weight": conv1_weight, "conv1_bias": conv1_bias, "conv2_weight": conv2_weight, "conv2_bias": conv2_bias, "norm1_gain": norm1_gain, "norm1_bias": norm1_bias, "qkv_weight": qkv_weight, "qkv_bias": qkv_bias, "out_weight": out_weight, "out_bias": out_bias, "norm2_gain": norm2_gain, "norm2_bias": norm2_bias, "up_weight": up_weight, "up_bias": up_bias, "down_weight": down_weight, "down_bias": down_bias, "cotangent": cotangent, "speech_mask": speech_mask}


@jax.custom_vjp
def low(v):
    return lax.optimization_barrier(v.astype(jnp.bfloat16)).astype(jnp.float32)

@jax.custom_vjp
def low_back(v):
    return v

def low_keep(v):
    return (low(v), None)

def low_pass(kept, grad):
    return (grad,)

def back_keep(v):
    return (v, None)

def back_low(kept, grad):
    return (low(grad),)
low.defvjp(low_keep, low_pass)
low_back.defvjp(back_keep, back_low)

def gelu_exact(values):
    return jax.nn.gelu(values, approximate=False)

def hi_dot(left_side, right_side):
    return jnp.dot(left_side, right_side, precision=lax.Precision.HIGHEST)

def layer_norm(values, scale_row, shift_row):
    center = values - lax.optimization_barrier(jnp.mean(values, axis=-1, keepdims=True))
    spread = lax.optimization_barrier(jnp.mean(center * center, axis=-1, keepdims=True))
    return center * lax.rsqrt(spread + 1e-05) * scale_row + shift_row

def sinusoids(frames, channels):
    half_width = channels // 2
    increment = math.log(10000.0) / (half_width - 1)
    inverse = jnp.exp(-increment * jnp.arange(half_width, dtype=jnp.float32))
    angles = jnp.arange(frames, dtype=jnp.float32)[:, None] * inverse[None, :]
    return jnp.concatenate([jnp.sin(angles), jnp.cos(angles)], axis=1)

def forward(mel_values, params):
    conv1_weight, conv1_bias, conv2_weight, conv2_bias, norm1_gain, norm1_bias, qkv_weight, qkv_bias, out_weight, out_bias, norm2_gain, norm2_bias, up_weight, up_bias, down_weight, down_bias = params
    frames = mel_values.shape[1] // 2
    head_size = D // HEADS
    padded = jnp.pad(mel_values, ((0, 0), (1, 1)))
    first_pre = conv1_bias
    for offset in range(3):
        first_pre = first_pre + jnp.einsum('ct,cd->td', padded[:, offset:offset + 2 * frames], conv1_weight[offset], precision=lax.Precision.HIGHEST)
    hidden = low(gelu_exact(low_back(first_pre)))
    shifted = jnp.pad(hidden, ((1, 0), (0, 0)))
    second_pre = conv2_bias
    for offset in range(3):
        second_pre = second_pre + hi_dot(shifted[offset:offset + 2 * frames:2], conv2_weight[offset])
    stream = gelu_exact(low_back(second_pre)) + sinusoids(frames, D)
    normed = low(layer_norm(stream, norm1_gain, norm1_bias))
    queries = low_back(low(hi_dot(normed, qkv_weight[0]) + qkv_bias[0]))
    key_rows = low_back(low(hi_dot(normed, qkv_weight[1])))
    value_rows = low_back(low(hi_dot(normed, qkv_weight[2]) + qkv_bias[1]))
    query_heads = queries.reshape(frames, HEADS, head_size)
    key_heads = key_rows.reshape(frames, HEADS, head_size)
    value_heads = value_rows.reshape(frames, HEADS, head_size)
    scores = jnp.einsum('qhe,khe->hqk', query_heads, key_heads, precision=lax.Precision.HIGHEST) * head_size ** (-0.5)
    scores = low_back(scores)
    probs = jax.nn.softmax(scores, axis=-1)
    mixture = jnp.einsum('hqk,khe->qhe', low(probs), value_heads, precision=lax.Precision.HIGHEST).reshape(frames, D)
    mixture = low_back(low(mixture))
    stream_mid = stream + low_back(hi_dot(mixture, out_weight) + out_bias)
    normed_two = low(layer_norm(stream_mid, norm2_gain, norm2_bias))
    inner_pre = low_back(hi_dot(normed_two, up_weight) + up_bias)
    active = low(gelu_exact(inner_pre))
    return stream_mid + low_back(hi_dot(active, down_weight) + down_bias)

def reference(mel_input, conv1_weight, conv1_bias, conv2_weight, conv2_bias, norm1_gain, norm1_bias, qkv_weight, qkv_bias, out_weight, out_bias, norm2_gain, norm2_bias, up_weight, up_bias, down_weight, down_bias, cotangent, speech_mask):
    params = tuple((weight.astype(jnp.float32) for weight in (conv1_weight, conv1_bias, conv2_weight, conv2_bias, norm1_gain, norm1_bias, qkv_weight, qkv_bias, out_weight, out_bias, norm2_gain, norm2_bias, up_weight, up_bias, down_weight, down_bias)))

    def per_clip(totals, inputs):
        mel_clip, cot_clip, mask_clip = inputs
        output, pullback = jax.vjp(forward, mel_clip.astype(jnp.float32), params)
        upstream = cot_clip.astype(jnp.float32) * mask_clip.astype(jnp.float32)[:, None]
        mel_part, param_grads = pullback(upstream)
        totals = tuple((total + piece for total, piece in zip(totals, param_grads)))
        return (totals, (output.astype(jnp.bfloat16), mel_part))
    zero_sums = tuple((jnp.zeros_like(weight) for weight in params))
    totals, (encoded, mel_grad) = lax.scan(per_clip, zero_sums, (mel_input, cotangent, speech_mask))
    return (encoded, mel_grad, totals[0], totals[1], totals[2], totals[3], totals[4], totals[5], totals[6], totals[7], totals[8], totals[9], totals[10], totals[11], totals[12], totals[13], totals[14], totals[15])
```

```python
import functools
import math

import jax
import jax.numpy as jnp
from jax import lax
from jax.experimental import pallas as pl
from jax.experimental.pallas import tpu as pltpu
from jax.sharding import PartitionSpec as P

HEAD = 64
BF = jnp.bfloat16
F32 = jnp.float32
MESH = pl.DeviceIdType.MESH
VMEM_LIMIT = 60 * 1024 * 1024
C1B, C2B, N1G, N1B, OUB, N2G, N2B, DNB, QB, VB, UPB = range(11)


class Box:
    pass


def dot(a, b, ca, cb):
    return lax.dot_general(a, b, (((ca,), (cb,)), ((), ())), preferred_element_type=F32)


def nn(a, b):
    return dot(a, b, 1, 0)


def nt(a, b):
    return dot(a, b, 1, 1)


def tn(a, b):
    return dot(a, b, 0, 0)


def rows_loop(total, step, body, unroll=1):
    step = min(step, total)

    def one(i, carry):
        body(pl.ds(pl.multiple_of(i * step, step), step))
        return carry

    lax.fori_loop(0, total // step, one, 0, unroll=unroll)


def gelu_parts(v):
    t = 1.0 / (1.0 + (0.3275911 / math.sqrt(2.0)) * jnp.abs(v))
    e = jnp.exp(-0.5 * v * v)
    poly = 1.061405429 * t - 1.453152027
    poly = poly * t + 1.421413741
    poly = poly * t - 0.284496736
    poly = poly * t + 0.254829592
    tail = (0.5 * t) * poly * e
    return jnp.where(v >= 0, 1.0 - tail, tail), e * (1.0 / math.sqrt(2.0 * math.pi))


def gelu_both(v):
    cdf, pdf = gelu_parts(v)
    return v * cdf, cdf + v * pdf


def normal(x):
    center = x - jnp.mean(x, axis=-1, keepdims=True)
    spread = jnp.mean(center * center, axis=-1, keepdims=True)
    inv = lax.rsqrt(spread + 1e-05)
    return center * inv, inv


def normal_pull(gy, hat, inv):
    return inv * (
        gy
        - jnp.mean(gy, axis=-1, keepdims=True)
        - hat * jnp.mean(gy * hat, axis=-1, keepdims=True)
    )


def vec(r, i):
    return r.vecs[i : i + 1, :]


def add_small(r, i, value):
    r.small[i : i + 1, :] += value


def col(value):
    return jnp.sum(value, axis=0, keepdims=True)


def stage_stem(r):
    T, D = r.stream.shape
    c = lax.axis_index("seq")
    m = lax.axis_index("mp")
    w1 = r.w1[...]
    first = jnp.logical_and(c == 0, m == 0)
    edge = nn(r.xh[...], w1) + vec(r, C1B)
    edge = gelu_both(edge)[0] * jnp.where(first, 0.0, 1.0)
    r.odd[0:8, :] = edge[0:8, :]
    r.tmp[...] = nn(r.xe[...], w1)

    def even(rows):
        value, slope = gelu_both(r.tmp[rows, :] + vec(r, C1B))
        r.he[rows, :] = value.astype(BF)
        r.dge[rows, :] = slope

    rows_loop(T, 32, even)
    r.tmp[...] = nn(r.xo[...], w1)

    def odd(rows):
        value, slope = gelu_both(r.tmp[rows, :] + vec(r, C1B))
        r.ho[rows, :] = value.astype(BF)
        r.odd[pl.ds(pl.multiple_of(rows.start + 8, 8), rows.size), :] = value
        r.dgo[rows, :] = slope

    rows_loop(T, 32, odd)
    r.hp[...] = r.odd[7 : 7 + T, :].astype(BF)
    r.tmp[...] = nn(r.hp[...], r.w2[0]) + nn(r.he[...], r.w2[1]) + nn(r.ho[...], r.w2[2])

    def second(rows):
        value, slope = gelu_both(r.tmp[rows, :] + vec(r, C2B))
        stream = value + r.pos[rows, :]
        r.dg2[rows, :] = slope
        r.stream[rows, :] = stream
        r.normed[rows, :] = (normal(stream)[0] * vec(r, N1G) + vec(r, N1B)).astype(BF)

    rows_loop(T, 32, second)


def stage_qkv(r):
    T, D = r.stream.shape
    half = D // 2
    normed = r.normed[...]
    for part, bias, scale in ((1, None, 1.0), (2, VB, 1.0), (0, QB, HEAD**-0.5)):
        for m in range(2):
            value = nn(normed, r.wqkv[m, part])
            if bias is not None:
                value = value + r.vecs[bias : bias + 1, m * half : (m + 1) * half]
            value = (value.astype(BF).astype(F32) * scale).T.astype(BF)
            if part == 0:
                r.qt[m * half : (m + 1) * half, :] = value
            else:
                r.kv[part - 1, m * half : (m + 1) * half, :] = value


def head_rows(h):
    return pl.ds(pl.multiple_of(h * HEAD, HEAD), HEAD)


def attend_block(r, kv, first):
    D, T = r.qt.shape

    def one(h, carry):
        rows = head_rows(h)
        s = tn(kv[0, rows, :], r.qt[rows, :])
        top = jnp.max(s, axis=0, keepdims=True)
        if not first:
            top = jnp.maximum(top, r.top[h])
        p = jnp.exp(s - top)
        total = jnp.sum(p, axis=0, keepdims=True)
        mixed = nn(kv[1, rows, :], p.astype(BF))
        if not first:
            keep = jnp.exp(r.top[h] - top)
            total = total + keep * r.total[h]
            mixed = mixed + keep * r.mixt[rows, :]
        r.top[h] = top
        r.total[h] = total
        r.mixt[rows, :] = mixed
        return carry

    lax.fori_loop(0, D // HEAD, one, 0)


def attend_end(r):
    D, T = r.qt.shape

    def one(h, carry):
        rows = head_rows(h)
        total = r.total[h]
        value = r.mixt[rows, :] * (1.0 / total)
        r.mixt[rows, :] = value
        r.mixb[rows, :] = value.astype(BF)
        r.top[h] = r.top[h] + jnp.log(total)
        return carry

    lax.fori_loop(0, D // HEAD, one, 0)


def stage_mid(r):
    T, D = r.stream.shape
    r.tmp[...] = tn(r.mixb[...], r.wo[...])

    def one(rows):
        mid = r.stream[rows, :] + r.tmp[rows, :] + vec(r, OUB)
        r.mid[rows, :] = mid
        r.ntwo[rows, :] = (normal(mid)[0] * vec(r, N2G) + vec(r, N2B)).astype(BF)

    rows_loop(T, 32, one)


def stage_ff(r):
    T, D = r.stream.shape
    parts = r.up.shape[0]
    width = r.up.shape[2]
    add_small(r, DNB, col(r.bg[...].astype(F32)))

    def chunk(j, carry):
        r.tmp[...] = nn(r.ntwo[...], r.up[j])
        r.tmp2[...] = nt(r.bg[...], r.down[j])
        bias = r.vecs[pl.ds(UPB + j, 1), :]

        def one(i, acc):
            rows = pl.ds(pl.multiple_of(i * 32, 32), 32)
            value, slope = gelu_both(r.tmp[rows, :] + bias)
            r.act[rows, :] = value.astype(BF)
            grad = (r.tmp2[rows, :] * slope).astype(BF)
            r.ing[rows, :] = grad
            return acc + col(grad.astype(F32))

        r.small[pl.ds(UPB + j, 1), :] = lax.fori_loop(0, T // 32, one, jnp.zeros((1, width), F32))
        act = r.act[...]
        ing = r.ing[...]
        out = nn(act, r.down[j])
        back = nt(ing, r.up[j])

        @pl.when(j == 0)
        def _():
            r.ffo[...] = out
            r.ntg[...] = back

        @pl.when(j > 0)
        def _():
            r.ffo[...] += out
            r.ntg[...] += back

        r.gdown[j] = tn(act, r.bg[...]).astype(BF)
        r.gup[j] = tn(r.ntwo[...], ing).astype(BF)
        return carry

    lax.fori_loop(0, parts, chunk, 0)


def stage_mid_pull(r):
    T, D = r.stream.shape

    def one(i, accs):
        rows = pl.ds(pl.multiple_of(i * 32, 32), 32)
        mid = r.mid[rows, :]
        r.enc[rows, :] = (mid + r.ffo[rows, :] + vec(r, DNB)).astype(BF)
        hat, inv = normal(mid)
        grad = r.ntg[rows, :]
        smg = r.bg[rows, :].astype(F32) + normal_pull(grad * vec(r, N2G), hat, inv)
        r.smg[rows, :] = smg
        attg = smg.astype(BF)
        r.attg[rows, :] = attg
        return accs[0] + col(grad * hat), accs[1] + col(grad), accs[2] + col(attg.astype(F32))

    zero = jnp.zeros((1, D), F32)
    gain, bias, out_bias = lax.fori_loop(0, T // 32, one, (zero, zero, zero))
    add_small(r, N2G, gain)
    add_small(r, N2B, bias)
    add_small(r, OUB, out_bias)
    attg = r.attg[...]
    r.dot[...] = nt(r.wo[...], attg).astype(BF)
    r.gout[...] = nn(r.mixb[...], attg).astype(BF)

    def head(h, carry):
        rows = head_rows(h)
        r.diag[h] = jnp.sum(r.dot[rows, :].astype(F32) * r.mixt[rows, :], axis=0, keepdims=True)
        return carry

    lax.fori_loop(0, D // HEAD, head, 0)


def pull_block(r, kv, dkv, first):
    D, T = r.qt.shape

    def one(h, carry):
        rows = head_rows(h)
        k, v, q, do = kv[0, rows, :], kv[1, rows, :], r.qt[rows, :], r.dot[rows, :]
        p = jnp.exp(tn(k, q) - r.top[h])
        ds = (p * (tn(v, do) - r.diag[h])).astype(BF)
        dkv[1, rows, :] = nt(do, p.astype(BF)).astype(dkv.dtype)
        dkv[0, rows, :] = nt(q, ds).astype(dkv.dtype)
        dq = nn(k, ds)
        if first:
            r.dqt[rows, :] = dq
        else:
            r.dqt[rows, :] += dq
        return carry

    lax.fori_loop(0, D // HEAD, one, 0)


def stage_qkv_pull(r):
    T, D = r.stream.shape
    half = D // 2
    normedt = r.normed[...].astype(F32).T.astype(BF)
    ones = jnp.ones((8, T), BF)
    total = None
    for part, ref in enumerate((r.dqb, r.dkb, r.dvb)):
        if part != 1:
            add_small(r, QB if part == 0 else VB, nt(ones, ref[...])[0:1, :])
        for m in range(2):
            piece = ref[m * half : (m + 1) * half, :]
            grad = nt(normedt, piece).astype(BF)
            r.gqkv[m, part, :, 0:half] = grad[0:half, :]
            r.gqkv[m, part, :, half : 2 * half] = grad[half : 2 * half, :]
            back = nn(r.wqkv[m, part], piece)
            total = back if total is None else total + back
    r.tmp[...] = total.T

    def one(i, accs):
        rows = pl.ds(pl.multiple_of(i * 32, 32), 32)
        hat, inv = normal(r.stream[rows, :])
        grad = r.tmp[rows, :]
        back = r.smg[rows, :] + normal_pull(grad * vec(r, N1G), hat, inv)
        sg = (back * r.dg2[rows, :]).astype(BF)
        r.sg[rows, :] = sg
        return accs[0] + col(grad * hat), accs[1] + col(grad), accs[2] + col(sg.astype(F32))

    zero = jnp.zeros((1, D), F32)
    gain, bias, c2b = lax.fori_loop(0, T // 32, one, (zero, zero, zero))
    add_small(r, N1G, gain)
    add_small(r, N1B, bias)
    add_small(r, C2B, c2b)


def stage_conv2_pull(r, next_row):
    T, D = r.stream.shape
    sg = r.sg[...]
    r.shift[0:T, :] = nt(sg, r.w2[0])
    r.shift[T : T + 16, :] = nt(next_row, r.w2[0])
    r.tmp[...] = nt(sg, r.w2[1])
    r.tmp2[...] = nt(sg, r.w2[2]) + r.shift[1 : T + 1, :]

    def one(i, acc):
        rows = pl.ds(pl.multiple_of(i * 32, 32), 32)
        even = (r.tmp[rows, :] * r.dge[rows, :]).astype(BF)
        odd = (r.tmp2[rows, :] * r.dgo[rows, :]).astype(BF)
        r.fe[rows, :] = even
        r.fo[rows, :] = odd
        return acc + col(even.astype(F32)) + col(odd.astype(F32))

    add_small(r, C1B, lax.fori_loop(0, T // 32, one, jnp.zeros((1, D), F32)))


def stage_conv_weights(r):
    sg = r.sg[...]
    r.gc2[0] = tn(r.hp[...], sg).astype(BF)
    r.gc2[1] = tn(r.he[...], sg).astype(BF)
    r.gc2[2] = tn(r.ho[...], sg).astype(BF)
    r.gc1[...] = (tn(r.xe[...], r.fe[...]) + tn(r.xo[...], r.fo[...])).astype(BF)


def stage_mel(r, next_row, prev_row):
    T, D = r.stream.shape
    fe, fo = r.fe[...], r.fo[...]
    r.wide[16 : 16 + T, :] = nt(fo, r.w1p[2])
    r.wide[0:16, :] = nt(prev_row, r.w1p[2])
    r.melg[:, 0:128] = nt(fe, r.w1p[1]) + nt(fo, r.w1p[0]) + r.wide[15 : 15 + T, :]
    r.wide[0:T, :] = nt(fe, r.w1p[0])
    r.wide[T : T + 16, :] = nt(next_row, r.w1p[0])
    r.melg[:, 128:256] = nt(fe, r.w1p[2]) + nt(fo, r.w1p[1]) + r.wide[1 : 1 + T, :]


def call(name, body, ins, outs, scratch, sems=(), **params):
    names_in, names_out, names_scr = list(ins), list(outs), list(scratch)

    def kernel(*refs):
        r = Box()
        names = names_in + names_out + names_scr + [n for n, _ in sems]
        for n, ref in zip(names, refs):
            setattr(r, n, ref)
        body(r)

    got = pl.pallas_call(
        kernel,
        name=name,
        out_shape=[jax.ShapeDtypeStruct(*outs[n]) for n in names_out],
        in_specs=[pl.BlockSpec(memory_space=pltpu.VMEM)] * len(ins),
        out_specs=[pl.BlockSpec(memory_space=pltpu.VMEM)] * len(outs),
        scratch_shapes=[pltpu.VMEM(*scratch[n]) for n in names_scr] + [s for _, s in sems],
        compiler_params=pltpu.CompilerParams(vmem_limit_bytes=VMEM_LIMIT, **params),
    )(*[ins[n] for n in names_in])
    return dict(zip(names_out, got))


def kernel_stem(r):
    stage_stem(r)
    stage_qkv(r)


def kernel_mid(r):
    r.small[...] = jnp.zeros_like(r.small)
    for b in range(4):
        attend_block(r, r.kvs.at[b], b == 0)
    attend_end(r)
    stage_mid(r)
    stage_ff(r)
    stage_mid_pull(r)
    for b in range(4):
        pull_block(r, r.kvs.at[b], r.dkvs.at[b], b == 0)
    r.dqb[...] = (r.dqt[...] * HEAD**-0.5).astype(BF)


def partners():
    c, m, d = lax.axis_index("seq"), lax.axis_index("mp"), lax.axis_index("dp")
    return (d, 1 - c, m), (d, c, 1 - m)


def rim_copies(r, source, slots, start):
    copies = []
    for i, target in enumerate(partners()):
        copies.append(
            pltpu.make_async_remote_copy(
                src_ref=source,
                dst_ref=slots.at[i],
                send_sem=r.send.at[start + i],
                recv_sem=r.recv.at[start + i],
                device_id=target,
                device_id_type=MESH,
            )
        )
    return copies


def quarter():
    c, m = lax.axis_index("seq"), lax.axis_index("mp")
    return 2 * c + jnp.bitwise_xor(c, m)


def pick_next(slots):
    q = quarter()
    by_y = jnp.where(q % 2 == 0, 1.0, 0.0)
    by_core = jnp.where(q == 1, 1.0, 0.0)
    return (slots[0].astype(F32) * by_core + slots[1].astype(F32) * by_y).astype(BF)


def pick_prev(slots):
    q = quarter()
    by_y = jnp.where(q % 2 == 1, 1.0, 0.0)
    by_core = jnp.where(q == 2, 1.0, 0.0)
    return (slots[0].astype(F32) * by_core + slots[1].astype(F32) * by_y).astype(BF)


def kernel_back(r):
    T, D = r.stream.shape
    barrier = pltpu.get_barrier_semaphore()
    for target in partners():
        pl.semaphore_signal(barrier, inc=1, device_id=target, device_id_type=MESH)
    pl.semaphore_wait(barrier, 2)
    r.small[...] = jnp.zeros_like(r.small)
    stage_qkv_pull(r)
    first = rim_copies(r, r.sg.at[0:16], r.slots.at[0], 0)
    for copy in first:
        copy.start()
    for copy in first:
        copy.wait()
    stage_conv2_pull(r, pick_next(r.slots.at[0]))
    second = rim_copies(r, r.fe.at[0:16], r.slots.at[1], 2)
    second += rim_copies(r, r.fo.at[T - 16 : T], r.slots.at[2], 4)
    for copy in second:
        copy.start()
    stage_conv_weights(r)
    for copy in second:
        copy.wait()
    stage_mel(r, pick_next(r.slots.at[1]), pick_prev(r.slots.at[2]))


def sinusoids(positions, channels):
    half_width = channels // 2
    increment = math.log(10000.0) / (half_width - 1)
    inverse = jnp.exp(-increment * jnp.arange(half_width, dtype=F32))
    angles = positions.astype(F32)[:, None] * inverse[None, :]
    return jnp.concatenate([jnp.sin(angles), jnp.cos(angles)], axis=1)


def on_device(
    mel_input,
    conv1_weight,
    conv1_bias,
    conv2_weight,
    conv2_bias,
    norm1_gain,
    norm1_bias,
    qkv_weight,
    qkv_bias,
    out_weight,
    out_bias,
    norm2_gain,
    norm2_bias,
    up_weight,
    up_bias,
    down_weight,
    down_bias,
    cotangent,
    speech_mask,
):
    mel = mel_input[0]
    mels, span = mel.shape
    T, D = cotangent.shape[1] // 2, cotangent.shape[2]
    F = 2 * up_weight.shape[1]
    NF = F // D
    H = D // HEAD
    half = D // 2
    c, m = lax.axis_index("seq"), lax.axis_index("mp")
    sub = jnp.bitwise_xor(c, m)

    low = lax.ppermute(mel[:, -2:], "seq", [(0, 1)])
    high = lax.ppermute(mel[:, :2], "seq", [(1, 0)])
    window = lax.dynamic_slice_in_dim(
        jnp.concatenate([low, mel, high], axis=1), sub * 2 * T, 2 * T + 4, axis=1
    )
    pairs = window.T.reshape(T + 2, 2 * mels)
    xe = jnp.concatenate([pairs[0:T, mels:], pairs[1 : T + 1]], axis=1)
    xo = jnp.concatenate([pairs[1 : T + 1], pairs[2 : T + 2, :mels]], axis=1)
    xh = jnp.concatenate([pairs[0:1], pairs[1:2, :mels]], axis=1)
    lanes = -(-3 * mels // 128) * 128
    xe = jnp.pad(xe, ((0, 0), (0, lanes - 3 * mels)))
    xo = jnp.pad(xo, ((0, 0), (0, lanes - 3 * mels)))
    xh = jnp.pad(xh, ((15, 0), (0, lanes - 3 * mels)))
    xh = jnp.roll(xh, 8, axis=0)
    w1 = jnp.pad(conv1_weight.reshape(3 * mels, D), ((0, lanes - 3 * mels), (0, 0)))
    w1p = jnp.pad(conv1_weight, ((0, 0), (0, 128 - mels), (0, 0)))
    pos = sinusoids((c * 2 + sub) * T + jnp.arange(T, dtype=jnp.int32), D)

    wqkv = lax.all_gather(qkv_weight, "mp", axis=0)
    wo = lax.all_gather(out_weight, "mp", axis=0, tiled=True)
    up = lax.all_gather(
        up_weight.reshape(D, NF // 2, D).transpose(1, 0, 2), "mp", axis=0, tiled=True
    )
    down = lax.all_gather(down_weight.reshape(NF // 2, D, D), "mp", axis=0, tiled=True)
    qb = lax.all_gather(qkv_bias, "mp", axis=1, tiled=True)
    ub = lax.all_gather(up_bias, "mp", axis=0, tiled=True).reshape(NF, D)
    table = [conv1_bias, conv2_bias, norm1_gain, norm1_bias, out_bias, norm2_gain, norm2_bias]
    table = jnp.stack(table + [down_bias, qb[0], qb[1]])
    vecs = jnp.concatenate([table, ub], axis=0).astype(F32)
    vecs = jnp.pad(vecs, ((0, 16 - vecs.shape[0]), (0, 0)))

    cot = lax.dynamic_slice_in_dim(cotangent[0], sub * T, T, axis=0)
    mask = lax.dynamic_slice_in_dim(speech_mask[0], sub * T, T, axis=0)
    bg = cot * mask.astype(BF)[:, None]

    td, dt = (T, D), (D, T)
    a = call(
        "stem",
        kernel_stem,
        dict(xe=xe, xo=xo, xh=xh, w1=w1, w2=conv2_weight, vecs=vecs, pos=pos, wqkv=wqkv),
        dict(
            he=(td, BF), ho=(td, BF), hp=(td, BF), dge=(td, F32), dgo=(td, F32), dg2=(td, F32),
            stream=(td, F32), normed=(td, BF), qt=(dt, BF), kv=((2, D, T), BF),
        ),
        dict(tmp=(td, F32), odd=((T + 8, D), F32)),
    )
    kvs = lax.all_gather(a["kv"], ("seq", "mp"), axis=0)
    b = call(
        "middle",
        kernel_mid,
        dict(kvs=kvs, qt=a["qt"], stream=a["stream"], wo=wo, up=up, down=down, bg=bg, vecs=vecs),
        dict(
            enc=(td, BF), gdown=((NF, D, D), BF), gup=((NF, D, D), BF), gout=((D, D), BF),
            small=((16, D), F32), smg=(td, F32), dqb=(dt, BF), dkvs=((4, 2, D, T), BF),
        ),
        dict(
            tmp=(td, F32), tmp2=(td, F32), top=((H, 1, T), F32), total=((H, 1, T), F32),
            mixt=(dt, F32), mixb=(dt, BF), mid=(td, F32), ntwo=(td, BF), act=(td, BF),
            ing=(td, BF), ffo=(td, F32), ntg=(td, F32), attg=(td, BF), dot=(dt, BF),
            diag=((H, 1, T), F32), dqt=(dt, F32),
        ),
    )
    dkv = lax.psum_scatter(b["dkvs"], ("seq", "mp"), scatter_dimension=0, tiled=True)[0]
    e = call(
        "back",
        kernel_back,
        dict(
            dqb=b["dqb"], dkb=dkv[0], dvb=dkv[1], smg=b["smg"], vecs=vecs, wqkv=wqkv, w2=conv2_weight,
            w1p=w1p, xe=xe, xo=xo, he=a["he"], ho=a["ho"], hp=a["hp"], dge=a["dge"], dgo=a["dgo"],
            dg2=a["dg2"], stream=a["stream"], normed=a["normed"],
        ),
        dict(
            gqkv=((2, 3, half, D), BF), gc2=((3, D, D), BF), gc1=((lanes, D), BF),
            small=((16, D), F32), melg=((T, 256), F32),
        ),
        dict(
            tmp=(td, F32), tmp2=(td, F32), sg=(td, BF), fe=(td, BF), fo=(td, BF),
            shift=((T + 16, D), F32), wide=((T + 16, 128), F32), slots=((3, 2, 16, D), BF),
        ),
        (("send", pltpu.SemaphoreType.DMA((6,))), ("recv", pltpu.SemaphoreType.DMA((6,)))),
        collective_id=1,
        has_side_effects=True,
    )

    packed = jnp.concatenate(
        [
            b["gdown"].reshape(2, -1, D),
            b["gup"].reshape(2, -1, D),
            b["gout"].reshape(2, -1, D),
            e["gqkv"].reshape(2, -1, D),
        ],
        axis=1,
    )
    mine = lax.psum_scatter(packed, "mp", scatter_dimension=0, tiled=True)[0]
    mine = lax.psum(mine, ("dp", "seq")).astype(F32)
    conv = jnp.concatenate([e["gc2"].reshape(-1, D), e["gc1"]], axis=0)
    conv = lax.psum(conv, ("dp", "seq", "mp")).astype(F32)
    small = lax.psum(b["small"] + e["small"], ("dp", "seq", "mp"))
    cut = [F // 2, F, F + half, F + half + 3 * half]
    grad_down = mine[: cut[0]]
    grad_up = mine[cut[0] : cut[1]].reshape(NF // 2, D, D).transpose(1, 0, 2).reshape(D, F // 2)
    grad_out = mine[cut[1] : cut[2]]
    grad_qkv = mine[cut[2] : cut[3]].reshape(3, half, 2, half).transpose(0, 2, 1, 3).reshape(3, D, half)
    grad_conv2 = conv[: 3 * D].reshape(3, D, D)
    grad_conv1 = conv[3 * D : 3 * D + 3 * mels].reshape(3, mels, D)
    own_half = lax.dynamic_slice_in_dim(small[QB : QB + 2], m * half, half, axis=1)
    own_up = lax.dynamic_slice_in_dim(
        small[UPB : UPB + NF], m * (NF // 2), NF // 2, axis=0
    ).reshape(-1)

    def ordered(value):
        both = lax.all_gather(value, "mp", axis=0)
        both = jnp.where(c == 0, both, both[::-1])
        return both.reshape((-1,) + value.shape[1:])

    encoded = ordered(b["enc"])[None]
    melg = ordered(e["melg"]).reshape(4 * T, 128)[:, :mels].T[None]
    return (
        encoded,
        melg,
        grad_conv1,
        small[C1B],
        grad_conv2,
        small[C2B],
        small[N1G],
        small[N1B],
        grad_qkv,
        own_half,
        grad_out,
        small[OUB],
        small[N2G],
        small[N2B],
        grad_up,
        own_up,
        grad_down,
        small[DNB],
    )


def solution(mesh):
    placed = (
        P("dp", None, "seq"),
        P(),
        P(),
        P(),
        P(),
        P(),
        P(),
        P(None, None, "mp"),
        P(None, "mp"),
        P("mp", None),
        P(),
        P(),
        P(),
        P(None, "mp"),
        P("mp"),
        P("mp", None),
        P(),
        P("dp", "seq", None),
        P("dp", "seq"),
    )
    return jax.shard_map(
        on_device,
        mesh=mesh,
        in_specs=placed,
        out_specs=(
            P("dp", "seq", None),
            P("dp", None, "seq"),
            P(),
            P(),
            P(),
            P(),
            P(),
            P(),
            P(None, None, "mp"),
            P(None, "mp"),
            P("mp", None),
            P(),
            P(),
            P(),
            P(None, "mp"),
            P("mp"),
            P("mp", None),
            P(),
        ),
        check_vma=False,
    )
```

```python
import functools
import math

import jax
import jax.numpy as jnp
from jax import lax
from jax.experimental import pallas as pl
from jax.experimental.pallas import tpu as pltpu
from jax.sharding import PartitionSpec as P

HEAD = 64
BF = jnp.bfloat16
F32 = jnp.float32
MESH = pl.DeviceIdType.MESH
VMEM_LIMIT = 60 * 1024 * 1024
C1B, C2B, N1G, N1B, OUB, N2G, N2B, DNB, QB, VB, UPB = range(11)


class Box:
    pass


def dot(a, b, ca, cb):
    return lax.dot_general(a, b, (((ca,), (cb,)), ((), ())), preferred_element_type=F32)


def nn(a, b):
    return dot(a, b, 1, 0)


def nt(a, b):
    return dot(a, b, 1, 1)


def tn(a, b):
    return dot(a, b, 0, 0)


def rows_loop(total, step, body, unroll=1):
    step = min(step, total)

    def one(i, carry):
        body(pl.ds(pl.multiple_of(i * step, step), step))
        return carry

    lax.fori_loop(0, total // step, one, 0, unroll=unroll)


def gelu_parts(v):
    t = 1.0 / (1.0 + (0.3275911 / math.sqrt(2.0)) * jnp.abs(v))
    e = jnp.exp(-0.5 * v * v)
    poly = 1.061405429 * t - 1.453152027
    poly = poly * t + 1.421413741
    poly = poly * t - 0.284496736
    poly = poly * t + 0.254829592
    tail = (0.5 * t) * poly * e
    return jnp.where(v >= 0, 1.0 - tail, tail), e * (1.0 / math.sqrt(2.0 * math.pi))


def gelu_both(v):
    cdf, pdf = gelu_parts(v)
    return v * cdf, cdf + v * pdf


def normal(x):
    center = x - jnp.mean(x, axis=-1, keepdims=True)
    spread = jnp.mean(center * center, axis=-1, keepdims=True)
    inv = lax.rsqrt(spread + 1e-05)
    return center * inv, inv


def normal_pull(gy, hat, inv):
    return inv * (
        gy
        - jnp.mean(gy, axis=-1, keepdims=True)
        - hat * jnp.mean(gy * hat, axis=-1, keepdims=True)
    )


def vec(r, i):
    return r.vecs[i : i + 1, :]


def add_small(r, i, value):
    r.small[i : i + 1, :] += value


def col(value):
    return jnp.sum(value, axis=0, keepdims=True)


def stage_stem(r):
    T, D = r.stream.shape
    c = lax.axis_index("seq")
    m = lax.axis_index("mp")
    w1 = r.w1[...]
    first = jnp.logical_and(c == 0, m == 0)
    edge = nn(r.xh[...], w1) + vec(r, C1B)
    edge = gelu_both(edge)[0] * jnp.where(first, 0.0, 1.0)
    r.odd[0:8, :] = edge[0:8, :]
    r.tmp[...] = nn(r.xe[...], w1)

    def even(rows):
        value, slope = gelu_both(r.tmp[rows, :] + vec(r, C1B))
        r.he[rows, :] = value.astype(BF)
        r.dge[rows, :] = slope

    rows_loop(T, 32, even)
    r.tmp[...] = nn(r.xo[...], w1)

    def odd(rows):
        value, slope = gelu_both(r.tmp[rows, :] + vec(r, C1B))
        r.ho[rows, :] = value.astype(BF)
        r.odd[pl.ds(pl.multiple_of(rows.start + 8, 8), rows.size), :] = value
        r.dgo[rows, :] = slope

    rows_loop(T, 32, odd)
    r.hp[...] = r.odd[7 : 7 + T, :].astype(BF)
    r.tmp[...] = nn(r.hp[...], r.w2[0]) + nn(r.he[...], r.w2[1]) + nn(r.ho[...], r.w2[2])

    def second(rows):
        value, slope = gelu_both(r.tmp[rows, :] + vec(r, C2B))
        stream = value + r.stream[rows, :]
        r.dg2[rows, :] = slope
        r.stream[rows, :] = stream
        r.normed[rows, :] = (normal(stream)[0] * vec(r, N1G) + vec(r, N1B)).astype(BF)

    rows_loop(T, 32, second)


def stage_qkv(r, parts):
    T, D = r.stream.shape
    half = D // 2
    normed = r.normed[...]
    for part in parts:
        bias, scale = ((QB, HEAD**-0.5), (None, 1.0), (VB, 1.0))[part]
        for m in range(2):
            value = nn(normed, r.wqkv[m, part])
            if bias is not None:
                value = value + r.vecs[bias : bias + 1, m * half : (m + 1) * half]
            value = (value.astype(BF).astype(F32) * scale).T.astype(BF)
            if part == 0:
                r.qt[m * half : (m + 1) * half, :] = value
            else:
                at = (part - 1) * D + m * half
                r.kv[at : at + half, :] = value


def head_rows(h):
    return pl.ds(pl.multiple_of(h * HEAD, HEAD), HEAD)


def block_rows(r, slot, part, h):
    D = r.qt.shape[0]
    return pl.ds(pl.multiple_of((2 * slot + part) * D + h * HEAD, HEAD), HEAD)


def attend_block(r, slot):
    D, T = r.qt.shape
    first = slot == 0

    def one(h, carry):
        rows = head_rows(h)
        s = tn(r.kv[block_rows(r, slot, 0, h), :], r.qt[rows, :])
        top = jnp.max(s, axis=0, keepdims=True)
        if not first:
            top = jnp.maximum(top, r.top[h])
        p = jnp.exp(s - top)
        total = jnp.sum(p, axis=0, keepdims=True)
        mixed = nn(r.kv[block_rows(r, slot, 1, h), :], p.astype(BF))
        if not first:
            keep = jnp.exp(r.top[h] - top)
            total = total + keep * r.total[h]
            mixed = mixed + keep * r.mixt[rows, :]
        r.top[h] = top
        r.total[h] = total
        r.mixt[rows, :] = mixed
        return carry

    lax.fori_loop(0, D // HEAD, one, 0)


def attend_end(r):
    D, T = r.qt.shape

    def one(h, carry):
        rows = head_rows(h)
        total = r.total[h]
        value = r.mixt[rows, :] * (1.0 / total)
        r.mixt[rows, :] = value
        r.mixb[rows, :] = value.astype(BF)
        r.top[h] = r.top[h] + jnp.log(total)
        return carry

    lax.fori_loop(0, D // HEAD, one, 0)


def stage_mid(r):
    T, D = r.stream.shape
    r.tmp[...] = tn(r.mixb[...], r.wo[...])

    def one(rows):
        mid = r.stream[rows, :] + r.tmp[rows, :] + vec(r, OUB)
        r.mid[rows, :] = mid
        r.ntwo[rows, :] = (normal(mid)[0] * vec(r, N2G) + vec(r, N2B)).astype(BF)

    rows_loop(T, 32, one)


def stage_ff(r):
    T, D = r.stream.shape
    side = r.up.shape[2] // D
    parts, width = 2 * side, D
    add_small(r, DNB, col(r.bg[...].astype(F32)))

    def chunk(j, carry):
        into, at = j // side, j % side
        up = r.up[into, :, pl.ds(pl.multiple_of(at * D, D), D)]
        down = r.down[pl.ds(pl.multiple_of(j * D, D), D), :]
        r.tmp[...] = nn(r.ntwo[...], up)
        r.tmp2[...] = nt(r.bg[...], down)
        bias = r.vecs[pl.ds(UPB + j, 1), :]

        def one(i, acc):
            rows = pl.ds(pl.multiple_of(i * 32, 32), 32)
            value, slope = gelu_both(r.tmp[rows, :] + bias)
            r.act[rows, :] = value.astype(BF)
            grad = (r.tmp2[rows, :] * slope).astype(BF)
            r.ing[rows, :] = grad
            return acc + col(grad.astype(F32))

        r.small[pl.ds(UPB + j, 1), :] = lax.fori_loop(0, T // 32, one, jnp.zeros((1, width), F32))
        act = r.act[...]
        ing = r.ing[...]
        out = nn(act, down)
        back = nt(ing, up)

        @pl.when(j == 0)
        def _():
            r.ffo[...] = out
            r.ntg[...] = back

        @pl.when(j > 0)
        def _():
            r.ffo[...] += out
            r.ntg[...] += back

        r.g_down[pl.ds(pl.multiple_of(j * D, D), D), :] = tn(act, r.bg[...]).astype(BF)
        base = into * (r.g_up.shape[0] // 2) + at * D
        r.g_up[pl.ds(pl.multiple_of(base, 16), D), :] = tn(r.ntwo[...], ing).astype(BF)
        return carry

    lax.fori_loop(0, parts, chunk, 0)


def stage_mid_pull(r):
    T, D = r.stream.shape

    def one(i, accs):
        rows = pl.ds(pl.multiple_of(i * 32, 32), 32)
        mid = r.mid[rows, :]
        r.enc[rows, :] = (mid + r.ffo[rows, :] + vec(r, DNB)).astype(BF)
        hat, inv = normal(mid)
        grad = r.ntg[rows, :]
        smg = r.bg[rows, :].astype(F32) + normal_pull(grad * vec(r, N2G), hat, inv)
        r.smg[rows, :] = smg
        attg = smg.astype(BF)
        r.attg[rows, :] = attg
        return accs[0] + col(grad * hat), accs[1] + col(grad), accs[2] + col(attg.astype(F32))

    zero = jnp.zeros((1, D), F32)
    gain, bias, out_bias = lax.fori_loop(0, T // 32, one, (zero, zero, zero))
    add_small(r, N2G, gain)
    add_small(r, N2B, bias)
    add_small(r, OUB, out_bias)
    attg = r.attg[...]
    r.dot[...] = nt(r.wo[...], attg).astype(BF)
    gout = nn(r.mixb[...], attg).astype(BF)
    rows, half = r.g_up.shape[0] // 2, D // 2
    r.g_up[rows - half : rows, :] = gout[0:half, :]
    r.g_up[2 * rows - half : 2 * rows, :] = gout[half:D, :]

    def head(h, carry):
        rows = head_rows(h)
        r.diag[h] = jnp.sum(r.dot[rows, :].astype(F32) * r.mixt[rows, :], axis=0, keepdims=True)
        return carry

    lax.fori_loop(0, D // HEAD, head, 0)


def pull_block(r, slot, dkv, hook):
    D, T = r.qt.shape
    first = slot == 3
    H = D // HEAD

    def one(h, carry):
        rows = head_rows(h)
        k, v = r.kv[block_rows(r, slot, 0, h), :], r.kv[block_rows(r, slot, 1, h), :]
        q, do = r.qt[rows, :], r.dot[rows, :]
        p = jnp.exp(tn(k, q) - r.top[h])
        ds = (p * (tn(v, do) - r.diag[h])).astype(BF)
        dkv[1, rows, :] = nt(do, p.astype(BF)).astype(dkv.dtype)
        dkv[0, rows, :] = nt(q, ds).astype(dkv.dtype)
        dq = nn(k, ds)
        if first:
            r.dqt[rows, :] = dq
        else:
            r.dqt[rows, :] += dq
        return carry

    for part in range(2):
        lax.fori_loop(part * H // 2, (part + 1) * H // 2, one, 0)
        hook()


def stage_qkv_weights(r):
    T, D = r.stream.shape
    half = D // 2
    normedt = r.normed[...].astype(F32).T.astype(BF)
    ones = jnp.ones((8, T), BF)
    for part, ref in enumerate((r.dqb, r.dkb, r.dvb)):
        if part != 1:
            add_small(r, QB if part == 0 else VB, nt(ones, ref[...])[0:1, :])
        for m in range(2):
            grad = nt(normedt, ref[m * half : (m + 1) * half, :]).astype(BF)
            at = (3 * m + part) * half
            r.g_qkv[at : at + half, 0:half] = grad[0:half, :]
            r.g_qkv[at : at + half, half:D] = grad[half:D, :]


def stage_qkv_pull(r):
    T, D = r.stream.shape
    half = D // 2
    total = None
    for part, ref in enumerate((r.dqb, r.dkb, r.dvb)):
        for m in range(2):
            back = nn(r.wqkv[m, part], ref[m * half : (m + 1) * half, :])
            total = back if total is None else total + back
    r.tmp[...] = total.T

    def one(i, accs):
        rows = pl.ds(pl.multiple_of(i * 32, 32), 32)
        hat, inv = normal(r.stream[rows, :])
        grad = r.tmp[rows, :]
        back = r.smg[rows, :] + normal_pull(grad * vec(r, N1G), hat, inv)
        sg = (back * r.dg2[rows, :]).astype(BF)
        r.sg[rows, :] = sg
        return accs[0] + col(grad * hat), accs[1] + col(grad), accs[2] + col(sg.astype(F32))

    zero = jnp.zeros((1, D), F32)
    gain, bias, c2b = lax.fori_loop(0, T // 32, one, (zero, zero, zero))
    add_small(r, N1G, gain)
    add_small(r, N1B, bias)
    add_small(r, C2B, c2b)


def stage_conv2_pull(r, next_row):
    T, D = r.stream.shape
    sg = r.sg[...]
    r.shift[0:T, :] = nt(sg, r.w2[0])
    r.shift[T : T + 16, :] = nt(next_row, r.w2[0])
    r.tmp[...] = nt(sg, r.w2[1])
    r.tmp2[...] = nt(sg, r.w2[2]) + r.shift[1 : T + 1, :]

    def one(i, acc):
        rows = pl.ds(pl.multiple_of(i * 32, 32), 32)
        even = (r.tmp[rows, :] * r.dge[rows, :]).astype(BF)
        odd = (r.tmp2[rows, :] * r.dgo[rows, :]).astype(BF)
        r.fe[rows, :] = even
        r.fo[rows, :] = odd
        return acc + col(even.astype(F32)) + col(odd.astype(F32))

    add_small(r, C1B, lax.fori_loop(0, T // 32, one, jnp.zeros((1, D), F32)))


def stage_conv2_weights(r):
    D = r.stream.shape[1]
    sg = r.sg[...]
    for i, tap in enumerate((r.hp, r.he, r.ho)):
        r.g_c2[i * D : (i + 1) * D, :] = tn(tap[...], sg).astype(BF)


def stage_conv1_weights(r):
    r.g_c1[...] = (tn(r.xe[...], r.fe[...]) + tn(r.xo[...], r.fo[...])).astype(BF)


def stage_mel(r, next_row, prev_row):
    T, D = r.stream.shape
    fe, fo = r.fe[...], r.fo[...]
    r.wide[16 : 16 + T, :] = nt(fo, r.w1p[2])
    r.wide[0:16, :] = nt(prev_row, r.w1p[2])
    r.melg[:, 0:128] = nt(fe, r.w1p[1]) + nt(fo, r.w1p[0]) + r.wide[15 : 15 + T, :]
    r.wide[0:T, :] = nt(fe, r.w1p[0])
    r.wide[T : T + 16, :] = nt(next_row, r.w1p[0])
    r.melg[:, 128:256] = nt(fe, r.w1p[2]) + nt(fo, r.w1p[1]) + r.wide[1 : 1 + T, :]


class Net:
    def __init__(self, r, bits):
        self.r, self.bits, self.used, self.used_here = r, bits, 0, 0
        self.d, self.c, self.m = (lax.axis_index(n) for n in ("dp", "seq", "mp"))

    def bit(self, dim):
        if dim == "c":
            return self.c
        if dim == "y":
            return self.m
        return (self.d // (1 << dim)) % 2

    def peer(self, dim):
        if dim == "c":
            return (self.d, 1 - self.c, self.m)
        if dim == "y":
            return (self.d, self.c, 1 - self.m)
        step = 1 << dim
        return (self.d + step - 2 * step * self.bit(dim), self.c, self.m)

    def greet(self):
        barrier = pltpu.get_barrier_semaphore()
        dims = ["c", "y"] + list(range(self.bits))
        for dim in dims:
            pl.semaphore_signal(barrier, inc=1, device_id=self.peer(dim), device_id_type=MESH)
        pl.semaphore_wait(barrier, len(dims))

    def send(self, src, dst, dim):
        i = self.used
        self.used += 1
        copy = pltpu.make_async_remote_copy(
            src_ref=src,
            dst_ref=dst,
            send_sem=self.r.send.at[i],
            recv_sem=self.r.recv.at[i],
            device_id=self.peer(dim),
            device_id_type=MESH,
        )
        copy.start()
        return copy

    def here(self, src, dst):
        i = self.used_here
        self.used_here += 1
        copy = pltpu.make_async_copy(src, dst, self.r.own.at[i])
        copy.start()
        return copy


def wait_all(copies):
    for copy in copies:
        copy.wait()


def rows16(start, size):
    return pl.ds(pl.multiple_of(start, 16), size)


def sum_plan(rows, halves, order):
    steps, need = [], 0
    for dim in order:
        if dim == "y" and halves == 2:
            steps.append((dim, "other", rows))
            halves = 1
        elif rows % 32 == 0:
            rows //= 2
            steps.append((dim, "halve", rows))
        else:
            steps.append((dim, "swap", rows))
        need += rows * halves
    return steps, need


def bucket_sum(net, g, got, done, halves, order):
    R = g.shape[0] // halves
    lo, rows, at, bases = 0, R, 0, [h * R for h in range(halves)]
    back = []
    for dim, kind, n in sum_plan(R, halves, order)[0]:
        b = net.bit(dim)
        keep = give = lo
        givers = bases
        if kind == "halve":
            keep, give = lo + b * n, lo + (1 - b) * n
            back.append((dim, n, lo))
        if kind == "other":
            givers, bases = [(1 - b) * R], [b * R]
        copies = [
            net.send(g.at[rows16(base + give, n)], got.at[rows16(at + i * n, n)], dim)
            for i, base in enumerate(givers)
        ]
        yield
        wait_all(copies)
        step = 32 if n % 32 == 0 else 16
        for i, base in enumerate(bases):

            def add(k, carry, base=base, keep=keep, at=at, i=i, n=n):
                mine = rows16(base + keep + k * step, step)
                value = g[mine, :].astype(F32) + got[rows16(at + i * n + k * step, step), :].astype(F32)
                g[mine, :] = value.astype(BF)
                return carry

            lax.fori_loop(0, n // step, add, 0)
        at += n * len(bases)
        lo, rows = keep, n
    for k in range(rows // 16):
        done[rows16(lo + 16 * k, 16), :] = g[rows16(bases[0] + lo + 16 * k, 16), :]
    for dim, n, before in reversed(back):
        part = rows16(lo, n)
        copy = net.send(done.at[part], done.at[part], dim)
        yield
        copy.wait()
        lo = before


def small_sum(net, value, slots, order):
    for i, dim in enumerate(order):
        copy = net.send(value, slots.at[i], dim)
        yield
        copy.wait()
        value[...] += slots[i]


def advance(*sums):
    for one in sums:
        next(one, None)


def drain(*sums):
    left = list(sums)
    while left:
        left = [one for one in left if next(one, left) is not left]


def quarter(net):
    return 2 * net.c + net.c + net.m - 2 * net.c * net.m


def choose(slots, by_core, by_y):
    core = jnp.where(by_core, 1.0, 0.0)
    y = jnp.where(by_y, 1.0, 0.0)
    return (slots[0].astype(F32) * core + slots[1].astype(F32) * y).astype(BF)


def pick_next(net, slots):
    q = quarter(net)
    return choose(slots, q == 1, q % 2 == 0)


def pick_prev(net, slots):
    q = quarter(net)
    return choose(slots, q == 2, q % 2 == 1)


def layer(r, bits):
    T, D = r.stream.shape
    half, F2 = D // 2, r.down_l.shape[0]
    net = Net(r, bits)
    c, m = net.c, net.m
    sub = c + m - 2 * c * m
    dims = list(range(bits))
    net.greet()

    own = [
        net.here(r.pos, r.stream),
        net.here(r.wqkv_l, r.wqkv.at[m]),
        net.here(r.wo_l, r.wo.at[rows16(m * half, half)]),
        net.here(r.up_l, r.up.at[m]),
        net.here(r.down_l, r.down.at[rows16(m * F2, F2)]),
    ]
    vec_copy = net.send(r.vecs_in.at[8:16], r.vec_got, "y")
    piece = rows16(c * half, half)
    qkv_y = net.send(r.wqkv_l.at[:, piece], r.wqkv.at[m, :, piece], "y")
    p = 2 * c + net.bit(0)
    ff_y = [
        net.send(r.wo_l.at[rows16(p * (half // 4), half // 4)], r.wo.at[rows16(m * half + p * (half // 4), half // 4)], "y"),
        net.send(r.up_l.at[rows16(p * (D // 4), D // 4)], r.up.at[m, rows16(p * (D // 4), D // 4)], "y"),
        net.send(r.down_l.at[rows16(p * (F2 // 4), F2 // 4)], r.down.at[rows16(m * F2 + p * (F2 // 4), F2 // 4)], "y"),
    ]

    def pass_on(at, parts, dim):
        wo = r.wo.at[rows16((1 - m) * half + at * (half // 4), parts * (half // 4))]
        up = r.up.at[1 - m, rows16(at * (D // 4), parts * (D // 4))]
        down = r.down.at[rows16((1 - m) * F2 + at * (F2 // 4), parts * (F2 // 4))]
        return [net.send(x, x, dim) for x in (wo, up, down)]

    r.small[...] = jnp.zeros_like(r.small)
    r.vecs[...] = r.vecs_in[...]
    own[0].wait()
    stage_stem(r)
    qkv_y.wait()
    arrived = r.wqkv.at[1 - m, :, piece]
    qkv_c = net.send(arrived, arrived, "c")
    vec_copy.wait()
    r.vecs[8:16, :] += r.vec_got[...]
    own[1].wait()
    qkv_c.wait()

    def block(slot, part):
        return r.kv.at[(2 * slot + part) * D : (2 * slot + part + 1) * D]

    kv_y, kv_c = [], []
    for part in range(2):
        stage_qkv(r, (1 + part,))
        kv_y.append(net.send(block(0, part), block(2, part), "y"))
        kv_c.append(net.send(block(0, part), block(1, part), "c"))
    stage_qkv(r, (0,))
    attend_block(r, 0)
    wait_all(ff_y)
    ff_x = pass_on(p, 1, 0)
    wait_all(kv_c)
    attend_block(r, 1)
    wait_all(ff_x)
    ff_c = pass_on(2 * c, 2, "c")
    wait_all(kv_y)
    kv_d = [net.send(block(2, part), block(3, part), "c") for part in range(2)]
    attend_block(r, 2)
    wait_all(kv_d)
    attend_block(r, 3)
    attend_end(r)
    wait_all(own[2:])
    wait_all(ff_c)
    stage_mid(r)
    stage_ff(r)
    down_sum = bucket_sum(net, r.g_down, r.got_down, r.done_down, 2, ["c"] + dims + ["y"])
    advance(down_sum)
    stage_mid_pull(r)
    rows_of_mine = rows16(sub * T, T)
    enc = [
        net.here(r.enc, r.enc_o.at[rows_of_mine]),
        net.send(r.enc, r.enc_o.at[rows_of_mine], "y"),
    ]
    up_sum = bucket_sum(net, r.g_up, r.got_up, r.done_up, 2, ["c"] + dims[1:] + dims[:1] + ["y"])
    advance(up_sum)

    turn = [0]

    def hook():
        turn[0] += 1
        advance(down_sum if turn[0] % 2 else up_sum)

    def halves(ref):
        return [ref.at[0], ref.at[1]]

    pull_block(r, 3, r.part_a, hook)
    to_c = [net.send(r.part_a, r.from_d, "c")]
    pull_block(r, 2, r.part_y, hook)
    wait_all(to_c)

    def join(i, carry):
        for part in range(2):
            rows = rows16(i * 32, 32)
            value = r.part_y[part, rows, :].astype(F32) + r.from_d[part, rows, :].astype(F32)
            r.part_y[part, rows, :] = value.astype(BF)
        return carry

    lax.fori_loop(0, D // 32, join, 0)
    to_y = net.send(r.part_y, r.from_y, "y")
    pull_block(r, 1, r.part_a, hook)
    to_s = net.send(r.part_a, r.from_s, "c")
    pull_block(r, 0, r.part_o, hook)
    r.dqb[...] = (r.dqt[...] * HEAD**-0.5).astype(BF)
    to_s.wait()
    to_y.wait()

    def total(i, carry):
        for part in range(2):
            rows = rows16(i * 32, 32)
            value = r.part_o[part, rows, :].astype(F32) + r.from_s[part, rows, :].astype(F32)
            r.part_o[part, rows, :] = (value + r.from_y[part, rows, :].astype(F32)).astype(BF)
        return carry

    lax.fori_loop(0, D // 32, total, 0)
    r.dkb, r.dvb = r.part_o.at[0], r.part_o.at[1]

    stage_qkv_weights(r)
    qkv_sum = bucket_sum(net, r.g_qkv, r.got_qkv, r.done_qkv, 2, ["c"] + dims[1:] + dims[:1] + ["y"])
    advance(qkv_sum, down_sum)
    stage_qkv_pull(r)
    rim = [net.send(r.sg.at[0:16], r.slots.at[0, i], dim) for i, dim in enumerate(("c", "y"))]
    stage_conv2_weights(r)
    c2_sum = bucket_sum(net, r.g_c2, r.got_c2, r.done_c2, 1, ["c"] + dims + ["y"])
    advance(c2_sum, qkv_sum, up_sum)
    wait_all(rim)
    stage_conv2_pull(r, pick_next(net, r.slots.at[0]))
    rim = [net.send(r.fe.at[0:16], r.slots.at[1, i], dim) for i, dim in enumerate(("c", "y"))]
    rim += [net.send(r.fo.at[T - 16 : T], r.slots.at[2, i], dim) for i, dim in enumerate(("c", "y"))]
    stage_conv1_weights(r)
    c1_sum = bucket_sum(net, r.g_c1, r.got_c1, r.done_c1, 1, ["c"] + dims + ["y"])
    vec_sum = small_sum(net, r.small, r.got_small, ["c"] + dims + ["y"])
    advance(c1_sum, vec_sum, c2_sum, qkv_sum, down_sum)
    wait_all(rim)
    stage_mel(r, pick_next(net, r.slots.at[1]), pick_prev(net, r.slots.at[2]))
    ends = [
        net.here(r.melg, r.mel_o.at[rows_of_mine]),
        net.send(r.melg, r.mel_o.at[rows_of_mine], "y"),
    ]
    drain(c2_sum, qkv_sum, c1_sum, vec_sum, up_sum, down_sum)

    side = F2 // D
    ends.append(net.here(r.done_down, r.down_o))
    for j in range(side):
        ends.append(net.here(r.done_up.at[j * D : (j + 1) * D], r.up_o.at[:, j * D : (j + 1) * D]))
    ends.append(net.here(r.done_up.at[side * D : side * D + half], r.out_o))
    for part in range(3):
        for j in range(2):
            ends.append(
                net.here(
                    r.done_qkv.at[part * half : (part + 1) * half, j * half : (j + 1) * half],
                    r.qkv_o.at[part, j * half : (j + 1) * half],
                )
            )
    ends.append(net.here(r.done_c2, r.c2_o))
    ends.append(net.here(r.done_c1, r.c1_o))
    ends.append(net.here(r.small, r.small_o))
    wait_all(enc)
    wait_all(ends)


def run_layer(bits, near, far, outs, T, D, F2, lanes):
    half, H = D // 2, D // HEAD
    td, dt = (T, D), (D, T)
    dims = list(range(bits))
    first, second = ["c"] + dims + ["y"], ["c"] + dims[1:] + dims[:1] + ["y"]
    buckets = dict(
        down=(F2, 2, first),
        up=(F2 + half, 2, second),
        qkv=(3 * half, 2, second),
        c2=(3 * D, 1, first),
        c1=(lanes, 1, first),
    )
    scratch = dict(
        wqkv=((2, 3, D, half), BF),
        wo=((D, D), BF),
        up=((2, D, F2), BF),
        down=((2 * F2, D), BF),
        vecs=((16, D), F32),
        vec_got=((8, D), F32),
        stream=(td, F32),
        he=(td, BF),
        ho=(td, BF),
        hp=(td, BF),
        dge=(td, F32),
        dgo=(td, F32),
        dg2=(td, F32),
        normed=(td, BF),
        qt=(dt, BF),
        kv=((8 * D, T), BF),
        mixt=(dt, F32),
        mixb=(dt, BF),
        dot=(dt, BF),
        top=((H, 1, T), F32),
        total=((H, 1, T), F32),
        diag=((H, 1, T), F32),
        tmp=(td, F32),
        tmp2=(td, F32),
        shift=((T + 16, D), F32),
        wide=((T + 16, 128), F32),
        mid=(td, F32),
        ntwo=(td, BF),
        act=(td, BF),
        ing=(td, BF),
        ffo=(td, F32),
        ntg=(td, F32),
        attg=(td, BF),
        dqb=(dt, BF),
        part_a=((2, D, T), BF),
        part_y=((2, D, T), BF),
        part_o=((2, D, T), BF),
        from_d=((2, D, T), BF),
        from_y=((2, D, T), BF),
        from_s=((2, D, T), BF),
        enc=(td, BF),
        melg=((T, 256), F32),
        small=((16, D), F32),
        got_small=((bits + 2, 16, D), F32),
        slots=((3, 2, 16, D), BF),
    )
    for n, (rows, halves, order) in buckets.items():
        if n not in ("qkv", "c2") or T != D:
            scratch["g_" + n] = ((rows * halves, D), BF)
        scratch["got_" + n] = ((sum_plan(rows, halves, order)[1], D), BF)
        scratch["done_" + n] = ((rows, D), BF)
    names = list(near) + list(far) + list(outs) + list(scratch) + ["send", "recv", "own"]

    def kernel(*refs):
        r = Box()
        for n, ref in zip(names, refs):
            setattr(r, n, ref)
        r.odd, r.smg, r.sg, r.fe, r.fo, r.dqt = r.shift, r.mid, r.ntwo, r.act, r.ing, r.ffo
        if T == D:
            r.g_qkv, r.g_c2 = r.kv.at[0 : 6 * half], r.kv.at[3 * D : 6 * D]
        layer(r, bits)

    vmem, anywhere = pl.BlockSpec(memory_space=pltpu.VMEM), pl.BlockSpec(memory_space=pl.ANY)
    got = pl.pallas_call(
        kernel,
        name="layer",
        out_shape=[jax.ShapeDtypeStruct(*o) for o in outs.values()],
        in_specs=[vmem] * len(near) + [anywhere] * len(far),
        out_specs=[anywhere] * len(outs),
        scratch_shapes=[pltpu.VMEM(*s) for s in scratch.values()]
        + [pltpu.SemaphoreType.DMA((160,)), pltpu.SemaphoreType.DMA((160,)), pltpu.SemaphoreType.DMA((32,))],
        compiler_params=pltpu.CompilerParams(
            vmem_limit_bytes=VMEM_LIMIT, collective_id=1, has_side_effects=True
        ),
    )(*near.values(), *far.values())
    return dict(zip(outs, got))


def sinusoids(positions, channels):
    half_width = channels // 2
    increment = math.log(10000.0) / (half_width - 1)
    inverse = jnp.exp(-increment * jnp.arange(half_width, dtype=F32))
    angles = positions.astype(F32)[:, None] * inverse[None, :]
    return jnp.concatenate([jnp.sin(angles), jnp.cos(angles)], axis=1)


def on_device(
    mel_input,
    conv1_weight,
    conv1_bias,
    conv2_weight,
    conv2_bias,
    norm1_gain,
    norm1_bias,
    qkv_weight,
    qkv_bias,
    out_weight,
    out_bias,
    norm2_gain,
    norm2_bias,
    up_weight,
    up_bias,
    down_weight,
    down_bias,
    cotangent,
    speech_mask,
):
    mel = mel_input[0]
    mels = mel.shape[0]
    T, D = cotangent.shape[1] // 2, cotangent.shape[2]
    F2 = up_weight.shape[1]
    side, half = F2 // D, D // 2
    bits = (lax.axis_size("dp") - 1).bit_length()
    c, m = lax.axis_index("seq"), lax.axis_index("mp")
    sub = jnp.bitwise_xor(c, m)

    low = lax.ppermute(mel[:, -2:], "seq", [(0, 1)])
    high = lax.ppermute(mel[:, :2], "seq", [(1, 0)])
    window = lax.dynamic_slice_in_dim(
        jnp.concatenate([low, mel, high], axis=1), sub * 2 * T, 2 * T + 4, axis=1
    )
    pairs = window.T.reshape(T + 2, 2 * mels)
    xe = jnp.concatenate([pairs[0:T, mels:], pairs[1 : T + 1]], axis=1)
    xo = jnp.concatenate([pairs[1 : T + 1], pairs[2 : T + 2, :mels]], axis=1)
    xh = jnp.concatenate([pairs[0:1], pairs[1:2, :mels]], axis=1)
    lanes = -(-3 * mels // 128) * 128
    xe = jnp.pad(xe, ((0, 0), (0, lanes - 3 * mels)))
    xo = jnp.pad(xo, ((0, 0), (0, lanes - 3 * mels)))
    xh = jnp.pad(xh, ((7, 8), (0, lanes - 3 * mels)))
    w1 = jnp.pad(conv1_weight.reshape(3 * mels, D), ((0, lanes - 3 * mels), (0, 0)))
    w1p = jnp.pad(conv1_weight, ((0, 0), (0, 128 - mels), (0, 0)))
    pos = sinusoids((c * 2 + sub) * T + jnp.arange(T, dtype=jnp.int32), D)

    table = [conv1_bias, conv2_bias, norm1_gain, norm1_bias, out_bias, norm2_gain, norm2_bias]
    table = jnp.stack(table + [down_bias]).astype(F32)
    mine = jnp.zeros((8, D), F32)
    mine = lax.dynamic_update_slice(mine, qkv_bias.astype(F32), (0, m * half))
    mine = lax.dynamic_update_slice(mine, up_bias.astype(F32).reshape(side, D), (2 + m * side, 0))
    vecs = jnp.concatenate([table, mine], axis=0)

    cot = lax.dynamic_slice_in_dim(cotangent[0], sub * T, T, axis=0)
    mask = lax.dynamic_slice_in_dim(speech_mask[0], sub * T, T, axis=0)
    bg = cot * mask.astype(BF)[:, None]

    got = run_layer(
        bits,
        dict(xe=xe, xo=xo, xh=xh, w1=w1, w1p=w1p, w2=conv2_weight, vecs_in=vecs, bg=bg),
        dict(pos=pos, wqkv_l=qkv_weight, wo_l=out_weight, up_l=up_weight, down_l=down_weight),
        dict(
            enc_o=((2 * T, D), BF),
            mel_o=((2 * T, 256), F32),
            down_o=((F2, D), BF),
            up_o=((D, F2), BF),
            out_o=((half, D), BF),
            qkv_o=((3, D, half), BF),
            c2_o=((3 * D, D), BF),
            c1_o=((lanes, D), BF),
            small_o=((16, D), F32),
        ),
        T,
        D,
        F2,
        lanes,
    )
    small = got["small_o"]
    own_half = lax.dynamic_slice_in_dim(small[QB : QB + 2], m * half, half, axis=1)
    own_up = lax.dynamic_slice_in_dim(small[UPB : UPB + 2 * side], m * side, side, axis=0).reshape(-1)
    melg = got["mel_o"].reshape(4 * T, 128)[:, :mels].T[None]
    return (
        got["enc_o"][None],
        melg,
        got["c1_o"][: 3 * mels].astype(F32).reshape(3, mels, D),
        small[C1B],
        got["c2_o"].astype(F32).reshape(3, D, D),
        small[C2B],
        small[N1G],
        small[N1B],
        got["qkv_o"].astype(F32),
        own_half,
        got["out_o"].astype(F32),
        small[OUB],
        small[N2G],
        small[N2B],
        got["up_o"].astype(F32),
        own_up,
        got["down_o"].astype(F32),
        small[DNB],
    )


def solution(mesh):
    placed = (
        P("dp", None, "seq"),
        P(),
        P(),
        P(),
        P(),
        P(),
        P(),
        P(None, None, "mp"),
        P(None, "mp"),
        P("mp", None),
        P(),
        P(),
        P(),
        P(None, "mp"),
        P("mp"),
        P("mp", None),
        P(),
        P("dp", "seq", None),
        P("dp", "seq"),
    )
    return jax.shard_map(
        on_device,
        mesh=mesh,
        in_specs=placed,
        out_specs=(
            P("dp", "seq", None),
            P("dp", None, "seq"),
            P(),
            P(),
            P(),
            P(),
            P(),
            P(),
            P(None, None, "mp"),
            P(None, "mp"),
            P("mp", None),
            P(),
            P(),
            P(),
            P(None, "mp"),
            P("mp"),
            P("mp", None),
            P(),
        ),
        check_vma=False,
    )
```

```python
import functools
import math

import jax
import jax.numpy as jnp
import numpy as np
from jax import lax
from jax.experimental import pallas as pl
from jax.experimental.pallas import tpu as pltpu
from jax.sharding import PartitionSpec as P

HEAD = 64
BF = jnp.bfloat16
F32 = jnp.float32
MESH = pl.DeviceIdType.MESH
VMEM_LIMIT = 60 * 1024 * 1024
C1B, C2B, N1G, N1B, OUB, N2G, N2B, DNB, QB, VB, UPB = range(11)


class Box:
    pass


def dot(a, b, ca, cb):
    return lax.dot_general(a, b, (((ca,), (cb,)), ((), ())), preferred_element_type=F32)


def nn(a, b):
    return dot(a, b, 1, 0)


def nt(a, b):
    return dot(a, b, 1, 1)


def tn(a, b):
    return dot(a, b, 0, 0)


def rows_loop(total, step, body, unroll=1):
    step = min(step, total)

    def one(i, carry):
        body(pl.ds(pl.multiple_of(i * step, step), step))
        return carry

    lax.fori_loop(0, total // step, one, 0, unroll=unroll)


def gelu_parts(v):
    t = 1.0 / (1.0 + (0.3275911 / math.sqrt(2.0)) * jnp.abs(v))
    e = jnp.exp(-0.5 * v * v)
    poly = 1.061405429 * t - 1.453152027
    poly = poly * t + 1.421413741
    poly = poly * t - 0.284496736
    poly = poly * t + 0.254829592
    tail = (0.5 * t) * poly * e
    return jnp.where(v >= 0, 1.0 - tail, tail), e * (1.0 / math.sqrt(2.0 * math.pi))


def gelu_both(v):
    cdf, pdf = gelu_parts(v)
    return v * cdf, cdf + v * pdf


def normal(x):
    center = x - jnp.mean(x, axis=-1, keepdims=True)
    spread = jnp.mean(center * center, axis=-1, keepdims=True)
    inv = lax.rsqrt(spread + 1e-05)
    return center * inv, inv


def normal_pull(gy, hat, inv):
    return inv * (
        gy
        - jnp.mean(gy, axis=-1, keepdims=True)
        - hat * jnp.mean(gy * hat, axis=-1, keepdims=True)
    )


def vec(r, i):
    return r.vecs[i : i + 1, :]


def add_small(r, i, value):
    r.small[i : i + 1, :] += value


def col(value):
    return jnp.sum(value, axis=0, keepdims=True)


def stage_mel_rows(r, sub):
    T, D = r.stream.shape
    row = lax.broadcasted_iota(jnp.int32, (256, 256), 0)
    lane = lax.broadcasted_iota(jnp.int32, (256, 256), 1)
    pick = jnp.where(lane == 2 * (row % 128) + row // 128, 1.0, 0.0).astype(BF)
    base = sub * 2 * T

    def lanes(start, size):
        return r.melbuf[:, pl.ds(pl.multiple_of(base + start, 128), size)]

    row = lax.broadcasted_iota(jnp.int32, (16, 128), 0)
    lane = lax.broadcasted_iota(jnp.int32, (16, 128), 1)

    def select(at, to):
        return jnp.where(jnp.logical_and(row == to, lane == at), 1.0, 0.0).astype(BF)

    before, after = lanes(0, 128), lanes(128 + 2 * T, 128)
    r.mele[0:8, :] = nt(select(126, 7), before)[0:8, :]
    r.melo[0:8, :] = nt(select(127, 7), before)[0:8, :]
    r.mele[T + 8 : T + 16, :] = nt(select(0, 0), after)[0:8, :]
    for k in range(T // 128):
        both = nt(pick, lanes(128 + 256 * k, 256))
        r.mele[8 + 128 * k : 136 + 128 * k, :] = both[0:128, :]
        r.melo[8 + 128 * k : 136 + 128 * k, :] = both[128:256, :]


def three(a, b, c):
    return jnp.concatenate([a, b, c], axis=1).astype(BF)


def stage_first(r, first):
    T, D = r.stream.shape
    for o in range(3):
        r.w1p[128 * o : 128 * o + r.w1.shape[1], :] = r.w1[o]
        r.w1p[128 * o + r.w1.shape[1] : 128 * (o + 1), :] = jnp.zeros((128 - r.w1.shape[1], D), BF)
    w1 = r.w1p[...]
    edge = nn(three(r.mele[0:16, :], r.melo[0:16, :], r.mele[1:17, :]), w1) + vec(r, C1B)
    edge = gelu_both(edge)[0] * jnp.where(first, 0.0, 1.0)
    r.odd[0:8, :] = edge[0:8, :]
    r.xe[...] = three(r.melo[7 : 7 + T, :], r.mele[8 : 8 + T, :], r.melo[8 : 8 + T, :])
    r.xo[...] = three(r.mele[8 : 8 + T, :], r.melo[8 : 8 + T, :], r.mele[9 : 9 + T, :])
    r.tmp[...] = nn(r.xe[...], w1)

    def even(rows):
        value, slope = gelu_both(r.tmp[rows, :] + vec(r, C1B))
        r.he[rows, :] = value.astype(BF)
        r.dge[rows, :] = slope

    rows_loop(T, 32, even)
    r.tmp[...] = nn(r.xo[...], w1)

    def odd(rows):
        value, slope = gelu_both(r.tmp[rows, :] + vec(r, C1B))
        r.ho[rows, :] = value.astype(BF)
        r.odd[pl.ds(pl.multiple_of(rows.start + 8, 8), rows.size), :] = value
        r.dgo[rows, :] = slope

    rows_loop(T, 32, odd)


def stage_second(r, place):
    T, D = r.stream.shape
    r.hp[...] = r.odd[7 : 7 + T, :].astype(BF)
    r.tmp[...] = nn(r.hp[...], r.w2[0]) + nn(r.he[...], r.w2[1]) + nn(r.ho[...], r.w2[2])
    fine = r.fine_s.shape[0]

    def second(rows):
        value, slope = gelu_both(r.tmp[rows, :] + vec(r, C2B))
        at = place * (T // fine) + rows.start // fine
        s0, c0 = r.coarse_s[pl.ds(at, 1), :], r.coarse_c[pl.ds(at, 1), :]
        s1, c1 = r.fine_s[...], r.fine_c[...]
        stream = value + jnp.concatenate([s0 * c1 + c0 * s1, c0 * c1 - s0 * s1], axis=1)
        r.dg2[rows, :] = slope
        r.stream[rows, :] = stream
        r.normed[rows, :] = (normal(stream)[0] * vec(r, N1G) + vec(r, N1B)).astype(BF)

    rows_loop(T, fine, second)


def stage_mask(r, sub):
    T, D = r.stream.shape
    row = r.mask[0:1, pl.ds(pl.multiple_of(sub * T, 128), T)].astype(F32)
    r.wide[0:T, :] = jnp.broadcast_to(row, (128, T)).T

    def one(rows):
        keep = r.wide[rows, :]
        keep = jnp.concatenate([keep] * (D // 128), axis=1)
        r.bg[rows, :] = (r.bg[rows, :].astype(F32) * keep).astype(BF)

    rows_loop(T, 32, one)


def stage_qkv(r, parts):
    T, D = r.stream.shape
    half = D // 2
    normed = r.normed[...]
    for part in parts:
        bias, scale = ((QB, HEAD**-0.5), (None, 1.0), (VB, 1.0))[part]
        for m in range(2):
            value = nn(normed, r.wqkv[m, part])
            if bias is not None:
                value = value + r.vecs[bias : bias + 1, m * half : (m + 1) * half]
            value = (value.astype(BF).astype(F32) * scale).T.astype(BF)
            if part == 0:
                r.qt[m * half : (m + 1) * half, :] = value
            else:
                at = (part - 1) * D + m * half
                r.kv[at : at + half, :] = value


def head_rows(h):
    return pl.ds(pl.multiple_of(h * HEAD, HEAD), HEAD)


def block_rows(r, slot, part, h):
    D = r.qt.shape[0]
    return pl.ds(pl.multiple_of((2 * slot + part) * D + h * HEAD, HEAD), HEAD)


def attend_block(r, slot):
    D, T = r.qt.shape
    first = slot == 0

    def one(h, carry):
        rows = head_rows(h)
        s = tn(r.kv[block_rows(r, slot, 0, h), :], r.qt[rows, :])
        top = jnp.max(s, axis=0, keepdims=True)
        if not first:
            top = jnp.maximum(top, r.top[h])
        p = jnp.exp(s - top)
        total = jnp.sum(p, axis=0, keepdims=True)
        mixed = nn(r.kv[block_rows(r, slot, 1, h), :], p.astype(BF))
        if not first:
            keep = jnp.exp(r.top[h] - top)
            total = total + keep * r.total[h]
            mixed = mixed + keep * r.mixt[rows, :]
        r.top[h] = top
        r.total[h] = total
        r.mixt[rows, :] = mixed
        return carry

    lax.fori_loop(0, D // HEAD, one, 0)


def attend_end(r):
    D, T = r.qt.shape

    def one(h, carry):
        rows = head_rows(h)
        total = r.total[h]
        value = r.mixt[rows, :] * (1.0 / total)
        r.mixt[rows, :] = value
        r.mixb[rows, :] = value.astype(BF)
        r.top[h] = r.top[h] + jnp.log(total)
        return carry

    lax.fori_loop(0, D // HEAD, one, 0)


def stage_mid(r):
    T, D = r.stream.shape
    r.tmp[...] = tn(r.mixb[...], r.wo[...])

    def one(rows):
        mid = r.stream[rows, :] + r.tmp[rows, :] + vec(r, OUB)
        r.mid[rows, :] = mid
        r.ntwo[rows, :] = (normal(mid)[0] * vec(r, N2G) + vec(r, N2B)).astype(BF)

    rows_loop(T, 32, one)


def stage_ff(r):
    T, D = r.stream.shape
    side = r.up.shape[2] // D
    parts, width = 2 * side, D
    add_small(r, DNB, col(r.bg[...].astype(F32)))

    def chunk(j, carry):
        into, at = j // side, j % side
        up = r.up[into, :, pl.ds(pl.multiple_of(at * D, D), D)]
        down = r.down[pl.ds(pl.multiple_of(j * D, D), D), :]
        r.tmp[...] = nn(r.ntwo[...], up)
        r.tmp2[...] = nt(r.bg[...], down)
        bias = r.vecs[pl.ds(UPB + j, 1), :]

        def one(i, acc):
            rows = pl.ds(pl.multiple_of(i * 32, 32), 32)
            value, slope = gelu_both(r.tmp[rows, :] + bias)
            r.act[rows, :] = value.astype(BF)
            grad = (r.tmp2[rows, :] * slope).astype(BF)
            r.ing[rows, :] = grad
            return acc + col(grad.astype(F32))

        r.small[pl.ds(UPB + j, 1), :] = lax.fori_loop(0, T // 32, one, jnp.zeros((1, width), F32))
        act = r.act[...]
        ing = r.ing[...]
        out = nn(act, down)
        back = nt(ing, up)

        @pl.when(j == 0)
        def _():
            r.ffo[...] = out
            r.ntg[...] = back

        @pl.when(j > 0)
        def _():
            r.ffo[...] += out
            r.ntg[...] += back

        r.g_down[pl.ds(pl.multiple_of(j * D, D), D), :] = tn(act, r.bg[...]).astype(BF)
        base = into * (r.g_up.shape[0] // 2) + at * D
        r.g_up[pl.ds(pl.multiple_of(base, 16), D), :] = tn(r.ntwo[...], ing).astype(BF)
        return carry

    lax.fori_loop(0, parts, chunk, 0)


def stage_mid_pull(r):
    T, D = r.stream.shape

    def one(i, accs):
        rows = pl.ds(pl.multiple_of(i * 32, 32), 32)
        mid = r.mid[rows, :]
        r.enc[rows, :] = (mid + r.ffo[rows, :] + vec(r, DNB)).astype(BF)
        hat, inv = normal(mid)
        grad = r.ntg[rows, :]
        smg = r.bg[rows, :].astype(F32) + normal_pull(grad * vec(r, N2G), hat, inv)
        r.smg[rows, :] = smg
        attg = smg.astype(BF)
        r.attg[rows, :] = attg
        return accs[0] + col(grad * hat), accs[1] + col(grad), accs[2] + col(attg.astype(F32))

    zero = jnp.zeros((1, D), F32)
    gain, bias, out_bias = lax.fori_loop(0, T // 32, one, (zero, zero, zero))
    add_small(r, N2G, gain)
    add_small(r, N2B, bias)
    add_small(r, OUB, out_bias)
    attg = r.attg[...]
    r.dot[...] = nt(r.wo[...], attg).astype(BF)
    gout = nn(r.mixb[...], attg).astype(BF)
    rows, half = r.g_up.shape[0] // 2, D // 2
    r.g_up[rows - half : rows, :] = gout[0:half, :]
    r.g_up[2 * rows - half : 2 * rows, :] = gout[half:D, :]

    def head(h, carry):
        rows = head_rows(h)
        r.diag[h] = jnp.sum(r.dot[rows, :].astype(F32) * r.mixt[rows, :], axis=0, keepdims=True)
        return carry

    lax.fori_loop(0, D // HEAD, head, 0)


def pull_block(r, slot, dkv, hook):
    D, T = r.qt.shape
    first = slot == 3
    H = D // HEAD

    def one(h, carry):
        rows = head_rows(h)
        k, v = r.kv[block_rows(r, slot, 0, h), :], r.kv[block_rows(r, slot, 1, h), :]
        q, do = r.qt[rows, :], r.dot[rows, :]
        p = jnp.exp(tn(k, q) - r.top[h])
        ds = (p * (tn(v, do) - r.diag[h])).astype(BF)
        dkv[1, rows, :] = nt(do, p.astype(BF)).astype(dkv.dtype)
        dkv[0, rows, :] = nt(q, ds).astype(dkv.dtype)
        dq = nn(k, ds)
        if first:
            r.dqt[rows, :] = dq
        else:
            r.dqt[rows, :] += dq
        return carry

    for part in range(4):
        lax.fori_loop(part * H // 4, (part + 1) * H // 4, one, 0)
        hook()


def stage_qkv_weights(r):
    T, D = r.stream.shape
    half = D // 2
    normedt = r.normed[...].astype(F32).T.astype(BF)
    ones = jnp.ones((8, T), BF)
    for part, ref in enumerate((r.dqb, r.dkb, r.dvb)):
        if part != 1:
            add_small(r, QB if part == 0 else VB, nt(ones, ref[...])[0:1, :])
        for m in range(2):
            grad = nt(normedt, ref[m * half : (m + 1) * half, :]).astype(BF)
            at = (3 * m + part) * half
            r.g_qkv[at : at + half, 0:half] = grad[0:half, :]
            r.g_qkv[at : at + half, half:D] = grad[half:D, :]


def stage_qkv_pull(r):
    T, D = r.stream.shape
    half = D // 2
    total = None
    for part, ref in enumerate((r.dqb, r.dkb, r.dvb)):
        for m in range(2):
            back = nn(r.wqkv[m, part], ref[m * half : (m + 1) * half, :])
            total = back if total is None else total + back
    r.tmp[...] = total.T

    def one(i, accs):
        rows = pl.ds(pl.multiple_of(i * 32, 32), 32)
        hat, inv = normal(r.stream[rows, :])
        grad = r.tmp[rows, :]
        back = r.smg[rows, :] + normal_pull(grad * vec(r, N1G), hat, inv)
        sg = (back * r.dg2[rows, :]).astype(BF)
        r.sg[rows, :] = sg
        return accs[0] + col(grad * hat), accs[1] + col(grad), accs[2] + col(sg.astype(F32))

    zero = jnp.zeros((1, D), F32)
    gain, bias, c2b = lax.fori_loop(0, T // 32, one, (zero, zero, zero))
    add_small(r, N1G, gain)
    add_small(r, N1B, bias)
    add_small(r, C2B, c2b)


def stage_conv2_pull(r, next_row):
    T, D = r.stream.shape
    sg = r.sg[...]
    r.shift[0:T, :] = nt(sg, r.w2[0])
    r.shift[T : T + 16, :] = nt(next_row, r.w2[0])
    r.tmp[...] = nt(sg, r.w2[1])
    r.tmp2[...] = nt(sg, r.w2[2]) + r.shift[1 : T + 1, :]

    def one(i, acc):
        rows = pl.ds(pl.multiple_of(i * 32, 32), 32)
        even = (r.tmp[rows, :] * r.dge[rows, :]).astype(BF)
        odd = (r.tmp2[rows, :] * r.dgo[rows, :]).astype(BF)
        r.fe[rows, :] = even
        r.fo[rows, :] = odd
        return acc + col(even.astype(F32)) + col(odd.astype(F32))

    add_small(r, C1B, lax.fori_loop(0, T // 32, one, jnp.zeros((1, D), F32)))


def stage_conv2_weights(r):
    D = r.stream.shape[1]
    sg = r.sg[...]
    for i, tap in enumerate((r.hp, r.he, r.ho)):
        value = tn(tap[...], sg).astype(BF)
        r.g_c2[i * D : (i + 1) * D, :] = value


def stage_conv1_weights(r):
    value = (tn(r.xe[...], r.fe[...]) + tn(r.xo[...], r.fo[...])).astype(BF)
    mels = r.w1.shape[1]
    for o in range(3):
        r.g_c1[mels * o : mels * (o + 1), :] = value[128 * o : 128 * o + mels, :]
    r.g_c1[3 * mels :, :] = jnp.zeros((r.g_c1.shape[0] - 3 * mels, r.g_c1.shape[1]), BF)


def stage_mel(r, next_row, prev_row):
    T, D = r.stream.shape
    fe, fo = r.fe[...], r.fo[...]
    w = [r.w1p[128 * o : 128 * (o + 1), :] for o in range(3)]
    r.wide[16 : 16 + T, :] = nt(fo, w[2])
    r.wide[0:16, :] = nt(prev_row, w[2])
    r.melg[:, 0:128] = (nt(fe, w[1]) + nt(fo, w[0]) + r.wide[15 : 15 + T, :]).astype(BF)
    r.wide[0:T, :] = nt(fe, w[0])
    r.wide[T : T + 16, :] = nt(next_row, w[0])
    r.melg[:, 128:256] = (nt(fe, w[2]) + nt(fo, w[1]) + r.wide[1 : 1 + T, :]).astype(BF)


class Net:
    def __init__(self, r, bits):
        self.r, self.bits, self.used, self.used_here = r, bits, 0, 0
        self.d, self.c, self.m = (lax.axis_index(n) for n in ("dp", "seq", "mp"))

    def bit(self, dim):
        if dim == "c":
            return self.c
        if dim == "y":
            return self.m
        return (self.d // (1 << dim)) % 2

    def peer(self, dim):
        if dim == "c":
            return (self.d, 1 - self.c, self.m)
        if dim == "y":
            return (self.d, self.c, 1 - self.m)
        step = 1 << dim
        return (self.d + step - 2 * step * self.bit(dim), self.c, self.m)

    def greet(self):
        barrier = pltpu.get_barrier_semaphore()
        dims = ["c", "y"] + list(range(self.bits))
        for dim in dims:
            pl.semaphore_signal(barrier, inc=1, device_id=self.peer(dim), device_id_type=MESH)
        pl.semaphore_wait(barrier, len(dims))

    def send(self, src, dst, dim):
        i = self.used
        self.used += 1
        copy = pltpu.make_async_remote_copy(
            src_ref=src,
            dst_ref=dst,
            send_sem=self.r.send.at[i],
            recv_sem=self.r.recv.at[i],
            device_id=self.peer(dim),
            device_id_type=MESH,
        )
        copy.start()
        return copy

    def here(self, src, dst):
        i = self.used_here
        self.used_here += 1
        copy = pltpu.make_async_copy(src, dst, self.r.own.at[i])
        copy.start()
        return copy


def wait_all(copies):
    for copy in copies:
        copy.wait()


def rows16(start, size):
    return pl.ds(pl.multiple_of(start, 16), size)


def sum_plan(rows, halves, order):
    steps, need = [], 0
    for dim in order:
        if dim == "y" and halves == 2:
            steps.append((dim, "other", rows))
            halves = 1
        elif rows % 32 == 0:
            rows //= 2
            steps.append((dim, "halve", rows))
        else:
            steps.append((dim, "swap", rows))
        need += rows * halves
    return steps, need


def bucket_sum(net, g, got, done, halves, order):
    R = g.shape[0] // halves
    lo, rows, at, bases = 0, R, 0, [h * R for h in range(halves)]
    back = []
    for dim, kind, n in sum_plan(R, halves, order)[0]:
        b = net.bit(dim)
        keep = give = lo
        givers = bases
        if kind == "halve":
            keep, give = lo + b * n, lo + (1 - b) * n
            back.append((dim, n, lo))
        if kind == "other":
            givers, bases = [(1 - b) * R], [b * R]
        copies = [
            net.send(g.at[rows16(base + give, n)], got.at[rows16(at + i * n, n)], dim)
            for i, base in enumerate(givers)
        ]
        yield
        wait_all(copies)
        step = 32 if n % 32 == 0 else 16
        for i, base in enumerate(bases):

            def add(k, carry, base=base, keep=keep, at=at, i=i, n=n):
                mine = rows16(base + keep + k * step, step)
                value = g[mine, :].astype(F32) + got[rows16(at + i * n + k * step, step), :].astype(F32)
                g[mine, :] = value.astype(BF)
                return carry

            lax.fori_loop(0, n // step, add, 0)
        at += n * len(bases)
        lo, rows = keep, n
    for k in range(rows // 16):
        done[rows16(lo + 16 * k, 16), :] = g[rows16(bases[0] + lo + 16 * k, 16), :]
    for dim, n, before in reversed(back):
        part = rows16(lo, n)
        copy = net.send(done.at[part], done.at[part], dim)
        yield
        copy.wait()
        lo = before


def small_sum(net, value, slots, order):
    for i, dim in enumerate(order):
        copy = net.send(value, slots.at[i], dim)
        yield
        copy.wait()
        value[...] += slots[i]


def advance(*sums):
    for one in sums:
        next(one, None)


def drain(*sums):
    left = list(sums)
    while left:
        left = [one for one in left if next(one, left) is not left]


def quarter(net):
    return 2 * net.c + net.c + net.m - 2 * net.c * net.m


def choose(slots, by_core, by_y):
    core = jnp.where(by_core, 1.0, 0.0)
    y = jnp.where(by_y, 1.0, 0.0)
    return (slots[0].astype(F32) * core + slots[1].astype(F32) * y).astype(BF)


def pick_next(net, slots):
    q = quarter(net)
    return choose(slots, q == 1, q % 2 == 0)


def pick_prev(net, slots):
    q = quarter(net)
    return choose(slots, q == 2, q % 2 == 1)


ROW_BIASES = ("c1b", "c2b", "n1g", "n1b", "oub", "n2g", "n2b", "dnb")


def orders(bits):
    dims = list(range(bits))
    z_first = dims[1:2] + dims[:1] + dims[2:]
    return dict(
        down=["c", "y"] + dims,
        up=["c"] + dims + ["y"],
        qkv=["c"] + z_first + ["y"],
        c2a=["c", "y"] + dims,
        c2b=["c"] + dims[:1] + ["y"] + dims[1:],
        c1=["c"] + dims + ["y"],
        vec=["c"] + dims + ["y"],
    )


def layer(r, bits):
    T, D = r.stream.shape
    half, F2 = D // 2, r.down_l.shape[0]
    side = F2 // D
    mels, span = r.w1.shape[1], 4 * T
    net = Net(r, bits)
    c, m = net.c, net.m
    sub = c + m - 2 * c * m
    order = orders(bits)
    rows_of_mine = rows16(sub * T, T)

    r.melbuf[...] = jnp.zeros_like(r.melbuf)
    r.vec_mine[...] = jnp.zeros_like(r.vec_mine)
    own_lanes = pl.ds(pl.multiple_of(m * half, 128), half)
    r.vec_mine[0:2, own_lanes] = r.qkvb[...].astype(F32)
    for k in range(side):
        r.vec_mine[pl.ds(2 + m * side + k, 1), :] = r.upb[k * D : (k + 1) * D].astype(F32).reshape(1, D)
    for k, n in enumerate(ROW_BIASES):
        r.vecs[k : k + 1, :] = getattr(r, n)[...].astype(F32).reshape(1, D)
    net.greet()
    mel_own = net.here(r.mel.at[0], r.melbuf.at[0:mels, 128 : 128 + span])
    src = pl.ds(pl.multiple_of((1 - c) * (span - 128), 128), 128)
    dst = pl.ds(pl.multiple_of(c * (span + 128), 128), 128)
    mel_rim = net.send(r.mel.at[0, :, src], r.melbuf.at[0:mels, dst], "c")
    piece = rows16(c * half, half)
    qkv_y = net.send(r.wqkv_l.at[:, piece], r.wqkv.at[m, :, piece], "y")
    vec_copy = net.send(r.vec_mine, r.vec_got, "y")
    w2_own = net.here(r.w2_l, r.w2)
    own = [
        net.here(r.wqkv_l, r.wqkv.at[m]),
        net.here(r.cot.at[0, rows_of_mine], r.bg),
        net.here(r.wo_l, r.wo.at[rows16(m * half, half)]),
        net.here(r.up_l, r.up.at[m]),
        net.here(r.down_l, r.down.at[rows16(m * F2, F2)]),
    ]

    p = 4 * c + 2 * net.bit(0) + net.bit(1) if bits > 1 else 2 * c + net.bit(0)
    cuts = 8 if bits > 1 else 4

    def ff_parts(of, at, count, local):
        def cut(n, base):
            return rows16(base + at * (n // cuts), count * (n // cuts))

        if local:
            return [r.wo_l.at[cut(half, 0)], r.up_l.at[cut(D, 0)], r.down_l.at[cut(F2, 0)]]
        return [r.wo.at[cut(half, of * half)], r.up.at[of, cut(D, 0)], r.down.at[cut(F2, of * F2)]]

    def pass_on(at, count, dim):
        return [net.send(x, x, dim) for x in ff_parts(1 - m, at, count, False)]

    r.small[...] = jnp.zeros_like(r.small)
    mel_own.wait()
    mel_rim.wait()
    stage_mel_rows(r, sub)
    stage_first(r, jnp.logical_and(c == 0, m == 0))
    qkv_y.wait()
    arrived = r.wqkv.at[1 - m, :, piece]
    qkv_c = net.send(arrived, arrived, "c")
    ff = [
        net.send(a, b, "y")
        for a, b in zip(ff_parts(m, p, 1, True), ff_parts(m, p, 1, False))
    ]
    w2_own.wait()
    stage_second(r, quarter(net))
    vec_copy.wait()
    r.vecs[8:16, :] = r.vec_mine[...] + r.vec_got[...]
    wait_all(own[0:1])
    qkv_c.wait()

    def block(slot, part):
        return r.kv.at[(2 * slot + part) * D : (2 * slot + part + 1) * D]

    kv_y, kv_c = [], []
    for part in range(2):
        stage_qkv(r, (1 + part,))
        kv_y.append(net.send(block(0, part), block(2, part), "y"))
        kv_c.append(net.send(block(0, part), block(1, part), "c"))
    stage_qkv(r, (0,))
    wait_all(ff)
    ff = pass_on(p, 1, 1) if bits > 1 else []
    wait_all(own[1:2])
    stage_mask(r, sub)
    attend_block(r, 0)
    wait_all(ff)
    ff = pass_on((p // 2) * 2 if bits > 1 else p, 2 if bits > 1 else 1, 0)
    wait_all(kv_c)
    attend_block(r, 1)
    wait_all(ff)
    ff = pass_on(c * (cuts // 2), cuts // 2, "c")
    wait_all(kv_y)
    kv_d = [net.send(block(2, part), block(3, part), "c") for part in range(2)]
    attend_block(r, 2)
    wait_all(kv_d)
    attend_block(r, 3)
    attend_end(r)
    wait_all(own[2:])
    wait_all(ff)
    stage_mid(r)
    stage_ff(r)

    def summed(n, halves):
        return bucket_sum(
            net, getattr(r, "g_" + n), getattr(r, "got_" + n), getattr(r, "done_" + n), halves, order[n]
        )

    down_sum = summed("down", 2)
    advance(down_sum)
    stage_mid_pull(r)
    up_sum = summed("up", 2)
    advance(up_sum, down_sum)
    enc = []

    def send_enc():
        enc.append(net.here(r.enc, r.enc_o.at[rows_of_mine]))
        enc.append(net.send(r.enc, r.enc_o.at[rows_of_mine], "y"))

    moves = {
        1: (up_sum,),
        4: (down_sum,),
        6: (up_sum, down_sum),
        9: (up_sum, down_sum),
        12: (up_sum, down_sum),
        13: (up_sum, down_sum),
        14: (up_sum, down_sum),
        15: (up_sum, down_sum),
        16: (up_sum, down_sum),
    }
    turn = [0]

    def hook():
        turn[0] += 1
        advance(*moves.get(turn[0], ()))
        if turn[0] == 4:
            send_enc()

    pull_block(r, 3, r.part_a, hook)
    to_c = net.send(r.part_a, r.from_d, "c")
    pull_block(r, 2, r.part_y, hook)
    to_c.wait()

    def join(i, carry):
        for part in range(2):
            rows = rows16(i * 32, 32)
            value = r.part_y[part, rows, :].astype(F32) + r.from_d[part, rows, :].astype(F32)
            r.part_y[part, rows, :] = value.astype(BF)
        return carry

    lax.fori_loop(0, D // 32, join, 0)
    to_y = net.send(r.part_y, r.from_y, "y")
    pull_block(r, 1, r.part_a, hook)
    to_s = net.send(r.part_a, r.from_s, "c")
    pull_block(r, 0, r.part_o, hook)
    r.dqb[...] = (r.dqt[...] * HEAD**-0.5).astype(BF)
    to_s.wait()
    to_y.wait()

    def total(i, carry):
        for part in range(2):
            rows = rows16(i * 32, 32)
            value = r.part_o[part, rows, :].astype(F32) + r.from_s[part, rows, :].astype(F32)
            r.part_o[part, rows, :] = (value + r.from_y[part, rows, :].astype(F32)).astype(BF)
        return carry

    lax.fori_loop(0, D // 32, total, 0)
    r.dkb, r.dvb = r.part_o.at[0], r.part_o.at[1]

    stage_qkv_weights(r)
    qkv_sum = summed("qkv", 2)
    advance(qkv_sum, up_sum)
    stage_qkv_pull(r)
    rim = [net.send(r.sg.at[0:16], r.slots.at[0, i], dim) for i, dim in enumerate(("c", "y"))]
    advance(qkv_sum)
    stage_conv2_weights(r)
    c2a_sum, c2b_sum = summed("c2a", 1), summed("c2b", 1)
    advance(c2a_sum, c2b_sum)
    wait_all(rim)
    stage_conv2_pull(r, pick_next(net, r.slots.at[0]))
    rim = [net.send(r.fe.at[0:16], r.slots.at[1, i], dim) for i, dim in enumerate(("c", "y"))]
    rim += [net.send(r.fo.at[T - 16 : T], r.slots.at[2, i], dim) for i, dim in enumerate(("c", "y"))]
    advance(c2a_sum, c2b_sum, qkv_sum)
    stage_conv1_weights(r)
    c1_sum = summed("c1", 1)
    vec_sum = small_sum(net, r.small, r.got_small, order["vec"])
    advance(c1_sum, vec_sum)
    wait_all(rim)
    stage_mel(r, pick_next(net, r.slots.at[1]), pick_prev(net, r.slots.at[2]))
    ends = [
        net.here(r.melg, r.mel_o.at[rows_of_mine]),
        net.send(r.melg, r.mel_o.at[rows_of_mine], "y"),
    ]
    drain(c1_sum, vec_sum, c2a_sum, c2b_sum, qkv_sum, up_sum, down_sum)

    ends.append(net.here(r.done_down, r.down_o))
    for j in range(side):
        ends.append(net.here(r.done_up.at[j * D : (j + 1) * D], r.up_o.at[:, j * D : (j + 1) * D]))
    ends.append(net.here(r.done_up.at[side * D : side * D + half], r.out_o))
    for part in range(3):
        for j in range(2):
            ends.append(
                net.here(
                    r.done_qkv.at[part * half : (part + 1) * half, j * half : (j + 1) * half],
                    r.qkv_o.at[part, j * half : (j + 1) * half],
                )
            )
    ends.append(net.here(r.done_c2a, r.c2_o.at[0 : 3 * half]))
    ends.append(net.here(r.done_c2b, r.c2_o.at[3 * half : 6 * half]))
    ends.append(net.here(r.done_c1, r.c1_o))
    ends.append(net.here(r.small, r.small_o))
    wait_all(enc)
    wait_all(ends)


def run_layer(bits, near, far, outs, T, D, F2, lanes):
    half, H = D // 2, D // HEAD
    td, dt = (T, D), (D, T)
    order = orders(bits)
    buckets = dict(down=(F2, 2), up=(F2 + half, 2), qkv=(3 * half, 2), c2a=(3 * half, 1), c2b=(3 * half, 1), c1=(lanes, 1))
    scratch = dict(
        melbuf=((128, 4 * T + 256), BF),
        mele=((T + 24, 128), F32),
        melo=((T + 24, 128), F32),
        xe=((T, 384), BF),
        xo=((T, 384), BF),
        w1p=((384, D), BF),
        w2=((3, D, D), BF),
        bg=(td, BF),
        wqkv=((2, 3, D, half), BF),
        wo=((D, D), BF),
        up=((2, D, F2), BF),
        down=((2 * F2, D), BF),
        vecs=((16, D), F32),
        vec_mine=((8, D), F32),
        vec_got=((8, D), F32),
        stream=(td, F32),
        he=(td, BF),
        ho=(td, BF),
        hp=(td, BF),
        dge=(td, F32),
        dgo=(td, F32),
        dg2=(td, F32),
        normed=(td, BF),
        qt=(dt, BF),
        kv=((8 * D, T), BF),
        mixt=(dt, F32),
        mixb=(dt, BF),
        dot=(dt, BF),
        top=((H, 1, T), F32),
        total=((H, 1, T), F32),
        diag=((H, 1, T), F32),
        tmp=(td, F32),
        tmp2=(td, F32),
        shift=((T + 16, D), F32),
        wide=((T + 16, 128), F32),
        mid=(td, F32),
        ntwo=(td, BF),
        act=(td, BF),
        ing=(td, BF),
        ffo=(td, F32),
        ntg=(td, F32),
        attg=(td, BF),
        dqb=(dt, BF),
        part_a=((2, D, T), BF),
        part_y=((2, D, T), BF),
        part_o=((2, D, T), BF),
        from_d=((2, D, T), BF),
        from_y=((2, D, T), BF),
        from_s=((2, D, T), BF),
        enc=(td, BF),
        melg=((T, 256), BF),
        small=((16, D), F32),
        got_small=((bits + 2, 16, D), F32),
        slots=((3, 2, 16, D), BF),
    )
    alias = T == D
    for n, (rows, halves) in buckets.items():
        if n == "c1" or n in ("down", "up"):
            scratch["g_" + n] = ((rows * halves, D), BF)
        scratch["got_" + n] = ((sum_plan(rows, halves, order[n])[1], D), BF)
        scratch["done_" + n] = ((rows, D), BF)
    if not alias:
        scratch.update(g_qkv=((6 * half, D), BF), g_c2=((6 * half, D), BF))
    names = list(near) + list(far) + list(outs) + list(scratch) + ["send", "recv", "own"]

    def kernel(*refs):
        r = Box()
        for n, ref in zip(names, refs):
            setattr(r, n, ref)
        r.odd, r.smg, r.sg, r.fe, r.fo, r.dqt = r.shift, r.mid, r.ntwo, r.act, r.ing, r.ffo
        if alias:
            r.g_qkv, r.g_c2 = r.kv.at[0 : 6 * half], r.kv.at[6 * half : 12 * half]
        r.g_c2a, r.g_c2b = r.g_c2.at[0 : 3 * half], r.g_c2.at[3 * half : 6 * half]
        layer(r, bits)

    vmem, anywhere = pl.BlockSpec(memory_space=pltpu.VMEM), pl.BlockSpec(memory_space=pl.ANY)
    got = pl.pallas_call(
        kernel,
        name="layer",
        out_shape=[jax.ShapeDtypeStruct(*o) for o in outs.values()],
        in_specs=[vmem] * len(near) + [anywhere] * len(far),
        out_specs=[anywhere] * len(outs),
        scratch_shapes=[pltpu.VMEM(*s) for s in scratch.values()]
        + [pltpu.SemaphoreType.DMA((200,)), pltpu.SemaphoreType.DMA((200,)), pltpu.SemaphoreType.DMA((40,))],
        compiler_params=pltpu.CompilerParams(
            vmem_limit_bytes=VMEM_LIMIT, collective_id=1, has_side_effects=True
        ),
    )(*near.values(), *far.values())
    return dict(zip(outs, got))


def run_finish(got, mels, side):
    T2, D = got["enc_o"].shape
    half = D // 2
    ins = list(got)
    outs = dict(
        enc=((1, T2, D), BF),
        mel=((1, mels, 2 * T2), F32),
        c1=((3, mels, D), F32),
        c2=((3, D, D), F32),
        qkv=((3, D, half), F32),
        out=((half, D), F32),
        up=((D, side * D), F32),
        down=((side * D, D), F32),
    )

    def kernel(*refs):
        r = Box()
        for n, ref in zip(ins + list(outs) + ["sem"], refs):
            setattr(r, n, ref)
        copy = pltpu.make_async_copy(r.enc_o, r.enc.at[0], r.sem)
        copy.start()

        def cast(src, dst):
            def one(rows):
                dst[rows, :] = src[rows, :].astype(F32)

            rows_loop(src.shape[0], 64, one)

        cast(r.down_o, r.down)
        cast(r.up_o, r.up)
        cast(r.out_o, r.out)
        for o in range(3):
            cast(r.qkv_o.at[o], r.qkv.at[o])
            cast(r.c2_o.at[o * D : (o + 1) * D], r.c2.at[o])
            r.c1[o] = r.c1_o[o * mels : (o + 1) * mels, :].astype(F32)
        row = lax.broadcasted_iota(jnp.int32, (128, 256), 0)
        lane = lax.broadcasted_iota(jnp.int32, (128, 256), 1)
        even = jnp.where(lane == 2 * row, 1.0, 0.0).astype(BF)
        odd = jnp.where(lane == 2 * row + 1, 1.0, 0.0).astype(BF)
        for k in range(T2 // 128):
            rows = slice(k * 128, (k + 1) * 128)
            value = tn(r.mel_o[rows, 0:128], even) + tn(r.mel_o[rows, 128:256], odd)
            r.mel[0, :, k * 256 : (k + 1) * 256] = value[0:mels, :]
        copy.wait()

    vmem, anywhere = pl.BlockSpec(memory_space=pltpu.VMEM), pl.BlockSpec(memory_space=pl.ANY)
    done = pl.pallas_call(
        kernel,
        name="finish",
        out_shape=[jax.ShapeDtypeStruct(*o) for o in outs.values()],
        in_specs=[anywhere if n == "enc_o" else vmem for n in ins],
        out_specs=[anywhere if n == "enc" else vmem for n in outs],
        scratch_shapes=[pltpu.SemaphoreType.DMA],
        compiler_params=pltpu.CompilerParams(vmem_limit_bytes=VMEM_LIMIT),
    )(*got.values())
    return dict(zip(outs, done))


def sine_tables(frames, channels, fine):
    half_width = channels // 2
    rate = np.exp(-(math.log(10000.0) / (half_width - 1)) * np.arange(half_width))
    small = np.arange(fine)[:, None] * rate[None, :]
    large = np.arange(0, frames, fine)[:, None] * rate[None, :]
    table = dict(fine_s=np.sin(small), fine_c=np.cos(small), coarse_s=np.sin(large), coarse_c=np.cos(large))
    return {n: jnp.asarray(t, F32) for n, t in table.items()}


def on_device(
    mel_input,
    conv1_weight,
    conv1_bias,
    conv2_weight,
    conv2_bias,
    norm1_gain,
    norm1_bias,
    qkv_weight,
    qkv_bias,
    out_weight,
    out_bias,
    norm2_gain,
    norm2_bias,
    up_weight,
    up_bias,
    down_weight,
    down_bias,
    cotangent,
    speech_mask,
):
    mels = mel_input.shape[1]
    T, D = cotangent.shape[1] // 2, cotangent.shape[2]
    F2 = up_weight.shape[1]
    side, half = F2 // D, D // 2
    bits = (lax.axis_size("dp") - 1).bit_length()
    m = lax.axis_index("mp")
    lanes = -(-3 * mels // 128) * 128
    near = dict(
        w1=conv1_weight,
        mask=speech_mask,
        qkvb=qkv_bias,
        upb=up_bias,
        c1b=conv1_bias,
        c2b=conv2_bias,
        n1g=norm1_gain,
        n1b=norm1_bias,
        oub=out_bias,
        n2g=norm2_gain,
        n2b=norm2_bias,
        dnb=down_bias,
    )
    near.update(sine_tables(4 * T, D, 32))
    got = run_layer(
        bits,
        near,
        dict(
            mel=mel_input,
            cot=cotangent,
            w2_l=conv2_weight,
            wqkv_l=qkv_weight,
            wo_l=out_weight,
            up_l=up_weight,
            down_l=down_weight,
        ),
        dict(
            enc_o=((2 * T, D), BF),
            mel_o=((2 * T, 256), BF),
            down_o=((F2, D), BF),
            up_o=((D, F2), BF),
            out_o=((half, D), BF),
            qkv_o=((3, D, half), BF),
            c2_o=((3 * D, D), BF),
            c1_o=((lanes, D), BF),
            small_o=((16, D), F32),
        ),
        T,
        D,
        F2,
        lanes,
    )
    small = got.pop("small_o")
    own_half = lax.dynamic_slice_in_dim(small[QB : QB + 2], m * half, half, axis=1)
    own_up = lax.dynamic_slice_in_dim(small[UPB : UPB + 2 * side], m * side, side, axis=0).reshape(-1)
    done = run_finish(got, mels, side)
    return (
        done["enc"],
        done["mel"],
        done["c1"],
        small[C1B],
        done["c2"],
        small[C2B],
        small[N1G],
        small[N1B],
        done["qkv"],
        own_half,
        done["out"],
        small[OUB],
        small[N2G],
        small[N2B],
        done["up"],
        own_up,
        done["down"],
        small[DNB],
    )


def solution(mesh):
    placed = (
        P("dp", None, "seq"),
        P(),
        P(),
        P(),
        P(),
        P(),
        P(),
        P(None, None, "mp"),
        P(None, "mp"),
        P("mp", None),
        P(),
        P(),
        P(),
        P(None, "mp"),
        P("mp"),
        P("mp", None),
        P(),
        P("dp", "seq", None),
        P("dp", "seq"),
    )
    return jax.shard_map(
        on_device,
        mesh=mesh,
        in_specs=placed,
        out_specs=(
            P("dp", "seq", None),
            P("dp", None, "seq"),
            P(),
            P(),
            P(),
            P(),
            P(),
            P(),
            P(None, None, "mp"),
            P(None, "mp"),
            P("mp", None),
            P(),
            P(),
            P(),
            P(None, "mp"),
            P("mp"),
            P("mp", None),
            P(),
        ),
        check_vma=False,
    )
```

```python
import functools
import math

import jax
import jax.numpy as jnp
import numpy as np
from jax import lax
from jax.experimental import pallas as pl
from jax.experimental.pallas import tpu as pltpu
from jax.sharding import PartitionSpec as P

HEAD = 64
BF = jnp.bfloat16
F32 = jnp.float32
MESH = pl.DeviceIdType.MESH
VMEM_LIMIT = 61 * 1024 * 1024
C1B, C2B, N1G, N1B, OUB, N2G, N2B, DNB, QB, VB, UPB = range(11)


class Box:
    pass


def dot(a, b, ca, cb):
    return lax.dot_general(a, b, (((ca,), (cb,)), ((), ())), preferred_element_type=F32)


def nn(a, b):
    return dot(a, b, 1, 0)


def nt(a, b):
    return dot(a, b, 1, 1)


def tn(a, b):
    return dot(a, b, 0, 0)


def rows_loop(total, step, body, unroll=1):
    step = min(step, total)

    def one(i, carry):
        body(pl.ds(pl.multiple_of(i * step, step), step))
        return carry

    lax.fori_loop(0, total // step, one, 0, unroll=unroll)


def gelu_parts(v):
    t = 1.0 / (1.0 + (0.3275911 / math.sqrt(2.0)) * jnp.abs(v))
    e = jnp.exp(-0.5 * v * v)
    poly = 1.061405429 * t - 1.453152027
    poly = poly * t + 1.421413741
    poly = poly * t - 0.284496736
    poly = poly * t + 0.254829592
    tail = (0.5 * t) * poly * e
    return jnp.where(v >= 0, 1.0 - tail, tail), e * (1.0 / math.sqrt(2.0 * math.pi))


def gelu_both(v):
    cdf, pdf = gelu_parts(v)
    return v * cdf, cdf + v * pdf


def normal(x):
    center = x - jnp.mean(x, axis=-1, keepdims=True)
    spread = jnp.mean(center * center, axis=-1, keepdims=True)
    inv = lax.rsqrt(spread + 1e-05)
    return center * inv, inv


def normal_pull(gy, hat, inv):
    return inv * (
        gy
        - jnp.mean(gy, axis=-1, keepdims=True)
        - hat * jnp.mean(gy * hat, axis=-1, keepdims=True)
    )


def vec(r, i):
    return r.vecs[i : i + 1, :]


def add_small(r, i, value):
    r.small[i : i + 1, :] += value


def col(value):
    return jnp.sum(value, axis=0, keepdims=True)


def stage_mel_rows(r, sub):
    T, D = r.stream.shape
    row = lax.broadcasted_iota(jnp.int32, (256, 256), 0)
    lane = lax.broadcasted_iota(jnp.int32, (256, 256), 1)
    pick = jnp.where(lane == 2 * (row % 128) + row // 128, 1.0, 0.0).astype(BF)
    base = sub * 2 * T

    def lanes(start, size):
        return r.melbuf[:, pl.ds(pl.multiple_of(base + start, 128), size)]

    row = lax.broadcasted_iota(jnp.int32, (16, 128), 0)
    lane = lax.broadcasted_iota(jnp.int32, (16, 128), 1)

    def select(at, to):
        return jnp.where(jnp.logical_and(row == to, lane == at), 1.0, 0.0).astype(BF)

    before, after = lanes(0, 128), lanes(128 + 2 * T, 128)
    r.mele[0:8, :] = nt(select(126, 7), before)[0:8, :]
    r.melo[0:8, :] = nt(select(127, 7), before)[0:8, :]
    r.mele[T + 8 : T + 16, :] = nt(select(0, 0), after)[0:8, :]
    for k in range(T // 128):
        both = nt(pick, lanes(128 + 256 * k, 256))
        r.mele[8 + 128 * k : 136 + 128 * k, :] = both[0:128, :]
        r.melo[8 + 128 * k : 136 + 128 * k, :] = both[128:256, :]


def three(a, b, c):
    return jnp.concatenate([a, b, c], axis=1).astype(BF)


def stage_first(r, first):
    T, D = r.stream.shape
    for o in range(3):
        r.w1p[128 * o : 128 * o + r.w1.shape[1], :] = r.w1[o]
        r.w1p[128 * o + r.w1.shape[1] : 128 * (o + 1), :] = jnp.zeros((128 - r.w1.shape[1], D), BF)
    w1 = r.w1p[...]
    edge = nn(three(r.mele[0:16, :], r.melo[0:16, :], r.mele[1:17, :]), w1) + vec(r, C1B)
    edge = gelu_both(edge)[0] * jnp.where(first, 0.0, 1.0)
    r.odd[0:8, :] = edge[0:8, :]
    r.xe[...] = three(r.melo[7 : 7 + T, :], r.mele[8 : 8 + T, :], r.melo[8 : 8 + T, :])
    r.xo[...] = three(r.mele[8 : 8 + T, :], r.melo[8 : 8 + T, :], r.mele[9 : 9 + T, :])
    r.tmp[...] = nn(r.xe[...], w1)

    def even(rows):
        value, slope = gelu_both(r.tmp[rows, :] + vec(r, C1B))
        r.he[rows, :] = value.astype(BF)
        r.dge[rows, :] = slope

    rows_loop(T, 32, even)
    r.tmp[...] = nn(r.xo[...], w1)

    def odd(rows):
        value, slope = gelu_both(r.tmp[rows, :] + vec(r, C1B))
        r.ho[rows, :] = value.astype(BF)
        r.odd[pl.ds(pl.multiple_of(rows.start + 8, 8), rows.size), :] = value
        r.dgo[rows, :] = slope

    rows_loop(T, 32, odd)


def stage_second(r, place):
    T, D = r.stream.shape
    r.hp[...] = r.odd[7 : 7 + T, :].astype(BF)
    r.tmp[...] = nn(r.hp[...], r.w2[0]) + nn(r.he[...], r.w2[1]) + nn(r.ho[...], r.w2[2])
    fine = r.fine_s.shape[0]

    def second(rows):
        value, slope = gelu_both(r.tmp[rows, :] + vec(r, C2B))
        at = place * (T // fine) + rows.start // fine
        s0, c0 = r.coarse_s[pl.ds(at, 1), :], r.coarse_c[pl.ds(at, 1), :]
        s1, c1 = r.fine_s[...], r.fine_c[...]
        stream = value + jnp.concatenate([s0 * c1 + c0 * s1, c0 * c1 - s0 * s1], axis=1)
        r.dg2[rows, :] = slope
        r.stream[rows, :] = stream
        r.normed[rows, :] = (normal(stream)[0] * vec(r, N1G) + vec(r, N1B)).astype(BF)

    rows_loop(T, fine, second)


def stage_mask(r, sub):
    T, D = r.stream.shape
    row = r.mask[0:1, pl.ds(pl.multiple_of(sub * T, 128), T)].astype(F32)
    r.wide[0:T, :] = jnp.broadcast_to(row, (128, T)).T

    def one(rows):
        keep = r.wide[rows, :]
        keep = jnp.concatenate([keep] * (D // 128), axis=1)
        r.bg[rows, :] = (r.bg[rows, :].astype(F32) * keep).astype(BF)

    rows_loop(T, 32, one)


def stage_qkv(r, parts):
    T, D = r.stream.shape
    half = D // 2
    normed = r.normed[...]
    for part in parts:
        bias, scale = ((QB, HEAD**-0.5), (None, 1.0), (VB, 1.0))[part]
        for m in range(2):
            value = nn(normed, r.wqkv[m, part])
            if bias is not None:
                value = value + r.vecs[bias : bias + 1, m * half : (m + 1) * half]
            value = (value.astype(BF).astype(F32) * scale).T.astype(BF)
            if part == 0:
                r.qt[m * half : (m + 1) * half, :] = value
            else:
                at = (part - 1) * D + m * half
                r.kv[at : at + half, :] = value


def head_rows(h):
    return pl.ds(pl.multiple_of(h * HEAD, HEAD), HEAD)


def block_rows(r, slot, part, h):
    D = r.qt.shape[0]
    return pl.ds(pl.multiple_of((2 * slot + part) * D + h * HEAD, HEAD), HEAD)


def attend_block(r, slot):
    D, T = r.qt.shape
    first = slot == 0

    def one(h, carry):
        rows = head_rows(h)
        s = tn(r.kv[block_rows(r, slot, 0, h), :], r.qt[rows, :])
        top = jnp.max(s, axis=0, keepdims=True)
        if not first:
            top = jnp.maximum(top, r.top[h])
        p = jnp.exp(s - top)
        total = jnp.sum(p, axis=0, keepdims=True)
        mixed = nn(r.kv[block_rows(r, slot, 1, h), :], p.astype(BF))
        if not first:
            keep = jnp.exp(r.top[h] - top)
            total = total + keep * r.total[h]
            mixed = mixed + keep * r.mixt[rows, :]
        r.top[h] = top
        r.total[h] = total
        r.mixt[rows, :] = mixed
        return carry

    lax.fori_loop(0, D // HEAD, one, 0)


def attend_end(r):
    D, T = r.qt.shape

    def one(h, carry):
        rows = head_rows(h)
        total = r.total[h]
        value = r.mixt[rows, :] * (1.0 / total)
        r.mixt[rows, :] = value
        r.mixb[rows, :] = value.astype(BF)
        r.top[h] = r.top[h] + jnp.log(total)
        return carry

    lax.fori_loop(0, D // HEAD, one, 0)


def stage_mid(r):
    T, D = r.stream.shape
    r.tmp[...] = tn(r.mixb[...], r.wo[...])

    def one(rows):
        mid = r.stream[rows, :] + r.tmp[rows, :] + vec(r, OUB)
        r.mid[rows, :] = mid
        r.ntwo[rows, :] = (normal(mid)[0] * vec(r, N2G) + vec(r, N2B)).astype(BF)

    rows_loop(T, 32, one)


def stage_ff(r):
    T, D = r.stream.shape
    side = r.up.shape[2] // D
    parts, width = 2 * side, D
    add_small(r, DNB, col(r.bg[...].astype(F32)))

    def chunk(j, carry):
        into, at = j // side, j % side
        up = r.up[into, :, pl.ds(pl.multiple_of(at * D, D), D)]
        down = r.down[pl.ds(pl.multiple_of(j * D, D), D), :]
        r.tmp[...] = nn(r.ntwo[...], up)
        r.tmp2[...] = nt(r.bg[...], down)
        bias = r.vecs[pl.ds(UPB + j, 1), :]

        def one(i, acc):
            rows = pl.ds(pl.multiple_of(i * 32, 32), 32)
            value, slope = gelu_both(r.tmp[rows, :] + bias)
            r.act[rows, :] = value.astype(BF)
            grad = (r.tmp2[rows, :] * slope).astype(BF)
            r.ing[rows, :] = grad
            return acc + col(grad.astype(F32))

        r.small[pl.ds(UPB + j, 1), :] = lax.fori_loop(0, T // 32, one, jnp.zeros((1, width), F32))
        act = r.act[...]
        ing = r.ing[...]
        out = nn(act, down)
        back = nt(ing, up)

        @pl.when(j == 0)
        def _():
            r.ffo[...] = out
            r.ntg[...] = back

        @pl.when(j > 0)
        def _():
            r.ffo[...] += out
            r.ntg[...] += back

        r.g_down[pl.ds(pl.multiple_of(j * D, D), D), :] = tn(act, r.bg[...]).astype(BF)
        base = into * (r.g_up.shape[0] // 2) + at * D
        r.g_up[pl.ds(pl.multiple_of(base, 16), D), :] = tn(r.ntwo[...], ing).astype(BF)
        return carry

    lax.fori_loop(0, parts, chunk, 0)


def stage_mid_pull(r):
    T, D = r.stream.shape

    def one(i, accs):
        rows = pl.ds(pl.multiple_of(i * 32, 32), 32)
        mid = r.mid[rows, :]
        enc = (mid + r.ffo[rows, :] + vec(r, DNB)).astype(BF)
        hat, inv = normal(mid)
        grad = r.ntg[rows, :]
        smg = r.bg[rows, :].astype(F32) + normal_pull(grad * vec(r, N2G), hat, inv)
        r.enc[rows, :] = enc
        r.smg[rows, :] = smg
        attg = smg.astype(BF)
        r.attg[rows, :] = attg
        return accs[0] + col(grad * hat), accs[1] + col(grad), accs[2] + col(attg.astype(F32))

    zero = jnp.zeros((1, D), F32)
    gain, bias, out_bias = lax.fori_loop(0, T // 32, one, (zero, zero, zero))
    add_small(r, N2G, gain)
    add_small(r, N2B, bias)
    add_small(r, OUB, out_bias)
    attg = r.attg[...]
    r.dot[...] = nt(r.wo[...], attg).astype(BF)
    gout = nn(r.mixb[...], attg).astype(BF)
    rows, half = r.g_up.shape[0] // 2, D // 2
    r.g_up[rows - half : rows, :] = gout[0:half, :]
    r.g_up[2 * rows - half : 2 * rows, :] = gout[half:D, :]

    def head(h, carry):
        rows = head_rows(h)
        r.diag[h] = jnp.sum(r.dot[rows, :].astype(F32) * r.mixt[rows, :], axis=0, keepdims=True)
        return carry

    lax.fori_loop(0, D // HEAD, head, 0)


def pull_block(r, slot, dkv, hook):
    D, T = r.qt.shape
    first = slot == 3
    H = D // HEAD

    def one(h, carry):
        rows = head_rows(h)
        k, v = r.kv[block_rows(r, slot, 0, h), :], r.kv[block_rows(r, slot, 1, h), :]
        q, do = r.qt[rows, :], r.dot[rows, :]
        p = jnp.exp(tn(k, q) - r.top[h])
        ds = (p * (tn(v, do) - r.diag[h])).astype(BF)
        dkv[1, rows, :] = nt(do, p.astype(BF)).astype(dkv.dtype)
        dkv[0, rows, :] = nt(q, ds).astype(dkv.dtype)
        dq = nn(k, ds)
        if first:
            r.dqt[rows, :] = dq
        else:
            r.dqt[rows, :] += dq
        return carry

    for part in range(4):
        lax.fori_loop(part * H // 4, (part + 1) * H // 4, one, 0)
        hook()


def stage_qkv_weights(r):
    T, D = r.stream.shape
    half = D // 2
    normedt = r.normed[...].astype(F32).T.astype(BF)
    ones = jnp.ones((8, T), BF)
    for part, ref in enumerate((r.dqb, r.dkb, r.dvb)):
        if part != 1:
            add_small(r, QB if part == 0 else VB, nt(ones, ref[...])[0:1, :])
        for m in range(2):
            grad = nt(normedt, ref[m * half : (m + 1) * half, :]).astype(BF)
            at = (3 * m + part) * half
            r.g_qkv[at : at + half, 0:half] = grad[0:half, :]
            r.g_qkv[at : at + half, half:D] = grad[half:D, :]


def stage_qkv_pull(r):
    T, D = r.stream.shape
    half = D // 2
    total = None
    for part, ref in enumerate((r.dqb, r.dkb, r.dvb)):
        for m in range(2):
            back = nn(r.wqkv[m, part], ref[m * half : (m + 1) * half, :])
            total = back if total is None else total + back
    r.tmp[...] = total.T

    def one(i, accs):
        rows = pl.ds(pl.multiple_of(i * 32, 32), 32)
        hat, inv = normal(r.stream[rows, :])
        grad = r.tmp[rows, :]
        back = r.smg[rows, :] + normal_pull(grad * vec(r, N1G), hat, inv)
        sg = (back * r.dg2[rows, :]).astype(BF)
        r.sg[rows, :] = sg
        return accs[0] + col(grad * hat), accs[1] + col(grad), accs[2] + col(sg.astype(F32))

    zero = jnp.zeros((1, D), F32)
    gain, bias, c2b = lax.fori_loop(0, T // 32, one, (zero, zero, zero))
    add_small(r, N1G, gain)
    add_small(r, N1B, bias)
    add_small(r, C2B, c2b)


def stage_conv2_pull(r, next_row):
    T, D = r.stream.shape
    sg = r.sg[...]
    r.shift[0:T, :] = nt(sg, r.w2[0])
    r.shift[T : T + 16, :] = nt(next_row, r.w2[0])
    r.tmp[...] = nt(sg, r.w2[1])
    r.tmp2[...] = nt(sg, r.w2[2]) + r.shift[1 : T + 1, :]

    def one(i, acc):
        rows = pl.ds(pl.multiple_of(i * 32, 32), 32)
        even = (r.tmp[rows, :] * r.dge[rows, :]).astype(BF)
        odd = (r.tmp2[rows, :] * r.dgo[rows, :]).astype(BF)
        r.fe[rows, :] = even
        r.fo[rows, :] = odd
        return acc + col(even.astype(F32)) + col(odd.astype(F32))

    add_small(r, C1B, lax.fori_loop(0, T // 32, one, jnp.zeros((1, D), F32)))


def stage_conv2_weights(r):
    D = r.stream.shape[1]
    sg = r.sg[...]
    for i, tap in enumerate((r.hp, r.he, r.ho)):
        value = tn(tap[...], sg).astype(BF)
        r.g_c2[i * D : (i + 1) * D, :] = value


def stage_conv1_weights(r):
    value = (tn(r.xe[...], r.fe[...]) + tn(r.xo[...], r.fo[...])).astype(BF)
    mels = r.w1.shape[1]
    for o in range(3):
        r.g_c1[mels * o : mels * (o + 1), :] = value[128 * o : 128 * o + mels, :]
    r.g_c1[3 * mels :, :] = jnp.zeros((r.g_c1.shape[0] - 3 * mels, r.g_c1.shape[1]), BF)


def stage_mel(r, next_row, prev_row):
    T, D = r.stream.shape
    fe, fo = r.fe[...], r.fo[...]
    w = [r.w1p[128 * o : 128 * (o + 1), :] for o in range(3)]
    r.wide[16 : 16 + T, :] = nt(fo, w[2])
    r.wide[0:16, :] = nt(prev_row, w[2])
    r.melg[:, 0:128] = (nt(fe, w[1]) + nt(fo, w[0]) + r.wide[15 : 15 + T, :]).astype(BF)
    r.wide[0:T, :] = nt(fe, w[0])
    r.wide[T : T + 16, :] = nt(next_row, w[0])
    r.melg[:, 128:256] = (nt(fe, w[2]) + nt(fo, w[1]) + r.wide[1 : 1 + T, :]).astype(BF)


class Net:
    def __init__(self, r, bits):
        self.r, self.bits, self.used, self.used_here = r, bits, 0, 0
        self.d, self.c, self.m = (lax.axis_index(n) for n in ("dp", "seq", "mp"))

    def bit(self, dim):
        if dim == "c":
            return self.c
        if dim == "y":
            return self.m
        return (self.d // (1 << dim)) % 2

    def peer(self, dim):
        if dim == "c":
            return (self.d, 1 - self.c, self.m)
        if dim == "y":
            return (self.d, self.c, 1 - self.m)
        step = 1 << dim
        return (self.d + step - 2 * step * self.bit(dim), self.c, self.m)

    def greet(self):
        barrier = pltpu.get_barrier_semaphore()
        dims = ["c", "y"] + list(range(self.bits))
        for dim in dims:
            pl.semaphore_signal(barrier, inc=1, device_id=self.peer(dim), device_id_type=MESH)
        pl.semaphore_wait(barrier, len(dims))

    def send(self, src, dst, dim):
        i = self.used
        self.used += 1
        copy = pltpu.make_async_remote_copy(
            src_ref=src,
            dst_ref=dst,
            send_sem=self.r.send.at[i],
            recv_sem=self.r.recv.at[i],
            device_id=self.peer(dim),
            device_id_type=MESH,
        )
        copy.start()
        return copy

    def here(self, src, dst):
        i = self.used_here
        self.used_here += 1
        copy = pltpu.make_async_copy(src, dst, self.r.own.at[i])
        copy.start()
        return copy


def wait_all(copies):
    for copy in copies:
        copy.wait()


def rows16(start, size):
    return pl.ds(pl.multiple_of(start, 16), size)


def sum_plan(rows, halves, order):
    steps, need = [], 0
    for dim in order:
        if dim == "y" and halves == 2:
            steps.append((dim, "other", rows))
            halves = 1
        elif rows % 32 == 0:
            rows //= 2
            steps.append((dim, "halve", rows))
        else:
            steps.append((dim, "swap", rows))
        need += rows * halves
    return steps, need


def bucket_sum(net, g, got, done, halves, order):
    R = g.shape[0] // halves
    lo, rows, at, bases = 0, R, 0, [h * R for h in range(halves)]
    back = []
    for dim, kind, n in sum_plan(R, halves, order)[0]:
        b = net.bit(dim)
        keep = give = lo
        givers = bases
        if kind == "halve":
            keep, give = lo + b * n, lo + (1 - b) * n
            back.append((dim, n, lo))
        if kind == "other":
            givers, bases = [(1 - b) * R], [b * R]
        copies = [
            net.send(g.at[rows16(base + give, n)], got.at[rows16(at + i * n, n)], dim)
            for i, base in enumerate(givers)
        ]
        yield
        wait_all(copies)
        step = 32 if n % 32 == 0 else 16
        for i, base in enumerate(bases):

            def add(k, carry, base=base, keep=keep, at=at, i=i, n=n):
                mine = rows16(base + keep + k * step, step)
                value = g[mine, :].astype(F32) + got[rows16(at + i * n + k * step, step), :].astype(F32)
                g[mine, :] = value.astype(BF)
                return carry

            lax.fori_loop(0, n // step, add, 0)
        at += n * len(bases)
        lo, rows = keep, n
    for k in range(rows // 16):
        done[rows16(lo + 16 * k, 16), :] = g[rows16(bases[0] + lo + 16 * k, 16), :]
    for dim, n, before in reversed(back):
        part = rows16(lo, n)
        copy = net.send(done.at[part], done.at[part], dim)
        yield
        copy.wait()
        lo = before


def small_sum(net, value, slots, order):
    for i, dim in enumerate(order):
        copy = net.send(value, slots.at[i], dim)
        yield
        copy.wait()
        value[...] += slots[i]


def advance(*sums):
    for one in sums:
        next(one, None)


def drain(*sums):
    left = list(sums)
    while left:
        left = [one for one in left if next(one, left) is not left]


def quarter(net):
    return 2 * net.c + net.c + net.m - 2 * net.c * net.m


def choose(slots, by_core, by_y):
    core = jnp.where(by_core, 1.0, 0.0)
    y = jnp.where(by_y, 1.0, 0.0)
    return (slots[0].astype(F32) * core + slots[1].astype(F32) * y).astype(BF)


def pick_next(net, slots):
    q = quarter(net)
    return choose(slots, q == 1, q % 2 == 0)


def pick_prev(net, slots):
    q = quarter(net)
    return choose(slots, q == 2, q % 2 == 1)


ROW_BIASES = ("c1b", "c2b", "n1g", "n1b", "oub", "n2g", "n2b", "dnb")


def orders(bits):
    dims = list(range(bits))
    z_first = dims[1:2] + dims[:1] + dims[2:]
    return dict(
        down=["c", "y"] + dims,
        up=["c"] + dims + ["y"],
        qkv=["c"] + z_first + ["y"],
        c2a=["c", "y"] + dims,
        c2b=["c"] + dims[:1] + ["y"] + dims[1:],
        c1=["c"] + dims + ["y"],
        vec=["c"] + dims + ["y"],
    )


def layer(r, bits):
    T, D = r.stream.shape
    half, F2 = D // 2, r.down_l.shape[0]
    side = F2 // D
    mels, span = r.w1.shape[1], 4 * T
    net = Net(r, bits)
    c, m = net.c, net.m
    sub = c + m - 2 * c * m
    order = orders(bits)
    rows_of_mine = rows16(sub * T, T)

    r.melbuf[...] = jnp.zeros_like(r.melbuf)
    r.vec_mine[...] = jnp.zeros_like(r.vec_mine)
    own_lanes = pl.ds(pl.multiple_of(m * half, 128), half)
    r.vec_mine[0:2, own_lanes] = r.qkvb[...].astype(F32)
    for k in range(side):
        r.vec_mine[pl.ds(2 + m * side + k, 1), :] = r.upb[k * D : (k + 1) * D].astype(F32).reshape(1, D)
    for k, n in enumerate(ROW_BIASES):
        r.vecs[k : k + 1, :] = getattr(r, n)[...].astype(F32).reshape(1, D)
    net.greet()
    mel_own = net.here(r.mel.at[0], r.melbuf.at[0:mels, 128 : 128 + span])
    qkv_own = net.here(r.wqkv_l, r.wqkv.at[m])
    w2_own = net.here(r.w2_l, r.w2)
    own = [
        net.here(r.wo_l, r.wo.at[rows16(m * half, half)]),
        net.here(r.up_l, r.up.at[m]),
        net.here(r.down_l, r.down.at[rows16(m * F2, F2)]),
        net.here(r.cot.at[0, rows_of_mine], r.bg),
    ]
    vec_copy = net.send(r.vec_mine, r.vec_got, "y")
    mel_own.wait()
    src = pl.ds(pl.multiple_of(128 + (1 - c) * (span - 128), 128), 128)
    dst = pl.ds(pl.multiple_of(c * (span + 128), 128), 128)
    mel_rim = net.send(r.melbuf.at[0:mels, src], r.melbuf.at[0:mels, dst], "c")
    piece = rows16(c * half, half)
    qkv_own.wait()
    mine = r.wqkv.at[m, :, piece]
    qkv_y = net.send(mine, mine, "y")

    p = 4 * c + 2 * net.bit(0) + net.bit(1) if bits > 1 else 2 * c + net.bit(0)
    cuts = 8 if bits > 1 else 4

    def pass_on(of, at, count, dim):
        def cut(n, base):
            return rows16(base + at * (n // cuts), count * (n // cuts))

        parts = [r.wo.at[cut(half, of * half)], r.up.at[of, cut(D, 0)], r.down.at[cut(F2, of * F2)]]
        return [net.send(x, x, dim) for x in parts]

    r.small[...] = jnp.zeros_like(r.small)
    mel_rim.wait()
    stage_mel_rows(r, sub)
    stage_first(r, jnp.logical_and(c == 0, m == 0))
    qkv_y.wait()
    arrived = r.wqkv.at[1 - m, :, piece]
    qkv_c = net.send(arrived, arrived, "c")
    wait_all(own)
    ff = pass_on(m, p, 1, "y")
    w2_own.wait()
    stage_second(r, quarter(net))
    vec_copy.wait()
    r.vecs[8:16, :] = r.vec_mine[...] + r.vec_got[...]
    qkv_c.wait()

    def block(slot, part):
        return r.kv.at[(2 * slot + part) * D : (2 * slot + part + 1) * D]

    kv_y, kv_c = [], []
    for part in range(2):
        stage_qkv(r, (1 + part,))
        kv_c.append(net.send(block(0, part), block(1, part), "c"))
        kv_y.append(net.send(block(0, part), block(2, part), "y"))
    stage_qkv(r, (0,))
    wait_all(ff)
    ff = pass_on(1 - m, p, 1, 1) if bits > 1 else []
    stage_mask(r, sub)
    attend_block(r, 0)
    wait_all(ff)
    ff = pass_on(1 - m, (p // 2) * 2 if bits > 1 else p, 2 if bits > 1 else 1, 0)
    wait_all(kv_c)
    attend_block(r, 1)
    wait_all(ff)
    ff = pass_on(1 - m, c * (cuts // 2), cuts // 2, "c")
    wait_all(kv_y)
    kv_d = [net.send(block(2, part), block(3, part), "c") for part in range(2)]
    attend_block(r, 2)
    wait_all(kv_d)
    attend_block(r, 3)
    attend_end(r)
    wait_all(ff)
    stage_mid(r)
    stage_ff(r)

    def summed(n, halves):
        return bucket_sum(
            net, getattr(r, "g_" + n), getattr(r, "got_" + n), getattr(r, "done_" + n), halves, order[n]
        )

    down_sum = summed("down", 2)
    advance(down_sum)
    stage_mid_pull(r)
    up_sum = summed("up", 2)
    advance(up_sum, down_sum)
    enc = []

    def send_enc():
        enc.append(net.here(r.enc, r.enc_o.at[rows_of_mine]))
        enc.append(net.send(r.enc, r.enc_got, "y"))

    moves = {
        1: (up_sum,),
        4: (down_sum,),
        6: (up_sum, down_sum),
        9: (up_sum, down_sum),
        12: (up_sum, down_sum),
        13: (up_sum, down_sum),
        14: (up_sum, down_sum),
        15: (up_sum, down_sum),
        16: (up_sum, down_sum),
    }
    turn = [0]

    def hook():
        turn[0] += 1
        advance(*moves.get(turn[0], ()))
        if turn[0] == 4:
            send_enc()

    pull_block(r, 3, r.part_a, hook)
    to_c = net.send(r.part_a, r.from_d, "c")
    pull_block(r, 2, r.part_y, hook)
    to_c.wait()

    def join(i, carry):
        for part in range(2):
            rows = rows16(i * 32, 32)
            value = r.part_y[part, rows, :].astype(F32) + r.from_d[part, rows, :].astype(F32)
            r.part_y[part, rows, :] = value.astype(BF)
        return carry

    lax.fori_loop(0, D // 32, join, 0)
    to_y = net.send(r.part_y, r.from_y, "y")
    pull_block(r, 1, r.part_a, hook)
    to_s = net.send(r.part_a, r.from_s, "c")
    pull_block(r, 0, r.part_o, hook)
    r.dqb[...] = (r.dqt[...] * HEAD**-0.5).astype(BF)
    to_s.wait()
    to_y.wait()

    def total(i, carry):
        for part in range(2):
            rows = rows16(i * 32, 32)
            value = r.part_o[part, rows, :].astype(F32) + r.from_s[part, rows, :].astype(F32)
            r.part_o[part, rows, :] = (value + r.from_y[part, rows, :].astype(F32)).astype(BF)
        return carry

    lax.fori_loop(0, D // 32, total, 0)
    r.dkb, r.dvb = r.part_o.at[0], r.part_o.at[1]

    stage_qkv_weights(r)
    qkv_sum = summed("qkv", 2)
    advance(qkv_sum, up_sum)
    stage_qkv_pull(r)
    rim = [net.send(r.sg.at[0:16], r.slots.at[0, i], dim) for i, dim in enumerate(("c", "y"))]
    advance(qkv_sum)
    stage_conv2_weights(r)
    c2a_sum, c2b_sum = summed("c2a", 1), summed("c2b", 1)
    advance(c2a_sum, c2b_sum)
    wait_all(rim)
    stage_conv2_pull(r, pick_next(net, r.slots.at[0]))
    rim = [net.send(r.fe.at[0:16], r.slots.at[1, i], dim) for i, dim in enumerate(("c", "y"))]
    rim += [net.send(r.fo.at[T - 16 : T], r.slots.at[2, i], dim) for i, dim in enumerate(("c", "y"))]
    advance(c2a_sum, c2b_sum, qkv_sum)
    stage_conv1_weights(r)
    c1_sum = summed("c1", 1)
    vec_sum = small_sum(net, r.small, r.got_small, order["vec"])
    advance(c1_sum, vec_sum)
    wait_all(rim)
    stage_mel(r, pick_next(net, r.slots.at[1]), pick_prev(net, r.slots.at[2]))
    rows_of_yours = rows16((1 - sub) * T, T)
    mel_y = net.send(r.melg, r.melg_got, "y")
    wait_all(enc)
    ends = [
        net.here(r.enc_got, r.enc_o.at[rows_of_yours]),
        net.here(r.melg, r.mel_o.at[rows_of_mine]),
    ]
    drain(c1_sum, vec_sum, c2a_sum, c2b_sum, qkv_sum, up_sum, down_sum)

    ends.append(net.here(r.done_down, r.down_o))
    for j in range(side):
        ends.append(net.here(r.done_up.at[j * D : (j + 1) * D], r.up_o.at[:, j * D : (j + 1) * D]))
    ends.append(net.here(r.done_up.at[side * D : side * D + half], r.out_o))
    for part in range(3):
        for j in range(2):
            ends.append(
                net.here(
                    r.done_qkv.at[part * half : (part + 1) * half, j * half : (j + 1) * half],
                    r.qkv_o.at[part, j * half : (j + 1) * half],
                )
            )
    ends.append(net.here(r.done_c2a, r.c2_o.at[0 : 3 * half]))
    ends.append(net.here(r.done_c2b, r.c2_o.at[3 * half : 6 * half]))
    ends.append(net.here(r.done_c1, r.c1_o))
    ends.append(net.here(r.small, r.small_o))
    mel_y.wait()
    ends.append(net.here(r.melg_got, r.mel_o.at[rows_of_yours]))
    wait_all(ends)


def run_layer(bits, near, far, outs, T, D, F2, lanes):
    half, H = D // 2, D // HEAD
    td, dt = (T, D), (D, T)
    order = orders(bits)
    buckets = dict(down=(F2, 2), up=(F2 + half, 2), qkv=(3 * half, 2), c2a=(3 * half, 1), c2b=(3 * half, 1), c1=(lanes, 1))
    scratch = dict(
        melbuf=((128, 4 * T + 256), BF),
        mele=((T + 24, 128), F32),
        melo=((T + 24, 128), F32),
        xe=((T, 384), BF),
        xo=((T, 384), BF),
        w1p=((384, D), BF),
        w2=((3, D, D), BF),
        bg=(td, BF),
        wqkv=((2, 3, D, half), BF),
        wo=((D, D), BF),
        up=((2, D, F2), BF),
        down=((2 * F2, D), BF),
        vecs=((16, D), F32),
        vec_mine=((8, D), F32),
        vec_got=((8, D), F32),
        stream=(td, F32),
        he=(td, BF),
        ho=(td, BF),
        hp=(td, BF),
        dge=(td, F32),
        dgo=(td, F32),
        dg2=(td, F32),
        normed=(td, BF),
        qt=(dt, BF),
        kv=((8 * D, T), BF),
        mixt=(dt, F32),
        mixb=(dt, BF),
        dot=(dt, BF),
        top=((H, 1, T), F32),
        total=((H, 1, T), F32),
        diag=((H, 1, T), F32),
        tmp=(td, F32),
        tmp2=(td, F32),
        shift=((T + 16, D), F32),
        wide=((T + 16, 128), F32),
        mid=(td, F32),
        ntwo=(td, BF),
        act=(td, BF),
        ing=(td, BF),
        ffo=(td, F32),
        ntg=(td, F32),
        attg=(td, BF),
        dqb=(dt, BF),
        part_a=((2, D, T), BF),
        part_y=((2, D, T), BF),
        part_o=((2, D, T), BF),
        from_d=((2, D, T), BF),
        from_y=((2, D, T), BF),
        from_s=((2, D, T), BF),
        enc_got=(td, BF),
        melg=((T, 256), BF),
        melg_got=((T, 256), BF),
        small=((16, D), F32),
        got_small=((bits + 2, 16, D), F32),
        slots=((3, 2, 16, D), BF),
    )
    alias = T == D
    for n, (rows, halves) in buckets.items():
        if n == "c1" or n in ("down", "up"):
            scratch["g_" + n] = ((rows * halves, D), BF)
        scratch["got_" + n] = ((sum_plan(rows, halves, order[n])[1], D), BF)
        scratch["done_" + n] = ((rows, D), BF)
    if not alias:
        scratch.update(g_qkv=((6 * half, D), BF), g_c2=((6 * half, D), BF))
    names = list(near) + list(far) + list(outs) + list(scratch) + ["send", "recv", "own"]

    def kernel(*refs):
        r = Box()
        for n, ref in zip(names, refs):
            setattr(r, n, ref)
        r.odd, r.smg, r.sg, r.fe, r.fo, r.dqt, r.enc = r.shift, r.mid, r.ntwo, r.act, r.ing, r.ffo, r.bg
        if alias:
            r.g_qkv, r.g_c2 = r.kv.at[0 : 6 * half], r.kv.at[6 * half : 12 * half]
        r.g_c2a, r.g_c2b = r.g_c2.at[0 : 3 * half], r.g_c2.at[3 * half : 6 * half]
        layer(r, bits)

    vmem, anywhere = pl.BlockSpec(memory_space=pltpu.VMEM), pl.BlockSpec(memory_space=pl.ANY)
    got = pl.pallas_call(
        kernel,
        name="layer",
        out_shape=[jax.ShapeDtypeStruct(*o) for o in outs.values()],
        in_specs=[vmem] * len(near) + [anywhere] * len(far),
        out_specs=[anywhere] * len(outs),
        scratch_shapes=[pltpu.VMEM(*s) for s in scratch.values()]
        + [pltpu.SemaphoreType.DMA((200,)), pltpu.SemaphoreType.DMA((200,)), pltpu.SemaphoreType.DMA((40,))],
        compiler_params=pltpu.CompilerParams(
            vmem_limit_bytes=VMEM_LIMIT, collective_id=1, has_side_effects=True
        ),
    )(*near.values(), *far.values())
    return dict(zip(outs, got))


def run_finish(got, mels, side):
    T2, D = got["enc_o"].shape
    half = D // 2
    ins = list(got)
    outs = dict(
        enc=((1, T2, D), BF),
        mel=((1, mels, 2 * T2), F32),
        c1=((3, mels, D), F32),
        c2=((3, D, D), F32),
        qkv=((3, D, half), F32),
        qkvb=((2, half), F32),
        out=((half, D), F32),
        up=((D, side * D), F32),
        upb=((side * D,), F32),
        down=((side * D, D), F32),
    )
    outs.update({n: ((D,), F32) for n in ROW_BIASES})

    def kernel(*refs):
        r = Box()
        for n, ref in zip(ins + list(outs), refs):
            setattr(r, n, ref)
        m = lax.axis_index("mp")

        def cast(src, dst):
            def one(rows):
                dst[rows, :] = src[rows, :].astype(dst.dtype)

            rows_loop(src.shape[0], 256, one)

        cast(r.enc_o, r.enc.at[0])
        cast(r.down_o, r.down)
        cast(r.up_o, r.up)
        cast(r.out_o, r.out)
        for o in range(3):
            cast(r.qkv_o.at[o], r.qkv.at[o])
            cast(r.c2_o.at[o * D : (o + 1) * D], r.c2.at[o])
            r.c1[o] = r.c1_o[o * mels : (o + 1) * mels, :].astype(F32)
        row = lax.broadcasted_iota(jnp.int32, (128, 256), 0)
        lane = lax.broadcasted_iota(jnp.int32, (128, 256), 1)
        even = jnp.where(lane == 2 * row, 1.0, 0.0).astype(BF)
        odd = jnp.where(lane == 2 * row + 1, 1.0, 0.0).astype(BF)
        for k in range(T2 // 128):
            rows = slice(k * 128, (k + 1) * 128)
            value = tn(r.mel_o[rows, 0:128], even) + tn(r.mel_o[rows, 128:256], odd)
            r.mel[0, :, k * 256 : (k + 1) * 256] = value[0:mels, :]
        for k, n in enumerate(ROW_BIASES):
            getattr(r, n)[...] = r.small_o[k : k + 1, :].reshape(D)
        r.qkvb[...] = r.small_o[QB : QB + 2, pl.ds(pl.multiple_of(m * half, 128), half)]
        for k in range(side):
            r.upb[k * D : (k + 1) * D] = r.small_o[pl.ds(UPB + m * side + k, 1), :].reshape(D)

    vmem = pl.BlockSpec(memory_space=pltpu.VMEM)
    done = pl.pallas_call(
        kernel,
        name="finish",
        out_shape=[jax.ShapeDtypeStruct(*o) for o in outs.values()],
        in_specs=[vmem] * len(ins),
        out_specs=[vmem] * len(outs),
        compiler_params=pltpu.CompilerParams(vmem_limit_bytes=VMEM_LIMIT),
    )(*got.values())
    return dict(zip(outs, done))


def sine_tables(frames, channels, fine):
    half_width = channels // 2
    rate = np.exp(-(math.log(10000.0) / (half_width - 1)) * np.arange(half_width))
    small = np.arange(fine)[:, None] * rate[None, :]
    large = np.arange(0, frames, fine)[:, None] * rate[None, :]
    table = dict(fine_s=np.sin(small), fine_c=np.cos(small), coarse_s=np.sin(large), coarse_c=np.cos(large))
    return {n: jnp.asarray(t, F32) for n, t in table.items()}


def on_device(
    mel_input,
    conv1_weight,
    conv1_bias,
    conv2_weight,
    conv2_bias,
    norm1_gain,
    norm1_bias,
    qkv_weight,
    qkv_bias,
    out_weight,
    out_bias,
    norm2_gain,
    norm2_bias,
    up_weight,
    up_bias,
    down_weight,
    down_bias,
    cotangent,
    speech_mask,
):
    mels = mel_input.shape[1]
    T, D = cotangent.shape[1] // 2, cotangent.shape[2]
    F2 = up_weight.shape[1]
    side, half = F2 // D, D // 2
    bits = (lax.axis_size("dp") - 1).bit_length()
    lanes = -(-3 * mels // 128) * 128
    near = dict(
        w1=conv1_weight,
        mask=speech_mask,
        qkvb=qkv_bias,
        upb=up_bias,
        c1b=conv1_bias,
        c2b=conv2_bias,
        n1g=norm1_gain,
        n1b=norm1_bias,
        oub=out_bias,
        n2g=norm2_gain,
        n2b=norm2_bias,
        dnb=down_bias,
    )
    near.update(sine_tables(4 * T, D, 32))
    got = run_layer(
        bits,
        near,
        dict(
            mel=mel_input,
            cot=cotangent,
            w2_l=conv2_weight,
            wqkv_l=qkv_weight,
            wo_l=out_weight,
            up_l=up_weight,
            down_l=down_weight,
        ),
        dict(
            enc_o=((2 * T, D), BF),
            mel_o=((2 * T, 256), BF),
            down_o=((F2, D), BF),
            up_o=((D, F2), BF),
            out_o=((half, D), BF),
            qkv_o=((3, D, half), BF),
            c2_o=((3 * D, D), BF),
            c1_o=((lanes, D), BF),
            small_o=((16, D), F32),
        ),
        T,
        D,
        F2,
        lanes,
    )
    done = run_finish(got, mels, side)
    names = ("enc", "mel", "c1", "c1b", "c2", "c2b", "n1g", "n1b", "qkv", "qkvb")
    names += ("out", "oub", "n2g", "n2b", "up", "upb", "down", "dnb")
    return tuple(done[n] for n in names)


def solution(mesh):
    placed = (
        P("dp", None, "seq"),
        P(),
        P(),
        P(),
        P(),
        P(),
        P(),
        P(None, None, "mp"),
        P(None, "mp"),
        P("mp", None),
        P(),
        P(),
        P(),
        P(None, "mp"),
        P("mp"),
        P("mp", None),
        P(),
        P("dp", "seq", None),
        P("dp", "seq"),
    )
    return jax.shard_map(
        on_device,
        mesh=mesh,
        in_specs=placed,
        out_specs=(
            P("dp", "seq", None),
            P("dp", None, "seq"),
            P(),
            P(),
            P(),
            P(),
            P(),
            P(),
            P(None, None, "mp"),
            P(None, "mp"),
            P("mp", None),
            P(),
            P(),
            P(),
            P(None, "mp"),
            P("mp"),
            P("mp", None),
            P(),
        ),
        check_vma=False,
    )
```

```python
import functools
import math

import jax
import jax.numpy as jnp
import numpy as np
from jax import lax
from jax.experimental import pallas as pl
from jax.experimental.pallas import tpu as pltpu
from jax.sharding import PartitionSpec as P

HEAD = 64
BF = jnp.bfloat16
F32 = jnp.float32
MESH = pl.DeviceIdType.MESH
VMEM_LIMIT = 61 * 1024 * 1024
C1B, C2B, N1G, N1B, OUB, N2G, N2B, DNB, QB, VB, UPB = range(11)


class Box:
    pass


def dot(a, b, ca, cb):
    return lax.dot_general(a, b, (((ca,), (cb,)), ((), ())), preferred_element_type=F32)


def nn(a, b):
    return dot(a, b, 1, 0)


def nt(a, b):
    return dot(a, b, 1, 1)


def tn(a, b):
    return dot(a, b, 0, 0)


def rows_loop(total, step, body, unroll=1):
    step = min(step, total)

    def one(i, carry):
        body(pl.ds(pl.multiple_of(i * step, step), step))
        return carry

    lax.fori_loop(0, total // step, one, 0, unroll=unroll)


def gelu_parts(v):
    t = 1.0 / (1.0 + (0.3275911 / math.sqrt(2.0)) * jnp.abs(v))
    e = jnp.exp(-0.5 * v * v)
    poly = 1.061405429 * t - 1.453152027
    poly = poly * t + 1.421413741
    poly = poly * t - 0.284496736
    poly = poly * t + 0.254829592
    tail = (0.5 * t) * poly * e
    return jnp.where(v >= 0, 1.0 - tail, tail), e * (1.0 / math.sqrt(2.0 * math.pi))


def gelu_both(v):
    cdf, pdf = gelu_parts(v)
    return v * cdf, cdf + v * pdf


def normal(x):
    center = x - jnp.mean(x, axis=-1, keepdims=True)
    spread = jnp.mean(center * center, axis=-1, keepdims=True)
    inv = lax.rsqrt(spread + 1e-05)
    return center * inv, inv


def normal_pull(gy, hat, inv):
    return inv * (
        gy
        - jnp.mean(gy, axis=-1, keepdims=True)
        - hat * jnp.mean(gy * hat, axis=-1, keepdims=True)
    )


def vec(r, i):
    return r.vecs[i : i + 1, :]


def add_small(r, i, value):
    r.small[i : i + 1, :] += value


def col(value):
    return jnp.sum(value, axis=0, keepdims=True)


def stage_mel_rows(r, sub):
    T, D = r.stream.shape
    row = lax.broadcasted_iota(jnp.int32, (256, 256), 0)
    lane = lax.broadcasted_iota(jnp.int32, (256, 256), 1)
    pick = jnp.where(lane == 2 * (row % 128) + row // 128, 1.0, 0.0).astype(BF)
    base = sub * 2 * T

    def lanes(start, size):
        return r.melbuf[:, pl.ds(pl.multiple_of(base + start, 128), size)]

    row = lax.broadcasted_iota(jnp.int32, (16, 128), 0)
    lane = lax.broadcasted_iota(jnp.int32, (16, 128), 1)

    def select(at, to):
        return jnp.where(jnp.logical_and(row == to, lane == at), 1.0, 0.0).astype(BF)

    before, after = lanes(0, 128), lanes(128 + 2 * T, 128)
    r.mele[0:8, :] = nt(select(126, 7), before)[0:8, :]
    r.melo[0:8, :] = nt(select(127, 7), before)[0:8, :]
    r.mele[T + 8 : T + 16, :] = nt(select(0, 0), after)[0:8, :]
    for k in range(T // 128):
        both = nt(pick, lanes(128 + 256 * k, 256))
        r.mele[8 + 128 * k : 136 + 128 * k, :] = both[0:128, :]
        r.melo[8 + 128 * k : 136 + 128 * k, :] = both[128:256, :]


def three(a, b, c):
    return jnp.concatenate([a, b, c], axis=1).astype(BF)


def stage_first(r, first):
    T, D = r.stream.shape
    for o in range(3):
        r.w1p[128 * o : 128 * o + r.w1.shape[1], :] = r.w1[o]
        r.w1p[128 * o + r.w1.shape[1] : 128 * (o + 1), :] = jnp.zeros((128 - r.w1.shape[1], D), BF)
    w1 = r.w1p[...]
    edge = nn(three(r.mele[0:16, :], r.melo[0:16, :], r.mele[1:17, :]), w1) + vec(r, C1B)
    edge = gelu_both(edge)[0] * jnp.where(first, 0.0, 1.0)
    r.odd[0:8, :] = edge[0:8, :]
    r.xe[...] = three(r.melo[7 : 7 + T, :], r.mele[8 : 8 + T, :], r.melo[8 : 8 + T, :])
    r.xo[...] = three(r.mele[8 : 8 + T, :], r.melo[8 : 8 + T, :], r.mele[9 : 9 + T, :])
    r.tmp[...] = nn(r.xe[...], w1)

    def even(rows):
        value, slope = gelu_both(r.tmp[rows, :] + vec(r, C1B))
        r.he[rows, :] = value.astype(BF)
        r.dge[rows, :] = slope

    rows_loop(T, 32, even)
    r.tmp[...] = nn(r.xo[...], w1)

    def odd(rows):
        value, slope = gelu_both(r.tmp[rows, :] + vec(r, C1B))
        r.ho[rows, :] = value.astype(BF)
        r.odd[pl.ds(pl.multiple_of(rows.start + 8, 8), rows.size), :] = value
        r.dgo[rows, :] = slope

    rows_loop(T, 32, odd)


def stage_second(r, place):
    T, D = r.stream.shape
    r.hp[...] = r.odd[7 : 7 + T, :].astype(BF)
    r.tmp[...] = nn(r.hp[...], r.w2[0]) + nn(r.he[...], r.w2[1]) + nn(r.ho[...], r.w2[2])
    fine = r.fine_s.shape[0]

    def second(rows):
        value, slope = gelu_both(r.tmp[rows, :] + vec(r, C2B))
        at = place * (T // fine) + rows.start // fine
        s0, c0 = r.coarse_s[pl.ds(at, 1), :], r.coarse_c[pl.ds(at, 1), :]
        s1, c1 = r.fine_s[...], r.fine_c[...]
        stream = value + jnp.concatenate([s0 * c1 + c0 * s1, c0 * c1 - s0 * s1], axis=1)
        r.dg2[rows, :] = slope
        r.stream[rows, :] = stream
        r.normed[rows, :] = (normal(stream)[0] * vec(r, N1G) + vec(r, N1B)).astype(BF)

    rows_loop(T, fine, second)


def stage_mask(r, sub):
    T, D = r.stream.shape
    row = r.mask[0:1, pl.ds(pl.multiple_of(sub * T, 128), T)].astype(F32)
    r.wide[0:T, :] = jnp.broadcast_to(row, (128, T)).T

    def one(rows):
        keep = r.wide[rows, :]
        keep = jnp.concatenate([keep] * (D // 128), axis=1)
        r.bg[rows, :] = (r.bg[rows, :].astype(F32) * keep).astype(BF)

    rows_loop(T, 32, one)


def stage_qkv(r, part):
    T, D = r.stream.shape
    half, qr = D // 2, D // 4
    bias, scale = ((QB, HEAD**-0.5), (None, 1.0), (VB, 1.0))[part]
    for h in range(2):
        value = nn(r.normed[...], r.wqkv[h, part])
        if bias is not None:
            value = value + r.vecs[bias : bias + 1, h * half : (h + 1) * half]
        value = (value.astype(BF).astype(F32) * scale).T.astype(BF)
        for k in range(2):
            at = (3 * (3 + k) + part) * half + h * qr
            r.kv[at : at + qr, :] = value[k * qr : (k + 1) * qr, :]


def at_head(start, h):
    return pl.ds(pl.multiple_of(start + h * HEAD, HEAD), HEAD)


def head_loop(steps, hooks, body):
    def one(step, carry):
        for at, todo in hooks.items():

            @pl.when(step == at)
            def _(todo=todo):
                for act in todo:
                    act()

        body(step)
        return carry

    lax.fori_loop(0, steps, one, 0)


def attend(r, c, hooks):
    S, T = r.kv.shape[0] // 15, r.kv.shape[1]
    heads = S // HEAD
    r.top[...] = jnp.full(r.top.shape, -jnp.inf, F32)
    r.total[...] = jnp.zeros(r.total.shape, F32)
    r.mixt[...] = jnp.zeros(r.mixt.shape, F32)

    def body(step):
        g, h = step // heads, step % heads
        own = (3 - g) // 3
        slot = own * (3 + c) + (1 - own) * ((g + 1) % 3)
        k = r.kv[at_head((3 * slot + 1) * S, h), :]
        v = r.kv[at_head((3 * slot + 2) * S, h), :]
        for i, home in enumerate((3 + c, 2)):
            q = r.kv[at_head(3 * home * S, h), :]
            s = tn(k, q)
            before = r.top[i * heads + h]
            top = jnp.maximum(before, jnp.max(s, axis=0, keepdims=True))
            p = jnp.exp(s - top)
            keep = jnp.exp(before - top)
            rows = at_head(i * S, h)
            r.top[i * heads + h] = top
            r.total[i * heads + h] = keep * r.total[i * heads + h] + jnp.sum(p, axis=0, keepdims=True)
            r.mixt[rows, :] = keep * r.mixt[rows, :] + nn(v, p.astype(BF))

    head_loop(4 * heads, hooks, body)


def attend_end(r, i):
    S = r.kv.shape[0] // 15
    heads = S // HEAD

    def one(h, carry):
        rows = at_head(i * S, h)
        total = r.total[i * heads + h]
        value = r.mixt[rows, :] * (1.0 / total)
        r.mixt[rows, :] = value
        r.mixb[rows, :] = value.astype(BF)
        r.top[i * heads + h] = r.top[i * heads + h] + jnp.log(total)
        return carry

    lax.fori_loop(0, heads, one, 0)


def stage_mid(r, c):
    T, D = r.stream.shape
    half = D // 2
    r.tmp[...] = tn(r.mixb[0:half, :], r.wo[rows16(c * half, half), :])
    r.tmp[...] += tn(r.mix_got[...], r.wo[rows16((1 - c) * half, half), :])

    def one(rows):
        mid = r.stream[rows, :] + r.tmp[rows, :] + vec(r, OUB)
        r.mid[rows, :] = mid
        r.ntwo[rows, :] = (normal(mid)[0] * vec(r, N2G) + vec(r, N2B)).astype(BF)

    rows_loop(T, 32, one)


def stage_ff(r):
    T, D = r.stream.shape
    side = r.up.shape[2] // D
    parts, width = 2 * side, D
    add_small(r, DNB, col(r.bg[...].astype(F32)))

    def chunk(j, carry):
        into, at = j // side, j % side
        up = r.up[into, :, pl.ds(pl.multiple_of(at * D, D), D)]
        down = r.down[pl.ds(pl.multiple_of(j * D, D), D), :]
        r.tmp[...] = nn(r.ntwo[...], up)
        r.tmp2[...] = nt(r.bg[...], down)
        bias = r.vecs[pl.ds(UPB + j, 1), :]

        def one(i, acc):
            rows = pl.ds(pl.multiple_of(i * 32, 32), 32)
            value, slope = gelu_both(r.tmp[rows, :] + bias)
            r.act[rows, :] = value.astype(BF)
            grad = (r.tmp2[rows, :] * slope).astype(BF)
            r.ing[rows, :] = grad
            return acc + col(grad.astype(F32))

        r.small[pl.ds(UPB + j, 1), :] = lax.fori_loop(0, T // 32, one, jnp.zeros((1, width), F32))
        act = r.act[...]
        ing = r.ing[...]
        out = nn(act, down)
        back = nt(ing, up)

        @pl.when(j == 0)
        def _():
            r.ffo[...] = out
            r.ntg[...] = back

        @pl.when(j > 0)
        def _():
            r.ffo[...] += out
            r.ntg[...] += back

        r.g_down[pl.ds(pl.multiple_of(j * D, D), D), :] = tn(act, r.bg[...]).astype(BF)
        base = into * (r.g_up.shape[0] // 2) + at * D
        r.g_up[pl.ds(pl.multiple_of(base, 16), D), :] = tn(r.ntwo[...], ing).astype(BF)
        return carry

    lax.fori_loop(0, parts, chunk, 0)


def stage_mid_pull(r):
    T, D = r.stream.shape

    def one(i, accs):
        rows = pl.ds(pl.multiple_of(i * 32, 32), 32)
        mid = r.mid[rows, :]
        enc = (mid + r.ffo[rows, :] + vec(r, DNB)).astype(BF)
        hat, inv = normal(mid)
        grad = r.ntg[rows, :]
        smg = r.bg[rows, :].astype(F32) + normal_pull(grad * vec(r, N2G), hat, inv)
        r.enc[rows, :] = enc
        r.smg[rows, :] = smg
        attg = smg.astype(BF)
        r.attg[rows, :] = attg
        return accs[0] + col(grad * hat), accs[1] + col(grad), accs[2] + col(attg.astype(F32))

    zero = jnp.zeros((1, D), F32)
    gain, bias, out_bias = lax.fori_loop(0, T // 32, one, (zero, zero, zero))
    add_small(r, N2G, gain)
    add_small(r, N2B, bias)
    add_small(r, OUB, out_bias)


def stage_do(r, c, own):
    half = r.attg.shape[1] // 2
    k = c if own else 1 - c
    value = nt(r.wo[rows16(k * half, half), :], r.attg[...]).astype(BF)
    if own:
        r.dot[0:half, :] = value
    else:
        r.dot_out[...] = value


def stage_out_weights(r, c):
    D = r.attg.shape[1]
    half, qr = D // 2, D // 4
    rows = r.g_up.shape[0] // 2
    for k, mix in ((c, r.mixb[0:half, :]), (1 - c, r.mix_got[...])):
        value = nn(mix, r.attg[...]).astype(BF)
        for h in range(2):
            r.g_up[rows16(h * rows + rows - half + k * qr, qr), :] = value[h * qr : (h + 1) * qr, :]


def stage_diag(r, i):
    S = r.kv.shape[0] // 15
    heads = S // HEAD

    def one(h, carry):
        rows = at_head(i * S, h)
        value = r.dot[rows, :].astype(F32) * r.mixt[rows, :]
        r.diag[i * heads + h] = jnp.sum(value, axis=0, keepdims=True)
        return carry

    lax.fori_loop(0, heads, one, 0)


def attend_pull(r, c, hooks):
    S, T = r.kv.shape[0] // 15, r.kv.shape[1]
    heads = S // HEAD
    r.dqt[...] = jnp.zeros(r.dqt.shape, F32)

    def body(step):
        g, h = step // heads, step % heads
        slot = g + (g // 3) * c
        k = r.kv[at_head((3 * slot + 1) * S, h), :]
        v = r.kv[at_head((3 * slot + 2) * S, h), :]
        dk, dv = None, None
        for i, home in enumerate((3 + c, 2)):
            q = r.kv[at_head(3 * home * S, h), :]
            rows = at_head(i * S, h)
            do = r.dot[rows, :]
            p = jnp.exp(tn(k, q) - r.top[i * heads + h])
            ds = (p * (tn(v, do) - r.diag[i * heads + h])).astype(BF)
            dv_i, dk_i = nt(do, p.astype(BF)), nt(q, ds)
            dk, dv = (dk_i, dv_i) if dk is None else (dk + dk_i, dv + dv_i)
            r.dqt[rows, :] += nn(k, ds)
        r.dkv[at_head(2 * g * S, h), :] = dk.astype(BF)
        r.dkv[at_head((2 * g + 1) * S, h), :] = dv.astype(BF)

    head_loop(4 * heads, hooks, body)


def piece_of(r, part, h):
    D, qr = r.attg.shape[1], r.attg.shape[1] // 4
    at = part * D + h * qr
    return jnp.concatenate([r.dsum[at : at + qr, :], r.dsum[at + 2 * qr : at + 3 * qr, :]], axis=0)


def stage_qkv_weights(r):
    T, D = r.stream.shape
    half = D // 2
    r.normedt[...] = r.normed[...].astype(F32).T.astype(BF)
    ones = jnp.ones((8, T), BF)
    for part in range(3):
        for h in range(2):
            piece = piece_of(r, part, h)
            if part != 1:
                row = QB if part == 0 else VB
                r.small[row : row + 1, h * half : (h + 1) * half] = nt(ones, piece)[0:1, :]
            grad = nt(r.normedt[...], piece).astype(BF)
            at = (3 * h + part) * half
            r.g_qkv[at : at + half, 0:half] = grad[0:half, :]
            r.g_qkv[at : at + half, half:D] = grad[half:D, :]


def stage_qkv_pull(r):
    T, D = r.stream.shape
    total = None
    for part in range(3):
        for h in range(2):
            back = nn(r.wqkv[h, part], piece_of(r, part, h))
            total = back if total is None else total + back
    r.tmp[...] = total.T

    def one(i, accs):
        rows = pl.ds(pl.multiple_of(i * 32, 32), 32)
        hat, inv = normal(r.stream[rows, :])
        grad = r.tmp[rows, :]
        back = r.smg[rows, :] + normal_pull(grad * vec(r, N1G), hat, inv)
        sg = (back * r.dg2[rows, :]).astype(BF)
        r.sg[rows, :] = sg
        return accs[0] + col(grad * hat), accs[1] + col(grad), accs[2] + col(sg.astype(F32))

    zero = jnp.zeros((1, D), F32)
    gain, bias, c2b = lax.fori_loop(0, T // 32, one, (zero, zero, zero))
    add_small(r, N1G, gain)
    add_small(r, N1B, bias)
    add_small(r, C2B, c2b)


def stage_conv2_pull(r, next_row):
    T, D = r.stream.shape
    sg = r.sg[...]
    r.shift[0:T, :] = nt(sg, r.w2[0])
    r.shift[T : T + 16, :] = nt(next_row, r.w2[0])
    r.tmp[...] = nt(sg, r.w2[1])
    r.tmp2[...] = nt(sg, r.w2[2]) + r.shift[1 : T + 1, :]

    def one(i, acc):
        rows = pl.ds(pl.multiple_of(i * 32, 32), 32)
        even = (r.tmp[rows, :] * r.dge[rows, :]).astype(BF)
        odd = (r.tmp2[rows, :] * r.dgo[rows, :]).astype(BF)
        r.fe[rows, :] = even
        r.fo[rows, :] = odd
        return acc + col(even.astype(F32)) + col(odd.astype(F32))

    add_small(r, C1B, lax.fori_loop(0, T // 32, one, jnp.zeros((1, D), F32)))


def stage_conv2_weights(r):
    D = r.stream.shape[1]
    sg = r.sg[...]
    for i, tap in enumerate((r.hp, r.he, r.ho)):
        value = tn(tap[...], sg).astype(BF)
        r.g_c2[i * D : (i + 1) * D, :] = value


def stage_conv1_weights(r):
    value = (tn(r.xe[...], r.fe[...]) + tn(r.xo[...], r.fo[...])).astype(BF)
    mels = r.w1.shape[1]
    for o in range(3):
        r.g_c1[mels * o : mels * (o + 1), :] = value[128 * o : 128 * o + mels, :]
    r.g_c1[3 * mels :, :] = jnp.zeros((r.g_c1.shape[0] - 3 * mels, r.g_c1.shape[1]), BF)


def stage_mel(r, next_row, prev_row):
    T, D = r.stream.shape
    fe, fo = r.fe[...], r.fo[...]
    w = [r.w1p[128 * o : 128 * (o + 1), :] for o in range(3)]
    r.wide[16 : 16 + T, :] = nt(fo, w[2])
    r.wide[0:16, :] = nt(prev_row, w[2])
    r.melg[:, 0:128] = (nt(fe, w[1]) + nt(fo, w[0]) + r.wide[15 : 15 + T, :]).astype(BF)
    r.wide[0:T, :] = nt(fe, w[0])
    r.wide[T : T + 16, :] = nt(next_row, w[0])
    r.melg[:, 128:256] = (nt(fe, w[2]) + nt(fo, w[1]) + r.wide[1 : 1 + T, :]).astype(BF)


class Net:
    def __init__(self, r, bits):
        self.r, self.bits, self.used, self.used_here = r, bits, 0, 0
        self.d, self.c, self.m = (lax.axis_index(n) for n in ("dp", "seq", "mp"))

    def bit(self, dim):
        if dim == "c":
            return self.c
        if dim == "y":
            return self.m
        return (self.d // (1 << dim)) % 2

    def peer(self, dim):
        if dim == "c":
            return (self.d, 1 - self.c, self.m)
        if dim == "y":
            return (self.d, self.c, 1 - self.m)
        if dim == "cy":
            return (self.d, 1 - self.c, 1 - self.m)
        step = 1 << dim
        return (self.d + step - 2 * step * self.bit(dim), self.c, self.m)

    def greet(self):
        barrier = pltpu.get_barrier_semaphore()
        dims = ["c", "y", "cy"] + list(range(self.bits))
        for dim in dims:
            pl.semaphore_signal(barrier, inc=1, device_id=self.peer(dim), device_id_type=MESH)
        pl.semaphore_wait(barrier, len(dims))

    def copy(self, src, dst, dim):
        i = self.used
        self.used += 1
        return pltpu.make_async_remote_copy(
            src_ref=src,
            dst_ref=dst,
            send_sem=self.r.send.at[i],
            recv_sem=self.r.recv.at[i],
            device_id=self.peer(dim),
            device_id_type=MESH,
        )

    def send(self, src, dst, dim):
        copy = self.copy(src, dst, dim)
        copy.start()
        return copy

    def here(self, src, dst):
        i = self.used_here
        self.used_here += 1
        copy = pltpu.make_async_copy(src, dst, self.r.own.at[i])
        copy.start()
        return copy


def start_all(copies):
    for copy in copies:
        copy.start()


def wait_all(copies):
    for copy in copies:
        copy.wait()


def rows16(start, size):
    return pl.ds(pl.multiple_of(start, 16), size)


def sum_plan(rows, halves, order):
    steps, need = [], 0
    for dim in order:
        if dim == "y" and halves == 2:
            steps.append((dim, "other", rows))
            halves = 1
        elif rows % 32 == 0:
            rows //= 2
            steps.append((dim, "halve", rows))
        else:
            steps.append((dim, "swap", rows))
        need += rows * halves
    return steps, need


class Track:
    def __init__(self, acts):
        self.acts = list(acts)

    def take(self):
        return [self.acts.pop(0)] if self.acts else []


def bucket_sum(net, g, got, done, halves, order):
    R = g.shape[0] // halves
    lo, rows, at, bases = 0, R, 0, [h * R for h in range(halves)]
    acts, back, end = [], [], None

    def start_after(end, copies):
        def act():
            if end is not None:
                end()
            for copy in copies:
                copy.start()

        return act

    def adder(copies, places, n):
        step = 64 if n % 64 == 0 else 32 if n % 32 == 0 else 16

        def end():
            wait_all(copies)
            for to, of in places:

                def add(k, carry, to=to, of=of):
                    mine = rows16(to + k * step, step)
                    value = g[mine, :].astype(F32) + got[rows16(of + k * step, step), :].astype(F32)
                    g[mine, :] = value.astype(BF)
                    return carry

                lax.fori_loop(0, n // step, add, 0)

        return end

    for dim, kind, n in sum_plan(R, halves, order)[0]:
        b = net.bit(dim)
        keep = give = lo
        givers = bases
        if kind == "halve":
            keep, give = lo + b * n, lo + (1 - b) * n
            back.append((dim, n, lo))
        if kind == "other":
            givers, bases = [(1 - b) * R], [b * R]
        copies = [
            net.copy(g.at[rows16(base + give, n)], got.at[rows16(at + i * n, n)], dim)
            for i, base in enumerate(givers)
        ]
        acts.append(start_after(end, copies))
        end = adder(copies, [(base + keep, at + i * n) for i, base in enumerate(bases)], n)
        at += n * len(bases)
        lo, rows = keep, n

    def settle(end=end, lo=lo, base=bases[0], rows=rows):
        end()
        for k in range(rows // 16):
            done[rows16(lo + 16 * k, 16), :] = g[rows16(base + lo + 16 * k, 16), :]

    end = settle
    for dim, n, before in reversed(back):
        part = rows16(lo, n)
        copy = net.copy(done.at[part], done.at[part], dim)
        acts.append(start_after(end, [copy]))
        end = copy.wait
        lo = before
    return Track(acts + [end])


def small_sum(net, value, slots, order):
    acts, end = [], None
    for i, dim in enumerate(order):
        copy = net.copy(value, slots.at[i], dim)

        def act(end=end, copy=copy):
            if end is not None:
                end()
            copy.start()

        def end(copy=copy, i=i):
            copy.wait()
            value[...] += slots[i]

        acts.append(act)
    return Track(acts + [end])


def advance(*sums):
    for one in sums:
        for act in one.take():
            act()


def drain(*sums):
    while any(one.acts for one in sums):
        advance(*sums)


def quarter(net):
    return 2 * net.c + net.c + net.m - 2 * net.c * net.m


def choose(slots, by_core, by_y):
    core = jnp.where(by_core, 1.0, 0.0)
    y = jnp.where(by_y, 1.0, 0.0)
    return (slots[0].astype(F32) * core + slots[1].astype(F32) * y).astype(BF)


def pick_next(net, slots):
    q = quarter(net)
    return choose(slots, q == 1, q % 2 == 0)


def pick_prev(net, slots):
    q = quarter(net)
    return choose(slots, q == 2, q % 2 == 1)


ROW_BIASES = ("c1b", "c2b", "n1g", "n1b", "oub", "n2g", "n2b", "dnb")


def orders(bits):
    dims = list(range(bits))
    z_first = dims[1:2] + dims[:1] + dims[2:]
    return dict(
        down=["c", "y"] + dims,
        up=["c"] + dims + ["y"],
        qkv=["c"] + z_first + ["y"],
        c2a=["c", "y"] + dims,
        c2b=["c"] + dims[:1] + ["y"] + dims[1:],
        c1=["c"] + dims + ["y"],
        vec=["c"] + dims + ["y"],
    )


def layer(r, bits):
    T, D = r.stream.shape
    half, F2 = D // 2, r.down_l.shape[0]
    side = F2 // D
    mels, span = r.w1.shape[1], 4 * T
    net = Net(r, bits)
    c, m = net.c, net.m
    sub = c + m - 2 * c * m
    order = orders(bits)
    rows_of_mine = rows16(sub * T, T)

    r.melbuf[...] = jnp.zeros_like(r.melbuf)
    r.vec_mine[...] = jnp.zeros_like(r.vec_mine)
    own_lanes = pl.ds(pl.multiple_of(m * half, 128), half)
    r.vec_mine[0:2, own_lanes] = r.qkvb[...].astype(F32)
    for k in range(side):
        r.vec_mine[pl.ds(2 + m * side + k, 1), :] = r.upb[k * D : (k + 1) * D].astype(F32).reshape(1, D)
    for k, n in enumerate(ROW_BIASES):
        r.vecs[k : k + 1, :] = getattr(r, n)[...].astype(F32).reshape(1, D)
    net.greet()
    mel_own = net.here(r.mel.at[0], r.melbuf.at[0:mels, 128 : 128 + span])
    qkv_own = net.here(r.wqkv_l, r.wqkv.at[m])
    w2_own = net.here(r.w2_l, r.w2)
    own = [
        net.here(r.wo_l.at[0 : D // 4], r.wo.at[rows16(m * (D // 4), D // 4)]),
        net.here(r.wo_l.at[D // 4 : half], r.wo.at[rows16(half + m * (D // 4), D // 4)]),
        net.here(r.up_l, r.up.at[m]),
        net.here(r.down_l, r.down.at[rows16(m * F2, F2)]),
        net.here(r.cot.at[0, rows_of_mine], r.bg),
    ]
    vec_copy = net.send(r.vec_mine, r.vec_got, "y")
    mel_own.wait()
    src = pl.ds(pl.multiple_of(128 + (1 - c) * (span - 128), 128), 128)
    dst = pl.ds(pl.multiple_of(c * (span + 128), 128), 128)
    mel_rim = net.send(r.melbuf.at[0:mels, src], r.melbuf.at[0:mels, dst], "c")
    piece = rows16(c * half, half)
    qkv_own.wait()
    mine = r.wqkv.at[m, :, piece]
    qkv_y = net.send(mine, mine, "y")

    p = 4 * c + 2 * net.bit(0) + net.bit(1) if bits > 1 else 2 * c + net.bit(0)
    cuts = 8 if bits > 1 else 4

    def pass_on(of, at, count, dim):
        def cut(n, base):
            return rows16(base + at * (n // cuts), count * (n // cuts))

        wo = rows16(c * half + of * (D // 4) + (at - c * (cuts // 2)) * (half // cuts), count * (half // cuts))
        parts = [r.wo.at[wo], r.up.at[of, cut(D, 0)], r.down.at[cut(F2, of * F2)]]
        return [net.copy(x, x, dim) for x in parts]

    r.small[...] = jnp.zeros_like(r.small)
    mel_rim.wait()
    stage_mel_rows(r, sub)
    stage_first(r, jnp.logical_and(c == 0, m == 0))
    qkv_y.wait()
    arrived = r.wqkv.at[1 - m, :, piece]
    qkv_c = net.send(arrived, arrived, "c")
    wait_all(own)
    ff_y = pass_on(m, p, 1, "y")
    start_all(ff_y)
    w2_own.wait()
    stage_second(r, quarter(net))
    vec_copy.wait()
    r.vecs[8:16, :] = r.vec_mine[...] + r.vec_got[...]
    qkv_c.wait()

    def block(slot, part, parts=1):
        return r.kv.at[rows16((3 * slot + part) * half, parts * half)]

    to_c, to_y, to_d = [], [], []
    for part in (0, 1, 2):
        stage_qkv(r, part)
        to_c.append(net.send(block(4 - c, part), block(2, part), "c"))
        if part > 0:
            to_y.append(net.send(block(3 + c, part), block(0, part), "y"))
            to_d.append(net.send(block(4 - c, part), block(1, part), "cy"))
    wait_all(ff_y)
    ff_z = pass_on(1 - m, p, 1, 1) if bits > 1 else []
    start_all(ff_z)
    ff_x = pass_on(1 - m, (p // 2) * 2 if bits > 1 else p, 2 if bits > 1 else 1, 0)
    ff_c = pass_on(1 - m, c * (cuts // 2), cuts // 2, "c")
    stage_mask(r, sub)
    to_c[0].wait()
    heads = half // HEAD
    attend(
        r,
        c,
        {
            heads: [lambda: wait_all(to_c[1:]), lambda: wait_all(ff_z), lambda: start_all(ff_x)],
            2 * heads: [lambda: wait_all(ff_x), lambda: start_all(ff_c), lambda: wait_all(to_y)],
            3 * heads: [lambda: wait_all(to_d)],
        },
    )
    attend_end(r, 1)
    mix_c = net.send(r.mixb.at[half:D], r.mix_got, "c")
    attend_end(r, 0)
    wait_all(ff_c)
    mix_c.wait()
    stage_mid(r, c)
    stage_ff(r)

    def summed(n, halves):
        refs = [getattr(r, kind + n) for kind in ("g_", "got_", "done_")]
        return bucket_sum(net, *refs, halves, order[n])

    down_sum = summed("down", 2)
    advance(down_sum)
    stage_mid_pull(r)
    stage_do(r, c, False)
    do_c = net.send(r.dot_out, r.dot.at[half:D], "c")
    stage_out_weights(r, c)
    up_sum = summed("up", 2)
    advance(up_sum, down_sum)
    stage_do(r, c, True)
    stage_diag(r, 0)
    do_c.wait()
    stage_diag(r, 1)
    enc = [
        net.copy(r.enc, r.enc_got, "y"),
        pltpu.make_async_copy(r.enc, r.enc_o.at[rows_of_mine], r.own.at[39]),
    ]

    both = half * 2
    home_y = net.copy(r.dkv.at[0:both], r.from_y, "y")
    home_d = net.copy(r.dkv.at[both : 2 * both], r.from_d, "cy")
    home_c = net.copy(r.dkv.at[2 * both : 3 * both], r.from_c.at[half:], "c")
    hooks = {}

    def at_step(step, *acts):
        hooks.setdefault(step * heads // 4, []).extend(acts)

    at_step(1, *up_sum.take())
    at_step(4, home_y.start, *down_sum.take())
    at_step(6, *up_sum.take(), *down_sum.take())
    at_step(8, home_d.start)
    at_step(9, *up_sum.take(), *down_sum.take())
    at_step(11, lambda: start_all(enc))
    at_step(12, home_c.start, *up_sum.take(), *down_sum.take())
    for step in (13, 14, 15):
        at_step(step, *up_sum.take(), *down_sum.take())
    attend_pull(r, c, hooks)
    r.dq_out[...] = (r.dqt[half:D, :] * HEAD**-0.5).astype(BF)
    dq_c = net.send(r.dq_out, r.from_c.at[0:half], "c")
    r.dsum[rows16(c * half, half), :] = (r.dqt[0:half, :] * HEAD**-0.5).astype(BF)
    home_y.wait()
    home_d.wait()
    home_c.wait()

    def total(i, carry):
        for part in range(2):
            rows = rows16(part * half + i * 32, 32)
            mine = r.dkv[rows16(3 * both + part * half + i * 32, 32), :].astype(F32) + r.from_y[rows, :].astype(F32)
            r.dsum[rows16((1 + part) * D + c * half + i * 32, 32), :] = mine.astype(BF)
            other = r.from_c[rows16((1 + part) * half + i * 32, 32), :].astype(F32) + r.from_d[rows, :].astype(F32)
            r.dsum[rows16((1 + part) * D + (1 - c) * half + i * 32, 32), :] = other.astype(BF)
        return carry

    lax.fori_loop(0, half // 32, total, 0)
    dq_c.wait()
    r.dsum[rows16((1 - c) * half, half), :] = r.from_c[0:half, :]

    stage_qkv_weights(r)
    qkv_sum = summed("qkv", 2)
    advance(qkv_sum, up_sum)
    stage_qkv_pull(r)
    rim = [net.send(r.sg.at[0:16], r.slots.at[0, i], dim) for i, dim in enumerate(("c", "y"))]
    advance(qkv_sum)
    stage_conv2_weights(r)
    c2a_sum, c2b_sum = summed("c2a", 1), summed("c2b", 1)
    advance(c2a_sum, c2b_sum)
    wait_all(rim)
    stage_conv2_pull(r, pick_next(net, r.slots.at[0]))
    rim = [net.send(r.fe.at[0:16], r.slots.at[1, i], dim) for i, dim in enumerate(("c", "y"))]
    rim += [net.send(r.fo.at[T - 16 : T], r.slots.at[2, i], dim) for i, dim in enumerate(("c", "y"))]
    advance(c2a_sum, c2b_sum, qkv_sum)
    stage_conv1_weights(r)
    c1_sum = summed("c1", 1)
    vec_sum = small_sum(net, r.small, r.got_small, order["vec"])
    advance(c1_sum, vec_sum)
    wait_all(rim)
    stage_mel(r, pick_next(net, r.slots.at[1]), pick_prev(net, r.slots.at[2]))
    rows_of_yours = rows16((1 - sub) * T, T)
    mel_y = net.send(r.melg, r.melg_got, "y")
    wait_all(enc)
    ends = [
        net.here(r.enc_got, r.enc_o.at[rows_of_yours]),
        net.here(r.melg, r.mel_o.at[rows_of_mine]),
    ]
    drain(c1_sum, vec_sum, c2a_sum, c2b_sum, qkv_sum, up_sum, down_sum)

    ends.append(net.here(r.done_down, r.down_o))
    for j in range(side):
        ends.append(net.here(r.done_up.at[j * D : (j + 1) * D], r.up_o.at[:, j * D : (j + 1) * D]))
    ends.append(net.here(r.done_up.at[side * D : side * D + half], r.out_o))
    for part in range(3):
        for j in range(2):
            ends.append(
                net.here(
                    r.done_qkv.at[part * half : (part + 1) * half, j * half : (j + 1) * half],
                    r.qkv_o.at[part, j * half : (j + 1) * half],
                )
            )
    ends.append(net.here(r.done_c2a, r.c2_o.at[0 : 3 * half]))
    ends.append(net.here(r.done_c2b, r.c2_o.at[3 * half : 6 * half]))
    ends.append(net.here(r.done_c1, r.c1_o))
    ends.append(net.here(r.small, r.small_o))
    mel_y.wait()
    ends.append(net.here(r.melg_got, r.mel_o.at[rows_of_yours]))
    wait_all(ends)


def run_layer(bits, near, far, outs, T, D, F2, lanes):
    half, H = D // 2, D // HEAD
    td, dt = (T, D), (D, T)
    order = orders(bits)
    buckets = dict(down=(F2, 2), up=(F2 + half, 2), qkv=(3 * half, 2), c2a=(3 * half, 1), c2b=(3 * half, 1), c1=(lanes, 1))
    scratch = dict(
        melbuf=((128, 4 * T + 256), BF),
        mele=((T + 24, 128), F32),
        melo=((T + 24, 128), F32),
        xe=((T, 384), BF),
        xo=((T, 384), BF),
        w1p=((384, D), BF),
        w2=((3, D, D), BF),
        bg=(td, BF),
        wqkv=((2, 3, D, half), BF),
        wo=((D, D), BF),
        up=((2, D, F2), BF),
        down=((2 * F2, D), BF),
        vecs=((16, D), F32),
        vec_mine=((8, D), F32),
        vec_got=((8, D), F32),
        stream=(td, F32),
        he=(td, BF),
        ho=(td, BF),
        hp=(td, BF),
        dge=(td, F32),
        dgo=(td, F32),
        dg2=(td, F32),
        normed=(td, BF),
        kv=((15 * half, T), BF),
        mixt=(dt, F32),
        mixb=(dt, BF),
        mix_got=((half, T), BF),
        dot=(dt, BF),
        dot_out=((half, T), BF),
        top=((H, 1, T), F32),
        total=((H, 1, T), F32),
        diag=((H, 1, T), F32),
        tmp=(td, F32),
        tmp2=(td, F32),
        shift=((T + 16, D), F32),
        wide=((T + 16, 128), F32),
        mid=(td, F32),
        ntwo=(td, BF),
        act=(td, BF),
        ing=(td, BF),
        ffo=(td, F32),
        ntg=(td, F32),
        attg=(td, BF),
        dqt=(dt, F32),
        dq_out=((half, T), BF),
        dkv=((8 * half, T), BF),
        from_y=((2 * half, T), BF),
        from_d=((2 * half, T), BF),
        from_c=((3 * half, T), BF),
        dsum=((3 * D, T), BF),
        enc_got=(td, BF),
        melg=((T, 256), BF),
        melg_got=((T, 256), BF),
        small=((16, D), F32),
        got_small=((bits + 2, 16, D), F32),
        slots=((3, 2, 16, D), BF),
    )
    alias = T == D
    for n, (rows, halves) in buckets.items():
        if n == "c1" or n in ("down", "up"):
            scratch["g_" + n] = ((rows * halves, D), BF)
        scratch["got_" + n] = ((sum_plan(rows, halves, order[n])[1], D), BF)
        scratch["done_" + n] = ((rows, D), BF)
    if not alias:
        scratch.update(g_qkv=((6 * half, D), BF), g_c2=((6 * half, D), BF), normedt=(dt, BF))
    names = list(near) + list(far) + list(outs) + list(scratch) + ["send", "recv", "own"]

    def kernel(*refs):
        r = Box()
        for n, ref in zip(names, refs):
            setattr(r, n, ref)
        r.odd, r.smg, r.sg, r.fe, r.fo, r.enc = r.shift, r.mid, r.ntwo, r.act, r.ing, r.bg
        r.normedt = r.mixb if alias else r.normedt
        if alias:
            r.g_qkv, r.g_c2 = r.kv.at[0 : 6 * half], r.kv.at[6 * half : 12 * half]
        r.g_c2a, r.g_c2b = r.g_c2.at[0 : 3 * half], r.g_c2.at[3 * half : 6 * half]
        layer(r, bits)

    vmem, anywhere = pl.BlockSpec(memory_space=pltpu.VMEM), pl.BlockSpec(memory_space=pl.ANY)
    got = pl.pallas_call(
        kernel,
        name="layer",
        out_shape=[jax.ShapeDtypeStruct(*o) for o in outs.values()],
        in_specs=[vmem] * len(near) + [anywhere] * len(far),
        out_specs=[anywhere] * len(outs),
        scratch_shapes=[pltpu.VMEM(*s) for s in scratch.values()]
        + [pltpu.SemaphoreType.DMA((200,)), pltpu.SemaphoreType.DMA((200,)), pltpu.SemaphoreType.DMA((40,))],
        compiler_params=pltpu.CompilerParams(
            vmem_limit_bytes=VMEM_LIMIT, collective_id=1, has_side_effects=True
        ),
    )(*near.values(), *far.values())
    return dict(zip(outs, got))


def run_finish(got, mels, side):
    T2, D = got["enc_o"].shape
    half = D // 2
    ins = list(got)
    outs = dict(
        enc=((1, T2, D), BF),
        mel=((1, mels, 2 * T2), F32),
        c1=((3, mels, D), F32),
        c2=((3, D, D), F32),
        qkv=((3, D, half), F32),
        qkvb=((2, half), F32),
        out=((half, D), F32),
        up=((D, side * D), F32),
        upb=((side * D,), F32),
        down=((side * D, D), F32),
    )
    outs.update({n: ((D,), F32) for n in ROW_BIASES})

    def kernel(*refs):
        r = Box()
        for n, ref in zip(ins + list(outs), refs):
            setattr(r, n, ref)
        m = lax.axis_index("mp")

        def cast(src, dst):
            def one(rows):
                dst[rows, :] = src[rows, :].astype(dst.dtype)

            rows_loop(src.shape[0], 256, one)

        cast(r.enc_o, r.enc.at[0])
        cast(r.down_o, r.down)
        cast(r.up_o, r.up)
        cast(r.out_o, r.out)
        for o in range(3):
            cast(r.qkv_o.at[o], r.qkv.at[o])
            cast(r.c2_o.at[o * D : (o + 1) * D], r.c2.at[o])
            r.c1[o] = r.c1_o[o * mels : (o + 1) * mels, :].astype(F32)
        row = lax.broadcasted_iota(jnp.int32, (128, 256), 0)
        lane = lax.broadcasted_iota(jnp.int32, (128, 256), 1)
        even = jnp.where(lane == 2 * row, 1.0, 0.0).astype(BF)
        odd = jnp.where(lane == 2 * row + 1, 1.0, 0.0).astype(BF)
        for k in range(T2 // 128):
            rows = slice(k * 128, (k + 1) * 128)
            value = tn(r.mel_o[rows, 0:128], even) + tn(r.mel_o[rows, 128:256], odd)
            r.mel[0, :, k * 256 : (k + 1) * 256] = value[0:mels, :]
        for k, n in enumerate(ROW_BIASES):
            getattr(r, n)[...] = r.small_o[k : k + 1, :].reshape(D)
        r.qkvb[...] = r.small_o[QB : QB + 2, pl.ds(pl.multiple_of(m * half, 128), half)]
        for k in range(side):
            r.upb[k * D : (k + 1) * D] = r.small_o[pl.ds(UPB + m * side + k, 1), :].reshape(D)

    vmem = pl.BlockSpec(memory_space=pltpu.VMEM)
    done = pl.pallas_call(
        kernel,
        name="finish",
        out_shape=[jax.ShapeDtypeStruct(*o) for o in outs.values()],
        in_specs=[vmem] * len(ins),
        out_specs=[vmem] * len(outs),
        compiler_params=pltpu.CompilerParams(vmem_limit_bytes=VMEM_LIMIT),
    )(*got.values())
    return dict(zip(outs, done))


def sine_tables(frames, channels, fine):
    half_width = channels // 2
    rate = np.exp(-(math.log(10000.0) / (half_width - 1)) * np.arange(half_width))
    small = np.arange(fine)[:, None] * rate[None, :]
    large = np.arange(0, frames, fine)[:, None] * rate[None, :]
    table = dict(fine_s=np.sin(small), fine_c=np.cos(small), coarse_s=np.sin(large), coarse_c=np.cos(large))
    return {n: jnp.asarray(t, F32) for n, t in table.items()}


def on_device(
    mel_input,
    conv1_weight,
    conv1_bias,
    conv2_weight,
    conv2_bias,
    norm1_gain,
    norm1_bias,
    qkv_weight,
    qkv_bias,
    out_weight,
    out_bias,
    norm2_gain,
    norm2_bias,
    up_weight,
    up_bias,
    down_weight,
    down_bias,
    cotangent,
    speech_mask,
):
    mels = mel_input.shape[1]
    T, D = cotangent.shape[1] // 2, cotangent.shape[2]
    F2 = up_weight.shape[1]
    side, half = F2 // D, D // 2
    bits = (lax.axis_size("dp") - 1).bit_length()
    lanes = -(-3 * mels // 128) * 128
    near = dict(
        w1=conv1_weight,
        mask=speech_mask,
        qkvb=qkv_bias,
        upb=up_bias,
        c1b=conv1_bias,
        c2b=conv2_bias,
        n1g=norm1_gain,
        n1b=norm1_bias,
        oub=out_bias,
        n2g=norm2_gain,
        n2b=norm2_bias,
        dnb=down_bias,
    )
    near.update(sine_tables(4 * T, D, 32))
    got = run_layer(
        bits,
        near,
        dict(
            mel=mel_input,
            cot=cotangent,
            w2_l=conv2_weight,
            wqkv_l=qkv_weight,
            wo_l=out_weight,
            up_l=up_weight,
            down_l=down_weight,
        ),
        dict(
            enc_o=((2 * T, D), BF),
            mel_o=((2 * T, 256), BF),
            down_o=((F2, D), BF),
            up_o=((D, F2), BF),
            out_o=((half, D), BF),
            qkv_o=((3, D, half), BF),
            c2_o=((3 * D, D), BF),
            c1_o=((lanes, D), BF),
            small_o=((16, D), F32),
        ),
        T,
        D,
        F2,
        lanes,
    )
    done = run_finish(got, mels, side)
    names = ("enc", "mel", "c1", "c1b", "c2", "c2b", "n1g", "n1b", "qkv", "qkvb")
    names += ("out", "oub", "n2g", "n2b", "up", "upb", "down", "dnb")
    return tuple(done[n] for n in names)


def solution(mesh):
    placed = (
        P("dp", None, "seq"),
        P(),
        P(),
        P(),
        P(),
        P(),
        P(),
        P(None, None, "mp"),
        P(None, "mp"),
        P("mp", None),
        P(),
        P(),
        P(),
        P(None, "mp"),
        P("mp"),
        P("mp", None),
        P(),
        P("dp", "seq", None),
        P("dp", "seq"),
    )
    return jax.shard_map(
        on_device,
        mesh=mesh,
        in_specs=placed,
        out_specs=(
            P("dp", "seq", None),
            P("dp", None, "seq"),
            P(),
            P(),
            P(),
            P(),
            P(),
            P(),
            P(None, None, "mp"),
            P(None, "mp"),
            P("mp", None),
            P(),
            P(),
            P(),
            P(None, "mp"),
            P("mp"),
            P("mp", None),
            P(),
        ),
        check_vma=False,
    )
```

```python
import functools
import math

import jax
import jax.numpy as jnp
import numpy as np
from jax import lax
from jax.experimental import pallas as pl
from jax.experimental.pallas import tpu as pltpu
from jax.sharding import PartitionSpec as P

HEAD = 64
BF = jnp.bfloat16
F32 = jnp.float32
MESH = pl.DeviceIdType.MESH
VMEM_LIMIT = 61 * 1024 * 1024
C1B, C2B, N1G, N1B, OUB, N2G, N2B, DNB, QB, VB, UPB = range(11)


class Box:
    pass


def dot(a, b, ca, cb):
    return lax.dot_general(a, b, (((ca,), (cb,)), ((), ())), preferred_element_type=F32)


def nn(a, b):
    return dot(a, b, 1, 0)


def nt(a, b):
    return dot(a, b, 1, 1)


def tn(a, b):
    return dot(a, b, 0, 0)


def rows_loop(total, step, body, unroll=1):
    step = min(step, total)

    def one(i, carry):
        body(pl.ds(pl.multiple_of(i * step, step), step))
        return carry

    lax.fori_loop(0, total // step, one, 0, unroll=unroll)


def gelu_parts(v):
    t = 1.0 / (1.0 + (0.3275911 / math.sqrt(2.0)) * jnp.abs(v))
    e = jnp.exp(-0.5 * v * v)
    poly = 1.061405429 * t - 1.453152027
    poly = poly * t + 1.421413741
    poly = poly * t - 0.284496736
    poly = poly * t + 0.254829592
    tail = (0.5 * t) * poly * e
    return jnp.where(v >= 0, 1.0 - tail, tail), e * (1.0 / math.sqrt(2.0 * math.pi))


def gelu_both(v):
    cdf, pdf = gelu_parts(v)
    return v * cdf, cdf + v * pdf


def normal(x):
    center = x - jnp.mean(x, axis=-1, keepdims=True)
    spread = jnp.mean(center * center, axis=-1, keepdims=True)
    inv = lax.rsqrt(spread + 1e-05)
    return center * inv, inv


def normal_pull(gy, hat, inv):
    return inv * (
        gy
        - jnp.mean(gy, axis=-1, keepdims=True)
        - hat * jnp.mean(gy * hat, axis=-1, keepdims=True)
    )


def vec(r, i):
    return r.vecs[i : i + 1, :]


def add_small(r, i, value):
    r.small[i : i + 1, :] += value


def col(value):
    return jnp.sum(value, axis=0, keepdims=True)


def stage_mel_rows(r, sub):
    T, D = r.stream.shape
    row = lax.broadcasted_iota(jnp.int32, (256, 256), 0)
    lane = lax.broadcasted_iota(jnp.int32, (256, 256), 1)
    pick = jnp.where(lane == 2 * (row % 128) + row // 128, 1.0, 0.0).astype(BF)
    base = sub * 2 * T

    def lanes(start, size):
        return r.melbuf[:, pl.ds(pl.multiple_of(base + start, 128), size)]

    row = lax.broadcasted_iota(jnp.int32, (16, 128), 0)
    lane = lax.broadcasted_iota(jnp.int32, (16, 128), 1)

    def select(at, to):
        return jnp.where(jnp.logical_and(row == to, lane == at), 1.0, 0.0).astype(BF)

    before, after = lanes(0, 128), lanes(128 + 2 * T, 128)
    r.mele[0:8, :] = nt(select(126, 7), before)[0:8, :]
    r.melo[0:8, :] = nt(select(127, 7), before)[0:8, :]
    r.mele[T + 8 : T + 16, :] = nt(select(0, 0), after)[0:8, :]
    for k in range(T // 128):
        both = nt(pick, lanes(128 + 256 * k, 256))
        r.mele[8 + 128 * k : 136 + 128 * k, :] = both[0:128, :]
        r.melo[8 + 128 * k : 136 + 128 * k, :] = both[128:256, :]


def three(a, b, c):
    return jnp.concatenate([a, b, c], axis=1).astype(BF)


def stage_first(r, first):
    T, D = r.stream.shape
    for o in range(3):
        r.w1p[128 * o : 128 * o + r.w1.shape[1], :] = r.w1[o]
        r.w1p[128 * o + r.w1.shape[1] : 128 * (o + 1), :] = jnp.zeros((128 - r.w1.shape[1], D), BF)
    w1 = r.w1p[...]
    edge = nn(three(r.mele[0:16, :], r.melo[0:16, :], r.mele[1:17, :]), w1) + vec(r, C1B)
    edge = gelu_both(edge)[0] * jnp.where(first, 0.0, 1.0)
    r.odd[0:8, :] = edge[0:8, :]
    r.xe[...] = three(r.melo[7 : 7 + T, :], r.mele[8 : 8 + T, :], r.melo[8 : 8 + T, :])
    r.xo[...] = three(r.mele[8 : 8 + T, :], r.melo[8 : 8 + T, :], r.mele[9 : 9 + T, :])
    r.tmp[...] = nn(r.xe[...], w1)

    def even(rows):
        value, slope = gelu_both(r.tmp[rows, :] + vec(r, C1B))
        r.he[rows, :] = value.astype(BF)
        r.dge[rows, :] = slope

    rows_loop(T, 32, even)
    r.tmp[...] = nn(r.xo[...], w1)

    def odd(rows):
        value, slope = gelu_both(r.tmp[rows, :] + vec(r, C1B))
        r.ho[rows, :] = value.astype(BF)
        r.odd[pl.ds(pl.multiple_of(rows.start + 8, 8), rows.size), :] = value
        r.dgo[rows, :] = slope

    rows_loop(T, 32, odd)


def stage_second(r, place):
    T, D = r.stream.shape
    r.hp[...] = r.odd[7 : 7 + T, :].astype(BF)
    r.tmp[...] = nn(r.hp[...], r.w2[0]) + nn(r.he[...], r.w2[1]) + nn(r.ho[...], r.w2[2])
    fine = r.fine_s.shape[0]

    def second(rows):
        value, slope = gelu_both(r.tmp[rows, :] + vec(r, C2B))
        at = place * (T // fine) + rows.start // fine
        s0, c0 = r.coarse_s[pl.ds(at, 1), :], r.coarse_c[pl.ds(at, 1), :]
        s1, c1 = r.fine_s[...], r.fine_c[...]
        stream = value + jnp.concatenate([s0 * c1 + c0 * s1, c0 * c1 - s0 * s1], axis=1)
        r.dg2[rows, :] = slope
        r.stream[rows, :] = stream
        r.normed[rows, :] = (normal(stream)[0] * vec(r, N1G) + vec(r, N1B)).astype(BF)

    rows_loop(T, fine, second)


def stage_mask(r, sub):
    T, D = r.stream.shape
    row = r.mask[0:1, pl.ds(pl.multiple_of(sub * T, 128), T)].astype(F32)
    r.wide[0:T, :] = jnp.broadcast_to(row, (128, T)).T

    def one(rows):
        keep = r.wide[rows, :]
        keep = jnp.concatenate([keep] * (D // 128), axis=1)
        r.bg[rows, :] = (r.bg[rows, :].astype(F32) * keep).astype(BF)

    rows_loop(T, 32, one)


def stage_qkv(r, part):
    T, D = r.stream.shape
    half, qr = D // 2, D // 4
    bias, scale = ((QB, HEAD**-0.5), (None, 1.0), (VB, 1.0))[part]
    for h in range(2):
        value = nn(r.normed[...], r.wqkv[h, part])
        if bias is not None:
            value = value + r.vecs[bias : bias + 1, h * half : (h + 1) * half]
        value = (value.astype(BF).astype(F32) * scale).T.astype(BF)
        for k in range(2):
            at = (3 * (3 + k) + part) * half + h * qr
            r.kv[at : at + qr, :] = value[k * qr : (k + 1) * qr, :]


def at_head(start, h):
    return pl.ds(pl.multiple_of(start + h * HEAD, HEAD), HEAD)


def head_loop(steps, hooks, body):
    def one(step, carry):
        for at, todo in hooks.items():

            @pl.when(step == at)
            def _(todo=todo):
                for act in todo:
                    act()

        body(step)
        return carry

    lax.fori_loop(0, steps, one, 0)


def attend(r, c, hooks):
    S, T = r.kv.shape[0] // 15, r.kv.shape[1]
    heads = S // HEAD
    r.top[...] = jnp.full(r.top.shape, -jnp.inf, F32)
    r.total[...] = jnp.zeros(r.total.shape, F32)
    r.mixt[...] = jnp.zeros(r.mixt.shape, F32)

    def body(step):
        g, h = step // heads, step % heads
        own = (3 - g) // 3
        slot = own * (3 + c) + (1 - own) * ((g + 1) % 3)
        k = r.kv[at_head((3 * slot + 1) * S, h), :]
        v = r.kv[at_head((3 * slot + 2) * S, h), :]
        for i, home in enumerate((3 + c, 2)):
            q = r.kv[at_head(3 * home * S, h), :]
            s = tn(k, q)
            before = r.top[i * heads + h]
            top = jnp.maximum(before, jnp.max(s, axis=0, keepdims=True))
            p = jnp.exp(s - top)
            keep = jnp.exp(before - top)
            rows = at_head(i * S, h)
            r.top[i * heads + h] = top
            r.total[i * heads + h] = keep * r.total[i * heads + h] + jnp.sum(p, axis=0, keepdims=True)
            r.mixt[rows, :] = keep * r.mixt[rows, :] + nn(v, p.astype(BF))

    head_loop(4 * heads, hooks, body)


def attend_end(r, i):
    S = r.kv.shape[0] // 15
    heads = S // HEAD

    def one(h, carry):
        rows = at_head(i * S, h)
        total = r.total[i * heads + h]
        value = r.mixt[rows, :] * (1.0 / total)
        r.mixt[rows, :] = value
        r.mixb[rows, :] = value.astype(BF)
        r.top[i * heads + h] = r.top[i * heads + h] + jnp.log(total)
        return carry

    lax.fori_loop(0, heads, one, 0)


def stage_mid(r, c):
    T, D = r.stream.shape
    half = D // 2
    r.tmp[...] = tn(r.mixb[0:half, :], r.wo[rows16(c * half, half), :])
    r.tmp[...] += tn(r.mix_got[...], r.wo[rows16((1 - c) * half, half), :])

    def one(rows):
        mid = r.stream[rows, :] + r.tmp[rows, :] + vec(r, OUB)
        r.mid[rows, :] = mid
        r.ntwo[rows, :] = (normal(mid)[0] * vec(r, N2G) + vec(r, N2B)).astype(BF)

    rows_loop(T, 32, one)


def stage_ff(r):
    T, D = r.stream.shape
    side = r.up.shape[2] // D
    parts, width = 2 * side, D
    add_small(r, DNB, col(r.bg[...].astype(F32)))

    def chunk(j, carry):
        into, at = j // side, j % side
        up = r.up[into, :, pl.ds(pl.multiple_of(at * D, D), D)]
        down = r.down[pl.ds(pl.multiple_of(j * D, D), D), :]
        r.tmp[...] = nn(r.ntwo[...], up)
        r.tmp2[...] = nt(r.bg[...], down)
        bias = r.vecs[pl.ds(UPB + j, 1), :]

        def one(i, acc):
            rows = pl.ds(pl.multiple_of(i * 32, 32), 32)
            value, slope = gelu_both(r.tmp[rows, :] + bias)
            r.act[rows, :] = value.astype(BF)
            grad = (r.tmp2[rows, :] * slope).astype(BF)
            r.ing[rows, :] = grad
            return acc + col(grad.astype(F32))

        r.small[pl.ds(UPB + j, 1), :] = lax.fori_loop(0, T // 32, one, jnp.zeros((1, width), F32))
        act = r.act[...]
        ing = r.ing[...]
        out = nn(act, down)
        back = nt(ing, up)

        @pl.when(j == 0)
        def _():
            r.ffo[...] = out
            r.ntg[...] = back

        @pl.when(j > 0)
        def _():
            r.ffo[...] += out
            r.ntg[...] += back

        r.g_down[pl.ds(pl.multiple_of(j * D, D), D), :] = tn(act, r.bg[...]).astype(BF)
        base = into * (r.g_up.shape[0] // 2) + at * D
        r.g_up[pl.ds(pl.multiple_of(base, 16), D), :] = tn(r.ntwo[...], ing).astype(BF)
        return carry

    lax.fori_loop(0, parts, chunk, 0)


def stage_mid_pull(r):
    T, D = r.stream.shape

    def one(i, accs):
        rows = pl.ds(pl.multiple_of(i * 32, 32), 32)
        mid = r.mid[rows, :]
        enc = (mid + r.ffo[rows, :] + vec(r, DNB)).astype(BF)
        hat, inv = normal(mid)
        grad = r.ntg[rows, :]
        smg = r.bg[rows, :].astype(F32) + normal_pull(grad * vec(r, N2G), hat, inv)
        r.enc[rows, :] = enc
        r.smg[rows, :] = smg
        attg = smg.astype(BF)
        r.attg[rows, :] = attg
        return accs[0] + col(grad * hat), accs[1] + col(grad), accs[2] + col(attg.astype(F32))

    zero = jnp.zeros((1, D), F32)
    gain, bias, out_bias = lax.fori_loop(0, T // 32, one, (zero, zero, zero))
    add_small(r, N2G, gain)
    add_small(r, N2B, bias)
    add_small(r, OUB, out_bias)


def stage_do(r, c, own):
    half = r.attg.shape[1] // 2
    k = c if own else 1 - c
    value = nt(r.wo[rows16(k * half, half), :], r.attg[...]).astype(BF)
    if own:
        r.dot[0:half, :] = value
    else:
        r.dot_out[...] = value


def stage_out_weights(r, c):
    D = r.attg.shape[1]
    half, qr = D // 2, D // 4
    rows = r.g_up.shape[0] // 2
    for k, mix in ((c, r.mixb[0:half, :]), (1 - c, r.mix_got[...])):
        value = nn(mix, r.attg[...]).astype(BF)
        for h in range(2):
            r.g_up[rows16(h * rows + rows - half + k * qr, qr), :] = value[h * qr : (h + 1) * qr, :]


def stage_diag(r, i):
    S = r.kv.shape[0] // 15
    heads = S // HEAD

    def one(h, carry):
        rows = at_head(i * S, h)
        value = r.dot[rows, :].astype(F32) * r.mixt[rows, :]
        r.diag[i * heads + h] = jnp.sum(value, axis=0, keepdims=True)
        return carry

    lax.fori_loop(0, heads, one, 0)


def attend_pull(r, c, hooks):
    S, T = r.kv.shape[0] // 15, r.kv.shape[1]
    heads = S // HEAD
    r.dqt[...] = jnp.zeros(r.dqt.shape, F32)

    def body(step):
        g, h = step // heads, step % heads
        slot = g + (g // 3) * c
        k = r.kv[at_head((3 * slot + 1) * S, h), :]
        v = r.kv[at_head((3 * slot + 2) * S, h), :]
        dk, dv = None, None
        for i, home in enumerate((3 + c, 2)):
            q = r.kv[at_head(3 * home * S, h), :]
            rows = at_head(i * S, h)
            do = r.dot[rows, :]
            p = jnp.exp(tn(k, q) - r.top[i * heads + h])
            ds = (p * (tn(v, do) - r.diag[i * heads + h])).astype(BF)
            dv_i, dk_i = nt(do, p.astype(BF)), nt(q, ds)
            dk, dv = (dk_i, dv_i) if dk is None else (dk + dk_i, dv + dv_i)
            r.dqt[rows, :] += nn(k, ds)
        r.dkv[at_head(2 * g * S, h), :] = dk.astype(BF)
        r.dkv[at_head((2 * g + 1) * S, h), :] = dv.astype(BF)

    head_loop(4 * heads, hooks, body)


def piece_of(r, part, h):
    D, qr = r.attg.shape[1], r.attg.shape[1] // 4
    at = part * D + h * qr
    return jnp.concatenate([r.dsum[at : at + qr, :], r.dsum[at + 2 * qr : at + 3 * qr, :]], axis=0)


def stage_qkv_weights(r):
    T, D = r.stream.shape
    half = D // 2
    r.normedt[...] = r.normed[...].astype(F32).T.astype(BF)
    ones = jnp.ones((8, T), BF)
    for part in range(3):
        for h in range(2):
            piece = piece_of(r, part, h)
            if part != 1:
                row = QB if part == 0 else VB
                r.small[row : row + 1, h * half : (h + 1) * half] = nt(ones, piece)[0:1, :]
            grad = nt(r.normedt[...], piece).astype(BF)
            at = (3 * h + part) * half
            r.g_qkv[at : at + half, 0:half] = grad[0:half, :]
            r.g_qkv[at : at + half, half:D] = grad[half:D, :]


def stage_qkv_pull(r):
    T, D = r.stream.shape
    total = None
    for part in range(3):
        for h in range(2):
            back = nn(r.wqkv[h, part], piece_of(r, part, h))
            total = back if total is None else total + back
    r.tmp[...] = total.T

    def one(i, accs):
        rows = pl.ds(pl.multiple_of(i * 32, 32), 32)
        hat, inv = normal(r.stream[rows, :])
        grad = r.tmp[rows, :]
        back = r.smg[rows, :] + normal_pull(grad * vec(r, N1G), hat, inv)
        sg = (back * r.dg2[rows, :]).astype(BF)
        r.sg[rows, :] = sg
        return accs[0] + col(grad * hat), accs[1] + col(grad), accs[2] + col(sg.astype(F32))

    zero = jnp.zeros((1, D), F32)
    gain, bias, c2b = lax.fori_loop(0, T // 32, one, (zero, zero, zero))
    add_small(r, N1G, gain)
    add_small(r, N1B, bias)
    add_small(r, C2B, c2b)


def stage_conv2_pull(r, next_row):
    T, D = r.stream.shape
    sg = r.sg[...]
    r.shift[0:T, :] = nt(sg, r.w2[0])
    r.shift[T : T + 16, :] = nt(next_row, r.w2[0])
    r.tmp[...] = nt(sg, r.w2[1])
    r.tmp2[...] = nt(sg, r.w2[2]) + r.shift[1 : T + 1, :]

    def one(i, acc):
        rows = pl.ds(pl.multiple_of(i * 32, 32), 32)
        even = (r.tmp[rows, :] * r.dge[rows, :]).astype(BF)
        odd = (r.tmp2[rows, :] * r.dgo[rows, :]).astype(BF)
        r.fe[rows, :] = even
        r.fo[rows, :] = odd
        return acc + col(even.astype(F32)) + col(odd.astype(F32))

    add_small(r, C1B, lax.fori_loop(0, T // 32, one, jnp.zeros((1, D), F32)))


def stage_conv2_weights(r):
    D = r.stream.shape[1]
    sg = r.sg[...]
    for i, tap in enumerate((r.hp, r.he, r.ho)):
        value = tn(tap[...], sg).astype(BF)
        r.g_c2[i * D : (i + 1) * D, :] = value


def stage_conv1_weights(r):
    value = (tn(r.xe[...], r.fe[...]) + tn(r.xo[...], r.fo[...])).astype(BF)
    mels = r.w1.shape[1]
    for o in range(3):
        r.g_c1[mels * o : mels * (o + 1), :] = value[128 * o : 128 * o + mels, :]
    r.g_c1[3 * mels :, :] = jnp.zeros((r.g_c1.shape[0] - 3 * mels, r.g_c1.shape[1]), BF)


def stage_mel(r, next_row, prev_row):
    T, D = r.stream.shape
    fe, fo = r.fe[...], r.fo[...]
    w = [r.w1p[128 * o : 128 * (o + 1), :] for o in range(3)]
    r.wide[16 : 16 + T, :] = nt(fo, w[2])
    r.wide[0:16, :] = nt(prev_row, w[2])
    r.melg[:, 0:128] = (nt(fe, w[1]) + nt(fo, w[0]) + r.wide[15 : 15 + T, :]).astype(BF)
    r.wide[0:T, :] = nt(fe, w[0])
    r.wide[T : T + 16, :] = nt(next_row, w[0])
    r.melg[:, 128:256] = (nt(fe, w[2]) + nt(fo, w[1]) + r.wide[1 : 1 + T, :]).astype(BF)


class Net:
    def __init__(self, r, bits):
        self.r, self.bits, self.used, self.used_here = r, bits, 0, 0
        self.d, self.c, self.m = (lax.axis_index(n) for n in ("dp", "seq", "mp"))

    def bit(self, dim):
        if dim == "c":
            return self.c
        if dim == "y":
            return self.m
        return (self.d // (1 << dim)) % 2

    def peer(self, dims):
        d = self.d
        for k in dims:
            if k not in ("c", "y"):
                d = d + (1 << k) - 2 * (1 << k) * self.bit(k)
        return (
            d,
            1 - self.c if "c" in dims else self.c,
            1 - self.m if "y" in dims else self.m,
        )

    def greet(self, partners):
        barrier = pltpu.get_barrier_semaphore()
        for dims in partners:
            pl.semaphore_signal(barrier, inc=1, device_id=self.peer(dims), device_id_type=MESH)
        pl.semaphore_wait(barrier, len(partners))

    def copy(self, src, dst, *dims):
        i = self.used
        self.used += 1
        return pltpu.make_async_remote_copy(
            src_ref=src,
            dst_ref=dst,
            send_sem=self.r.send.at[i],
            recv_sem=self.r.recv.at[i],
            device_id=self.peer(dims),
            device_id_type=MESH,
        )

    def send(self, src, dst, *dims):
        copy = self.copy(src, dst, *dims)
        copy.start()
        return copy

    def here(self, src, dst):
        i = self.used_here
        self.used_here += 1
        copy = pltpu.make_async_copy(src, dst, self.r.own.at[i])
        copy.start()
        return copy


def start_all(copies):
    for copy in copies:
        copy.start()


def wait_all(copies):
    for copy in copies:
        copy.wait()


def rows16(start, size):
    return pl.ds(pl.multiple_of(start, 16), size)


def subsets(dims):
    found = [()]
    for dim in dims:
        found += [one + (dim,) for one in found]
    return found[1:]


def sum_plan(rows, halves, order):
    steps, need = [], 0
    for dims in order:
        by_half = halves == 2 and "y" in dims
        cutting = [dim for dim in dims if not (by_half and dim == "y")]
        if rows % (16 << len(cutting)):
            cutting = []
        rows >>= len(cutting)
        if by_half:
            halves = 1
        steps.append((dims, cutting, rows, halves, by_half))
        need += rows * halves * len(subsets(dims))
    return steps, need


class Track:
    def __init__(self, acts):
        self.acts = list(acts)

    def take(self):
        return [self.acts.pop(0)] if self.acts else []


def bucket_sum(net, g, got, done, halves, order):
    R = g.shape[0] // halves
    lo, rows, at, bases = 0, R, 0, [h * R for h in range(halves)]
    acts, back, end = [], [], None

    def start_after(end, copies):
        def act():
            if end is not None:
                end()
            for copy in copies:
                copy.start()

        return act

    def adder(copies, places, n):
        step = 64 if n % 64 == 0 else 32 if n % 32 == 0 else 16

        def end():
            wait_all(copies)
            for to, ofs in places:

                def add(k, carry, to=to, ofs=ofs):
                    mine = rows16(to + k * step, step)
                    value = g[mine, :].astype(F32)
                    for of in ofs:
                        value = value + got[rows16(of + k * step, step), :].astype(F32)
                    g[mine, :] = value.astype(BF)
                    return carry

                lax.fori_loop(0, n // step, add, 0)

        return end

    for dims, cutting, n, _, by_half in sum_plan(R, halves, order)[0]:

        def part_of(other):
            start = lo
            for i, dim in enumerate(reversed(cutting)):
                b = net.bit(dim)
                start = start + (1 - b if dim in other else b) * (n << i)
            return start

        keep = part_of(())
        if by_half:
            bases = [net.m * R]
        copies, ofs = [], [[] for _ in bases]
        for other in subsets(dims):
            sources = [(1 - net.m) * R] if by_half and "y" in other else bases
            for i, base in enumerate(sources):
                src = g.at[rows16(base + part_of(other), n)]
                copies.append(net.copy(src, got.at[rows16(at, n)], *other))
                ofs[i].append(at)
                at += n
        acts.append(start_after(end, copies))
        end = adder(copies, [(base + keep, of) for base, of in zip(bases, ofs)], n)
        if cutting:
            back.append((cutting, n, lo))
        lo, rows = keep, n

    def settle(end=end, lo=lo, base=bases[0], rows=rows):
        end()
        for k in range(rows // 16):
            done[rows16(lo + 16 * k, 16), :] = g[rows16(base + lo + 16 * k, 16), :]

    end = settle
    for cutting, n, before in reversed(back):
        part = rows16(lo, n)
        copies = [net.copy(done.at[part], done.at[part], *other) for other in subsets(cutting)]
        acts.append(start_after(end, copies))
        end = functools.partial(wait_all, copies)
        lo = before
    return Track(acts + [end])


def small_sum(net, value, slots, order):
    acts, end, at = [], None, 0
    for dims in order:
        copies = [net.copy(value, slots.at[at + i], *other) for i, other in enumerate(subsets(dims))]

        def act(end=end, copies=copies):
            if end is not None:
                end()
            start_all(copies)

        def end(copies=copies, at=at):
            wait_all(copies)
            total = value[...]
            for i in range(len(copies)):
                total = total + slots[at + i]
            value[...] = total

        at += len(copies)
        acts.append(act)
    return Track(acts + [end])


def advance(*sums):
    for one in sums:
        for act in one.take():
            act()


def drain(*sums):
    while any(one.acts for one in sums):
        advance(*sums)


def quarter(net):
    return 2 * net.c + net.c + net.m - 2 * net.c * net.m


def choose(slots, by_core, by_y):
    core = jnp.where(by_core, 1.0, 0.0)
    y = jnp.where(by_y, 1.0, 0.0)
    return (slots[0].astype(F32) * core + slots[1].astype(F32) * y).astype(BF)


def pick_next(net, slots):
    q = quarter(net)
    return choose(slots, q == 1, q % 2 == 0)


def pick_prev(net, slots):
    q = quarter(net)
    return choose(slots, q == 2, q % 2 == 1)


ROW_BIASES = ("c1b", "c2b", "n1g", "n1b", "oub", "n2g", "n2b", "dnb")


def orders(bits):
    pairs = [tuple(range(k, min(k + 2, bits))) for k in range(1, bits, 2)]
    wide, near = [("c",), ("y", 0)], [("c", "y", 0)]
    return dict(
        down=wide + pairs,
        up=[("c",)] + pairs + [("y", 0)],
        qkv=wide + pairs,
        c2=wide + pairs,
        c1=near + pairs,
        vec=near + pairs,
    )


def layer(r, bits):
    T, D = r.stream.shape
    half, F2 = D // 2, r.down_l.shape[0]
    side = F2 // D
    mels, span = r.w1.shape[1], 4 * T
    net = Net(r, bits)
    c, m = net.c, net.m
    sub = c + m - 2 * c * m
    order = orders(bits)
    rows_of_mine = rows16(sub * T, T)

    r.melbuf[...] = jnp.zeros_like(r.melbuf)
    mel_own = net.here(r.mel.at[0], r.melbuf.at[0:mels, 128 : 128 + span])
    qkv_own = net.here(r.wqkv_l, r.wqkv.at[m])
    w2_own = net.here(r.w2_l, r.w2)
    own = [
        net.here(r.wo_l.at[0 : D // 4], r.wo.at[rows16(m * (D // 4), D // 4)]),
        net.here(r.wo_l.at[D // 4 : half], r.wo.at[rows16(half + m * (D // 4), D // 4)]),
        net.here(r.up_l, r.up.at[m]),
        net.here(r.down_l, r.down.at[rows16(m * F2, F2)]),
        net.here(r.cot.at[0, rows_of_mine], r.bg),
    ]
    r.vec_mine[...] = jnp.zeros_like(r.vec_mine)
    own_lanes = pl.ds(pl.multiple_of(m * half, 128), half)
    r.vec_mine[0:2, own_lanes] = r.qkvb[...].astype(F32)
    for k in range(side):
        r.vec_mine[pl.ds(2 + m * side + k, 1), :] = r.upb[k * D : (k + 1) * D].astype(F32).reshape(1, D)
    for k, n in enumerate(ROW_BIASES):
        r.vecs[k : k + 1, :] = getattr(r, n)[...].astype(F32).reshape(1, D)
    partners = [one for dims in order["c1"] for one in subsets(dims)]
    net.greet(partners)
    vec_copy = net.send(r.vec_mine, r.vec_got, "y")
    mel_own.wait()
    src = pl.ds(pl.multiple_of(128 + (1 - c) * (span - 128), 128), 128)
    dst = pl.ds(pl.multiple_of(c * (span + 128), 128), 128)
    mel_rim = net.send(r.melbuf.at[0:mels, src], r.melbuf.at[0:mels, dst], "c")
    piece = rows16(c * half, half)
    qkv_own.wait()
    mine = r.wqkv.at[m, :, piece]
    qkv_y = net.send(mine, mine, "y")

    p = 4 * c + 2 * net.bit(0) + net.bit(1) if bits > 1 else 2 * c + net.bit(0)
    cuts = 8 if bits > 1 else 4

    def pass_on(of, at, count, dim):
        def cut(n, base):
            return rows16(base + at * (n // cuts), count * (n // cuts))

        wo = rows16(c * half + of * (D // 4) + (at - c * (cuts // 2)) * (half // cuts), count * (half // cuts))
        parts = [r.wo.at[wo], r.up.at[of, cut(D, 0)], r.down.at[cut(F2, of * F2)]]
        return [net.copy(x, x, dim) for x in parts]

    r.small[...] = jnp.zeros_like(r.small)
    mel_rim.wait()
    stage_mel_rows(r, sub)
    stage_first(r, jnp.logical_and(c == 0, m == 0))
    qkv_y.wait()
    arrived = r.wqkv.at[1 - m, :, piece]
    qkv_c = net.send(arrived, arrived, "c")
    wait_all(own)
    ff_y = pass_on(m, p, 1, "y")
    start_all(ff_y)
    w2_own.wait()
    stage_second(r, quarter(net))
    vec_copy.wait()
    r.vecs[8:16, :] = r.vec_mine[...] + r.vec_got[...]
    qkv_c.wait()

    def block(slot, part, parts=1):
        return r.kv.at[rows16((3 * slot + part) * half, parts * half)]

    to_c, to_y, to_d = [], [], []
    for part in (1, 2, 0):
        stage_qkv(r, part)
        to_c.insert(0, net.send(block(4 - c, part), block(2, part), "c"))
        if part > 0:
            to_y.append(net.send(block(3 + c, part), block(0, part), "y"))
            to_d.append(net.send(block(4 - c, part), block(1, part), "c", "y"))
    wait_all(ff_y)
    ff_z = pass_on(1 - m, p, 1, 1) if bits > 1 else []
    start_all(ff_z)
    ff_x = pass_on(1 - m, (p // 2) * 2 if bits > 1 else p, 2 if bits > 1 else 1, 0)
    ff_c = pass_on(1 - m, c * (cuts // 2), cuts // 2, "c")
    stage_mask(r, sub)
    to_c[0].wait()
    heads = half // HEAD
    attend(
        r,
        c,
        {
            heads: [lambda: wait_all(to_c[1:]), lambda: wait_all(ff_z), lambda: start_all(ff_x)],
            2 * heads: [lambda: wait_all(ff_x), lambda: start_all(ff_c), lambda: wait_all(to_y)],
            3 * heads: [lambda: wait_all(to_d)],
        },
    )
    attend_end(r, 1)
    mix_c = net.send(r.mixb.at[half:D], r.mix_got, "c")
    attend_end(r, 0)
    wait_all(ff_c)
    mix_c.wait()
    stage_mid(r, c)
    stage_ff(r)

    def summed(n, halves):
        refs = [getattr(r, kind + n) for kind in ("g_", "got_", "done_")]
        return bucket_sum(net, *refs, halves, order[n])

    down_sum = summed("down", 2)
    advance(down_sum)
    stage_mid_pull(r)
    stage_do(r, c, False)
    do_c = net.send(r.dot_out, r.dot.at[half:D], "c")
    stage_out_weights(r, c)
    up_sum = summed("up", 2)
    advance(up_sum, down_sum)
    stage_do(r, c, True)
    stage_diag(r, 0)
    do_c.wait()
    stage_diag(r, 1)
    enc = [
        net.copy(r.enc, r.enc_got, "y"),
        pltpu.make_async_copy(r.enc, r.enc_o.at[rows_of_mine], r.own.at[39]),
    ]

    both = half * 2
    home_y = net.copy(r.dkv.at[0:both], r.from_y, "y")
    home_d = net.copy(r.dkv.at[both : 2 * both], r.from_d, "c", "y")
    home_c = net.copy(r.dkv.at[2 * both : 3 * both], r.from_c.at[half:], "c")
    hooks = {}

    def at_step(step, *acts):
        hooks.setdefault(step * heads // 4, []).extend(acts)

    at_step(1, *up_sum.take())
    at_step(4, home_y.start, *down_sum.take())
    at_step(8, home_d.start, *down_sum.take())
    at_step(11, lambda: start_all(enc), *up_sum.take(), *down_sum.take())
    at_step(12, home_c.start)
    at_step(13, *up_sum.take(), *down_sum.take())
    at_step(15, *up_sum.take(), *down_sum.take())
    attend_pull(r, c, hooks)
    r.dq_out[...] = (r.dqt[half:D, :] * HEAD**-0.5).astype(BF)
    dq_c = net.send(r.dq_out, r.from_c.at[0:half], "c")
    r.dsum[rows16(c * half, half), :] = (r.dqt[0:half, :] * HEAD**-0.5).astype(BF)
    home_y.wait()
    home_d.wait()
    home_c.wait()

    def total(i, carry):
        for part in range(2):
            rows = rows16(part * half + i * 32, 32)
            mine = r.dkv[rows16(3 * both + part * half + i * 32, 32), :].astype(F32) + r.from_y[rows, :].astype(F32)
            r.dsum[rows16((1 + part) * D + c * half + i * 32, 32), :] = mine.astype(BF)
            other = r.from_c[rows16((1 + part) * half + i * 32, 32), :].astype(F32) + r.from_d[rows, :].astype(F32)
            r.dsum[rows16((1 + part) * D + (1 - c) * half + i * 32, 32), :] = other.astype(BF)
        return carry

    lax.fori_loop(0, half // 32, total, 0)
    dq_c.wait()
    r.dsum[rows16((1 - c) * half, half), :] = r.from_c[0:half, :]

    stage_qkv_weights(r)
    qkv_sum = summed("qkv", 2)
    advance(qkv_sum, up_sum)
    stage_qkv_pull(r)
    rim = [net.send(r.sg.at[0:16], r.slots.at[0, i], dim) for i, dim in enumerate(("c", "y"))]
    advance(qkv_sum)
    stage_conv2_weights(r)
    c2_sum = summed("c2", 1)
    advance(c2_sum)
    wait_all(rim)
    stage_conv2_pull(r, pick_next(net, r.slots.at[0]))
    rim = [net.send(r.fe.at[0:16], r.slots.at[1, i], dim) for i, dim in enumerate(("c", "y"))]
    rim += [net.send(r.fo.at[T - 16 : T], r.slots.at[2, i], dim) for i, dim in enumerate(("c", "y"))]
    advance(c2_sum)
    stage_conv1_weights(r)
    c1_sum = summed("c1", 1)
    vec_sum = small_sum(net, r.small, r.got_small, order["vec"])
    advance(c1_sum, vec_sum, qkv_sum)
    wait_all(rim)
    stage_mel(r, pick_next(net, r.slots.at[1]), pick_prev(net, r.slots.at[2]))
    rows_of_yours = rows16((1 - sub) * T, T)
    mel_y = net.send(r.melg, r.melg_got, "y")
    wait_all(enc)
    ends = [
        net.here(r.enc_got, r.enc_o.at[rows_of_yours]),
        net.here(r.melg, r.mel_o.at[rows_of_mine]),
    ]
    drain(c1_sum, vec_sum, c2_sum, qkv_sum, up_sum, down_sum)

    ends.append(net.here(r.done_down, r.down_o))
    for j in range(side):
        ends.append(net.here(r.done_up.at[j * D : (j + 1) * D], r.up_o.at[:, j * D : (j + 1) * D]))
    ends.append(net.here(r.done_up.at[side * D : side * D + half], r.out_o))
    for part in range(3):
        for j in range(2):
            ends.append(
                net.here(
                    r.done_qkv.at[part * half : (part + 1) * half, j * half : (j + 1) * half],
                    r.qkv_o.at[part, j * half : (j + 1) * half],
                )
            )
    ends.append(net.here(r.done_c2, r.c2_o))
    ends.append(net.here(r.done_c1, r.c1_o))
    ends.append(net.here(r.small, r.small_o))
    mel_y.wait()
    ends.append(net.here(r.melg_got, r.mel_o.at[rows_of_yours]))
    wait_all(ends)


def run_layer(bits, near, far, outs, T, D, F2, lanes):
    half, H = D // 2, D // HEAD
    td, dt = (T, D), (D, T)
    order = orders(bits)
    buckets = dict(down=(F2, 2), up=(F2 + half, 2), qkv=(3 * half, 2), c2=(6 * half, 1), c1=(lanes, 1))
    scratch = dict(
        melbuf=((128, 4 * T + 256), BF),
        mele=((T + 24, 128), F32),
        melo=((T + 24, 128), F32),
        xe=((T, 384), BF),
        xo=((T, 384), BF),
        w1p=((384, D), BF),
        w2=((3, D, D), BF),
        bg=(td, BF),
        wqkv=((2, 3, D, half), BF),
        wo=((D, D), BF),
        up=((2, D, F2), BF),
        down=((2 * F2, D), BF),
        vecs=((16, D), F32),
        vec_mine=((8, D), F32),
        vec_got=((8, D), F32),
        stream=(td, F32),
        he=(td, BF),
        ho=(td, BF),
        hp=(td, BF),
        dge=(td, F32),
        dgo=(td, F32),
        dg2=(td, F32),
        normed=(td, BF),
        kv=((15 * half, T), BF),
        mixt=(dt, F32),
        mixb=(dt, BF),
        mix_got=((half, T), BF),
        dot=(dt, BF),
        dot_out=((half, T), BF),
        top=((H, 1, T), F32),
        total=((H, 1, T), F32),
        diag=((H, 1, T), F32),
        tmp=(td, F32),
        tmp2=(td, F32),
        shift=((T + 16, D), F32),
        wide=((T + 16, 128), F32),
        mid=(td, F32),
        ntwo=(td, BF),
        act=(td, BF),
        ing=(td, BF),
        ffo=(td, F32),
        ntg=(td, F32),
        attg=(td, BF),
        dqt=(dt, F32),
        dq_out=((half, T), BF),
        dkv=((8 * half, T), BF),
        from_y=((2 * half, T), BF),
        from_d=((2 * half, T), BF),
        from_c=((3 * half, T), BF),
        dsum=((3 * D, T), BF),
        enc_got=(td, BF),
        melg=((T, 256), BF),
        melg_got=((T, 256), BF),
        small=((16, D), F32),
        got_small=((sum(len(subsets(dims)) for dims in order["vec"]), 16, D), F32),
        slots=((3, 2, 16, D), BF),
    )
    alias = T == D
    for n, (rows, halves) in buckets.items():
        if n == "c1" or n in ("down", "up"):
            scratch["g_" + n] = ((rows * halves, D), BF)
        scratch["got_" + n] = ((sum_plan(rows, halves, order[n])[1], D), BF)
        scratch["done_" + n] = ((rows, D), BF)
    if not alias:
        scratch.update(g_qkv=((6 * half, D), BF), g_c2=((6 * half, D), BF), normedt=(dt, BF))
    names = list(near) + list(far) + list(outs) + list(scratch) + ["send", "recv", "own"]

    def kernel(*refs):
        r = Box()
        for n, ref in zip(names, refs):
            setattr(r, n, ref)
        r.odd, r.smg, r.sg, r.fe, r.fo, r.enc = r.shift, r.mid, r.ntwo, r.act, r.ing, r.bg
        r.normedt = r.mixb if alias else r.normedt
        if alias:
            r.g_qkv, r.g_c2 = r.kv.at[0 : 6 * half], r.kv.at[6 * half : 12 * half]
        layer(r, bits)

    vmem, anywhere = pl.BlockSpec(memory_space=pltpu.VMEM), pl.BlockSpec(memory_space=pl.ANY)
    got = pl.pallas_call(
        kernel,
        name="layer",
        out_shape=[jax.ShapeDtypeStruct(*o) for o in outs.values()],
        in_specs=[vmem] * len(near) + [anywhere] * len(far),
        out_specs=[anywhere] * len(outs),
        scratch_shapes=[pltpu.VMEM(*s) for s in scratch.values()]
        + [pltpu.SemaphoreType.DMA((200,)), pltpu.SemaphoreType.DMA((200,)), pltpu.SemaphoreType.DMA((40,))],
        compiler_params=pltpu.CompilerParams(
            vmem_limit_bytes=VMEM_LIMIT, collective_id=1, has_side_effects=True
        ),
    )(*near.values(), *far.values())
    return dict(zip(outs, got))


def run_finish(got, mels, side):
    T2, D = got["enc_o"].shape
    half = D // 2
    ins = list(got)
    outs = dict(
        enc=((1, T2, D), BF),
        mel=((1, mels, 2 * T2), F32),
        c1=((3, mels, D), F32),
        c2=((3, D, D), F32),
        qkv=((3, D, half), F32),
        qkvb=((2, half), F32),
        out=((half, D), F32),
        up=((D, side * D), F32),
        upb=((side * D,), F32),
        down=((side * D, D), F32),
    )
    outs.update({n: ((D,), F32) for n in ROW_BIASES})

    def kernel(*refs):
        r = Box()
        for n, ref in zip(ins + list(outs), refs):
            setattr(r, n, ref)
        m = lax.axis_index("mp")

        def cast(src, dst):
            def one(rows):
                dst[rows, :] = src[rows, :].astype(dst.dtype)

            rows_loop(src.shape[0], 256, one)

        cast(r.enc_o, r.enc.at[0])
        cast(r.down_o, r.down)
        cast(r.up_o, r.up)
        cast(r.out_o, r.out)
        for o in range(3):
            cast(r.qkv_o.at[o], r.qkv.at[o])
            cast(r.c2_o.at[o * D : (o + 1) * D], r.c2.at[o])
            r.c1[o] = r.c1_o[o * mels : (o + 1) * mels, :].astype(F32)
        row = lax.broadcasted_iota(jnp.int32, (128, 256), 0)
        lane = lax.broadcasted_iota(jnp.int32, (128, 256), 1)
        even = jnp.where(lane == 2 * row, 1.0, 0.0).astype(BF)
        odd = jnp.where(lane == 2 * row + 1, 1.0, 0.0).astype(BF)
        for k in range(T2 // 128):
            rows = slice(k * 128, (k + 1) * 128)
            value = tn(r.mel_o[rows, 0:128], even) + tn(r.mel_o[rows, 128:256], odd)
            r.mel[0, :, k * 256 : (k + 1) * 256] = value[0:mels, :]
        for k, n in enumerate(ROW_BIASES):
            getattr(r, n)[...] = r.small_o[k : k + 1, :].reshape(D)
        r.qkvb[...] = r.small_o[QB : QB + 2, pl.ds(pl.multiple_of(m * half, 128), half)]
        for k in range(side):
            r.upb[k * D : (k + 1) * D] = r.small_o[pl.ds(UPB + m * side + k, 1), :].reshape(D)

    vmem = pl.BlockSpec(memory_space=pltpu.VMEM)
    done = pl.pallas_call(
        kernel,
        name="finish",
        out_shape=[jax.ShapeDtypeStruct(*o) for o in outs.values()],
        in_specs=[vmem] * len(ins),
        out_specs=[vmem] * len(outs),
        compiler_params=pltpu.CompilerParams(vmem_limit_bytes=VMEM_LIMIT),
    )(*got.values())
    return dict(zip(outs, done))


def sine_tables(frames, channels, fine):
    half_width = channels // 2
    rate = np.exp(-(math.log(10000.0) / (half_width - 1)) * np.arange(half_width))
    small = np.arange(fine)[:, None] * rate[None, :]
    large = np.arange(0, frames, fine)[:, None] * rate[None, :]
    table = dict(fine_s=np.sin(small), fine_c=np.cos(small), coarse_s=np.sin(large), coarse_c=np.cos(large))
    return {n: jnp.asarray(t, F32) for n, t in table.items()}


def on_device(
    mel_input,
    conv1_weight,
    conv1_bias,
    conv2_weight,
    conv2_bias,
    norm1_gain,
    norm1_bias,
    qkv_weight,
    qkv_bias,
    out_weight,
    out_bias,
    norm2_gain,
    norm2_bias,
    up_weight,
    up_bias,
    down_weight,
    down_bias,
    cotangent,
    speech_mask,
):
    mels = mel_input.shape[1]
    T, D = cotangent.shape[1] // 2, cotangent.shape[2]
    F2 = up_weight.shape[1]
    side, half = F2 // D, D // 2
    bits = (lax.axis_size("dp") - 1).bit_length()
    lanes = -(-3 * mels // 128) * 128
    near = dict(
        w1=conv1_weight,
        mask=speech_mask,
        qkvb=qkv_bias,
        upb=up_bias,
        c1b=conv1_bias,
        c2b=conv2_bias,
        n1g=norm1_gain,
        n1b=norm1_bias,
        oub=out_bias,
        n2g=norm2_gain,
        n2b=norm2_bias,
        dnb=down_bias,
    )
    near.update(sine_tables(4 * T, D, 32))
    got = run_layer(
        bits,
        near,
        dict(
            mel=mel_input,
            cot=cotangent,
            w2_l=conv2_weight,
            wqkv_l=qkv_weight,
            wo_l=out_weight,
            up_l=up_weight,
            down_l=down_weight,
        ),
        dict(
            enc_o=((2 * T, D), BF),
            mel_o=((2 * T, 256), BF),
            down_o=((F2, D), BF),
            up_o=((D, F2), BF),
            out_o=((half, D), BF),
            qkv_o=((3, D, half), BF),
            c2_o=((3 * D, D), BF),
            c1_o=((lanes, D), BF),
            small_o=((16, D), F32),
        ),
        T,
        D,
        F2,
        lanes,
    )
    done = run_finish(got, mels, side)
    names = ("enc", "mel", "c1", "c1b", "c2", "c2b", "n1g", "n1b", "qkv", "qkvb")
    names += ("out", "oub", "n2g", "n2b", "up", "upb", "down", "dnb")
    return tuple(done[n] for n in names)


def solution(mesh):
    placed = (
        P("dp", None, "seq"),
        P(),
        P(),
        P(),
        P(),
        P(),
        P(),
        P(None, None, "mp"),
        P(None, "mp"),
        P("mp", None),
        P(),
        P(),
        P(),
        P(None, "mp"),
        P("mp"),
        P("mp", None),
        P(),
        P("dp", "seq", None),
        P("dp", "seq"),
    )
    return jax.shard_map(
        on_device,
        mesh=mesh,
        in_specs=placed,
        out_specs=(
            P("dp", "seq", None),
            P("dp", None, "seq"),
            P(),
            P(),
            P(),
            P(),
            P(),
            P(),
            P(None, None, "mp"),
            P(None, "mp"),
            P("mp", None),
            P(),
            P(),
            P(),
            P(None, "mp"),
            P("mp"),
            P("mp", None),
            P(),
        ),
        check_vma=False,
    )
```

```python
import functools
import math

import jax
import jax.numpy as jnp
import numpy as np
from jax import lax
from jax.experimental import pallas as pl
from jax.experimental.pallas import tpu as pltpu
from jax.sharding import PartitionSpec as P

HEAD = 64
BF = jnp.bfloat16
F32 = jnp.float32
MESH = pl.DeviceIdType.MESH
VMEM_LIMIT = 61 * 1024 * 1024
C1B, C2B, N1G, N1B, OUB, N2G, N2B, DNB, QB, VB, UPB = range(11)


class Box:
    pass


def dot(a, b, ca, cb):
    return lax.dot_general(a, b, (((ca,), (cb,)), ((), ())), preferred_element_type=F32)


def nn(a, b):
    return dot(a, b, 1, 0)


def nt(a, b):
    return dot(a, b, 1, 1)


def tn(a, b):
    return dot(a, b, 0, 0)


def rows_loop(total, step, body, unroll=1):
    step = min(step, total)

    def one(i, carry):
        body(pl.ds(pl.multiple_of(i * step, step), step))
        return carry

    lax.fori_loop(0, total // step, one, 0, unroll=unroll)


def gelu_parts(v):
    t = 1.0 / (1.0 + (0.3275911 / math.sqrt(2.0)) * jnp.abs(v))
    e = jnp.exp(-0.5 * v * v)
    poly = 1.061405429 * t - 1.453152027
    poly = poly * t + 1.421413741
    poly = poly * t - 0.284496736
    poly = poly * t + 0.254829592
    tail = (0.5 * t) * poly * e
    return jnp.where(v >= 0, 1.0 - tail, tail), e * (1.0 / math.sqrt(2.0 * math.pi))


def gelu_both(v):
    cdf, pdf = gelu_parts(v)
    return v * cdf, cdf + v * pdf


def normal(x):
    center = x - jnp.mean(x, axis=-1, keepdims=True)
    spread = jnp.mean(center * center, axis=-1, keepdims=True)
    inv = lax.rsqrt(spread + 1e-05)
    return center * inv, inv


def normal_pull(gy, hat, inv):
    return inv * (
        gy
        - jnp.mean(gy, axis=-1, keepdims=True)
        - hat * jnp.mean(gy * hat, axis=-1, keepdims=True)
    )


def vec(r, i):
    return r.vecs[i : i + 1, :]


def add_small(r, i, value):
    r.small[i : i + 1, :] += value


def col(value):
    return jnp.sum(value, axis=0, keepdims=True)


def stage_mel_rows(r, sub):
    T, D = r.stream.shape
    row = lax.broadcasted_iota(jnp.int32, (256, 256), 0)
    lane = lax.broadcasted_iota(jnp.int32, (256, 256), 1)
    pick = jnp.where(lane == 2 * (row % 128) + row // 128, 1.0, 0.0).astype(BF)
    base = sub * 2 * T

    def lanes(start, size):
        return r.melbuf[:, pl.ds(pl.multiple_of(base + start, 128), size)]

    row = lax.broadcasted_iota(jnp.int32, (16, 128), 0)
    lane = lax.broadcasted_iota(jnp.int32, (16, 128), 1)

    def select(at, to):
        return jnp.where(jnp.logical_and(row == to, lane == at), 1.0, 0.0).astype(BF)

    before, after = lanes(0, 128), lanes(128 + 2 * T, 128)
    r.mele[0:8, :] = nt(select(126, 7), before)[0:8, :]
    r.melo[0:8, :] = nt(select(127, 7), before)[0:8, :]
    r.mele[T + 8 : T + 16, :] = nt(select(0, 0), after)[0:8, :]
    for k in range(T // 128):
        both = nt(pick, lanes(128 + 256 * k, 256))
        r.mele[8 + 128 * k : 136 + 128 * k, :] = both[0:128, :]
        r.melo[8 + 128 * k : 136 + 128 * k, :] = both[128:256, :]


def three(a, b, c):
    return jnp.concatenate([a, b, c], axis=1).astype(BF)


def stage_first(r, first):
    T, D = r.stream.shape
    for o in range(3):
        r.w1p[128 * o : 128 * o + r.w1.shape[1], :] = r.w1[o]
        r.w1p[128 * o + r.w1.shape[1] : 128 * (o + 1), :] = jnp.zeros((128 - r.w1.shape[1], D), BF)
    w1 = r.w1p[...]
    edge = nn(three(r.mele[0:16, :], r.melo[0:16, :], r.mele[1:17, :]), w1) + vec(r, C1B)
    edge = gelu_both(edge)[0] * jnp.where(first, 0.0, 1.0)
    r.odd[0:8, :] = edge[0:8, :]
    r.xe[...] = three(r.melo[7 : 7 + T, :], r.mele[8 : 8 + T, :], r.melo[8 : 8 + T, :])
    r.xo[...] = three(r.mele[8 : 8 + T, :], r.melo[8 : 8 + T, :], r.mele[9 : 9 + T, :])
    r.tmp[...] = nn(r.xe[...], w1)

    def even(rows):
        value, slope = gelu_both(r.tmp[rows, :] + vec(r, C1B))
        r.he[rows, :] = value.astype(BF)
        r.dge[rows, :] = slope

    rows_loop(T, 32, even)
    r.tmp[...] = nn(r.xo[...], w1)

    def odd(rows):
        value, slope = gelu_both(r.tmp[rows, :] + vec(r, C1B))
        r.ho[rows, :] = value.astype(BF)
        r.odd[pl.ds(pl.multiple_of(rows.start + 8, 8), rows.size), :] = value
        r.dgo[rows, :] = slope

    rows_loop(T, 32, odd)


def stage_second(r, place):
    T, D = r.stream.shape
    r.hp[...] = r.odd[7 : 7 + T, :].astype(BF)
    r.tmp[...] = nn(r.hp[...], r.w2[0]) + nn(r.he[...], r.w2[1]) + nn(r.ho[...], r.w2[2])
    fine = r.fine_s.shape[0]

    def second(rows):
        value, slope = gelu_both(r.tmp[rows, :] + vec(r, C2B))
        at = place * (T // fine) + rows.start // fine
        s0, c0 = r.coarse_s[pl.ds(at, 1), :], r.coarse_c[pl.ds(at, 1), :]
        s1, c1 = r.fine_s[...], r.fine_c[...]
        stream = value + jnp.concatenate([s0 * c1 + c0 * s1, c0 * c1 - s0 * s1], axis=1)
        r.dg2[rows, :] = slope
        r.stream[rows, :] = stream
        r.normed[rows, :] = (normal(stream)[0] * vec(r, N1G) + vec(r, N1B)).astype(BF)

    rows_loop(T, fine, second)


def stage_mask(r, sub):
    T, D = r.stream.shape
    row = r.mask[0:1, pl.ds(pl.multiple_of(sub * T, 128), T)].astype(F32)
    r.wide[0:T, :] = jnp.broadcast_to(row, (128, T)).T

    def one(rows):
        keep = r.wide[rows, :]
        keep = jnp.concatenate([keep] * (D // 128), axis=1)
        r.bg[rows, :] = (r.bg[rows, :].astype(F32) * keep).astype(BF)

    rows_loop(T, 32, one)


def stage_qkv(r, part):
    T, D = r.stream.shape
    half, qr = D // 2, D // 4
    bias, scale = ((QB, HEAD**-0.5), (None, 1.0), (VB, 1.0))[part]
    for h in range(2):
        value = nn(r.normed[...], r.wqkv[h, part])
        if bias is not None:
            value = value + r.vecs[bias : bias + 1, h * half : (h + 1) * half]
        value = (value.astype(BF).astype(F32) * scale).T.astype(BF)
        for k in range(2):
            at = (3 * (3 + k) + part) * half + h * qr
            r.kv[at : at + qr, :] = value[k * qr : (k + 1) * qr, :]


def at_head(start, h):
    return pl.ds(pl.multiple_of(start + h * HEAD, HEAD), HEAD)


def head_loop(steps, hooks, body):
    def one(step, carry):
        for at, todo in hooks.items():

            @pl.when(step == at)
            def _(todo=todo):
                for act in todo:
                    act()

        body(step)
        return carry

    lax.fori_loop(0, steps, one, 0)


def attend(r, c, hooks):
    S, T = r.kv.shape[0] // 15, r.kv.shape[1]
    heads = S // HEAD
    r.top[...] = jnp.full(r.top.shape, -jnp.inf, F32)
    r.total[...] = jnp.zeros(r.total.shape, F32)
    r.mixt[...] = jnp.zeros(r.mixt.shape, F32)

    def body(step):
        g, h = step // heads, step % heads
        own = (3 - g) // 3
        slot = own * (3 + c) + (1 - own) * ((g + 1) % 3)
        k = r.kv[at_head((3 * slot + 1) * S, h), :]
        v = r.kv[at_head((3 * slot + 2) * S, h), :]
        for i, home in enumerate((3 + c, 2)):
            q = r.kv[at_head(3 * home * S, h), :]
            s = tn(k, q)
            before = r.top[i * heads + h]
            top = jnp.maximum(before, jnp.max(s, axis=0, keepdims=True))
            p = jnp.exp(s - top)
            keep = jnp.exp(before - top)
            rows = at_head(i * S, h)
            r.top[i * heads + h] = top
            r.total[i * heads + h] = keep * r.total[i * heads + h] + jnp.sum(p, axis=0, keepdims=True)
            r.mixt[rows, :] = keep * r.mixt[rows, :] + nn(v, p.astype(BF))

    head_loop(4 * heads, hooks, body)


def attend_end(r, i):
    S = r.kv.shape[0] // 15
    heads = S // HEAD

    def one(h, carry):
        rows = at_head(i * S, h)
        total = r.total[i * heads + h]
        value = r.mixt[rows, :] * (1.0 / total)
        r.mixt[rows, :] = value
        r.mixb[rows, :] = value.astype(BF)
        r.top[i * heads + h] = r.top[i * heads + h] + jnp.log(total)
        return carry

    lax.fori_loop(0, heads, one, 0)


def stage_mid(r, c):
    T, D = r.stream.shape
    half = D // 2
    r.tmp[...] = tn(r.mixb[0:half, :], r.wo[rows16(c * half, half), :])
    r.tmp[...] += tn(r.mix_got[...], r.wo[rows16((1 - c) * half, half), :])

    def one(rows):
        mid = r.stream[rows, :] + r.tmp[rows, :] + vec(r, OUB)
        r.mid[rows, :] = mid
        r.ntwo[rows, :] = (normal(mid)[0] * vec(r, N2G) + vec(r, N2B)).astype(BF)

    rows_loop(T, 32, one)


def stage_ff(r, hooks):
    T, D = r.stream.shape
    side = r.up.shape[2] // D
    parts, width = 2 * side, D
    add_small(r, DNB, col(r.bg[...].astype(F32)))

    def chunk(t):
        into, at = t % 2, t // 2
        j = into * side + at
        up = r.up[into, :, pl.ds(pl.multiple_of(at * D, D), D)]
        down = r.down[pl.ds(pl.multiple_of(j * D, D), D), :]
        r.tmp[...] = nn(r.ntwo[...], up)
        r.tmp2[...] = nt(r.bg[...], down)
        bias = r.vecs[pl.ds(UPB + j, 1), :]

        def one(i, acc):
            rows = pl.ds(pl.multiple_of(i * 32, 32), 32)
            value, slope = gelu_both(r.tmp[rows, :] + bias)
            r.act[rows, :] = value.astype(BF)
            grad = (r.tmp2[rows, :] * slope).astype(BF)
            r.ing[rows, :] = grad
            return acc + col(grad.astype(F32))

        r.small[pl.ds(UPB + j, 1), :] = lax.fori_loop(0, T // 32, one, jnp.zeros((1, width), F32))
        act = r.act[...]
        ing = r.ing[...]
        out = nn(act, down)
        back = nt(ing, up)

        r.ffo[...] += out
        r.ntg[...] += back
        rows = pl.ds(pl.multiple_of(t * D, D), D)
        r.g_down[rows, :] = tn(act, r.bg[...]).astype(BF)
        r.g_up[rows, :] = tn(r.ntwo[...], ing).astype(BF)

    r.ffo[...] = jnp.zeros_like(r.ffo)
    r.ntg[...] = jnp.zeros_like(r.ntg)
    head_loop(parts, hooks, chunk)


def stage_mid_pull(r):
    T, D = r.stream.shape

    def one(i, accs):
        rows = pl.ds(pl.multiple_of(i * 32, 32), 32)
        mid = r.mid[rows, :]
        enc = (mid + r.ffo[rows, :] + vec(r, DNB)).astype(BF)
        hat, inv = normal(mid)
        grad = r.ntg[rows, :]
        smg = r.bg[rows, :].astype(F32) + normal_pull(grad * vec(r, N2G), hat, inv)
        r.enc[rows, :] = enc
        r.smg[rows, :] = smg
        attg = smg.astype(BF)
        r.attg[rows, :] = attg
        return accs[0] + col(grad * hat), accs[1] + col(grad), accs[2] + col(attg.astype(F32))

    zero = jnp.zeros((1, D), F32)
    gain, bias, out_bias = lax.fori_loop(0, T // 32, one, (zero, zero, zero))
    add_small(r, N2G, gain)
    add_small(r, N2B, bias)
    add_small(r, OUB, out_bias)


def stage_do(r, c, own):
    half = r.attg.shape[1] // 2
    k = c if own else 1 - c
    value = nt(r.wo[rows16(k * half, half), :], r.attg[...]).astype(BF)
    if own:
        r.dot[0:half, :] = value
    else:
        r.dot_out[...] = value


def stage_out_weights(r, c):
    D = r.attg.shape[1]
    half, qr = D // 2, D // 4
    for k, mix in ((c, r.mixb[0:half, :]), (1 - c, r.mix_got[...])):
        value = nn(mix, r.attg[...]).astype(BF)
        for h in range(2):
            r.g_out[rows16(h * half + k * qr, qr), :] = value[h * qr : (h + 1) * qr, :]


def stage_diag(r, i):
    S = r.kv.shape[0] // 15
    heads = S // HEAD

    def one(h, carry):
        rows = at_head(i * S, h)
        value = r.dot[rows, :].astype(F32) * r.mixt[rows, :]
        r.diag[i * heads + h] = jnp.sum(value, axis=0, keepdims=True)
        return carry

    lax.fori_loop(0, heads, one, 0)


def attend_pull(r, c, hooks):
    S, T = r.kv.shape[0] // 15, r.kv.shape[1]
    heads = S // HEAD
    r.dqt[...] = jnp.zeros(r.dqt.shape, F32)

    def body(step):
        g, h = step // heads, step % heads
        slot = g + (g // 3) * c
        k = r.kv[at_head((3 * slot + 1) * S, h), :]
        v = r.kv[at_head((3 * slot + 2) * S, h), :]
        dk, dv = None, None
        for i, home in enumerate((3 + c, 2)):
            q = r.kv[at_head(3 * home * S, h), :]
            rows = at_head(i * S, h)
            do = r.dot[rows, :]
            p = jnp.exp(tn(k, q) - r.top[i * heads + h])
            ds = (p * (tn(v, do) - r.diag[i * heads + h])).astype(BF)
            dv_i, dk_i = nt(do, p.astype(BF)), nt(q, ds)
            dk, dv = (dk_i, dv_i) if dk is None else (dk + dk_i, dv + dv_i)
            r.dqt[rows, :] += nn(k, ds)
        r.dkv[at_head(2 * g * S, h), :] = dk.astype(BF)
        r.dkv[at_head((2 * g + 1) * S, h), :] = dv.astype(BF)

    head_loop(4 * heads, hooks, body)


def piece_of(r, part, h):
    D, qr = r.attg.shape[1], r.attg.shape[1] // 4
    at = part * D + h * qr
    return jnp.concatenate([r.dsum[at : at + qr, :], r.dsum[at + 2 * qr : at + 3 * qr, :]], axis=0)


def stage_qkv_weights(r, part):
    T, D = r.stream.shape
    half = D // 2
    ones = jnp.ones((8, T), BF)
    for h in range(2):
        piece = piece_of(r, part, h)
        if part != 1:
            row = QB if part == 0 else VB
            r.small[row : row + 1, h * half : (h + 1) * half] = nt(ones, piece)[0:1, :]
        grad = nt(r.normedt[...], piece).astype(BF)
        at = (2 * part + h) * half
        r.g_qkv[at : at + half, 0:half] = grad[0:half, :]
        r.g_qkv[at : at + half, half:D] = grad[half:D, :]


def stage_qkv_pull(r):
    T, D = r.stream.shape
    total = None
    for part in range(3):
        for h in range(2):
            back = nn(r.wqkv[h, part], piece_of(r, part, h))
            total = back if total is None else total + back
    r.tmp[...] = total.T


def stage_norm_pull(r):
    T, D = r.stream.shape

    def one(i, accs):
        rows = pl.ds(pl.multiple_of(i * 32, 32), 32)
        hat, inv = normal(r.stream[rows, :])
        grad = r.tmp[rows, :]
        back = r.smg[rows, :] + normal_pull(grad * vec(r, N1G), hat, inv)
        sg = (back * r.dg2[rows, :]).astype(BF)
        r.sg[rows, :] = sg
        return accs[0] + col(grad * hat), accs[1] + col(grad), accs[2] + col(sg.astype(F32))

    zero = jnp.zeros((1, D), F32)
    gain, bias, c2b = lax.fori_loop(0, T // 32, one, (zero, zero, zero))
    add_small(r, N1G, gain)
    add_small(r, N1B, bias)
    add_small(r, C2B, c2b)


def stage_conv2_pull(r, next_row):
    T, D = r.stream.shape
    sg = r.sg[...]
    r.shift[0:T, :] = nt(sg, r.w2[0])
    r.shift[T : T + 16, :] = nt(next_row, r.w2[0])
    r.tmp[...] = nt(sg, r.w2[1])
    r.tmp2[...] = nt(sg, r.w2[2]) + r.shift[1 : T + 1, :]


def stage_first_pull(r):
    T, D = r.stream.shape

    def one(i, acc):
        rows = pl.ds(pl.multiple_of(i * 32, 32), 32)
        even = (r.tmp[rows, :] * r.dge[rows, :]).astype(BF)
        odd = (r.tmp2[rows, :] * r.dgo[rows, :]).astype(BF)
        r.fe[rows, :] = even
        r.fo[rows, :] = odd
        return acc + col(even.astype(F32)) + col(odd.astype(F32))

    add_small(r, C1B, lax.fori_loop(0, T // 32, one, jnp.zeros((1, D), F32)))


def stage_conv2_weights(r, i):
    D = r.stream.shape[1]
    tap = (r.hp, r.he, r.ho)[i]
    r.g_c2[i * D : (i + 1) * D, :] = tn(tap[...], r.sg[...]).astype(BF)


def stage_conv1_weights(r):
    value = (tn(r.xe[...], r.fe[...]) + tn(r.xo[...], r.fo[...])).astype(BF)
    mels = r.w1.shape[1]
    for o in range(3):
        r.g_c1[mels * o : mels * (o + 1), :] = value[128 * o : 128 * o + mels, :]
    r.g_c1[3 * mels :, :] = jnp.zeros((r.g_c1.shape[0] - 3 * mels, r.g_c1.shape[1]), BF)


def stage_mel(r, next_row, prev_row):
    T, D = r.stream.shape
    fe, fo = r.fe[...], r.fo[...]
    w = [r.w1p[128 * o : 128 * (o + 1), :] for o in range(3)]
    r.wide[16 : 16 + T, :] = nt(fo, w[2])
    r.wide[0:16, :] = nt(prev_row, w[2])
    r.melg[:, 0:128] = (nt(fe, w[1]) + nt(fo, w[0]) + r.wide[15 : 15 + T, :]).astype(BF)
    r.wide[0:T, :] = nt(fe, w[0])
    r.wide[T : T + 16, :] = nt(next_row, w[0])
    r.melg[:, 128:256] = (nt(fe, w[2]) + nt(fo, w[1]) + r.wide[1 : 1 + T, :]).astype(BF)


class Net:
    def __init__(self, r, bits):
        self.r, self.bits, self.used, self.used_here = r, bits, 0, 0
        self.d, self.c, self.m = (lax.axis_index(n) for n in ("dp", "seq", "mp"))

    def bit(self, dim):
        if dim == "c":
            return self.c
        if dim == "y":
            return self.m
        return (self.d // (1 << dim)) % 2

    def peer(self, dims):
        d = self.d
        for k in dims:
            if k not in ("c", "y"):
                d = d + (1 << k) - 2 * (1 << k) * self.bit(k)
        return (
            d,
            1 - self.c if "c" in dims else self.c,
            1 - self.m if "y" in dims else self.m,
        )

    def greet(self, partners):
        barrier = pltpu.get_barrier_semaphore()
        for dims in partners:
            pl.semaphore_signal(barrier, inc=1, device_id=self.peer(dims), device_id_type=MESH)
        pl.semaphore_wait(barrier, len(partners))

    def copy(self, src, dst, *dims):
        i = self.used
        self.used += 1
        return pltpu.make_async_remote_copy(
            src_ref=src,
            dst_ref=dst,
            send_sem=self.r.send.at[i],
            recv_sem=self.r.recv.at[i],
            device_id=self.peer(dims),
            device_id_type=MESH,
        )

    def send(self, src, dst, *dims):
        copy = self.copy(src, dst, *dims)
        copy.start()
        return copy

    def here(self, src, dst):
        i = self.used_here
        self.used_here += 1
        copy = pltpu.make_async_copy(src, dst, self.r.own.at[i])
        copy.start()
        return copy


def start_all(copies):
    for copy in copies:
        copy.start()


def wait_all(copies):
    for copy in copies:
        copy.wait()


def rows16(start, size):
    return pl.ds(pl.multiple_of(start, 16), size)


def subsets(dims):
    found = [()]
    for dim in dims:
        found += [one + (dim,) for one in found]
    return found[1:]


def sum_plan(rows, halves, order):
    steps, need = [], 0
    for dims in order:
        by_half = halves == 2 and "y" in dims
        cutting = [dim for dim in dims if not (by_half and dim == "y")]
        if rows % (16 << len(cutting)):
            cutting = []
        rows >>= len(cutting)
        if by_half:
            halves = 1
        steps.append((dims, cutting, rows, halves, by_half))
        need += rows * halves * len(subsets(dims))
    return steps, need


class Track:
    def __init__(self, acts):
        self.acts = list(acts)

    def take(self):
        return [self.acts.pop(0)] if self.acts else []


def bucket_sum(net, g, got, done, halves, order):
    R = g.shape[0] // halves
    lo, rows, at, bases = 0, R, 0, [h * R for h in range(halves)]
    acts, back, end = [], [], None

    def start_after(end, copies):
        def act():
            if end is not None:
                end()
            for copy in copies:
                copy.start()

        return act

    def adder(copies, places, n):
        step = 64 if n % 64 == 0 else 32 if n % 32 == 0 else 16

        def end():
            wait_all(copies)
            for to, ofs in places:

                def add(k, carry, to=to, ofs=ofs):
                    mine = rows16(to + k * step, step)
                    value = g[mine, :].astype(F32)
                    for of in ofs:
                        value = value + got[rows16(of + k * step, step), :].astype(F32)
                    g[mine, :] = value.astype(BF)
                    return carry

                lax.fori_loop(0, n // step, add, 0)

        return end

    for dims, cutting, n, _, by_half in sum_plan(R, halves, order)[0]:

        def part_of(other):
            start = lo
            for i, dim in enumerate(reversed(cutting)):
                b = net.bit(dim)
                start = start + (1 - b if dim in other else b) * (n << i)
            return start

        keep = part_of(())
        if by_half:
            bases = [net.m * R]
        copies, ofs = [], [[] for _ in bases]
        for other in subsets(dims):
            sources = [(1 - net.m) * R] if by_half and "y" in other else bases
            for i, base in enumerate(sources):
                src = g.at[rows16(base + part_of(other), n)]
                copies.append(net.copy(src, got.at[rows16(at, n)], *other))
                ofs[i].append(at)
                at += n
        acts.append(start_after(end, copies))
        end = adder(copies, [(base + keep, of) for base, of in zip(bases, ofs)], n)
        if cutting:
            back.append((cutting, n, lo))
        lo, rows = keep, n

    def settle(end=end, lo=lo, base=bases[0], rows=rows):
        end()
        for k in range(rows // 16):
            done[rows16(lo + 16 * k, 16), :] = g[rows16(base + lo + 16 * k, 16), :]

    end = settle
    for cutting, n, before in reversed(back):
        part = rows16(lo, n)
        copies = [net.copy(done.at[part], done.at[part], *other) for other in subsets(cutting)]
        acts.append(start_after(end, copies))
        end = functools.partial(wait_all, copies)
        lo = before
    return Track(acts + [end])


def small_sum(net, value, slots, order):
    acts, end, at = [], None, 0
    for dims in order:
        copies = [net.copy(value, slots.at[at + i], *other) for i, other in enumerate(subsets(dims))]

        def act(end=end, copies=copies):
            if end is not None:
                end()
            start_all(copies)

        def end(copies=copies, at=at):
            wait_all(copies)
            total = value[...]
            for i in range(len(copies)):
                total = total + slots[at + i]
            value[...] = total

        at += len(copies)
        acts.append(act)
    return Track(acts + [end])


def advance(*sums):
    for one in sums:
        for act in one.take():
            act()


def drain(*sums):
    while any(one.acts for one in sums):
        advance(*sums)


def quarter(net):
    return 2 * net.c + net.c + net.m - 2 * net.c * net.m


def choose(slots, by_core, by_y):
    core = jnp.where(by_core, 1.0, 0.0)
    y = jnp.where(by_y, 1.0, 0.0)
    return (slots[0].astype(F32) * core + slots[1].astype(F32) * y).astype(BF)


def pick_next(net, slots):
    q = quarter(net)
    return choose(slots, q == 1, q % 2 == 0)


def pick_prev(net, slots):
    q = quarter(net)
    return choose(slots, q == 2, q % 2 == 1)


ROW_BIASES = ("c1b", "c2b", "n1g", "n1b", "oub", "n2g", "n2b", "dnb")


ORDERS = dict(
    down=("xczwy", "zcxwy"),
    up=("xyzwc", "zyxwc"),
    out=("cxzwy",),
    qkv=("xczwy", "zxcwy", "ycxzw"),
    c2=("cxyzw", "yzcxw", "xyzcw"),
    c1=("zcxyw",),
    vec=("cyxzw",),
)


def orders(name, bits):
    dims = dict(c=["c"], y=["y"], x=[0], z=list(range(1, min(2, bits))), w=list(range(2, bits)))
    return [[(dim,) for ch in spec for dim in dims[ch]] for spec in ORDERS[name]]


def layer(r, bits):
    T, D = r.stream.shape
    half, F2 = D // 2, r.down_l.shape[0]
    side = F2 // D
    mels, span = r.w1.shape[1], 4 * T
    net = Net(r, bits)
    c, m = net.c, net.m
    sub = c + m - 2 * c * m
    rows_of_mine = rows16(sub * T, T)

    r.melbuf[...] = jnp.zeros_like(r.melbuf)
    mel_own = net.here(r.mel.at[0], r.melbuf.at[0:mels, 128 : 128 + span])
    qkv_own = net.here(r.wqkv_l, r.wqkv.at[m])
    w2_own = net.here(r.w2_l, r.w2)
    own = [
        net.here(r.wo_l.at[0 : D // 4], r.wo.at[rows16(m * (D // 4), D // 4)]),
        net.here(r.wo_l.at[D // 4 : half], r.wo.at[rows16(half + m * (D // 4), D // 4)]),
        net.here(r.up_l, r.up.at[m]),
        net.here(r.down_l, r.down.at[rows16(m * F2, F2)]),
        net.here(r.cot.at[0, rows_of_mine], r.bg),
    ]
    r.vec_mine[...] = jnp.zeros_like(r.vec_mine)
    own_lanes = pl.ds(pl.multiple_of(m * half, 128), half)
    r.vec_mine[0:2, own_lanes] = r.qkvb[...].astype(F32)
    for k in range(side):
        r.vec_mine[pl.ds(2 + m * side + k, 1), :] = r.upb[k * D : (k + 1) * D].astype(F32).reshape(1, D)
    for k, n in enumerate(ROW_BIASES):
        r.vecs[k : k + 1, :] = getattr(r, n)[...].astype(F32).reshape(1, D)
    net.greet([("c",), ("y",), ("c", "y")] + [(k,) for k in range(bits)])
    vec_copy = net.send(r.vec_mine, r.vec_got, "y")
    mel_own.wait()
    src = pl.ds(pl.multiple_of(128 + (1 - c) * (span - 128), 128), 128)
    dst = pl.ds(pl.multiple_of(c * (span + 128), 128), 128)
    mel_rim = net.send(r.melbuf.at[0:mels, src], r.melbuf.at[0:mels, dst], "c")
    piece = rows16(c * half, half)
    qkv_own.wait()
    mine = r.wqkv.at[m, :, piece]
    qkv_y = net.send(mine, mine, "y")

    p = 4 * c + 2 * net.bit(0) + net.bit(1) if bits > 1 else 2 * c + net.bit(0)
    cuts = 8 if bits > 1 else 4

    def pass_on(of, at, count, dim):
        def cut(n, base):
            return rows16(base + at * (n // cuts), count * (n // cuts))

        wo = rows16(c * half + of * (D // 4) + (at - c * (cuts // 2)) * (half // cuts), count * (half // cuts))
        parts = [r.wo.at[wo], r.up.at[of, cut(D, 0)], r.down.at[cut(F2, of * F2)]]
        return [net.copy(x, x, dim) for x in parts]

    r.small[...] = jnp.zeros_like(r.small)
    mel_rim.wait()
    stage_mel_rows(r, sub)
    stage_first(r, jnp.logical_and(c == 0, m == 0))
    qkv_y.wait()
    arrived = r.wqkv.at[1 - m, :, piece]
    qkv_c = net.send(arrived, arrived, "c")
    wait_all(own)
    ff_y = pass_on(m, p, 1, "y")
    start_all(ff_y)
    w2_own.wait()
    stage_second(r, quarter(net))
    vec_copy.wait()
    r.vecs[8:16, :] = r.vec_mine[...] + r.vec_got[...]
    qkv_c.wait()

    def block(slot, part, parts=1):
        return r.kv.at[rows16((3 * slot + part) * half, parts * half)]

    to_y, to_d = [], []
    for part in (1, 2):
        stage_qkv(r, part)
        to_y.append(net.send(block(3 + c, part), block(0, part), "y"))
        to_d.append(net.send(block(4 - c, part), block(1, part), "c", "y"))
    stage_qkv(r, 0)
    to_c = [net.send(block(4 - c, part), block(2, part), "c") for part in range(3)]
    wait_all(ff_y)
    ff_z = pass_on(1 - m, p, 1, 1) if bits > 1 else []
    start_all(ff_z)
    ff_x = pass_on(1 - m, (p // 2) * 2 if bits > 1 else p, 2 if bits > 1 else 1, 0)
    ff_c = pass_on(1 - m, c * (cuts // 2), cuts // 2, "c")
    stage_mask(r, sub)
    to_c[0].wait()
    heads = half // HEAD
    attend(
        r,
        c,
        {
            heads: [lambda: wait_all(to_c[1:]), lambda: wait_all(ff_z), lambda: start_all(ff_x)],
            2 * heads: [lambda: wait_all(ff_x), lambda: start_all(ff_c), lambda: wait_all(to_y)],
            3 * heads: [lambda: wait_all(to_d)],
        },
    )
    attend_end(r, 1)
    mix_c = net.send(r.mixb.at[half:D], r.mix_got, "c")
    attend_end(r, 0)
    wait_all(ff_c)
    mix_c.wait()
    stage_mid(r, c)

    def summed(n, part, rows, halves):
        views = [
            getattr(r, "g_" + n).at[part * rows * halves : (part + 1) * rows * halves],
            getattr(r, "got_%s%d" % (n, part)),
            getattr(r, "done_" + n).at[part * rows : (part + 1) * rows],
        ]
        return bucket_sum(net, *views, halves, orders(n, bits)[part])

    down = [summed("down", part, D, 2) for part in range(side)]
    up = [summed("up", part, D, 2) for part in range(side)]
    hooks = {}
    for part in range(side - 1):
        hooks[2 * part + 2] = down[part].take() + up[part].take()
    stage_ff(r, hooks)
    stage_mid_pull(r)
    stage_do(r, c, False)
    do_c = net.send(r.dot_out, r.dot.at[half:D], "c")
    advance(down[-1], up[-1])
    stage_out_weights(r, c)
    out = summed("out", 0, half, 2)
    advance(out)
    stage_do(r, c, True)
    stage_diag(r, 0)
    do_c.wait()
    stage_diag(r, 1)
    enc = [
        net.copy(r.enc, r.enc_got, "y"),
        pltpu.make_async_copy(r.enc, r.enc_o.at[rows_of_mine], r.own.at[39]),
    ]

    both = half * 2
    home_y = net.copy(r.dkv.at[0:both], r.from_y, "y")
    home_d = net.copy(r.dkv.at[both : 2 * both], r.from_d, "c", "y")
    home_c = net.copy(r.dkv.at[2 * both : 3 * both], r.from_c.at[half:], "c")
    hooks = {}

    def at_step(step, *acts):
        hooks.setdefault(step * heads // 4, []).extend(acts)

    at_step(4, home_y.start)
    at_step(8, home_d.start)
    at_step(11, lambda: start_all(enc))
    at_step(12, home_c.start)
    tracks = (down[:1] + up[:1], down[1:] + up[1:] + [out])
    for step in range(1, 16):
        for one in tracks[(step + 1) % 2]:
            at_step(step, *one.take())
    attend_pull(r, c, hooks)
    r.dq_out[...] = (r.dqt[half:D, :] * HEAD**-0.5).astype(BF)
    dq_c = net.send(r.dq_out, r.from_c.at[0:half], "c")
    r.dsum[rows16(c * half, half), :] = (r.dqt[0:half, :] * HEAD**-0.5).astype(BF)
    home_y.wait()
    home_d.wait()
    home_c.wait()

    def total(i, carry):
        for part in range(2):
            rows = rows16(part * half + i * 32, 32)
            mine = r.dkv[rows16(3 * both + part * half + i * 32, 32), :].astype(F32) + r.from_y[rows, :].astype(F32)
            r.dsum[rows16((1 + part) * D + c * half + i * 32, 32), :] = mine.astype(BF)
            other = r.from_c[rows16((1 + part) * half + i * 32, 32), :].astype(F32) + r.from_d[rows, :].astype(F32)
            r.dsum[rows16((1 + part) * D + (1 - c) * half + i * 32, 32), :] = other.astype(BF)
        return carry

    lax.fori_loop(0, half // 32, total, 0)
    dq_c.wait()
    r.dsum[rows16((1 - c) * half, half), :] = r.from_c[0:half, :]

    qkv = [summed("qkv", part, half, 2) for part in range(3)]
    c2 = [summed("c2", part, D, 1) for part in range(3)]
    c1 = summed("c1", 0, r.g_c1.shape[0], 1)
    vecs = small_sum(net, r.small, r.got_small, orders("vec", bits)[0])
    rest = down + up + [out]
    r.normedt[...] = r.normed[...].astype(F32).T.astype(BF)
    for part in (1, 2, 0):
        stage_qkv_weights(r, part)
        advance(qkv[part])
    stage_qkv_pull(r)
    advance(*qkv, *rest)
    stage_norm_pull(r)
    rim = [net.send(r.sg.at[0:16], r.slots.at[0, i], dim) for i, dim in enumerate(("c", "y"))]
    for part in range(3):
        stage_conv2_weights(r, part)
        advance(c2[part])
    advance(*qkv)
    wait_all(rim)
    stage_conv2_pull(r, pick_next(net, r.slots.at[0]))
    advance(*c2, *qkv, *rest)
    stage_first_pull(r)
    rim = [net.send(r.fe.at[0:16], r.slots.at[1, i], dim) for i, dim in enumerate(("c", "y"))]
    rim += [net.send(r.fo.at[T - 16 : T], r.slots.at[2, i], dim) for i, dim in enumerate(("c", "y"))]
    stage_conv1_weights(r)
    advance(c1, vecs, *c2, *qkv)
    wait_all(rim)
    stage_mel(r, pick_next(net, r.slots.at[1]), pick_prev(net, r.slots.at[2]))
    rows_of_yours = rows16((1 - sub) * T, T)
    mel_y = net.send(r.melg, r.melg_got, "y")
    wait_all(enc)
    ends = [
        net.here(r.enc_got, r.enc_o.at[rows_of_yours]),
        net.here(r.melg, r.mel_o.at[rows_of_mine]),
    ]
    drain(c1, vecs, *c2, *qkv, *rest)

    ends.append(net.here(r.done_down, r.down_o))
    for j in range(side):
        ends.append(net.here(r.done_up.at[j * D : (j + 1) * D], r.up_o.at[:, j * D : (j + 1) * D]))
    ends.append(net.here(r.done_out, r.out_o))
    for part in range(3):
        for j in range(2):
            ends.append(
                net.here(
                    r.done_qkv.at[part * half : (part + 1) * half, j * half : (j + 1) * half],
                    r.qkv_o.at[part, j * half : (j + 1) * half],
                )
            )
    ends.append(net.here(r.done_c2, r.c2_o))
    ends.append(net.here(r.done_c1, r.c1_o))
    ends.append(net.here(r.small, r.small_o))
    mel_y.wait()
    ends.append(net.here(r.melg_got, r.mel_o.at[rows_of_yours]))
    wait_all(ends)


def run_layer(bits, near, far, outs, T, D, F2, lanes):
    half, H = D // 2, D // HEAD
    td, dt = (T, D), (D, T)
    buckets = dict(down=(D, 2, F2 // D), up=(D, 2, F2 // D), out=(half, 2, 1), qkv=(half, 2, 3), c2=(D, 1, 3), c1=(lanes, 1, 1))
    scratch = dict(
        melbuf=((128, 4 * T + 256), BF),
        mele=((T + 24, 128), F32),
        melo=((T + 24, 128), F32),
        xe=((T, 384), BF),
        xo=((T, 384), BF),
        w1p=((384, D), BF),
        w2=((3, D, D), BF),
        bg=(td, BF),
        wqkv=((2, 3, D, half), BF),
        wo=((D, D), BF),
        up=((2, D, F2), BF),
        down=((2 * F2, D), BF),
        vecs=((16, D), F32),
        vec_mine=((8, D), F32),
        vec_got=((8, D), F32),
        stream=(td, F32),
        he=(td, BF),
        ho=(td, BF),
        hp=(td, BF),
        dge=(td, F32),
        dgo=(td, F32),
        dg2=(td, F32),
        normed=(td, BF),
        kv=((15 * half, T), BF),
        mixt=(dt, F32),
        mixb=(dt, BF),
        mix_got=((half, T), BF),
        dot=(dt, BF),
        dot_out=((half, T), BF),
        top=((H, 1, T), F32),
        total=((H, 1, T), F32),
        diag=((H, 1, T), F32),
        tmp=(td, F32),
        tmp2=(td, F32),
        shift=((T + 16, D), F32),
        wide=((T + 16, 128), F32),
        mid=(td, F32),
        ntwo=(td, BF),
        act=(td, BF),
        ing=(td, BF),
        ffo=(td, F32),
        ntg=(td, F32),
        attg=(td, BF),
        dqt=(dt, F32),
        dq_out=((half, T), BF),
        dkv=((8 * half, T), BF),
        from_y=((2 * half, T), BF),
        from_d=((2 * half, T), BF),
        from_c=((3 * half, T), BF),
        dsum=((3 * D, T), BF),
        enc_got=(td, BF),
        melg=((T, 256), BF),
        melg_got=((T, 256), BF),
        small=((16, D), F32),
        got_small=((bits + 2, 16, D), F32),
        slots=((3, 2, 16, D), BF),
    )
    alias = T == D
    for n, (rows, halves, parts) in buckets.items():
        if n not in ("qkv", "c2"):
            scratch["g_" + n] = ((rows * halves * parts, D), BF)
        for part in range(parts):
            need = sum_plan(rows, halves, orders(n, bits)[part])[1]
            scratch["got_%s%d" % (n, part)] = ((need, D), BF)
        scratch["done_" + n] = ((rows * parts, D), BF)
    if not alias:
        scratch.update(g_qkv=((6 * half, D), BF), g_c2=((6 * half, D), BF), normedt=(dt, BF))
    names = list(near) + list(far) + list(outs) + list(scratch) + ["send", "recv", "own"]

    def kernel(*refs):
        r = Box()
        for n, ref in zip(names, refs):
            setattr(r, n, ref)
        r.odd, r.smg, r.sg, r.fe, r.fo, r.enc = r.shift, r.mid, r.ntwo, r.act, r.ing, r.bg
        r.normedt = r.mixb if alias else r.normedt
        if alias:
            r.g_qkv, r.g_c2 = r.kv.at[0 : 6 * half], r.kv.at[6 * half : 12 * half]
        layer(r, bits)

    vmem, anywhere = pl.BlockSpec(memory_space=pltpu.VMEM), pl.BlockSpec(memory_space=pl.ANY)
    got = pl.pallas_call(
        kernel,
        name="layer",
        out_shape=[jax.ShapeDtypeStruct(*o) for o in outs.values()],
        in_specs=[vmem] * len(near) + [anywhere] * len(far),
        out_specs=[anywhere] * len(outs),
        scratch_shapes=[pltpu.VMEM(*s) for s in scratch.values()]
        + [pltpu.SemaphoreType.DMA((256,)), pltpu.SemaphoreType.DMA((256,)), pltpu.SemaphoreType.DMA((40,))],
        compiler_params=pltpu.CompilerParams(
            vmem_limit_bytes=VMEM_LIMIT, collective_id=1, has_side_effects=True
        ),
    )(*near.values(), *far.values())
    return dict(zip(outs, got))


def run_finish(got, mels, side):
    T2, D = got["enc_o"].shape
    half = D // 2
    ins = list(got)
    outs = dict(
        enc=((1, T2, D), BF),
        mel=((1, mels, 2 * T2), F32),
        c1=((3, mels, D), F32),
        c2=((3, D, D), F32),
        qkv=((3, D, half), F32),
        qkvb=((2, half), F32),
        out=((half, D), F32),
        up=((D, side * D), F32),
        upb=((side * D,), F32),
        down=((side * D, D), F32),
    )
    outs.update({n: ((D,), F32) for n in ROW_BIASES})

    def kernel(*refs):
        r = Box()
        for n, ref in zip(ins + list(outs), refs):
            setattr(r, n, ref)
        m = lax.axis_index("mp")

        def cast(src, dst):
            def one(rows):
                dst[rows, :] = src[rows, :].astype(dst.dtype)

            rows_loop(src.shape[0], 256, one)

        cast(r.enc_o, r.enc.at[0])
        cast(r.down_o, r.down)
        cast(r.up_o, r.up)
        cast(r.out_o, r.out)
        for o in range(3):
            cast(r.qkv_o.at[o], r.qkv.at[o])
            cast(r.c2_o.at[o * D : (o + 1) * D], r.c2.at[o])
            r.c1[o] = r.c1_o[o * mels : (o + 1) * mels, :].astype(F32)
        row = lax.broadcasted_iota(jnp.int32, (128, 256), 0)
        lane = lax.broadcasted_iota(jnp.int32, (128, 256), 1)
        even = jnp.where(lane == 2 * row, 1.0, 0.0).astype(BF)
        odd = jnp.where(lane == 2 * row + 1, 1.0, 0.0).astype(BF)
        for k in range(T2 // 128):
            rows = slice(k * 128, (k + 1) * 128)
            value = tn(r.mel_o[rows, 0:128], even) + tn(r.mel_o[rows, 128:256], odd)
            r.mel[0, :, k * 256 : (k + 1) * 256] = value[0:mels, :]
        for k, n in enumerate(ROW_BIASES):
            getattr(r, n)[...] = r.small_o[k : k + 1, :].reshape(D)
        r.qkvb[...] = r.small_o[QB : QB + 2, pl.ds(pl.multiple_of(m * half, 128), half)]
        for k in range(side):
            r.upb[k * D : (k + 1) * D] = r.small_o[pl.ds(UPB + m * side + k, 1), :].reshape(D)

    vmem = pl.BlockSpec(memory_space=pltpu.VMEM)
    done = pl.pallas_call(
        kernel,
        name="finish",
        out_shape=[jax.ShapeDtypeStruct(*o) for o in outs.values()],
        in_specs=[vmem] * len(ins),
        out_specs=[vmem] * len(outs),
        compiler_params=pltpu.CompilerParams(vmem_limit_bytes=VMEM_LIMIT),
    )(*got.values())
    return dict(zip(outs, done))


def sine_tables(frames, channels, fine):
    half_width = channels // 2
    rate = np.exp(-(math.log(10000.0) / (half_width - 1)) * np.arange(half_width))
    small = np.arange(fine)[:, None] * rate[None, :]
    large = np.arange(0, frames, fine)[:, None] * rate[None, :]
    table = dict(fine_s=np.sin(small), fine_c=np.cos(small), coarse_s=np.sin(large), coarse_c=np.cos(large))
    return {n: jnp.asarray(t, F32) for n, t in table.items()}


def on_device(
    mel_input,
    conv1_weight,
    conv1_bias,
    conv2_weight,
    conv2_bias,
    norm1_gain,
    norm1_bias,
    qkv_weight,
    qkv_bias,
    out_weight,
    out_bias,
    norm2_gain,
    norm2_bias,
    up_weight,
    up_bias,
    down_weight,
    down_bias,
    cotangent,
    speech_mask,
):
    mels = mel_input.shape[1]
    T, D = cotangent.shape[1] // 2, cotangent.shape[2]
    F2 = up_weight.shape[1]
    side, half = F2 // D, D // 2
    bits = (lax.axis_size("dp") - 1).bit_length()
    lanes = -(-3 * mels // 128) * 128
    near = dict(
        w1=conv1_weight,
        mask=speech_mask,
        qkvb=qkv_bias,
        upb=up_bias,
        c1b=conv1_bias,
        c2b=conv2_bias,
        n1g=norm1_gain,
        n1b=norm1_bias,
        oub=out_bias,
        n2g=norm2_gain,
        n2b=norm2_bias,
        dnb=down_bias,
    )
    near.update(sine_tables(4 * T, D, 32))
    got = run_layer(
        bits,
        near,
        dict(
            mel=mel_input,
            cot=cotangent,
            w2_l=conv2_weight,
            wqkv_l=qkv_weight,
            wo_l=out_weight,
            up_l=up_weight,
            down_l=down_weight,
        ),
        dict(
            enc_o=((2 * T, D), BF),
            mel_o=((2 * T, 256), BF),
            down_o=((F2, D), BF),
            up_o=((D, F2), BF),
            out_o=((half, D), BF),
            qkv_o=((3, D, half), BF),
            c2_o=((3 * D, D), BF),
            c1_o=((lanes, D), BF),
            small_o=((16, D), F32),
        ),
        T,
        D,
        F2,
        lanes,
    )
    done = run_finish(got, mels, side)
    names = ("enc", "mel", "c1", "c1b", "c2", "c2b", "n1g", "n1b", "qkv", "qkvb")
    names += ("out", "oub", "n2g", "n2b", "up", "upb", "down", "dnb")
    return tuple(done[n] for n in names)


def solution(mesh):
    placed = (
        P("dp", None, "seq"),
        P(),
        P(),
        P(),
        P(),
        P(),
        P(),
        P(None, None, "mp"),
        P(None, "mp"),
        P("mp", None),
        P(),
        P(),
        P(),
        P(None, "mp"),
        P("mp"),
        P("mp", None),
        P(),
        P("dp", "seq", None),
        P("dp", "seq"),
    )
    return jax.shard_map(
        on_device,
        mesh=mesh,
        in_specs=placed,
        out_specs=(
            P("dp", "seq", None),
            P("dp", None, "seq"),
            P(),
            P(),
            P(),
            P(),
            P(),
            P(),
            P(None, None, "mp"),
            P(None, "mp"),
            P("mp", None),
            P(),
            P(),
            P(),
            P(None, "mp"),
            P("mp"),
            P("mp", None),
            P(),
        ),
        check_vma=False,
    )
```

```python
import functools
import math

import jax
import jax.numpy as jnp
import numpy as np
from jax import lax
from jax.experimental import pallas as pl
from jax.experimental.pallas import tpu as pltpu
from jax.sharding import PartitionSpec as P

HEAD = 64
BF = jnp.bfloat16
F32 = jnp.float32
MESH = pl.DeviceIdType.MESH
VMEM_LIMIT = 61 * 1024 * 1024
C1B, C2B, N1G, N1B, OUB, N2G, N2B, DNB, QB, VB, UPB = range(11)


class Box:
    pass


def dot(a, b, ca, cb):
    return lax.dot_general(a, b, (((ca,), (cb,)), ((), ())), preferred_element_type=F32)


def nn(a, b):
    return dot(a, b, 1, 0)


def nt(a, b):
    return dot(a, b, 1, 1)


def tn(a, b):
    return dot(a, b, 0, 0)


def rows_loop(total, step, body, unroll=1):
    step = min(step, total)

    def one(i, carry):
        body(pl.ds(pl.multiple_of(i * step, step), step))
        return carry

    lax.fori_loop(0, total // step, one, 0, unroll=unroll)


def gelu_parts(v):
    t = 1.0 / (1.0 + (0.3275911 / math.sqrt(2.0)) * jnp.abs(v))
    e = jnp.exp(-0.5 * v * v)
    poly = 1.061405429 * t - 1.453152027
    poly = poly * t + 1.421413741
    poly = poly * t - 0.284496736
    poly = poly * t + 0.254829592
    tail = (0.5 * t) * poly * e
    return jnp.where(v >= 0, 1.0 - tail, tail), e * (1.0 / math.sqrt(2.0 * math.pi))


def gelu_both(v):
    cdf, pdf = gelu_parts(v)
    return v * cdf, cdf + v * pdf


def normal(x):
    center = x - jnp.mean(x, axis=-1, keepdims=True)
    spread = jnp.mean(center * center, axis=-1, keepdims=True)
    inv = lax.rsqrt(spread + 1e-05)
    return center * inv, inv


def normal_pull(gy, hat, inv):
    return inv * (
        gy
        - jnp.mean(gy, axis=-1, keepdims=True)
        - hat * jnp.mean(gy * hat, axis=-1, keepdims=True)
    )


def vec(r, i):
    return r.vecs[i : i + 1, :]


def add_small(r, i, value):
    r.small[i : i + 1, :] += value


def col(value):
    return jnp.sum(value, axis=0, keepdims=True)


def stage_mel_rows(r, sub):
    T, D = r.stream.shape
    row = lax.broadcasted_iota(jnp.int32, (256, 256), 0)
    lane = lax.broadcasted_iota(jnp.int32, (256, 256), 1)
    pick = jnp.where(lane == 2 * (row % 128) + row // 128, 1.0, 0.0).astype(BF)
    base = sub * 2 * T

    def lanes(start, size):
        return r.melbuf[:, pl.ds(pl.multiple_of(base + start, 128), size)]

    row = lax.broadcasted_iota(jnp.int32, (16, 128), 0)
    lane = lax.broadcasted_iota(jnp.int32, (16, 128), 1)

    def select(at, to):
        return jnp.where(jnp.logical_and(row == to, lane == at), 1.0, 0.0).astype(BF)

    before, after = lanes(0, 128), lanes(128 + 2 * T, 128)
    r.mele[0:8, :] = nt(select(126, 7), before)[0:8, :]
    r.melo[0:8, :] = nt(select(127, 7), before)[0:8, :]
    r.mele[T + 8 : T + 16, :] = nt(select(0, 0), after)[0:8, :]
    for k in range(T // 128):
        both = nt(pick, lanes(128 + 256 * k, 256))
        r.mele[8 + 128 * k : 136 + 128 * k, :] = both[0:128, :]
        r.melo[8 + 128 * k : 136 + 128 * k, :] = both[128:256, :]


def three(a, b, c):
    return jnp.concatenate([a, b, c], axis=1).astype(BF)


def stage_first(r, first):
    T, D = r.stream.shape
    for o in range(3):
        r.w1p[128 * o : 128 * o + r.w1.shape[1], :] = r.w1[o]
        r.w1p[128 * o + r.w1.shape[1] : 128 * (o + 1), :] = jnp.zeros((128 - r.w1.shape[1], D), BF)
    w1 = r.w1p[...]
    edge = nn(three(r.mele[0:16, :], r.melo[0:16, :], r.mele[1:17, :]), w1) + vec(r, C1B)
    edge = gelu_both(edge)[0] * jnp.where(first, 0.0, 1.0)
    r.odd[0:8, :] = edge[0:8, :]
    r.xe[...] = three(r.melo[7 : 7 + T, :], r.mele[8 : 8 + T, :], r.melo[8 : 8 + T, :])
    r.xo[...] = three(r.mele[8 : 8 + T, :], r.melo[8 : 8 + T, :], r.mele[9 : 9 + T, :])
    r.tmp[...] = nn(r.xe[...], w1)

    def even(rows):
        value, slope = gelu_both(r.tmp[rows, :] + vec(r, C1B))
        r.he[rows, :] = value.astype(BF)
        r.dge[rows, :] = slope

    rows_loop(T, 32, even)


def stage_odd(r):
    T, D = r.stream.shape
    r.tmp[...] = nn(r.xo[...], r.w1p[...])

    def odd(rows):
        value, slope = gelu_both(r.tmp[rows, :] + vec(r, C1B))
        r.ho[rows, :] = value.astype(BF)
        r.odd[pl.ds(pl.multiple_of(rows.start + 8, 8), rows.size), :] = value
        r.dgo[rows, :] = slope

    rows_loop(T, 32, odd)


def stage_second(r, place):
    T, D = r.stream.shape
    r.hp[...] = r.odd[7 : 7 + T, :].astype(BF)
    r.tmp[...] = nn(r.hp[...], r.w2[0]) + nn(r.he[...], r.w2[1]) + nn(r.ho[...], r.w2[2])
    fine = r.fine_s.shape[0]

    def second(rows):
        value, slope = gelu_both(r.tmp[rows, :] + vec(r, C2B))
        at = place * (T // fine) + rows.start // fine
        s0, c0 = r.coarse_s[pl.ds(at, 1), :], r.coarse_c[pl.ds(at, 1), :]
        s1, c1 = r.fine_s[...], r.fine_c[...]
        stream = value + jnp.concatenate([s0 * c1 + c0 * s1, c0 * c1 - s0 * s1], axis=1)
        r.dg2[rows, :] = slope
        r.stream[rows, :] = stream
        r.normed[rows, :] = (normal(stream)[0] * vec(r, N1G) + vec(r, N1B)).astype(BF)

    rows_loop(T, fine, second)


def stage_mask(r, sub):
    T, D = r.stream.shape
    row = r.mask[0:1, pl.ds(pl.multiple_of(sub * T, 128), T)].astype(F32)
    r.wide[0:T, :] = jnp.broadcast_to(row, (128, T)).T

    def one(rows):
        keep = r.wide[rows, :]
        keep = jnp.concatenate([keep] * (D // 128), axis=1)
        r.bg[rows, :] = (r.bg[rows, :].astype(F32) * keep).astype(BF)

    rows_loop(T, 32, one)


def stage_qkv(r, part, h):
    T, D = r.stream.shape
    half, qr = D // 2, D // 4
    bias, scale = ((QB, HEAD**-0.5), (None, 1.0), (VB, 1.0))[part]
    value = nn(r.normed[...], r.wqkv[h, part])
    if bias is not None:
        value = value + r.vecs[bias : bias + 1, pl.ds(pl.multiple_of(h * half, half), half)]
    value = (value.astype(BF).astype(F32) * scale).T.astype(BF)
    for k in range(2):
        r.kv[rows16((3 * (3 + k) + part) * half + h * qr, qr), :] = value[k * qr : (k + 1) * qr, :]


def at_head(start, h):
    return pl.ds(pl.multiple_of(start + h * HEAD, HEAD), HEAD)


def head_loop(steps, hooks, body):
    def one(step, carry):
        for at, todo in hooks.items():
            if not todo:
                continue

            @pl.when(step == at)
            def _(todo=todo):
                for act in todo:
                    act()

        body(step)
        return carry

    lax.fori_loop(0, steps, one, 0)


def attend(r, c, m, hooks):
    S, T = r.kv.shape[0] // 15, r.kv.shape[1]
    heads = S // HEAD
    r.top[...] = jnp.full(r.top.shape, -jnp.inf, F32)
    r.total[...] = jnp.zeros(r.total.shape, F32)
    r.mixt[...] = jnp.zeros(r.mixt.shape, F32)

    def body(step):
        quarter, u, pair = step // heads, step % heads, heads // 2
        g = 2 * (quarter // 2) + u // pair
        h = (m + (1 - 2 * m) * ((quarter + 1) // 2 % 2)) * pair + u % pair
        own = (3 - g) // 3
        slot = own * (3 + c) + (1 - own) * ((g + 1) % 3)
        k = r.kv[at_head((3 * slot + 1) * S, h), :]
        v = r.kv[at_head((3 * slot + 2) * S, h), :]
        for i, home in enumerate((3 + c, 2)):
            q = r.kv[at_head(3 * home * S, h), :]
            s = tn(k, q)
            before = r.top[i * heads + h]
            top = jnp.maximum(before, jnp.max(s, axis=0, keepdims=True))
            p = jnp.exp(s - top)
            keep = jnp.exp(before - top)
            rows = at_head(i * S, h)
            r.top[i * heads + h] = top
            r.total[i * heads + h] = keep * r.total[i * heads + h] + jnp.sum(p, axis=0, keepdims=True)
            r.mixt[rows, :] = keep * r.mixt[rows, :] + nn(v, p.astype(BF))

    head_loop(4 * heads, hooks, body)


def attend_end(r, i):
    S = r.kv.shape[0] // 15
    heads = S // HEAD

    def one(h, carry):
        rows = at_head(i * S, h)
        total = r.total[i * heads + h]
        value = r.mixt[rows, :] * (1.0 / total)
        r.mixt[rows, :] = value
        r.mixb[rows, :] = value.astype(BF)
        r.top[i * heads + h] = r.top[i * heads + h] + jnp.log(total)
        return carry

    lax.fori_loop(0, heads, one, 0)


def stage_mid(r, c):
    T, D = r.stream.shape
    half = D // 2
    r.tmp[...] = tn(r.mixb[0:half, :], r.wo[rows16(c * half, half), :])
    r.tmp[...] += tn(r.mix_got[...], r.wo[rows16((1 - c) * half, half), :])

    def one(rows):
        mid = r.stream[rows, :] + r.tmp[rows, :] + vec(r, OUB)
        r.mid[rows, :] = mid
        r.ntwo[rows, :] = (normal(mid)[0] * vec(r, N2G) + vec(r, N2B)).astype(BF)

    rows_loop(T, 32, one)


def stage_ff(r, hooks):
    T, D = r.stream.shape
    side = r.up.shape[2] // D
    parts, width = 2 * side, D
    add_small(r, DNB, col(r.bg[...].astype(F32)))

    def chunk(t):
        into, at = t % 2, t // 2
        j = into * side + at
        up = r.up[into, :, pl.ds(pl.multiple_of(at * D, D), D)]
        down = r.down[pl.ds(pl.multiple_of(j * D, D), D), :]
        r.tmp[...] = nn(r.ntwo[...], up)
        r.tmp2[...] = nt(r.bg[...], down)
        bias = r.vecs[pl.ds(UPB + j, 1), :]

        def one(i, acc):
            rows = pl.ds(pl.multiple_of(i * 32, 32), 32)
            value, slope = gelu_both(r.tmp[rows, :] + bias)
            r.act[rows, :] = value.astype(BF)
            grad = (r.tmp2[rows, :] * slope).astype(BF)
            r.ing[rows, :] = grad
            return acc + col(grad.astype(F32))

        r.small[pl.ds(UPB + j, 1), :] = lax.fori_loop(0, T // 32, one, jnp.zeros((1, width), F32))
        act = r.act[...]
        ing = r.ing[...]
        out = nn(act, down)
        back = nt(ing, up)

        r.ffo[...] += out
        r.ntg[...] += back
        rows = pl.ds(pl.multiple_of(t * D, D), D)
        r.g_down[rows, :] = tn(act, r.bg[...]).astype(BF)
        r.g_up[rows, :] = tn(r.ntwo[...], ing).astype(BF)

    r.ffo[...] = jnp.zeros_like(r.ffo)
    r.ntg[...] = jnp.zeros_like(r.ntg)
    head_loop(parts, hooks, chunk)


def stage_mid_pull(r):
    T, D = r.stream.shape

    def one(i, accs):
        rows = pl.ds(pl.multiple_of(i * 32, 32), 32)
        mid = r.mid[rows, :]
        enc = (mid + r.ffo[rows, :] + vec(r, DNB)).astype(BF)
        hat, inv = normal(mid)
        grad = r.ntg[rows, :]
        smg = r.bg[rows, :].astype(F32) + normal_pull(grad * vec(r, N2G), hat, inv)
        r.enc[rows, :] = enc
        r.smg[rows, :] = smg
        attg = smg.astype(BF)
        r.attg[rows, :] = attg
        return accs[0] + col(grad * hat), accs[1] + col(grad), accs[2] + col(attg.astype(F32))

    zero = jnp.zeros((1, D), F32)
    gain, bias, out_bias = lax.fori_loop(0, T // 32, one, (zero, zero, zero))
    add_small(r, N2G, gain)
    add_small(r, N2B, bias)
    add_small(r, OUB, out_bias)


def stage_do(r, c, own):
    half = r.attg.shape[1] // 2
    k = c if own else 1 - c
    value = nt(r.wo[rows16(k * half, half), :], r.attg[...]).astype(BF)
    if own:
        r.dot[0:half, :] = value
    else:
        r.dot_out[...] = value


def stage_out_weights(r, c):
    D = r.attg.shape[1]
    half, qr = D // 2, D // 4
    for k, mix in ((c, r.mixb[0:half, :]), (1 - c, r.mix_got[...])):
        value = nn(mix, r.attg[...]).astype(BF)
        for h in range(2):
            r.g_out[rows16(h * half + k * qr, qr), :] = value[h * qr : (h + 1) * qr, :]


def stage_diag(r, i):
    S = r.kv.shape[0] // 15
    heads = S // HEAD

    def one(h, carry):
        rows = at_head(i * S, h)
        value = r.dot[rows, :].astype(F32) * r.mixt[rows, :]
        r.diag[i * heads + h] = jnp.sum(value, axis=0, keepdims=True)
        return carry

    lax.fori_loop(0, heads, one, 0)


def attend_pull(r, c, hooks):
    S, T = r.kv.shape[0] // 15, r.kv.shape[1]
    heads = S // HEAD
    r.dqt[...] = jnp.zeros(r.dqt.shape, F32)

    def body(step):
        g, h = step // heads, step % heads
        slot = g + (g // 3) * c
        k = r.kv[at_head((3 * slot + 1) * S, h), :]
        v = r.kv[at_head((3 * slot + 2) * S, h), :]
        dk, dv = None, None
        for i, home in enumerate((3 + c, 2)):
            q = r.kv[at_head(3 * home * S, h), :]
            rows = at_head(i * S, h)
            do = r.dot[rows, :]
            p = jnp.exp(tn(k, q) - r.top[i * heads + h])
            ds = (p * (tn(v, do) - r.diag[i * heads + h])).astype(BF)
            dv_i, dk_i = nt(do, p.astype(BF)), nt(q, ds)
            dk, dv = (dk_i, dv_i) if dk is None else (dk + dk_i, dv + dv_i)
            r.dqt[rows, :] += nn(k, ds)
        r.dkv[at_head(2 * g * S, h), :] = dk.astype(BF)
        r.dkv[at_head((2 * g + 1) * S, h), :] = dv.astype(BF)

    head_loop(4 * heads, hooks, body)


def piece_of(r, part, h):
    D, qr = r.attg.shape[1], r.attg.shape[1] // 4
    at = part * D + h * qr
    return jnp.concatenate([r.dsum[at : at + qr, :], r.dsum[at + 2 * qr : at + 3 * qr, :]], axis=0)


def stage_qkv_weights(r, part):
    T, D = r.stream.shape
    half = D // 2
    ones = jnp.ones((8, T), BF)
    for h in range(2):
        piece = piece_of(r, part, h)
        if part != 1:
            row = QB if part == 0 else VB
            r.small[row : row + 1, h * half : (h + 1) * half] = nt(ones, piece)[0:1, :]
        grad = nt(r.normedt[...], piece).astype(BF)
        at = (2 * part + h) * half
        r.g_qkv[at : at + half, 0:half] = grad[0:half, :]
        r.g_qkv[at : at + half, half:D] = grad[half:D, :]


def stage_qkv_pull(r):
    T, D = r.stream.shape
    total = None
    for part in range(3):
        for h in range(2):
            back = nn(r.wqkv[h, part], piece_of(r, part, h))
            total = back if total is None else total + back
    r.tmp[...] = total.T


def stage_norm_pull(r):
    T, D = r.stream.shape

    def one(i, accs):
        rows = pl.ds(pl.multiple_of(i * 32, 32), 32)
        hat, inv = normal(r.stream[rows, :])
        grad = r.tmp[rows, :]
        back = r.smg[rows, :] + normal_pull(grad * vec(r, N1G), hat, inv)
        sg = (back * r.dg2[rows, :]).astype(BF)
        r.sg[rows, :] = sg
        return accs[0] + col(grad * hat), accs[1] + col(grad), accs[2] + col(sg.astype(F32))

    zero = jnp.zeros((1, D), F32)
    gain, bias, c2b = lax.fori_loop(0, T // 32, one, (zero, zero, zero))
    add_small(r, N1G, gain)
    add_small(r, N1B, bias)
    add_small(r, C2B, c2b)


def stage_conv2_pull(r, next_row):
    T, D = r.stream.shape
    sg = r.sg[...]
    r.shift[0:T, :] = nt(sg, r.w2[0])
    r.shift[T : T + 16, :] = nt(next_row, r.w2[0])
    r.tmp[...] = nt(sg, r.w2[1])
    r.tmp2[...] = nt(sg, r.w2[2]) + r.shift[1 : T + 1, :]


def stage_first_pull(r):
    T, D = r.stream.shape

    def one(i, acc):
        rows = pl.ds(pl.multiple_of(i * 32, 32), 32)
        even = (r.tmp[rows, :] * r.dge[rows, :]).astype(BF)
        odd = (r.tmp2[rows, :] * r.dgo[rows, :]).astype(BF)
        r.fe[rows, :] = even
        r.fo[rows, :] = odd
        return acc + col(even.astype(F32)) + col(odd.astype(F32))

    add_small(r, C1B, lax.fori_loop(0, T // 32, one, jnp.zeros((1, D), F32)))


def stage_conv2_weights(r, i):
    D = r.stream.shape[1]
    tap = (r.hp, r.he, r.ho)[i]
    r.g_c2[i * D : (i + 1) * D, :] = tn(tap[...], r.sg[...]).astype(BF)


def stage_conv1_weights(r):
    value = (tn(r.xe[...], r.fe[...]) + tn(r.xo[...], r.fo[...])).astype(BF)
    mels = r.w1.shape[1]
    for o in range(3):
        r.g_c1[mels * o : mels * (o + 1), :] = value[128 * o : 128 * o + mels, :]
    r.g_c1[3 * mels :, :] = jnp.zeros((r.g_c1.shape[0] - 3 * mels, r.g_c1.shape[1]), BF)


def stage_mel(r, next_row, prev_row):
    T, D = r.stream.shape
    fe, fo = r.fe[...], r.fo[...]
    w = [r.w1p[128 * o : 128 * (o + 1), :] for o in range(3)]
    r.wide[16 : 16 + T, :] = nt(fo, w[2])
    r.wide[0:16, :] = nt(prev_row, w[2])
    r.melg[:, 0:128] = (nt(fe, w[1]) + nt(fo, w[0]) + r.wide[15 : 15 + T, :]).astype(BF)
    r.wide[0:T, :] = nt(fe, w[0])
    r.wide[T : T + 16, :] = nt(next_row, w[0])
    r.melg[:, 128:256] = (nt(fe, w[2]) + nt(fo, w[1]) + r.wide[1 : 1 + T, :]).astype(BF)


class Net:
    def __init__(self, r, bits):
        self.r, self.bits, self.used, self.used_here = r, bits, 0, 0
        self.d, self.c, self.m = (lax.axis_index(n) for n in ("dp", "seq", "mp"))

    def bit(self, dim):
        if dim == "c":
            return self.c
        if dim == "y":
            return self.m
        return (self.d // (1 << dim)) % 2

    def peer(self, dims):
        d = self.d
        for k in dims:
            if k not in ("c", "y"):
                d = d + (1 << k) - 2 * (1 << k) * self.bit(k)
        return (
            d,
            1 - self.c if "c" in dims else self.c,
            1 - self.m if "y" in dims else self.m,
        )

    def greet(self, partners):
        barrier = pltpu.get_barrier_semaphore()
        for dims in partners:
            pl.semaphore_signal(barrier, inc=1, device_id=self.peer(dims), device_id_type=MESH)
        pl.semaphore_wait(barrier, len(partners))

    def copy(self, src, dst, *dims):
        i = self.used
        self.used += 1
        return pltpu.make_async_remote_copy(
            src_ref=src,
            dst_ref=dst,
            send_sem=self.r.send.at[i],
            recv_sem=self.r.recv.at[i],
            device_id=self.peer(dims),
            device_id_type=MESH,
        )

    def send(self, src, dst, *dims):
        copy = self.copy(src, dst, *dims)
        copy.start()
        return copy

    def here(self, src, dst):
        i = self.used_here
        self.used_here += 1
        copy = pltpu.make_async_copy(src, dst, self.r.own.at[i])
        copy.start()
        return copy


def start_all(copies):
    for copy in copies:
        copy.start()


def wait_all(copies):
    for copy in copies:
        copy.wait()


def rows16(start, size):
    return pl.ds(pl.multiple_of(start, 16), size)


def subsets(dims):
    found = [()]
    for dim in dims:
        found += [one + (dim,) for one in found]
    return found[1:]


def sum_plan(rows, halves, order):
    steps, need = [], 0
    for dims in order:
        by_half = halves == 2 and "y" in dims
        cutting = [dim for dim in dims if not (by_half and dim == "y")]
        if rows % (16 << len(cutting)):
            cutting = []
        rows >>= len(cutting)
        if by_half:
            halves = 1
        steps.append((dims, cutting, rows, halves, by_half))
        need += rows * halves * len(subsets(dims))
    return steps, need


class Track:
    def __init__(self, acts):
        self.acts = list(acts)

    def take(self):
        return [self.acts.pop(0)] if self.acts else []


def bucket_sum(net, g, got, done, halves, order):
    R = g.shape[0] // halves
    lo, rows, at, bases = 0, R, 0, [h * R for h in range(halves)]
    acts, back, end = [], [], None

    def start_after(end, copies):
        def act():
            if end is not None:
                end()
            for copy in copies:
                copy.start()

        return act

    def adder(copies, places, n):
        step = 64 if n % 64 == 0 else 32 if n % 32 == 0 else 16

        def end():
            wait_all(copies)
            for to, ofs in places:

                def add(k, carry, to=to, ofs=ofs):
                    mine = rows16(to + k * step, step)
                    value = g[mine, :].astype(F32)
                    for of in ofs:
                        value = value + got[rows16(of + k * step, step), :].astype(F32)
                    g[mine, :] = value.astype(BF)
                    return carry

                lax.fori_loop(0, n // step, add, 0)

        return end

    for dims, cutting, n, _, by_half in sum_plan(R, halves, order)[0]:

        def part_of(other):
            start = lo
            for i, dim in enumerate(reversed(cutting)):
                b = net.bit(dim)
                start = start + (1 - b if dim in other else b) * (n << i)
            return start

        keep = part_of(())
        if by_half:
            bases = [net.m * R]
        copies, ofs = [], [[] for _ in bases]
        for other in subsets(dims):
            sources = [(1 - net.m) * R] if by_half and "y" in other else bases
            for i, base in enumerate(sources):
                src = g.at[rows16(base + part_of(other), n)]
                copies.append(net.copy(src, got.at[rows16(at, n)], *other))
                ofs[i].append(at)
                at += n
        acts.append(start_after(end, copies))
        end = adder(copies, [(base + keep, of) for base, of in zip(bases, ofs)], n)
        if cutting:
            back.append((cutting, n, lo))
        lo, rows = keep, n

    def settle(end=end, lo=lo, base=bases[0], rows=rows):
        end()
        for k in range(rows // 16):
            done[rows16(lo + 16 * k, 16), :] = g[rows16(base + lo + 16 * k, 16), :]

    end = settle
    for cutting, n, before in reversed(back):
        part = rows16(lo, n)
        copies = [net.copy(done.at[part], done.at[part], *other) for other in subsets(cutting)]
        acts.append(start_after(end, copies))
        end = functools.partial(wait_all, copies)
        lo = before
    return Track(acts + [end])


def small_sum(net, value, slots, order):
    acts, end, at = [], None, 0
    for dims in order:
        copies = [net.copy(value, slots.at[at + i], *other) for i, other in enumerate(subsets(dims))]

        def act(end=end, copies=copies):
            if end is not None:
                end()
            start_all(copies)

        def end(copies=copies, at=at):
            wait_all(copies)
            total = value[...]
            for i in range(len(copies)):
                total = total + slots[at + i]
            value[...] = total

        at += len(copies)
        acts.append(act)
    return Track(acts + [end])


def ready(*names):
    pass


def advance(*sums):
    for one in sums:
        for act in one.take():
            act()


def drain(*sums):
    while any(one.acts for one in sums):
        advance(*sums)


def quarter(net):
    return 2 * net.c + net.c + net.m - 2 * net.c * net.m


def choose(slots, by_core, by_y):
    core = jnp.where(by_core, 1.0, 0.0)
    y = jnp.where(by_y, 1.0, 0.0)
    return (slots[0].astype(F32) * core + slots[1].astype(F32) * y).astype(BF)


def pick_next(net, slots):
    q = quarter(net)
    return choose(slots, q == 1, q % 2 == 0)


def pick_prev(net, slots):
    q = quarter(net)
    return choose(slots, q == 2, q % 2 == 1)


ROW_BIASES = ("c1b", "c2b", "n1g", "n1b", "oub", "n2g", "n2b", "dnb")


ORDERS = dict(
    down=("ycwzx", "cyxzw"),
    up=("cxzyw", "cyzwx"),
    out=("cyzxw",),
    qkv=("cyzxw", "czyxw", "cxzyw"),
    c2=("cxywz", "cyzxw", "czxyw"),
    c1=("cxyzw",),
    vec=("cyxzw",),
)
SCHEDULE = dict(
    ff2=("down0", "up0"),
    ff3=("up0",),
    ffo=("down1", "up1"),
    out=("down1", "up0", "up1", "out0"),
    pull0=("down0",),
    pull1=("down0", "up0", "out0"),
    pull4=("down0", "up0"),
    pull6=("down0", "down1", "up0", "up1", "out0"),
    pull7=("down0",),
    pull8=("down0", "down1", "up0", "out0"),
    pull9=("up1", "out0"),
    pull11=("down0", "down1", "up0", "out0"),
    pull12=("up1",),
    pull13=("down1", "up0", "up1", "out0"),
    pull14=("up0",),
    pull15=("down0", "down1", "up1", "out0"),
    home=("down0",),
    qkvw1=("qkv1",),
    qkvw2=("qkv2",),
    qkvw0=("down1", "up1", "out0", "qkv0"),
    norm=("qkv1", "qkv2"),
    c2=("out0", "qkv0"),
    c2w0=("c20",),
    c2w1=("down1", "c21"),
    c2w2=("up1", "c22"),
    first=("qkv1", "qkv2", "c20"),
    c1=("down1", "up1", "qkv0", "c21", "c22"),
    c1w=("qkv1", "qkv2", "c10", "vec"),
    mel=("qkv0", "qkv1", "c20", "c10", "vec"),
    end=(
        "qkv2", "c21", "c22", "qkv0", "qkv1", "qkv2", "c10", "vec", "c22", "c20", "vec", "qkv0",
        "qkv1", "qkv2", "c21", "c10", "c22", "c20", "qkv1", "c21", "qkv0", "c10", "vec", "c22",
        "qkv0", "qkv2", "c20", "c21", "c10", "qkv2", "c22", "qkv2", "c20", "c21", "c10", "vec",
        "c22", "qkv1", "c21", "qkv0", "c10", "c20", "qkv1", "c22", "qkv0", "c21", "c20", "c10",
        "c10", "c22", "c21", "c20", "c22", "c21", "c20",
    ),
)


def orders(name, bits):
    dims = dict(c=["c"], y=["y"], x=[0], z=list(range(1, min(2, bits))), w=list(range(2, bits)))
    return [[(dim,) for ch in spec for dim in dims[ch]] for spec in ORDERS[name]]


def layer(r, bits):
    T, D = r.stream.shape
    half, F2 = D // 2, r.down_l.shape[0]
    side = F2 // D
    mels, span = r.w1.shape[1], 4 * T
    net = Net(r, bits)
    c, m = net.c, net.m
    sub = c + m - 2 * c * m
    rows_of_mine = rows16(sub * T, T)

    r.melbuf[...] = jnp.zeros_like(r.melbuf)
    mel_own = net.here(r.mel.at[0], r.melbuf.at[0:mels, 128 : 128 + span])
    qkv_own = net.here(r.wqkv_l, r.wqkv.at[m])
    w2_own = net.here(r.w2_l, r.w2)
    own = [
        net.here(r.wo_l.at[0 : D // 4], r.wo.at[rows16(m * (D // 4), D // 4)]),
        net.here(r.wo_l.at[D // 4 : half], r.wo.at[rows16(half + m * (D // 4), D // 4)]),
        net.here(r.up_l, r.up.at[m]),
        net.here(r.down_l, r.down.at[rows16(m * F2, F2)]),
        net.here(r.cot.at[0, rows_of_mine], r.bg),
    ]
    r.vec_mine[...] = jnp.zeros_like(r.vec_mine)
    own_lanes = pl.ds(pl.multiple_of(m * half, 128), half)
    r.vec_mine[0:2, own_lanes] = r.qkvb[...].astype(F32)
    for k in range(side):
        r.vec_mine[pl.ds(2 + m * side + k, 1), :] = r.upb[k * D : (k + 1) * D].astype(F32).reshape(1, D)
    for k, n in enumerate(ROW_BIASES):
        r.vecs[k : k + 1, :] = getattr(r, n)[...].astype(F32).reshape(1, D)
    net.greet([("c",), ("y",), ("c", "y")] + [(k,) for k in range(bits)])
    vec_copy = net.send(r.vec_mine, r.vec_got, "y")
    mel_own.wait()
    src = pl.ds(pl.multiple_of(128 + (1 - c) * (span - 128), 128), 128)
    dst = pl.ds(pl.multiple_of(c * (span + 128), 128), 128)
    mel_rim = net.send(r.melbuf.at[0:mels, src], r.melbuf.at[0:mels, dst], "c")
    p = 4 * c + 2 * net.bit(0) + net.bit(1) if bits > 1 else 2 * c + net.bit(0)
    cuts = 8 if bits > 1 else 4

    def pass_on(of, at, count, dim):
        def cut(n, base):
            return rows16(base + at * (n // cuts), count * (n // cuts))

        wo = rows16(c * half + of * (D // 4) + (at - c * (cuts // 2)) * (half // cuts), count * (half // cuts))
        parts = [r.wo.at[wo], r.up.at[of, cut(D, 0)], r.down.at[cut(F2, of * F2)]]
        return [net.copy(x, x, dim) for x in parts]

    def pass_qkv(of, at, count, dim):
        rows = r.wqkv.at[of, :, rows16(at * (D // cuts), count * (D // cuts))]
        return net.copy(rows, rows, dim)

    two = 2 if bits > 1 else 1
    qkv_y = pass_qkv(m, p, 1, "y")
    qkv_z = [pass_qkv(1 - m, p, 1, 1)] if bits > 1 else []
    qkv_x = pass_qkv(1 - m, (p // two) * two, two, 0)
    qkv_c = pass_qkv(1 - m, c * (cuts // 2), cuts // 2, "c")
    ff_y = pass_on(m, p, 1, "y")
    ff_z = pass_on(1 - m, p, 1, 1) if bits > 1 else []
    ff_x = pass_on(1 - m, (p // two) * two, two, 0)
    ff_c = pass_on(1 - m, c * (cuts // 2), cuts // 2, "c")
    qkv_own.wait()
    qkv_y.start()
    wait_all(own)
    r.small[...] = jnp.zeros_like(r.small)
    mel_rim.wait()
    stage_mel_rows(r, sub)
    start_all(ff_y)
    stage_first(r, jnp.logical_and(c == 0, m == 0))
    qkv_y.wait()
    start_all(qkv_z)
    stage_odd(r)
    wait_all(qkv_z)
    qkv_x.start()
    wait_all(ff_y)
    start_all(ff_z)
    w2_own.wait()
    stage_second(r, quarter(net))
    vec_copy.wait()
    r.vecs[8:16, :] = r.vec_mine[...] + r.vec_got[...]
    qkv_x.wait()
    qkv_c.start()

    def block(slot, part, h):
        return r.kv.at[rows16((3 * slot + part) * half + h * (half // 2), half // 2)]

    def project(h):
        far = []
        for part in (1, 2):
            stage_qkv(r, part, h)
            far.append(net.copy(block(3 + c, part, h), block(0, part, h), "y"))
            far.append(net.copy(block(4 - c, part, h), block(1, part, h), "c", "y"))
            start_all(far[-2:])
        stage_qkv(r, 0, h)
        near = [net.copy(block(4 - c, part, h), block(2, part, h), "c") for part in range(3)]
        start_all(near)
        return far, near

    far_own, near_own = project(m)
    stage_mask(r, sub)
    wait_all(near_own)
    heads = half // HEAD
    far_other = [
        net.copy(block(own, part, 1 - m), block(to, part, 1 - m), *dims)
        for part in (1, 2)
        for own, to, dims in ((3 + c, 0, ("y",)), (4 - c, 1, ("c", "y")))
    ]
    near_other = [net.copy(block(4 - c, part, 1 - m), block(2, part, 1 - m), "c") for part in range(3)]

    def project_other():
        qkv_c.wait()
        stage_qkv(r, 1, 1 - m)
        start_all(far_other[0:2])
        stage_qkv(r, 2, 1 - m)
        start_all(far_other[2:4])
        stage_qkv(r, 0, 1 - m)
        start_all(near_other)

    hooks = {
        heads - 1: [project_other],
        heads: [lambda: wait_all(near_other), lambda: wait_all(ff_z), lambda: start_all(ff_x)],
        2 * heads: [lambda: wait_all(far_own)],
        5 * heads // 2: [lambda: wait_all(ff_x), lambda: start_all(ff_c)],
        3 * heads: [lambda: wait_all(far_other)],
    }
    attend(r, c, m, hooks)
    attend_end(r, 1)
    mix_c = net.send(r.mixb.at[half:D], r.mix_got, "c")
    attend_end(r, 0)
    wait_all(ff_c)
    mix_c.wait()
    stage_mid(r, c)

    def summed(n, part, rows, halves):
        views = [
            getattr(r, "g_" + n).at[part * rows * halves : (part + 1) * rows * halves],
            getattr(r, "got_%s%d" % (n, part)),
            getattr(r, "done_" + n).at[part * rows : (part + 1) * rows],
        ]
        return bucket_sum(net, *views, halves, orders(n, bits)[part])

    tracks = {}
    for n, rows, halves, parts in (
        ("down", D, 2, side),
        ("up", D, 2, side),
        ("out", half, 2, 1),
        ("qkv", half, 2, 3),
        ("c2", D, 1, 3),
        ("c1", r.g_c1.shape[0], 1, 1),
    ):
        for part in range(parts):
            tracks["%s%d" % (n, part)] = summed(n, part, rows, halves)
    tracks["vec"] = small_sum(net, r.small, r.got_small, orders("vec", bits)[0])

    def acts_at(name):
        return [act for n in SCHEDULE.get(name, ()) if n in tracks for act in tracks[n].take()]

    def point(name):
        for act in acts_at(name):
            act()

    hooks = {}
    for step in range(2 * side):
        if step and step % 2 == 0:
            ready("down%d" % (step // 2 - 1), "up%d" % (step // 2 - 1))
        hooks[step] = acts_at("ff%d" % step)
    stage_ff(r, hooks)
    ready("down%d" % (side - 1), "up%d" % (side - 1))
    point("ffo")
    stage_mid_pull(r)
    stage_do(r, c, False)
    do_c = net.send(r.dot_out, r.dot.at[half:D], "c")
    point("mid")
    stage_out_weights(r, c)
    ready("out0")
    point("out")
    stage_do(r, c, True)
    stage_diag(r, 0)
    do_c.wait()
    stage_diag(r, 1)
    enc = [
        net.copy(r.enc, r.enc_got, "y"),
        pltpu.make_async_copy(r.enc, r.enc_o.at[rows_of_mine], r.own.at[39]),
    ]

    both = half * 2
    home_y = net.copy(r.dkv.at[0:both], r.from_y, "y")
    home_d = net.copy(r.dkv.at[both : 2 * both], r.from_d, "c", "y")
    home_c = net.copy(r.dkv.at[2 * both : 3 * both], r.from_c.at[half:], "c")
    hooks = {}

    def at_step(step, *acts):
        hooks.setdefault(step * heads // 4, []).extend(acts)

    at_step(4, home_y.start)
    at_step(8, home_d.start)
    at_step(11, lambda: start_all(enc))
    at_step(12, home_c.start)
    for step in range(16):
        at_step(step, *acts_at("pull%d" % step))
    attend_pull(r, c, hooks)
    r.dq_out[...] = (r.dqt[half:D, :] * HEAD**-0.5).astype(BF)
    dq_c = net.send(r.dq_out, r.from_c.at[0:half], "c")
    r.dsum[rows16(c * half, half), :] = (r.dqt[0:half, :] * HEAD**-0.5).astype(BF)
    point("home")
    home_y.wait()
    home_d.wait()
    home_c.wait()

    def total(i, carry):
        for part in range(2):
            rows = rows16(part * half + i * 32, 32)
            mine = r.dkv[rows16(3 * both + part * half + i * 32, 32), :].astype(F32) + r.from_y[rows, :].astype(F32)
            r.dsum[rows16((1 + part) * D + c * half + i * 32, 32), :] = mine.astype(BF)
            other = r.from_c[rows16((1 + part) * half + i * 32, 32), :].astype(F32) + r.from_d[rows, :].astype(F32)
            r.dsum[rows16((1 + part) * D + (1 - c) * half + i * 32, 32), :] = other.astype(BF)
        return carry

    lax.fori_loop(0, half // 32, total, 0)
    dq_c.wait()
    r.dsum[rows16((1 - c) * half, half), :] = r.from_c[0:half, :]

    r.normedt[...] = r.normed[...].astype(F32).T.astype(BF)
    for part in (1, 2, 0):
        stage_qkv_weights(r, part)
        ready("qkv%d" % part)
        point("qkvw%d" % part)
    stage_qkv_pull(r)
    point("norm")
    stage_norm_pull(r)
    rim = [net.send(r.sg.at[0:16], r.slots.at[0, i], dim) for i, dim in enumerate(("c", "y"))]
    point("c2")
    for part in range(3):
        stage_conv2_weights(r, part)
        ready("c2%d" % part)
        point("c2w%d" % part)
    wait_all(rim)
    stage_conv2_pull(r, pick_next(net, r.slots.at[0]))
    point("first")
    stage_first_pull(r)
    rim = [net.send(r.fe.at[0:16], r.slots.at[1, i], dim) for i, dim in enumerate(("c", "y"))]
    rim += [net.send(r.fo.at[T - 16 : T], r.slots.at[2, i], dim) for i, dim in enumerate(("c", "y"))]
    point("c1")
    stage_conv1_weights(r)
    ready("c10", "vec")
    point("c1w")
    wait_all(rim)
    stage_mel(r, pick_next(net, r.slots.at[1]), pick_prev(net, r.slots.at[2]))
    rows_of_yours = rows16((1 - sub) * T, T)
    mel_y = net.send(r.melg, r.melg_got, "y")
    point("mel")
    wait_all(enc)
    ends = [
        net.here(r.enc_got, r.enc_o.at[rows_of_yours]),
        net.here(r.melg, r.mel_o.at[rows_of_mine]),
    ]
    point("end")
    drain(*tracks.values())

    ends.append(net.here(r.done_down, r.down_o))
    for j in range(side):
        ends.append(net.here(r.done_up.at[j * D : (j + 1) * D], r.up_o.at[:, j * D : (j + 1) * D]))
    ends.append(net.here(r.done_out, r.out_o))
    for part in range(3):
        for j in range(2):
            ends.append(
                net.here(
                    r.done_qkv.at[part * half : (part + 1) * half, j * half : (j + 1) * half],
                    r.qkv_o.at[part, j * half : (j + 1) * half],
                )
            )
    ends.append(net.here(r.done_c2, r.c2_o))
    ends.append(net.here(r.done_c1, r.c1_o))
    ends.append(net.here(r.small, r.small_o))
    mel_y.wait()
    ends.append(net.here(r.melg_got, r.mel_o.at[rows_of_yours]))
    wait_all(ends)


def run_layer(bits, near, far, outs, T, D, F2, lanes):
    half, H = D // 2, D // HEAD
    td, dt = (T, D), (D, T)
    buckets = dict(down=(D, 2, F2 // D), up=(D, 2, F2 // D), out=(half, 2, 1), qkv=(half, 2, 3), c2=(D, 1, 3), c1=(lanes, 1, 1))
    scratch = dict(
        melbuf=((128, 4 * T + 256), BF),
        mele=((T + 24, 128), F32),
        melo=((T + 24, 128), F32),
        xe=((T, 384), BF),
        xo=((T, 384), BF),
        w1p=((384, D), BF),
        w2=((3, D, D), BF),
        bg=(td, BF),
        wqkv=((2, 3, D, half), BF),
        wo=((D, D), BF),
        up=((2, D, F2), BF),
        down=((2 * F2, D), BF),
        vecs=((16, D), F32),
        vec_mine=((8, D), F32),
        vec_got=((8, D), F32),
        stream=(td, F32),
        he=(td, BF),
        ho=(td, BF),
        hp=(td, BF),
        dge=(td, F32),
        dgo=(td, F32),
        dg2=(td, F32),
        normed=(td, BF),
        kv=((15 * half, T), BF),
        mixt=(dt, F32),
        mixb=(dt, BF),
        mix_got=((half, T), BF),
        dot=(dt, BF),
        dot_out=((half, T), BF),
        top=((H, 1, T), F32),
        total=((H, 1, T), F32),
        diag=((H, 1, T), F32),
        tmp=(td, F32),
        tmp2=(td, F32),
        shift=((T + 16, D), F32),
        wide=((T + 16, 128), F32),
        mid=(td, F32),
        ntwo=(td, BF),
        act=(td, BF),
        ing=(td, BF),
        ffo=(td, F32),
        ntg=(td, F32),
        attg=(td, BF),
        dqt=(dt, F32),
        dq_out=((half, T), BF),
        dkv=((8 * half, T), BF),
        from_y=((2 * half, T), BF),
        from_d=((2 * half, T), BF),
        from_c=((3 * half, T), BF),
        dsum=((3 * D, T), BF),
        enc_got=(td, BF),
        melg=((T, 256), BF),
        melg_got=((T, 256), BF),
        small=((16, D), F32),
        got_small=((bits + 2, 16, D), F32),
        slots=((3, 2, 16, D), BF),
    )
    alias = T == D
    for n, (rows, halves, parts) in buckets.items():
        if n not in ("qkv", "c2"):
            scratch["g_" + n] = ((rows * halves * parts, D), BF)
        for part in range(parts):
            need = sum_plan(rows, halves, orders(n, bits)[part])[1]
            scratch["got_%s%d" % (n, part)] = ((need, D), BF)
        scratch["done_" + n] = ((rows * parts, D), BF)
    if not alias:
        scratch.update(g_qkv=((6 * half, D), BF), g_c2=((6 * half, D), BF), normedt=(dt, BF))
    names = list(near) + list(far) + list(outs) + list(scratch) + ["send", "recv", "own"]

    def kernel(*refs):
        r = Box()
        for n, ref in zip(names, refs):
            setattr(r, n, ref)
        r.odd, r.smg, r.sg, r.fe, r.fo, r.enc = r.shift, r.mid, r.ntwo, r.act, r.ing, r.bg
        r.normedt = r.mixb if alias else r.normedt
        if alias:
            r.g_qkv, r.g_c2 = r.kv.at[0 : 6 * half], r.kv.at[6 * half : 12 * half]
        layer(r, bits)

    vmem, anywhere = pl.BlockSpec(memory_space=pltpu.VMEM), pl.BlockSpec(memory_space=pl.ANY)
    got = pl.pallas_call(
        kernel,
        name="layer",
        out_shape=[jax.ShapeDtypeStruct(*o) for o in outs.values()],
        in_specs=[vmem] * len(near) + [anywhere] * len(far),
        out_specs=[anywhere] * len(outs),
        scratch_shapes=[pltpu.VMEM(*s) for s in scratch.values()]
        + [pltpu.SemaphoreType.DMA((256,)), pltpu.SemaphoreType.DMA((256,)), pltpu.SemaphoreType.DMA((40,))],
        compiler_params=pltpu.CompilerParams(
            vmem_limit_bytes=VMEM_LIMIT, collective_id=1, has_side_effects=True
        ),
    )(*near.values(), *far.values())
    return dict(zip(outs, got))


def run_finish(got, mels, side):
    T2, D = got["enc_o"].shape
    half = D // 2
    ins = list(got)
    outs = dict(
        enc=((1, T2, D), BF),
        mel=((1, mels, 2 * T2), F32),
        c1=((3, mels, D), F32),
        c2=((3, D, D), F32),
        qkv=((3, D, half), F32),
        qkvb=((2, half), F32),
        out=((half, D), F32),
        up=((D, side * D), F32),
        upb=((side * D,), F32),
        down=((side * D, D), F32),
    )
    outs.update({n: ((D,), F32) for n in ROW_BIASES})

    def kernel(*refs):
        r = Box()
        for n, ref in zip(ins + list(outs), refs):
            setattr(r, n, ref)
        m = lax.axis_index("mp")

        def cast(src, dst):
            def one(rows):
                dst[rows, :] = src[rows, :].astype(dst.dtype)

            rows_loop(src.shape[0], 256, one)

        cast(r.enc_o, r.enc.at[0])
        cast(r.down_o, r.down)
        cast(r.up_o, r.up)
        cast(r.out_o, r.out)
        for o in range(3):
            cast(r.qkv_o.at[o], r.qkv.at[o])
            cast(r.c2_o.at[o * D : (o + 1) * D], r.c2.at[o])
            r.c1[o] = r.c1_o[o * mels : (o + 1) * mels, :].astype(F32)
        row = lax.broadcasted_iota(jnp.int32, (128, 256), 0)
        lane = lax.broadcasted_iota(jnp.int32, (128, 256), 1)
        even = jnp.where(lane == 2 * row, 1.0, 0.0).astype(BF)
        odd = jnp.where(lane == 2 * row + 1, 1.0, 0.0).astype(BF)
        for k in range(T2 // 128):
            rows = slice(k * 128, (k + 1) * 128)
            value = tn(r.mel_o[rows, 0:128], even) + tn(r.mel_o[rows, 128:256], odd)
            r.mel[0, :, k * 256 : (k + 1) * 256] = value[0:mels, :]
        for k, n in enumerate(ROW_BIASES):
            getattr(r, n)[...] = r.small_o[k : k + 1, :].reshape(D)
        r.qkvb[...] = r.small_o[QB : QB + 2, pl.ds(pl.multiple_of(m * half, 128), half)]
        for k in range(side):
            r.upb[k * D : (k + 1) * D] = r.small_o[pl.ds(UPB + m * side + k, 1), :].reshape(D)

    vmem = pl.BlockSpec(memory_space=pltpu.VMEM)
    done = pl.pallas_call(
        kernel,
        name="finish",
        out_shape=[jax.ShapeDtypeStruct(*o) for o in outs.values()],
        in_specs=[vmem] * len(ins),
        out_specs=[vmem] * len(outs),
        compiler_params=pltpu.CompilerParams(vmem_limit_bytes=VMEM_LIMIT),
    )(*got.values())
    return dict(zip(outs, done))


def sine_tables(frames, channels, fine):
    half_width = channels // 2
    rate = np.exp(-(math.log(10000.0) / (half_width - 1)) * np.arange(half_width))
    small = np.arange(fine)[:, None] * rate[None, :]
    large = np.arange(0, frames, fine)[:, None] * rate[None, :]
    table = dict(fine_s=np.sin(small), fine_c=np.cos(small), coarse_s=np.sin(large), coarse_c=np.cos(large))
    return {n: jnp.asarray(t, F32) for n, t in table.items()}


def on_device(
    mel_input,
    conv1_weight,
    conv1_bias,
    conv2_weight,
    conv2_bias,
    norm1_gain,
    norm1_bias,
    qkv_weight,
    qkv_bias,
    out_weight,
    out_bias,
    norm2_gain,
    norm2_bias,
    up_weight,
    up_bias,
    down_weight,
    down_bias,
    cotangent,
    speech_mask,
):
    mels = mel_input.shape[1]
    T, D = cotangent.shape[1] // 2, cotangent.shape[2]
    F2 = up_weight.shape[1]
    side, half = F2 // D, D // 2
    bits = (lax.axis_size("dp") - 1).bit_length()
    lanes = -(-3 * mels // 128) * 128
    near = dict(
        w1=conv1_weight,
        mask=speech_mask,
        qkvb=qkv_bias,
        upb=up_bias,
        c1b=conv1_bias,
        c2b=conv2_bias,
        n1g=norm1_gain,
        n1b=norm1_bias,
        oub=out_bias,
        n2g=norm2_gain,
        n2b=norm2_bias,
        dnb=down_bias,
    )
    near.update(sine_tables(4 * T, D, 32))
    got = run_layer(
        bits,
        near,
        dict(
            mel=mel_input,
            cot=cotangent,
            w2_l=conv2_weight,
            wqkv_l=qkv_weight,
            wo_l=out_weight,
            up_l=up_weight,
            down_l=down_weight,
        ),
        dict(
            enc_o=((2 * T, D), BF),
            mel_o=((2 * T, 256), BF),
            down_o=((F2, D), BF),
            up_o=((D, F2), BF),
            out_o=((half, D), BF),
            qkv_o=((3, D, half), BF),
            c2_o=((3 * D, D), BF),
            c1_o=((lanes, D), BF),
            small_o=((16, D), F32),
        ),
        T,
        D,
        F2,
        lanes,
    )
    done = run_finish(got, mels, side)
    names = ("enc", "mel", "c1", "c1b", "c2", "c2b", "n1g", "n1b", "qkv", "qkvb")
    names += ("out", "oub", "n2g", "n2b", "up", "upb", "down", "dnb")
    return tuple(done[n] for n in names)


def solution(mesh):
    placed = (
        P("dp", None, "seq"),
        P(),
        P(),
        P(),
        P(),
        P(),
        P(),
        P(None, None, "mp"),
        P(None, "mp"),
        P("mp", None),
        P(),
        P(),
        P(),
        P(None, "mp"),
        P("mp"),
        P("mp", None),
        P(),
        P("dp", "seq", None),
        P("dp", "seq"),
    )
    return jax.shard_map(
        on_device,
        mesh=mesh,
        in_specs=placed,
        out_specs=(
            P("dp", "seq", None),
            P("dp", None, "seq"),
            P(),
            P(),
            P(),
            P(),
            P(),
            P(),
            P(None, None, "mp"),
            P(None, "mp"),
            P("mp", None),
            P(),
            P(),
            P(),
            P(None, "mp"),
            P("mp"),
            P("mp", None),
            P(),
        ),
        check_vma=False,
    )
```

```python
import functools
import math

import jax
import jax.numpy as jnp
import numpy as np
from jax import lax
from jax.experimental import pallas as pl
from jax.experimental.pallas import tpu as pltpu
from jax.sharding import PartitionSpec as P

HEAD = 64
BF = jnp.bfloat16
F32 = jnp.float32
MESH = pl.DeviceIdType.MESH
VMEM_LIMIT = 61 * 1024 * 1024
C1B, C2B, N1G, N1B, OUB, N2G, N2B, DNB, QB, VB, UPB = range(11)


class Box:
    pass


def dot(a, b, ca, cb):
    return lax.dot_general(a, b, (((ca,), (cb,)), ((), ())), preferred_element_type=F32)


def nn(a, b):
    return dot(a, b, 1, 0)


def nt(a, b):
    return dot(a, b, 1, 1)


def tn(a, b):
    return dot(a, b, 0, 0)


def rows_loop(total, step, body, unroll=1):
    step = min(step, total)

    def one(i, carry):
        body(pl.ds(pl.multiple_of(i * step, step), step))
        return carry

    lax.fori_loop(0, total // step, one, 0, unroll=unroll)


def gelu_parts(v):
    t = 1.0 / (1.0 + (0.3275911 / math.sqrt(2.0)) * jnp.abs(v))
    e = jnp.exp(-0.5 * v * v)
    poly = 1.061405429 * t - 1.453152027
    poly = poly * t + 1.421413741
    poly = poly * t - 0.284496736
    poly = poly * t + 0.254829592
    tail = (0.5 * t) * poly * e
    return jnp.where(v >= 0, 1.0 - tail, tail), e * (1.0 / math.sqrt(2.0 * math.pi))


def gelu_both(v):
    cdf, pdf = gelu_parts(v)
    return v * cdf, cdf + v * pdf


def normal(x):
    center = x - jnp.mean(x, axis=-1, keepdims=True)
    spread = jnp.mean(center * center, axis=-1, keepdims=True)
    inv = lax.rsqrt(spread + 1e-05)
    return center * inv, inv


def normal_pull(gy, hat, inv):
    return inv * (
        gy
        - jnp.mean(gy, axis=-1, keepdims=True)
        - hat * jnp.mean(gy * hat, axis=-1, keepdims=True)
    )


def vec(r, i):
    return r.vecs[i : i + 1, :]


def add_small(r, i, value):
    r.small[i : i + 1, :] += value


def col(value):
    return jnp.sum(value, axis=0, keepdims=True)


def stage_mel_rows(r, sub, rim_came):
    T, D = r.stream.shape
    row = lax.broadcasted_iota(jnp.int32, (256, 256), 0)
    lane = lax.broadcasted_iota(jnp.int32, (256, 256), 1)
    pick = jnp.where(lane == 2 * (row % 128) + row // 128, 1.0, 0.0).astype(BF)
    base = sub * 2 * T

    def lanes(start, size):
        return r.melbuf[:, pl.ds(pl.multiple_of(base + start, 128), size)]

    row = lax.broadcasted_iota(jnp.int32, (16, 128), 0)
    lane = lax.broadcasted_iota(jnp.int32, (16, 128), 1)

    def select(at, to):
        return jnp.where(jnp.logical_and(row == to, lane == at), 1.0, 0.0).astype(BF)

    for k in range(T // 128):
        both = nt(pick, lanes(128 + 256 * k, 256))
        r.mele[8 + 128 * k : 136 + 128 * k, :] = both[0:128, :]
        r.melo[8 + 128 * k : 136 + 128 * k, :] = both[128:256, :]
    rim_came()
    before, after = lanes(0, 128), lanes(128 + 2 * T, 128)
    r.mele[0:8, :] = nt(select(126, 7), before)[0:8, :]
    r.melo[0:8, :] = nt(select(127, 7), before)[0:8, :]
    r.mele[T + 8 : T + 16, :] = nt(select(0, 0), after)[0:8, :]


def three(a, b, c):
    return jnp.concatenate([a, b, c], axis=1).astype(BF)


def stage_first(r, first):
    T, D = r.stream.shape
    for o in range(3):
        r.w1p[128 * o : 128 * o + r.w1.shape[1], :] = r.w1[o]
        r.w1p[128 * o + r.w1.shape[1] : 128 * (o + 1), :] = jnp.zeros((128 - r.w1.shape[1], D), BF)
    w1 = r.w1p[...]
    edge = nn(three(r.mele[0:16, :], r.melo[0:16, :], r.mele[1:17, :]), w1) + vec(r, C1B)
    edge = gelu_both(edge)[0] * jnp.where(first, 0.0, 1.0)
    r.odd[0:8, :] = edge[0:8, :]
    r.xe[...] = three(r.melo[7 : 7 + T, :], r.mele[8 : 8 + T, :], r.melo[8 : 8 + T, :])
    r.xo[...] = three(r.mele[8 : 8 + T, :], r.melo[8 : 8 + T, :], r.mele[9 : 9 + T, :])
    r.tmp[...] = nn(r.xe[...], w1)

    def even(rows):
        value, slope = gelu_both(r.tmp[rows, :] + vec(r, C1B))
        r.he[rows, :] = value.astype(BF)
        r.dge[rows, :] = slope

    rows_loop(T, 32, even)


def stage_odd(r):
    T, D = r.stream.shape
    r.tmp[...] = nn(r.xo[...], r.w1p[...])

    def odd(rows):
        value, slope = gelu_both(r.tmp[rows, :] + vec(r, C1B))
        r.ho[rows, :] = value.astype(BF)
        r.odd[pl.ds(pl.multiple_of(rows.start + 8, 8), rows.size), :] = value
        r.dgo[rows, :] = slope

    rows_loop(T, 32, odd)


def stage_second(r, place):
    T, D = r.stream.shape
    r.hp[...] = r.odd[7 : 7 + T, :].astype(BF)
    r.tmp[...] = nn(r.hp[...], r.w2[0]) + nn(r.he[...], r.w2[1]) + nn(r.ho[...], r.w2[2])
    fine = r.fine_s.shape[0]

    def second(rows):
        value, slope = gelu_both(r.tmp[rows, :] + vec(r, C2B))
        at = place * (T // fine) + rows.start // fine
        s0, c0 = r.coarse_s[pl.ds(at, 1), :], r.coarse_c[pl.ds(at, 1), :]
        s1, c1 = r.fine_s[...], r.fine_c[...]
        stream = value + jnp.concatenate([s0 * c1 + c0 * s1, c0 * c1 - s0 * s1], axis=1)
        r.dg2[rows, :] = slope
        r.stream[rows, :] = stream
        r.normed[rows, :] = (normal(stream)[0] * vec(r, N1G) + vec(r, N1B)).astype(BF)

    rows_loop(T, fine, second)


def stage_mask(r, sub):
    T, D = r.stream.shape
    row = r.mask[0:1, pl.ds(pl.multiple_of(sub * T, 128), T)].astype(F32)
    r.wide[0:T, :] = jnp.broadcast_to(row, (128, T)).T

    def one(rows):
        keep = r.wide[rows, :]
        keep = jnp.concatenate([keep] * (D // 128), axis=1)
        r.bg[rows, :] = (r.bg[rows, :].astype(F32) * keep).astype(BF)

    rows_loop(T, 32, one)


def stage_qkv(r, part, h):
    T, D = r.stream.shape
    half, qr = D // 2, D // 4
    bias, scale = ((QB, HEAD**-0.5), (None, 1.0), (VB, 1.0))[part]
    value = nn(r.normed[...], r.wqkv[h, part])
    if bias is not None:
        value = value + r.vecs[bias : bias + 1, pl.ds(pl.multiple_of(h * half, half), half)]
    value = (value.astype(BF).astype(F32) * scale).T.astype(BF)
    for k in range(2):
        r.kv[rows16((3 * (3 + k) + part) * half + h * qr, qr), :] = value[k * qr : (k + 1) * qr, :]


def at_head(start, h):
    return pl.ds(pl.multiple_of(start + h * HEAD, HEAD), HEAD)


def head_loop(steps, hooks, body):
    def one(step, carry):
        for at, todo in hooks.items():
            if not todo:
                continue

            @pl.when(step == at)
            def _(todo=todo):
                for act in todo:
                    act()

        body(step)
        return carry

    lax.fori_loop(0, steps, one, 0)


def attend(r, c, m, hooks):
    S, T = r.kv.shape[0] // 15, r.kv.shape[1]
    heads = S // HEAD
    r.top[...] = jnp.full(r.top.shape, -jnp.inf, F32)
    r.total[...] = jnp.zeros(r.total.shape, F32)
    r.mixt[...] = jnp.zeros(r.mixt.shape, F32)

    def body(step):
        quarter, u, pair = step // heads, step % heads, heads // 2
        g = 2 * (quarter // 2) + u // pair
        h = (m + (1 - 2 * m) * ((quarter + 1) // 2 % 2)) * pair + u % pair
        own = (3 - g) // 3
        slot = own * (3 + c) + (1 - own) * ((g + 1) % 3)
        k = r.kv[at_head((3 * slot + 1) * S, h), :]
        v = r.kv[at_head((3 * slot + 2) * S, h), :]
        for i, home in enumerate((3 + c, 2)):
            q = r.kv[at_head(3 * home * S, h), :]
            s = tn(k, q)
            before = r.top[i * heads + h]
            top = jnp.maximum(before, jnp.max(s, axis=0, keepdims=True))
            p = jnp.exp(s - top)
            keep = jnp.exp(before - top)
            rows = at_head(i * S, h)
            r.top[i * heads + h] = top
            r.total[i * heads + h] = keep * r.total[i * heads + h] + jnp.sum(p, axis=0, keepdims=True)
            r.mixt[rows, :] = keep * r.mixt[rows, :] + nn(v, p.astype(BF))

    head_loop(4 * heads, hooks, body)


def attend_end(r, i):
    S = r.kv.shape[0] // 15
    heads = S // HEAD

    def one(h, carry):
        rows = at_head(i * S, h)
        total = r.total[i * heads + h]
        value = r.mixt[rows, :] * (1.0 / total)
        r.mixt[rows, :] = value
        r.mixb[rows, :] = value.astype(BF)
        r.top[i * heads + h] = r.top[i * heads + h] + jnp.log(total)
        return carry

    lax.fori_loop(0, heads, one, 0)


def stage_mid(r, c, mix_came, weights_came):
    T, D = r.stream.shape
    half = D // 2
    weights_came()
    r.tmp[...] = tn(r.mixb[0:half, :], r.wo[rows16(c * half, half), :])
    mix_came()
    r.tmp[...] += tn(r.mix_got[...], r.wo[rows16((1 - c) * half, half), :])

    def one(rows):
        mid = r.stream[rows, :] + r.tmp[rows, :] + vec(r, OUB)
        r.mid[rows, :] = mid
        r.ntwo[rows, :] = (normal(mid)[0] * vec(r, N2G) + vec(r, N2B)).astype(BF)

    rows_loop(T, 32, one)


def stage_ff(r, hooks):
    T, D = r.stream.shape
    side = r.up.shape[2] // D
    parts, width = 2 * side, D

    def chunk(t):
        into, at = t % 2, t // 2
        j = into * side + at
        up = r.up[into, :, pl.ds(pl.multiple_of(at * D, D), D)]
        down = r.down[pl.ds(pl.multiple_of(j * D, D), D), :]
        r.tmp[...] = nn(r.ntwo[...], up)
        r.tmp2[...] = nt(r.bg[...], down)
        bias = r.vecs[pl.ds(UPB + j, 1), :]

        def one(i, acc):
            rows = pl.ds(pl.multiple_of(i * 32, 32), 32)
            value, slope = gelu_both(r.tmp[rows, :] + bias)
            r.act[rows, :] = value.astype(BF)
            grad = (r.tmp2[rows, :] * slope).astype(BF)
            r.ing[rows, :] = grad
            return acc + col(grad.astype(F32))

        r.small[pl.ds(UPB + j, 1), :] = lax.fori_loop(0, T // 32, one, jnp.zeros((1, width), F32))
        act = r.act[...]
        ing = r.ing[...]
        out = nn(act, down)
        back = nt(ing, up)

        r.ffo[...] += out
        r.ntg[...] += back
        rows = pl.ds(pl.multiple_of(t * D, D), D)
        r.g_down[rows, :] = tn(act, r.bg[...]).astype(BF)
        r.g_up[rows, :] = tn(r.ntwo[...], ing).astype(BF)

    r.ffo[...] = jnp.zeros_like(r.ffo)
    r.ntg[...] = jnp.zeros_like(r.ntg)
    head_loop(parts, hooks, chunk)


def stage_mid_pull(r):
    T, D = r.stream.shape

    def one(i, accs):
        rows = pl.ds(pl.multiple_of(i * 32, 32), 32)
        mid = r.mid[rows, :]
        enc = (mid + r.ffo[rows, :] + vec(r, DNB)).astype(BF)
        hat, inv = normal(mid)
        grad = r.ntg[rows, :]
        smg = r.bg[rows, :].astype(F32) + normal_pull(grad * vec(r, N2G), hat, inv)
        r.enc[rows, :] = enc
        r.smg[rows, :] = smg
        attg = smg.astype(BF)
        r.attg[rows, :] = attg
        return accs[0] + col(grad * hat), accs[1] + col(grad), accs[2] + col(attg.astype(F32))

    zero = jnp.zeros((1, D), F32)
    gain, bias, out_bias = lax.fori_loop(0, T // 32, one, (zero, zero, zero))
    add_small(r, N2G, gain)
    add_small(r, N2B, bias)
    add_small(r, OUB, out_bias)


def stage_do(r, c, own):
    half = r.attg.shape[1] // 2
    k = c if own else 1 - c
    value = nt(r.wo[rows16(k * half, half), :], r.attg[...]).astype(BF)
    if own:
        r.dot[0:half, :] = value
    else:
        r.dot_out[...] = value


def stage_out_weights(r, c):
    D = r.attg.shape[1]
    half, qr = D // 2, D // 4
    for k, mix in ((c, r.mixb[0:half, :]), (1 - c, r.mix_got[...])):
        value = nn(mix, r.attg[...]).astype(BF)
        for h in range(2):
            r.g_out[rows16(h * half + k * qr, qr), :] = value[h * qr : (h + 1) * qr, :]


def stage_diag(r, i):
    S = r.kv.shape[0] // 15
    heads = S // HEAD

    def one(h, carry):
        rows = at_head(i * S, h)
        value = r.dot[rows, :].astype(F32) * r.mixt[rows, :]
        r.diag[i * heads + h] = jnp.sum(value, axis=0, keepdims=True)
        return carry

    lax.fori_loop(0, heads, one, 0)


def attend_pull(r, c, hooks):
    S, T = r.kv.shape[0] // 15, r.kv.shape[1]
    heads = S // HEAD
    r.dqt[...] = jnp.zeros(r.dqt.shape, F32)

    def body(step):
        g, h = step // heads, step % heads
        slot = g + (g // 3) * c
        k = r.kv[at_head((3 * slot + 1) * S, h), :]
        v = r.kv[at_head((3 * slot + 2) * S, h), :]
        dk, dv = None, None
        for i, home in enumerate((3 + c, 2)):
            q = r.kv[at_head(3 * home * S, h), :]
            rows = at_head(i * S, h)
            do = r.dot[rows, :]
            p = jnp.exp(tn(k, q) - r.top[i * heads + h])
            ds = (p * (tn(v, do) - r.diag[i * heads + h])).astype(BF)
            dv_i, dk_i = nt(do, p.astype(BF)), nt(q, ds)
            dk, dv = (dk_i, dv_i) if dk is None else (dk + dk_i, dv + dv_i)
            r.dqt[rows, :] += nn(k, ds)
        r.dkv[at_head(2 * g * S, h), :] = dk.astype(BF)
        r.dkv[at_head((2 * g + 1) * S, h), :] = dv.astype(BF)

    head_loop(4 * heads, hooks, body)


def piece_of(r, part, h):
    D, qr = r.attg.shape[1], r.attg.shape[1] // 4
    at = part * D + h * qr
    return jnp.concatenate([r.dsum[at : at + qr, :], r.dsum[at + 2 * qr : at + 3 * qr, :]], axis=0)


def stage_qkv_weights(r, part):
    T, D = r.stream.shape
    half = D // 2
    ones = jnp.ones((8, T), BF)
    for h in range(2):
        piece = piece_of(r, part, h)
        if part != 1:
            row = QB if part == 0 else VB
            r.small[row : row + 1, h * half : (h + 1) * half] = nt(ones, piece)[0:1, :]
        grad = nt(r.normedt[...], piece).astype(BF)
        at = (2 * part + h) * half
        r.g_qkv[at : at + half, 0:half] = grad[0:half, :]
        r.g_qkv[at : at + half, half:D] = grad[half:D, :]


def stage_qkv_pull(r):
    T, D = r.stream.shape
    total = None
    for part in range(3):
        for h in range(2):
            back = nn(r.wqkv[h, part], piece_of(r, part, h))
            total = back if total is None else total + back
    r.tmp[...] = total.T


def stage_norm_pull(r):
    T, D = r.stream.shape

    def one(i, accs):
        rows = pl.ds(pl.multiple_of(i * 32, 32), 32)
        hat, inv = normal(r.stream[rows, :])
        grad = r.tmp[rows, :]
        back = r.smg[rows, :] + normal_pull(grad * vec(r, N1G), hat, inv)
        sg = (back * r.dg2[rows, :]).astype(BF)
        r.sg[rows, :] = sg
        return accs[0] + col(grad * hat), accs[1] + col(grad), accs[2] + col(sg.astype(F32))

    zero = jnp.zeros((1, D), F32)
    gain, bias, c2b = lax.fori_loop(0, T // 32, one, (zero, zero, zero))
    add_small(r, N1G, gain)
    add_small(r, N1B, bias)
    add_small(r, C2B, c2b)


def stage_conv2_pull(r, next_row):
    T, D = r.stream.shape
    sg = r.sg[...]
    r.shift[0:T, :] = nt(sg, r.w2[0])
    r.shift[T : T + 16, :] = nt(next_row, r.w2[0])
    r.tmp[...] = nt(sg, r.w2[1])
    r.tmp2[...] = nt(sg, r.w2[2]) + r.shift[1 : T + 1, :]


def stage_first_pull(r):
    T, D = r.stream.shape

    def one(i, acc):
        rows = pl.ds(pl.multiple_of(i * 32, 32), 32)
        even = (r.tmp[rows, :] * r.dge[rows, :]).astype(BF)
        odd = (r.tmp2[rows, :] * r.dgo[rows, :]).astype(BF)
        r.fe[rows, :] = even
        r.fo[rows, :] = odd
        return acc + col(even.astype(F32)) + col(odd.astype(F32))

    add_small(r, C1B, lax.fori_loop(0, T // 32, one, jnp.zeros((1, D), F32)))


def stage_conv2_weights(r, i):
    D = r.stream.shape[1]
    tap = (r.hp, r.he, r.ho)[i]
    r.g_c2[i * D : (i + 1) * D, :] = tn(tap[...], r.sg[...]).astype(BF)


def stage_conv1_weights(r):
    value = (tn(r.xe[...], r.fe[...]) + tn(r.xo[...], r.fo[...])).astype(BF)
    mels = r.w1.shape[1]
    for o in range(3):
        r.g_c1[mels * o : mels * (o + 1), :] = value[128 * o : 128 * o + mels, :]
    r.g_c1[3 * mels :, :] = jnp.zeros((r.g_c1.shape[0] - 3 * mels, r.g_c1.shape[1]), BF)


def stage_mel(r, next_row, prev_row):
    T, D = r.stream.shape
    fe, fo = r.fe[...], r.fo[...]
    w = [r.w1p[128 * o : 128 * (o + 1), :] for o in range(3)]
    r.wide[16 : 16 + T, :] = nt(fo, w[2])
    r.wide[0:16, :] = nt(prev_row, w[2])
    r.melg[:, 0:128] = (nt(fe, w[1]) + nt(fo, w[0]) + r.wide[15 : 15 + T, :]).astype(BF)
    r.wide[0:T, :] = nt(fe, w[0])
    r.wide[T : T + 16, :] = nt(next_row, w[0])
    r.melg[:, 128:256] = (nt(fe, w[2]) + nt(fo, w[1]) + r.wide[1 : 1 + T, :]).astype(BF)


class Net:
    def __init__(self, r, bits):
        self.r, self.bits, self.used, self.used_here = r, bits, 0, 0
        self.d, self.c, self.m = (lax.axis_index(n) for n in ("dp", "seq", "mp"))

    def bit(self, dim):
        if dim == "c":
            return self.c
        if dim == "y":
            return self.m
        return (self.d // (1 << dim)) % 2

    def peer(self, dims):
        d = self.d
        for k in dims:
            if k not in ("c", "y"):
                d = d + (1 << k) - 2 * (1 << k) * self.bit(k)
        return (
            d,
            1 - self.c if "c" in dims else self.c,
            1 - self.m if "y" in dims else self.m,
        )

    def greet(self, partners):
        barrier = pltpu.get_barrier_semaphore()
        for dims in partners:
            pl.semaphore_signal(barrier, inc=1, device_id=self.peer(dims), device_id_type=MESH)
        pl.semaphore_wait(barrier, len(partners))

    def copy(self, src, dst, *dims):
        i = self.used
        self.used += 1
        return pltpu.make_async_remote_copy(
            src_ref=src,
            dst_ref=dst,
            send_sem=self.r.send.at[i],
            recv_sem=self.r.recv.at[i],
            device_id=self.peer(dims),
            device_id_type=MESH,
        )

    def send(self, src, dst, *dims):
        copy = self.copy(src, dst, *dims)
        copy.start()
        return copy

    def here(self, src, dst):
        i = self.used_here
        self.used_here += 1
        copy = pltpu.make_async_copy(src, dst, self.r.own.at[i])
        copy.start()
        return copy


def start_all(copies):
    for copy in copies:
        copy.start()


def wait_all(copies):
    for copy in copies:
        copy.wait()


def rows16(start, size):
    return pl.ds(pl.multiple_of(start, 16), size)


def subsets(dims):
    found = [()]
    for dim in dims:
        found += [one + (dim,) for one in found]
    return found[1:]


def sum_plan(rows, halves, order):
    steps, need = [], 0
    for dims in order:
        by_half = halves == 2 and "y" in dims
        cutting = [dim for dim in dims if not (by_half and dim == "y")]
        if rows % (16 << len(cutting)):
            cutting = []
        rows >>= len(cutting)
        if by_half:
            halves = 1
        steps.append((dims, cutting, rows, halves, by_half))
        need += rows * halves * len(subsets(dims))
    return steps, need


class Track:
    def __init__(self, acts):
        self.acts = list(acts)

    def take(self):
        return [self.acts.pop(0)] if self.acts else []


def bucket_sum(net, g, got, done, halves, order):
    R = g.shape[0] // halves
    lo, rows, at, bases = 0, R, 0, [h * R for h in range(halves)]
    acts, back, end = [], [], None

    def start_after(end, copies):
        def act():
            if end is not None:
                end()
            for copy in copies:
                copy.start()

        return act

    def adder(copies, places, n):
        step = 64 if n % 64 == 0 else 32 if n % 32 == 0 else 16

        def end():
            wait_all(copies)
            for to, ofs in places:

                def add(k, carry, to=to, ofs=ofs):
                    mine = rows16(to + k * step, step)
                    value = g[mine, :].astype(F32)
                    for of in ofs:
                        value = value + got[rows16(of + k * step, step), :].astype(F32)
                    g[mine, :] = value.astype(BF)
                    return carry

                lax.fori_loop(0, n // step, add, 0)

        return end

    for dims, cutting, n, _, by_half in sum_plan(R, halves, order)[0]:

        def part_of(other):
            start = lo
            for i, dim in enumerate(reversed(cutting)):
                b = net.bit(dim)
                start = start + (1 - b if dim in other else b) * (n << i)
            return start

        keep = part_of(())
        if by_half:
            bases = [net.m * R]
        copies, ofs = [], [[] for _ in bases]
        for other in subsets(dims):
            sources = [(1 - net.m) * R] if by_half and "y" in other else bases
            for i, base in enumerate(sources):
                src = g.at[rows16(base + part_of(other), n)]
                copies.append(net.copy(src, got.at[rows16(at, n)], *other))
                ofs[i].append(at)
                at += n
        acts.append(start_after(end, copies))
        end = adder(copies, [(base + keep, of) for base, of in zip(bases, ofs)], n)
        if cutting:
            back.append((cutting, n, lo))
        lo, rows = keep, n

    def settle(end=end, lo=lo, base=bases[0], rows=rows):
        end()
        for k in range(rows // 16):
            done[rows16(lo + 16 * k, 16), :] = g[rows16(base + lo + 16 * k, 16), :]

    end = settle
    for cutting, n, before in reversed(back):
        part = rows16(lo, n)
        copies = [net.copy(done.at[part], done.at[part], *other) for other in subsets(cutting)]
        acts.append(start_after(end, copies))
        end = functools.partial(wait_all, copies)
        lo = before
    return Track(acts + [end])


def small_sum(net, value, slots, order):
    acts, end, at = [], None, 0
    for dims in order:
        copies = [net.copy(value, slots.at[at + i], *other) for i, other in enumerate(subsets(dims))]

        def act(end=end, copies=copies):
            if end is not None:
                end()
            start_all(copies)

        def end(copies=copies, at=at):
            wait_all(copies)
            total = value[...]
            for i in range(len(copies)):
                total = total + slots[at + i]
            value[...] = total

        at += len(copies)
        acts.append(act)
    return Track(acts + [end])


def ready(*names):
    pass


def advance(*sums):
    for one in sums:
        for act in one.take():
            act()


def drain(*sums):
    while any(one.acts for one in sums):
        advance(*sums)


def quarter(net):
    return 2 * net.c + net.c + net.m - 2 * net.c * net.m


def choose(slots, by_core, by_y):
    core = jnp.where(by_core, 1.0, 0.0)
    y = jnp.where(by_y, 1.0, 0.0)
    return (slots[0].astype(F32) * core + slots[1].astype(F32) * y).astype(BF)


def pick_next(net, slots):
    q = quarter(net)
    return choose(slots, q == 1, q % 2 == 0)


def pick_prev(net, slots):
    q = quarter(net)
    return choose(slots, q == 2, q % 2 == 1)


ROW_BIASES = ("c1b", "c2b", "n1g", "n1b", "oub", "n2g", "n2b", "dnb")


ORDERS = dict(
    down=("c x y w z", "c zy w x"),
    up=("c xy wz", "c zy x w"),
    out=("c zy wx",),
    qkv=("c y z x w", "c xz yw", "c z x y w"),
    c2=("c z xy w", "c yx z w", "c x zy w"),
    c1=("c y xz w",),
    vec=("c w x y z",),
)
SCHEDULE = dict(
    ff2=("down0", "up0"),
    ffo=("down0", "down1", "up0", "up1"),
    out=("down1", "up1", "out0"),
    pull1=("out0",),
    pull2=("down0",),
    pull4=("up0",),
    pull6=("down1", "up1", "out0"),
    pull7=("down0", "up0"),
    pull8=("up1", "out0"),
    pull10=("down1",),
    pull11=("up0", "up1", "out0"),
    pull12=("down0", "down1"),
    pull13=("up0", "up1", "out0"),
    pull14=("down0", "down1"),
    pull15=("up0", "up1", "out0"),
    home=("down0",),
    qkvw1=("down1", "up1", "qkv1"),
    qkvw2=("qkv2",),
    qkvw0=("down0", "qkv0"),
    norm=("up1", "qkv1"),
    c2=("down1", "qkv0", "qkv2"),
    c2w0=("c20",),
    c2w1=("c21",),
    c2w2=("c22",),
    first=("down0", "down1", "qkv1", "c20", "c21", "c22"),
    c1=("qkv0", "qkv2"),
    c1w=("down0", "c10", "vec"),
    mel=("qkv0", "qkv1", "qkv2", "c20", "c21", "c10", "vec"),
    end=(
        "c22", "qkv1", "qkv0", "c21", "vec", "qkv2", "c20", "c22", "qkv0", "qkv1", "c10", "c21",
        "vec", "qkv2", "c20", "qkv1", "c22", "qkv0", "vec", "c10", "c21", "qkv2", "c20", "c22",
        "qkv0", "c10", "vec", "c21", "qkv2", "c20", "c22", "c10", "qkv0", "c21", "qkv2", "qkv0",
        "c10", "c20", "c22", "c21", "qkv2", "c10", "c20", "c22",
    ),
)


def orders(name, bits):
    dims = dict(c=["c"], y=["y"], x=[0], z=list(range(1, min(2, bits))), w=list(range(2, min(3, bits))))
    found = []
    for spec in ORDERS[name]:
        groups = [tuple(dim for ch in group for dim in dims[ch]) for group in spec.split()]
        found.append([group for group in groups if group] + [(dim,) for dim in range(3, bits)])
    return found


def partners(bits):
    found = [("c",), ("y",), ("c", "y")] + [(dim,) for dim in range(bits)]
    for name in ORDERS:
        for order in orders(name, bits):
            for dims in order:
                found += [one for one in subsets(dims) if set(one) not in [set(x) for x in found]]
    return found


def layer(r, bits):
    T, D = r.stream.shape
    half, F2 = D // 2, r.down_l.shape[0]
    side = F2 // D
    mels, span = r.w1.shape[1], 4 * T
    net = Net(r, bits)
    c, m = net.c, net.m
    sub = c + m - 2 * c * m
    rows_of_mine = rows16(sub * T, T)

    r.melbuf[...] = jnp.zeros_like(r.melbuf)
    mel_own = net.here(r.mel.at[0], r.melbuf.at[0:mels, 128 : 128 + span])
    qkv_own = net.here(r.wqkv_l, r.wqkv.at[m])
    w2_own = net.here(r.w2_l, r.w2)
    own = [
        net.here(r.wo_l.at[0 : D // 4], r.wo.at[rows16(m * (D // 4), D // 4)]),
        net.here(r.wo_l.at[D // 4 : half], r.wo.at[rows16(half + m * (D // 4), D // 4)]),
        net.here(r.up_l, r.up.at[m]),
        net.here(r.down_l, r.down.at[rows16(m * F2, F2)]),
        net.here(r.cot.at[0, rows_of_mine], r.bg),
    ]
    r.vec_mine[...] = jnp.zeros_like(r.vec_mine)
    own_lanes = pl.ds(pl.multiple_of(m * half, 128), half)
    r.vec_mine[0:2, own_lanes] = r.qkvb[...].astype(F32)
    for k in range(side):
        r.vec_mine[pl.ds(2 + m * side + k, 1), :] = r.upb[k * D : (k + 1) * D].astype(F32).reshape(1, D)
    for k, n in enumerate(ROW_BIASES):
        r.vecs[k : k + 1, :] = getattr(r, n)[...].astype(F32).reshape(1, D)
    net.greet(partners(bits))
    vec_copy = net.send(r.vec_mine, r.vec_got, "y")
    mel_own.wait()
    src = pl.ds(pl.multiple_of(128 + (1 - c) * (span - 128), 128), 128)
    dst = pl.ds(pl.multiple_of(c * (span + 128), 128), 128)
    mel_rim = net.send(r.melbuf.at[0:mels, src], r.melbuf.at[0:mels, dst], "c")
    p = 4 * c + 2 * net.bit(0) + net.bit(1) if bits > 1 else 2 * c + net.bit(0)
    cuts = 8 if bits > 1 else 4

    def pass_on(of, at, count, dim):
        def cut(n, base):
            return rows16(base + at * (n // cuts), count * (n // cuts))

        wo = rows16(c * half + of * (D // 4) + (at - c * (cuts // 2)) * (half // cuts), count * (half // cuts))
        parts = [r.wo.at[wo], r.up.at[of, cut(D, 0)], r.down.at[cut(F2, of * F2)]]
        return [net.copy(x, x, dim) for x in parts]

    def pass_qkv(of, at, count, dim):
        rows = r.wqkv.at[of, :, rows16(at * (D // 4), count * (D // 4))]
        return net.copy(rows, rows, dim)

    two = 2 if bits > 1 else 1
    qkv_y = pass_qkv(m, 2 * c + net.bit(0), 1, "y")
    qkv_x = pass_qkv(1 - m, 2 * c + net.bit(0), 1, 0)
    qkv_c = pass_qkv(1 - m, 2 * c, 2, "c")
    ff_y = pass_on(m, p, 1, "y")
    ff_z = pass_on(1 - m, p, 1, 1) if bits > 1 else []
    ff_x = pass_on(1 - m, (p // two) * two, two, 0)
    ff_c = pass_on(1 - m, c * (cuts // 2), cuts // 2, "c")
    qkv_own.wait()
    qkv_y.start()
    wait_all(own)
    r.small[...] = jnp.zeros_like(r.small)
    stage_mel_rows(r, sub, mel_rim.wait)
    start_all(ff_y)
    stage_first(r, jnp.logical_and(c == 0, m == 0))
    stage_odd(r)
    qkv_y.wait()
    qkv_x.start()
    w2_own.wait()
    stage_second(r, quarter(net))
    wait_all(ff_y)
    start_all(ff_z)
    vec_copy.wait()
    r.vecs[8:16, :] = r.vec_mine[...] + r.vec_got[...]

    def block(slot, part, h):
        return r.kv.at[rows16((3 * slot + part) * half + h * (half // 2), half // 2)]

    def project(h):
        far, near = [], []
        for part in (1, 2, 0):
            stage_qkv(r, part, h)
            if part:
                far.append(net.send(block(3 + c, part, h), block(0, part, h), "y"))
                far.append(net.send(block(4 - c, part, h), block(1, part, h), "c", "y"))
            near.append(net.send(block(4 - c, part, h), block(2, part, h), "c"))
        return far, near

    far_own, near_own = project(m)
    qkv_x.wait()
    qkv_c.start()
    stage_mask(r, sub)
    add_small(r, DNB, col(r.bg[...].astype(F32)))
    r.normedt[...] = r.normed[...].astype(F32).T.astype(BF)
    wait_all(near_own)
    heads = half // HEAD
    far_other = [
        net.copy(block(own, part, 1 - m), block(to, part, 1 - m), *dims)
        for part in (1, 2)
        for own, to, dims in ((3 + c, 0, ("y",)), (4 - c, 1, ("c", "y")))
    ]
    near_other = [net.copy(block(4 - c, part, 1 - m), block(2, part, 1 - m), "c") for part in range(3)]

    def project_other():
        qkv_c.wait()
        stage_qkv(r, 1, 1 - m)
        start_all(far_other[0:2])
        stage_qkv(r, 2, 1 - m)
        start_all(far_other[2:4])
        stage_qkv(r, 0, 1 - m)
        start_all(near_other)

    hooks = {
        heads - 1: [project_other],
        heads: [lambda: wait_all(near_other), lambda: wait_all(ff_z), lambda: start_all(ff_x)],
        2 * heads: [lambda: wait_all(far_own)],
        5 * heads // 2: [lambda: wait_all(ff_x), lambda: start_all(ff_c)],
        3 * heads: [lambda: wait_all(far_other)],
    }
    attend(r, c, m, hooks)
    attend_end(r, 1)
    mix_c = net.send(r.mixb.at[half:D], r.mix_got, "c")
    attend_end(r, 0)
    stage_mid(r, c, mix_c.wait, lambda: wait_all(ff_c))

    def summed(n, part, rows, halves):
        views = [
            getattr(r, "g_" + n).at[part * rows * halves : (part + 1) * rows * halves],
            getattr(r, "got_%s%d" % (n, part)),
            getattr(r, "done_" + n).at[part * rows : (part + 1) * rows],
        ]
        return bucket_sum(net, *views, halves, orders(n, bits)[part])

    tracks = {}
    for n, rows, halves, parts in (
        ("down", D, 2, side),
        ("up", D, 2, side),
        ("out", half, 2, 1),
        ("qkv", half, 2, 3),
        ("c2", D, 1, 3),
        ("c1", r.g_c1.shape[0], 1, 1),
    ):
        for part in range(parts):
            tracks["%s%d" % (n, part)] = summed(n, part, rows, halves)
    tracks["vec"] = small_sum(net, r.small, r.got_small, orders("vec", bits)[0])

    def acts_at(name):
        return [act for n in SCHEDULE.get(name, ()) if n in tracks for act in tracks[n].take()]

    def point(name):
        for act in acts_at(name):
            act()

    hooks = {}
    for step in range(2 * side):
        if step and step % 2 == 0:
            ready("down%d" % (step // 2 - 1), "up%d" % (step // 2 - 1))
        hooks[step] = acts_at("ff%d" % step)
    stage_ff(r, hooks)
    ready("down%d" % (side - 1), "up%d" % (side - 1))
    point("ffo")
    stage_mid_pull(r)
    stage_do(r, c, False)
    do_c = net.send(r.dot_out, r.dot.at[half:D], "c")
    point("mid")
    stage_out_weights(r, c)
    ready("out0")
    point("out")
    stage_do(r, c, True)
    stage_diag(r, 0)
    do_c.wait()
    stage_diag(r, 1)
    enc = [
        net.copy(r.enc, r.enc_got, "y"),
        pltpu.make_async_copy(r.enc, r.enc_o.at[rows_of_mine], r.own.at[39]),
    ]

    both = half * 2
    home_y = net.copy(r.dkv.at[0:both], r.from_y, "y")
    home_d = net.copy(r.dkv.at[both : 2 * both], r.from_d, "c", "y")
    home_c = net.copy(r.dkv.at[2 * both : 3 * both], r.from_c.at[half:], "c")
    hooks = {}

    def at_step(step, *acts):
        hooks.setdefault(step * heads // 4, []).extend(acts)

    at_step(4, home_y.start)
    at_step(8, home_d.start)
    at_step(11, lambda: start_all(enc))
    at_step(12, home_c.start)
    for step in range(16):
        at_step(step, *acts_at("pull%d" % step))
    attend_pull(r, c, hooks)
    r.dq_out[...] = (r.dqt[half:D, :] * HEAD**-0.5).astype(BF)
    dq_c = net.send(r.dq_out, r.from_c.at[0:half], "c")
    r.dsum[rows16(c * half, half), :] = (r.dqt[0:half, :] * HEAD**-0.5).astype(BF)
    point("home")
    home_y.wait()
    home_d.wait()
    home_c.wait()

    def total(i, carry):
        for part in range(2):
            rows = rows16(part * half + i * 32, 32)
            mine = r.dkv[rows16(3 * both + part * half + i * 32, 32), :].astype(F32) + r.from_y[rows, :].astype(F32)
            r.dsum[rows16((1 + part) * D + c * half + i * 32, 32), :] = mine.astype(BF)
            other = r.from_c[rows16((1 + part) * half + i * 32, 32), :].astype(F32) + r.from_d[rows, :].astype(F32)
            r.dsum[rows16((1 + part) * D + (1 - c) * half + i * 32, 32), :] = other.astype(BF)
        return carry

    lax.fori_loop(0, half // 32, total, 0)
    dq_c.wait()
    r.dsum[rows16((1 - c) * half, half), :] = r.from_c[0:half, :]

    for part in (1, 2, 0):
        stage_qkv_weights(r, part)
        ready("qkv%d" % part)
        point("qkvw%d" % part)
    stage_qkv_pull(r)
    point("norm")
    stage_norm_pull(r)
    rim = [net.send(r.sg.at[0:16], r.slots.at[0, i], dim) for i, dim in enumerate(("c", "y"))]
    point("c2")
    for part in range(3):
        stage_conv2_weights(r, part)
        ready("c2%d" % part)
        point("c2w%d" % part)
    wait_all(rim)
    stage_conv2_pull(r, pick_next(net, r.slots.at[0]))
    point("first")
    stage_first_pull(r)
    rim = [net.send(r.fe.at[0:16], r.slots.at[1, i], dim) for i, dim in enumerate(("c", "y"))]
    rim += [net.send(r.fo.at[T - 16 : T], r.slots.at[2, i], dim) for i, dim in enumerate(("c", "y"))]
    point("c1")
    stage_conv1_weights(r)
    ready("c10", "vec")
    point("c1w")
    wait_all(rim)
    stage_mel(r, pick_next(net, r.slots.at[1]), pick_prev(net, r.slots.at[2]))
    rows_of_yours = rows16((1 - sub) * T, T)
    mel_y = net.send(r.melg, r.melg_got, "y")
    point("mel")
    wait_all(enc)
    ends = [
        net.here(r.enc_got, r.enc_o.at[rows_of_yours]),
        net.here(r.melg, r.mel_o.at[rows_of_mine]),
    ]
    point("end")
    drain(*tracks.values())

    ends.append(net.here(r.done_down, r.down_o))
    for j in range(side):
        ends.append(net.here(r.done_up.at[j * D : (j + 1) * D], r.up_o.at[:, j * D : (j + 1) * D]))
    ends.append(net.here(r.done_out, r.out_o))
    for part in range(3):
        for j in range(2):
            ends.append(
                net.here(
                    r.done_qkv.at[part * half : (part + 1) * half, j * half : (j + 1) * half],
                    r.qkv_o.at[part, j * half : (j + 1) * half],
                )
            )
    ends.append(net.here(r.done_c2, r.c2_o))
    ends.append(net.here(r.done_c1, r.c1_o))
    ends.append(net.here(r.small, r.small_o))
    mel_y.wait()
    ends.append(net.here(r.melg_got, r.mel_o.at[rows_of_yours]))
    wait_all(ends)


def run_layer(bits, near, far, outs, T, D, F2, lanes):
    half, H = D // 2, D // HEAD
    td, dt = (T, D), (D, T)
    buckets = dict(down=(D, 2, F2 // D), up=(D, 2, F2 // D), out=(half, 2, 1), qkv=(half, 2, 3), c2=(D, 1, 3), c1=(lanes, 1, 1))
    scratch = dict(
        melbuf=((128, 4 * T + 256), BF),
        mele=((T + 24, 128), F32),
        melo=((T + 24, 128), F32),
        xe=((T, 384), BF),
        xo=((T, 384), BF),
        w1p=((384, D), BF),
        w2=((3, D, D), BF),
        bg=(td, BF),
        wqkv=((2, 3, D, half), BF),
        wo=((D, D), BF),
        up=((2, D, F2), BF),
        down=((2 * F2, D), BF),
        vecs=((16, D), F32),
        vec_mine=((8, D), F32),
        vec_got=((8, D), F32),
        stream=(td, F32),
        he=(td, BF),
        ho=(td, BF),
        hp=(td, BF),
        dge=(td, F32),
        dgo=(td, F32),
        dg2=(td, F32),
        normed=(td, BF),
        kv=((15 * half, T), BF),
        mixt=(dt, F32),
        mixb=(dt, BF),
        normedt=(dt, BF),
        mix_got=((half, T), BF),
        dot=(dt, BF),
        dot_out=((half, T), BF),
        top=((H, 1, T), F32),
        total=((H, 1, T), F32),
        diag=((H, 1, T), F32),
        tmp=(td, F32),
        tmp2=(td, F32),
        shift=((T + 16, D), F32),
        wide=((T + 16, 128), F32),
        mid=(td, F32),
        ntwo=(td, BF),
        act=(td, BF),
        ing=(td, BF),
        ffo=(td, F32),
        ntg=(td, F32),
        attg=(td, BF),
        dqt=(dt, F32),
        dq_out=((half, T), BF),
        dkv=((8 * half, T), BF),
        from_y=((2 * half, T), BF),
        from_d=((2 * half, T), BF),
        from_c=((3 * half, T), BF),
        dsum=((3 * D, T), BF),
        enc_got=(td, BF),
        melg=((T, 256), BF),
        melg_got=((T, 256), BF),
        small=((16, D), F32),
        got_small=((sum(len(subsets(dims)) for dims in orders("vec", bits)[0]), 16, D), F32),
        slots=((3, 2, 16, D), BF),
    )
    alias = T == D
    for n, (rows, halves, parts) in buckets.items():
        if n not in ("qkv", "c2"):
            scratch["g_" + n] = ((rows * halves * parts, D), BF)
        for part in range(parts):
            need = sum_plan(rows, halves, orders(n, bits)[part])[1]
            scratch["got_%s%d" % (n, part)] = ((need, D), BF)
        scratch["done_" + n] = ((rows * parts, D), BF)
    if not alias:
        scratch.update(g_qkv=((6 * half, D), BF), g_c2=((6 * half, D), BF))
    names = list(near) + list(far) + list(outs) + list(scratch) + ["send", "recv", "own"]

    def kernel(*refs):
        r = Box()
        for n, ref in zip(names, refs):
            setattr(r, n, ref)
        r.odd, r.smg, r.sg, r.fe, r.fo, r.enc = r.shift, r.mid, r.ntwo, r.act, r.ing, r.bg
        if alias:
            r.g_qkv, r.g_c2 = r.kv.at[0 : 6 * half], r.kv.at[6 * half : 12 * half]
        layer(r, bits)

    vmem, anywhere = pl.BlockSpec(memory_space=pltpu.VMEM), pl.BlockSpec(memory_space=pl.ANY)
    got = pl.pallas_call(
        kernel,
        name="layer",
        out_shape=[jax.ShapeDtypeStruct(*o) for o in outs.values()],
        in_specs=[vmem] * len(near) + [anywhere] * len(far),
        out_specs=[anywhere] * len(outs),
        scratch_shapes=[pltpu.VMEM(*s) for s in scratch.values()]
        + [pltpu.SemaphoreType.DMA((256,)), pltpu.SemaphoreType.DMA((256,)), pltpu.SemaphoreType.DMA((40,))],
        compiler_params=pltpu.CompilerParams(
            vmem_limit_bytes=VMEM_LIMIT, collective_id=1, has_side_effects=True
        ),
    )(*near.values(), *far.values())
    return dict(zip(outs, got))


def run_finish(got, mels, side):
    T2, D = got["enc_o"].shape
    half = D // 2
    ins = list(got)
    outs = dict(
        enc=((1, T2, D), BF),
        mel=((1, mels, 2 * T2), F32),
        c1=((3, mels, D), F32),
        c2=((3, D, D), F32),
        qkv=((3, D, half), F32),
        qkvb=((2, half), F32),
        out=((half, D), F32),
        up=((D, side * D), F32),
        upb=((side * D,), F32),
        down=((side * D, D), F32),
    )
    outs.update({n: ((D,), F32) for n in ROW_BIASES})

    def kernel(*refs):
        r = Box()
        for n, ref in zip(ins + list(outs), refs):
            setattr(r, n, ref)
        m = lax.axis_index("mp")

        def cast(src, dst):
            def one(rows):
                dst[rows, :] = src[rows, :].astype(dst.dtype)

            rows_loop(src.shape[0], 256, one)

        cast(r.enc_o, r.enc.at[0])
        cast(r.down_o, r.down)
        cast(r.up_o, r.up)
        cast(r.out_o, r.out)
        for o in range(3):
            cast(r.qkv_o.at[o], r.qkv.at[o])
            cast(r.c2_o.at[o * D : (o + 1) * D], r.c2.at[o])
            r.c1[o] = r.c1_o[o * mels : (o + 1) * mels, :].astype(F32)
        row = lax.broadcasted_iota(jnp.int32, (128, 256), 0)
        lane = lax.broadcasted_iota(jnp.int32, (128, 256), 1)
        even = jnp.where(lane == 2 * row, 1.0, 0.0).astype(BF)
        odd = jnp.where(lane == 2 * row + 1, 1.0, 0.0).astype(BF)
        for k in range(T2 // 128):
            rows = slice(k * 128, (k + 1) * 128)
            value = tn(r.mel_o[rows, 0:128], even) + tn(r.mel_o[rows, 128:256], odd)
            r.mel[0, :, k * 256 : (k + 1) * 256] = value[0:mels, :]
        for k, n in enumerate(ROW_BIASES):
            getattr(r, n)[...] = r.small_o[k : k + 1, :].reshape(D)
        r.qkvb[...] = r.small_o[QB : QB + 2, pl.ds(pl.multiple_of(m * half, 128), half)]
        for k in range(side):
            r.upb[k * D : (k + 1) * D] = r.small_o[pl.ds(UPB + m * side + k, 1), :].reshape(D)

    vmem = pl.BlockSpec(memory_space=pltpu.VMEM)
    done = pl.pallas_call(
        kernel,
        name="finish",
        out_shape=[jax.ShapeDtypeStruct(*o) for o in outs.values()],
        in_specs=[vmem] * len(ins),
        out_specs=[vmem] * len(outs),
        compiler_params=pltpu.CompilerParams(vmem_limit_bytes=VMEM_LIMIT),
    )(*got.values())
    return dict(zip(outs, done))


def sine_tables(frames, channels, fine):
    half_width = channels // 2
    rate = np.exp(-(math.log(10000.0) / (half_width - 1)) * np.arange(half_width))
    small = np.arange(fine)[:, None] * rate[None, :]
    large = np.arange(0, frames, fine)[:, None] * rate[None, :]
    table = dict(fine_s=np.sin(small), fine_c=np.cos(small), coarse_s=np.sin(large), coarse_c=np.cos(large))
    return {n: jnp.asarray(t, F32) for n, t in table.items()}


def on_device(
    mel_input,
    conv1_weight,
    conv1_bias,
    conv2_weight,
    conv2_bias,
    norm1_gain,
    norm1_bias,
    qkv_weight,
    qkv_bias,
    out_weight,
    out_bias,
    norm2_gain,
    norm2_bias,
    up_weight,
    up_bias,
    down_weight,
    down_bias,
    cotangent,
    speech_mask,
):
    mels = mel_input.shape[1]
    T, D = cotangent.shape[1] // 2, cotangent.shape[2]
    F2 = up_weight.shape[1]
    side, half = F2 // D, D // 2
    bits = (lax.axis_size("dp") - 1).bit_length()
    lanes = -(-3 * mels // 128) * 128
    near = dict(
        w1=conv1_weight,
        mask=speech_mask,
        qkvb=qkv_bias,
        upb=up_bias,
        c1b=conv1_bias,
        c2b=conv2_bias,
        n1g=norm1_gain,
        n1b=norm1_bias,
        oub=out_bias,
        n2g=norm2_gain,
        n2b=norm2_bias,
        dnb=down_bias,
    )
    near.update(sine_tables(4 * T, D, 32))
    got = run_layer(
        bits,
        near,
        dict(
            mel=mel_input,
            cot=cotangent,
            w2_l=conv2_weight,
            wqkv_l=qkv_weight,
            wo_l=out_weight,
            up_l=up_weight,
            down_l=down_weight,
        ),
        dict(
            enc_o=((2 * T, D), BF),
            mel_o=((2 * T, 256), BF),
            down_o=((F2, D), BF),
            up_o=((D, F2), BF),
            out_o=((half, D), BF),
            qkv_o=((3, D, half), BF),
            c2_o=((3 * D, D), BF),
            c1_o=((lanes, D), BF),
            small_o=((16, D), F32),
        ),
        T,
        D,
        F2,
        lanes,
    )
    done = run_finish(got, mels, side)
    names = ("enc", "mel", "c1", "c1b", "c2", "c2b", "n1g", "n1b", "qkv", "qkvb")
    names += ("out", "oub", "n2g", "n2b", "up", "upb", "down", "dnb")
    return tuple(done[n] for n in names)


def solution(mesh):
    placed = (
        P("dp", None, "seq"),
        P(),
        P(),
        P(),
        P(),
        P(),
        P(),
        P(None, None, "mp"),
        P(None, "mp"),
        P("mp", None),
        P(),
        P(),
        P(),
        P(None, "mp"),
        P("mp"),
        P("mp", None),
        P(),
        P("dp", "seq", None),
        P("dp", "seq"),
    )
    return jax.shard_map(
        on_device,
        mesh=mesh,
        in_specs=placed,
        out_specs=(
            P("dp", "seq", None),
            P("dp", None, "seq"),
            P(),
            P(),
            P(),
            P(),
            P(),
            P(),
            P(None, None, "mp"),
            P(None, "mp"),
            P("mp", None),
            P(),
            P(),
            P(),
            P(None, "mp"),
            P("mp"),
            P("mp", None),
            P(),
        ),
        check_vma=False,
    )
```

```python
import functools
import math

import jax
import jax.numpy as jnp
import numpy as np
from jax import lax
from jax.experimental import pallas as pl
from jax.experimental.pallas import tpu as pltpu
from jax.sharding import PartitionSpec as P

HEAD = 64
BF = jnp.bfloat16
F32 = jnp.float32
MESH = pl.DeviceIdType.MESH
VMEM_LIMIT = 61 * 1024 * 1024
C1B, C2B, N1G, N1B, OUB, N2G, N2B, DNB, QB, VB, UPB = range(11)


class Box:
    pass


def dot(a, b, ca, cb):
    return lax.dot_general(a, b, (((ca,), (cb,)), ((), ())), preferred_element_type=F32)


def nn(a, b):
    return dot(a, b, 1, 0)


def nt(a, b):
    return dot(a, b, 1, 1)


def tn(a, b):
    return dot(a, b, 0, 0)


def rows_loop(total, step, body, unroll=1):
    step = min(step, total)

    def one(i, carry):
        body(pl.ds(pl.multiple_of(i * step, step), step))
        return carry

    lax.fori_loop(0, total // step, one, 0, unroll=unroll)


def gelu_parts(v):
    t = 1.0 / (1.0 + (0.3275911 / math.sqrt(2.0)) * jnp.abs(v))
    e = jnp.exp(-0.5 * v * v)
    poly = 1.061405429 * t - 1.453152027
    poly = poly * t + 1.421413741
    poly = poly * t - 0.284496736
    poly = poly * t + 0.254829592
    tail = (0.5 * t) * poly * e
    return jnp.where(v >= 0, 1.0 - tail, tail), e * (1.0 / math.sqrt(2.0 * math.pi))


def gelu_both(v):
    cdf, pdf = gelu_parts(v)
    return v * cdf, cdf + v * pdf


def normal(x):
    center = x - jnp.mean(x, axis=-1, keepdims=True)
    spread = jnp.mean(center * center, axis=-1, keepdims=True)
    inv = lax.rsqrt(spread + 1e-05)
    return center * inv, inv


def normal_pull(gy, hat, inv):
    return inv * (
        gy
        - jnp.mean(gy, axis=-1, keepdims=True)
        - hat * jnp.mean(gy * hat, axis=-1, keepdims=True)
    )


def vec(r, i):
    return r.vecs[i : i + 1, :]


def add_small(r, i, value):
    r.small[i : i + 1, :] += value


def col(value):
    return jnp.sum(value, axis=0, keepdims=True)


def stage_mel_rows(r, sub, rim_came):
    T, D = r.stream.shape
    row = lax.broadcasted_iota(jnp.int32, (256, 256), 0)
    lane = lax.broadcasted_iota(jnp.int32, (256, 256), 1)
    pick = jnp.where(lane == 2 * (row % 128) + row // 128, 1.0, 0.0).astype(BF)
    base = sub * 2 * T

    def lanes(start, size):
        return r.melbuf[:, pl.ds(pl.multiple_of(base + start, 128), size)]

    row = lax.broadcasted_iota(jnp.int32, (16, 128), 0)
    lane = lax.broadcasted_iota(jnp.int32, (16, 128), 1)

    def select(at, to):
        return jnp.where(jnp.logical_and(row == to, lane == at), 1.0, 0.0).astype(BF)

    for k in range(T // 128):
        both = nt(pick, lanes(128 + 256 * k, 256))
        r.mele[8 + 128 * k : 136 + 128 * k, :] = both[0:128, :]
        r.melo[8 + 128 * k : 136 + 128 * k, :] = both[128:256, :]
    rim_came()
    before, after = lanes(0, 128), lanes(128 + 2 * T, 128)
    r.mele[0:8, :] = nt(select(126, 7), before)[0:8, :]
    r.melo[0:8, :] = nt(select(127, 7), before)[0:8, :]
    r.mele[T + 8 : T + 16, :] = nt(select(0, 0), after)[0:8, :]


def three(a, b, c):
    return jnp.concatenate([a, b, c], axis=1).astype(BF)


def stage_first(r, first):
    T, D = r.stream.shape
    for o in range(3):
        r.w1p[128 * o : 128 * o + r.w1.shape[1], :] = r.w1[o]
        r.w1p[128 * o + r.w1.shape[1] : 128 * (o + 1), :] = jnp.zeros((128 - r.w1.shape[1], D), BF)
    w1 = r.w1p[...]
    edge = nn(three(r.mele[0:16, :], r.melo[0:16, :], r.mele[1:17, :]), w1) + vec(r, C1B)
    edge = gelu_both(edge)[0] * jnp.where(first, 0.0, 1.0)
    r.odd[0:8, :] = edge[0:8, :]
    r.xe[...] = three(r.melo[7 : 7 + T, :], r.mele[8 : 8 + T, :], r.melo[8 : 8 + T, :])
    r.xo[...] = three(r.mele[8 : 8 + T, :], r.melo[8 : 8 + T, :], r.mele[9 : 9 + T, :])
    r.tmp[...] = nn(r.xe[...], w1)

    def even(rows):
        value, slope = gelu_both(r.tmp[rows, :] + vec(r, C1B))
        r.he[rows, :] = value.astype(BF)
        r.dge[rows, :] = slope

    rows_loop(T, 32, even)


def stage_odd(r):
    T, D = r.stream.shape
    r.tmp[...] = nn(r.xo[...], r.w1p[...])

    def odd(rows):
        value, slope = gelu_both(r.tmp[rows, :] + vec(r, C1B))
        r.ho[rows, :] = value.astype(BF)
        r.odd[pl.ds(pl.multiple_of(rows.start + 8, 8), rows.size), :] = value
        r.dgo[rows, :] = slope

    rows_loop(T, 32, odd)


def stage_second(r, place):
    T, D = r.stream.shape
    r.hp[...] = r.odd[7 : 7 + T, :].astype(BF)
    r.tmp[...] = nn(r.hp[...], r.w2[0]) + nn(r.he[...], r.w2[1]) + nn(r.ho[...], r.w2[2])
    fine = r.fine_s.shape[0]

    def second(rows):
        value, slope = gelu_both(r.tmp[rows, :] + vec(r, C2B))
        at = place * (T // fine) + rows.start // fine
        s0, c0 = r.coarse_s[pl.ds(at, 1), :], r.coarse_c[pl.ds(at, 1), :]
        s1, c1 = r.fine_s[...], r.fine_c[...]
        stream = value + jnp.concatenate([s0 * c1 + c0 * s1, c0 * c1 - s0 * s1], axis=1)
        r.dg2[rows, :] = slope
        r.stream[rows, :] = stream
        r.normed[rows, :] = (normal(stream)[0] * vec(r, N1G) + vec(r, N1B)).astype(BF)

    rows_loop(T, fine, second)


def stage_mask(r, sub):
    T, D = r.stream.shape
    row = r.mask[0:1, pl.ds(pl.multiple_of(sub * T, 128), T)].astype(F32)
    r.wide[0:T, :] = jnp.broadcast_to(row, (128, T)).T

    def one(rows):
        keep = r.wide[rows, :]
        keep = jnp.concatenate([keep] * (D // 128), axis=1)
        r.bg[rows, :] = (r.bg[rows, :].astype(F32) * keep).astype(BF)

    rows_loop(T, 32, one)


def stage_qkv(r, part, h):
    T, D = r.stream.shape
    half, qr = D // 2, D // 4
    bias, scale = ((QB, HEAD**-0.5), (None, 1.0), (VB, 1.0))[part]
    value = nn(r.normed[...], r.wqkv[h, part])
    if bias is not None:
        value = value + r.vecs[bias : bias + 1, pl.ds(pl.multiple_of(h * half, half), half)]
    value = (value.astype(BF).astype(F32) * scale).T.astype(BF)
    for k in range(2):
        r.kv[rows16((3 * (3 + k) + part) * half + h * qr, qr), :] = value[k * qr : (k + 1) * qr, :]


def at_head(start, h):
    return pl.ds(pl.multiple_of(start + h * HEAD, HEAD), HEAD)


def head_loop(steps, hooks, body):
    def one(step, carry):
        for at, todo in hooks.items():
            if not todo:
                continue

            @pl.when(step == at)
            def _(todo=todo):
                for act in todo:
                    act()

        body(step)
        return carry

    lax.fori_loop(0, steps, one, 0)


def attend(r, c, m, hooks):
    S, T = r.kv.shape[0] // 15, r.kv.shape[1]
    heads = S // HEAD
    r.top[...] = jnp.full(r.top.shape, -jnp.inf, F32)
    r.total[...] = jnp.zeros(r.total.shape, F32)
    r.mixt[...] = jnp.zeros(r.mixt.shape, F32)

    def body(step):
        quarter, u, pair = step // heads, step % heads, heads // 2
        g = 2 * (quarter // 2) + u // pair
        h = (m + (1 - 2 * m) * ((quarter + 1) // 2 % 2)) * pair + u % pair
        own = (3 - g) // 3
        slot = own * (3 + c) + (1 - own) * ((g + 1) % 3)
        k = r.kv[at_head((3 * slot + 1) * S, h), :]
        v = r.kv[at_head((3 * slot + 2) * S, h), :]
        for i, home in enumerate((3 + c, 2)):
            q = r.kv[at_head(3 * home * S, h), :]
            s = tn(k, q)
            before = r.top[i * heads + h]
            top = jnp.maximum(before, jnp.max(s, axis=0, keepdims=True))
            p = jnp.exp(s - top)
            keep = jnp.exp(before - top)
            rows = at_head(i * S, h)
            r.top[i * heads + h] = top
            r.total[i * heads + h] = keep * r.total[i * heads + h] + jnp.sum(p, axis=0, keepdims=True)
            r.mixt[rows, :] = keep * r.mixt[rows, :] + nn(v, p.astype(BF))

    head_loop(4 * heads, hooks, body)


def attend_end(r, i):
    S = r.kv.shape[0] // 15
    heads = S // HEAD

    def one(h, carry):
        rows = at_head(i * S, h)
        total = r.total[i * heads + h]
        value = r.mixt[rows, :] * (1.0 / total)
        r.mixt[rows, :] = value
        r.mixb[rows, :] = value.astype(BF)
        r.top[i * heads + h] = r.top[i * heads + h] + jnp.log(total)
        return carry

    lax.fori_loop(0, heads, one, 0)


def stage_mid(r, c, mix_came, weights_came):
    T, D = r.stream.shape
    half = D // 2
    weights_came()
    r.tmp[...] = tn(r.mixb[0:half, :], r.wo[rows16(c * half, half), :])
    mix_came()
    r.tmp[...] += tn(r.mix_got[...], r.wo[rows16((1 - c) * half, half), :])

    def one(rows):
        mid = r.stream[rows, :] + r.tmp[rows, :] + vec(r, OUB)
        r.mid[rows, :] = mid
        r.ntwo[rows, :] = (normal(mid)[0] * vec(r, N2G) + vec(r, N2B)).astype(BF)

    rows_loop(T, 32, one)


def stage_ff(r, hooks):
    T, D = r.stream.shape
    side = r.up.shape[2] // D
    parts, width = 2 * side, D

    def chunk(t):
        into, at = t % 2, t // 2
        j = into * side + at
        up = r.up[into, :, pl.ds(pl.multiple_of(at * D, D), D)]
        down = r.down[pl.ds(pl.multiple_of(j * D, D), D), :]
        r.tmp[...] = nn(r.ntwo[...], up)
        r.tmp2[...] = nt(r.bg[...], down)
        bias = r.vecs[pl.ds(UPB + j, 1), :]

        def one(i, acc):
            rows = pl.ds(pl.multiple_of(i * 32, 32), 32)
            value, slope = gelu_both(r.tmp[rows, :] + bias)
            r.act[rows, :] = value.astype(BF)
            grad = (r.tmp2[rows, :] * slope).astype(BF)
            r.ing[rows, :] = grad
            return acc + col(grad.astype(F32))

        r.small[pl.ds(UPB + j, 1), :] = lax.fori_loop(0, T // 32, one, jnp.zeros((1, width), F32))
        act = r.act[...]
        ing = r.ing[...]
        out = nn(act, down)
        back = nt(ing, up)

        r.ffo[...] += out
        r.ntg[...] += back
        rows = pl.ds(pl.multiple_of(t * D, D), D)
        r.g_down[rows, :] = tn(act, r.bg[...]).astype(BF)
        r.g_up[rows, :] = tn(r.ntwo[...], ing).astype(BF)

    r.ffo[...] = jnp.zeros_like(r.ffo)
    r.ntg[...] = jnp.zeros_like(r.ntg)
    head_loop(parts, hooks, chunk)


def stage_mid_pull(r):
    T, D = r.stream.shape

    def one(i, accs):
        rows = pl.ds(pl.multiple_of(i * 32, 32), 32)
        mid = r.mid[rows, :]
        enc = (mid + r.ffo[rows, :] + vec(r, DNB)).astype(BF)
        hat, inv = normal(mid)
        grad = r.ntg[rows, :]
        smg = r.bg[rows, :].astype(F32) + normal_pull(grad * vec(r, N2G), hat, inv)
        r.enc[rows, :] = enc
        r.smg[rows, :] = smg
        attg = smg.astype(BF)
        r.attg[rows, :] = attg
        return accs[0] + col(grad * hat), accs[1] + col(grad), accs[2] + col(attg.astype(F32))

    zero = jnp.zeros((1, D), F32)
    gain, bias, out_bias = lax.fori_loop(0, T // 32, one, (zero, zero, zero))
    add_small(r, N2G, gain)
    add_small(r, N2B, bias)
    add_small(r, OUB, out_bias)


def stage_do(r, c, own):
    half = r.attg.shape[1] // 2
    k = c if own else 1 - c
    value = nt(r.wo[rows16(k * half, half), :], r.attg[...]).astype(BF)
    if own:
        r.dot[0:half, :] = value
    else:
        r.dot_out[...] = value


def stage_out_weights(r, c):
    D = r.attg.shape[1]
    half, qr = D // 2, D // 4
    for k, mix in ((c, r.mixb[0:half, :]), (1 - c, r.mix_got[...])):
        value = nn(mix, r.attg[...]).astype(BF)
        for h in range(2):
            r.g_out[rows16(h * half + k * qr, qr), :] = value[h * qr : (h + 1) * qr, :]


def stage_diag(r, i):
    S = r.kv.shape[0] // 15
    heads = S // HEAD

    def one(h, carry):
        rows = at_head(i * S, h)
        value = r.dot[rows, :].astype(F32) * r.mixt[rows, :]
        r.diag[i * heads + h] = jnp.sum(value, axis=0, keepdims=True)
        return carry

    lax.fori_loop(0, heads, one, 0)


def attend_pull(r, c, hooks):
    S, T = r.kv.shape[0] // 15, r.kv.shape[1]
    heads = S // HEAD
    r.dqt[...] = jnp.zeros(r.dqt.shape, F32)

    def body(step):
        g, h = step // heads, step % heads
        slot = g + (g // 3) * c
        k = r.kv[at_head((3 * slot + 1) * S, h), :]
        v = r.kv[at_head((3 * slot + 2) * S, h), :]
        qs = [r.kv[at_head(3 * home * S, h), :] for home in (3 + c, 2)]
        dos = [r.dot[at_head(i * S, h), :] for i in range(2)]
        for i in range(2):
            top, diag = r.top[i * heads + h], r.diag[i * heads + h]
            for at in range(0, T, 128):
                rows, cols = slice(at, at + 128), slice(i * T, (i + 1) * T)
                p = jnp.exp(tn(k[:, rows], qs[i]) - top)
                r.pb[rows, cols] = p.astype(BF)
                r.ds[rows, cols] = (p * (tn(v[:, rows], dos[i]) - diag)).astype(BF)
        both = [jnp.concatenate(one, axis=1) for one in (qs, dos)]
        r.dkv[at_head(2 * g * S, h), :] = nt(both[0], r.ds[...]).astype(BF)
        r.dkv[at_head((2 * g + 1) * S, h), :] = nt(both[1], r.pb[...]).astype(BF)
        dq = nn(k, r.ds[...])
        for i in range(2):
            r.dqt[at_head(i * S, h), :] += dq[:, i * T : (i + 1) * T]

    head_loop(4 * heads, hooks, body)


def piece_of(r, part, h):
    D, qr = r.attg.shape[1], r.attg.shape[1] // 4
    at = part * D + h * qr
    return jnp.concatenate([r.dsum[at : at + qr, :], r.dsum[at + 2 * qr : at + 3 * qr, :]], axis=0)


def stage_qkv_weights(r, part):
    T, D = r.stream.shape
    half = D // 2
    ones = jnp.ones((8, T), BF)
    for h in range(2):
        piece = piece_of(r, part, h)
        if part != 1:
            row = QB if part == 0 else VB
            r.small[row : row + 1, h * half : (h + 1) * half] = nt(ones, piece)[0:1, :]
        grad = nt(r.normedt[...], piece).astype(BF)
        at = (2 * part + h) * half
        r.g_qkv[at : at + half, 0:half] = grad[0:half, :]
        r.g_qkv[at : at + half, half:D] = grad[half:D, :]


def stage_qkv_pull(r):
    T, D = r.stream.shape
    total = None
    for part in range(3):
        for h in range(2):
            back = nn(r.wqkv[h, part], piece_of(r, part, h))
            total = back if total is None else total + back
    r.tmp[...] = total.T


def stage_norm_pull(r):
    T, D = r.stream.shape

    def one(i, accs):
        rows = pl.ds(pl.multiple_of(i * 32, 32), 32)
        hat, inv = normal(r.stream[rows, :])
        grad = r.tmp[rows, :]
        back = r.smg[rows, :] + normal_pull(grad * vec(r, N1G), hat, inv)
        sg = (back * r.dg2[rows, :]).astype(BF)
        r.sg[rows, :] = sg
        return accs[0] + col(grad * hat), accs[1] + col(grad), accs[2] + col(sg.astype(F32))

    zero = jnp.zeros((1, D), F32)
    gain, bias, c2b = lax.fori_loop(0, T // 32, one, (zero, zero, zero))
    add_small(r, N1G, gain)
    add_small(r, N1B, bias)
    add_small(r, C2B, c2b)


def stage_conv2_pull(r, next_row):
    T, D = r.stream.shape
    sg = r.sg[...]
    r.shift[0:T, :] = nt(sg, r.w2[0])
    r.shift[T : T + 16, :] = nt(next_row, r.w2[0])
    r.tmp[...] = nt(sg, r.w2[1])
    r.tmp2[...] = nt(sg, r.w2[2]) + r.shift[1 : T + 1, :]


def stage_first_pull(r):
    T, D = r.stream.shape

    def one(i, acc):
        rows = pl.ds(pl.multiple_of(i * 32, 32), 32)
        even = (r.tmp[rows, :] * r.dge[rows, :]).astype(BF)
        odd = (r.tmp2[rows, :] * r.dgo[rows, :]).astype(BF)
        r.fe[rows, :] = even
        r.fo[rows, :] = odd
        return acc + col(even.astype(F32)) + col(odd.astype(F32))

    add_small(r, C1B, lax.fori_loop(0, T // 32, one, jnp.zeros((1, D), F32)))


def stage_conv2_weights(r, i):
    D = r.stream.shape[1]
    tap = (r.hp, r.he, r.ho)[i]
    r.g_c2[i * D : (i + 1) * D, :] = tn(tap[...], r.sg[...]).astype(BF)


def stage_conv1_weights(r):
    value = (tn(r.xe[...], r.fe[...]) + tn(r.xo[...], r.fo[...])).astype(BF)
    mels = r.w1.shape[1]
    for o in range(3):
        r.g_c1[mels * o : mels * (o + 1), :] = value[128 * o : 128 * o + mels, :]
    r.g_c1[3 * mels :, :] = jnp.zeros((r.g_c1.shape[0] - 3 * mels, r.g_c1.shape[1]), BF)


def stage_mel(r, next_row, prev_row):
    T, D = r.stream.shape
    fe, fo = r.fe[...], r.fo[...]
    w = [r.w1p[128 * o : 128 * (o + 1), :] for o in range(3)]
    r.wide[16 : 16 + T, :] = nt(fo, w[2])
    r.wide[0:16, :] = nt(prev_row, w[2])
    r.melg[:, 0:128] = (nt(fe, w[1]) + nt(fo, w[0]) + r.wide[15 : 15 + T, :]).astype(BF)
    r.wide[0:T, :] = nt(fe, w[0])
    r.wide[T : T + 16, :] = nt(next_row, w[0])
    r.melg[:, 128:256] = (nt(fe, w[2]) + nt(fo, w[1]) + r.wide[1 : 1 + T, :]).astype(BF)


class Net:
    def __init__(self, r, bits):
        self.r, self.bits, self.used, self.used_here = r, bits, 0, 0
        self.d, self.c, self.m = (lax.axis_index(n) for n in ("dp", "seq", "mp"))

    def bit(self, dim):
        if dim == "c":
            return self.c
        if dim == "y":
            return self.m
        return (self.d // (1 << dim)) % 2

    def peer(self, dims):
        d = self.d
        for k in dims:
            if k not in ("c", "y"):
                d = d + (1 << k) - 2 * (1 << k) * self.bit(k)
        return (
            d,
            1 - self.c if "c" in dims else self.c,
            1 - self.m if "y" in dims else self.m,
        )

    def greet(self, partners):
        barrier = pltpu.get_barrier_semaphore()
        for dims in partners:
            pl.semaphore_signal(barrier, inc=1, device_id=self.peer(dims), device_id_type=MESH)
        pl.semaphore_wait(barrier, len(partners))

    def copy(self, src, dst, *dims):
        i = self.used
        self.used += 1
        return pltpu.make_async_remote_copy(
            src_ref=src,
            dst_ref=dst,
            send_sem=self.r.send.at[i],
            recv_sem=self.r.recv.at[i],
            device_id=self.peer(dims),
            device_id_type=MESH,
        )

    def send(self, src, dst, *dims):
        copy = self.copy(src, dst, *dims)
        copy.start()
        return copy

    def here(self, src, dst):
        i = self.used_here
        self.used_here += 1
        copy = pltpu.make_async_copy(src, dst, self.r.own.at[i])
        copy.start()
        return copy


def start_all(copies):
    for copy in copies:
        copy.start()


def wait_all(copies):
    for copy in copies:
        copy.wait()


def rows16(start, size):
    return pl.ds(pl.multiple_of(start, 16), size)


def subsets(dims):
    found = [()]
    for dim in dims:
        found += [one + (dim,) for one in found]
    return found[1:]


def sum_plan(rows, halves, order):
    steps, need = [], 0
    for dims in order:
        by_half = halves == 2 and "y" in dims
        cutting = [dim for dim in dims if not (by_half and dim == "y")]
        if rows % (16 << len(cutting)):
            cutting = []
        rows >>= len(cutting)
        if by_half:
            halves = 1
        steps.append((dims, cutting, rows, halves, by_half))
        need += rows * halves * len(subsets(dims))
    return steps, need


class Track:
    def __init__(self, acts):
        self.acts = list(acts)

    def take(self):
        return [self.acts.pop(0)] if self.acts else []


def bucket_sum(net, g, got, done, halves, order):
    R = g.shape[0] // halves
    lo, rows, at, bases = 0, R, 0, [h * R for h in range(halves)]
    acts, back, end = [], [], None

    def start_after(end, copies):
        def act():
            if end is not None:
                end()
            for copy in copies:
                copy.start()

        return act

    def adder(copies, places, n):
        step = 64 if n % 64 == 0 else 32 if n % 32 == 0 else 16

        def end():
            wait_all(copies)
            for to, ofs in places:

                def add(k, carry, to=to, ofs=ofs):
                    mine = rows16(to + k * step, step)
                    value = g[mine, :].astype(F32)
                    for of in ofs:
                        value = value + got[rows16(of + k * step, step), :].astype(F32)
                    g[mine, :] = value.astype(BF)
                    return carry

                lax.fori_loop(0, n // step, add, 0)

        return end

    for dims, cutting, n, _, by_half in sum_plan(R, halves, order)[0]:

        def part_of(other):
            start = lo
            for i, dim in enumerate(reversed(cutting)):
                b = net.bit(dim)
                start = start + (1 - b if dim in other else b) * (n << i)
            return start

        keep = part_of(())
        if by_half:
            bases = [net.m * R]
        copies, ofs = [], [[] for _ in bases]
        for other in subsets(dims):
            sources = [(1 - net.m) * R] if by_half and "y" in other else bases
            for i, base in enumerate(sources):
                src = g.at[rows16(base + part_of(other), n)]
                copies.append(net.copy(src, got.at[rows16(at, n)], *other))
                ofs[i].append(at)
                at += n
        acts.append(start_after(end, copies))
        end = adder(copies, [(base + keep, of) for base, of in zip(bases, ofs)], n)
        if cutting:
            back.append((cutting, n, lo))
        lo, rows = keep, n

    def settle(end=end, lo=lo, base=bases[0], rows=rows):
        end()
        for k in range(rows // 16):
            done[rows16(lo + 16 * k, 16), :] = g[rows16(base + lo + 16 * k, 16), :]

    end = settle
    for cutting, n, before in reversed(back):
        part = rows16(lo, n)
        copies = [net.copy(done.at[part], done.at[part], *other) for other in subsets(cutting)]
        acts.append(start_after(end, copies))
        end = functools.partial(wait_all, copies)
        lo = before
    return Track(acts + [end])


def small_sum(net, value, slots, order):
    acts, end, at = [], None, 0
    for dims in order:
        copies = [net.copy(value, slots.at[at + i], *other) for i, other in enumerate(subsets(dims))]

        def act(end=end, copies=copies):
            if end is not None:
                end()
            start_all(copies)

        def end(copies=copies, at=at):
            wait_all(copies)
            total = value[...]
            for i in range(len(copies)):
                total = total + slots[at + i]
            value[...] = total

        at += len(copies)
        acts.append(act)
    return Track(acts + [end])


def ready(*names):
    pass


def advance(*sums):
    for one in sums:
        for act in one.take():
            act()


def drain(*sums):
    while any(one.acts for one in sums):
        advance(*sums)


def quarter(net):
    return 2 * net.c + net.c + net.m - 2 * net.c * net.m


def choose(slots, by_core, by_y):
    core = jnp.where(by_core, 1.0, 0.0)
    y = jnp.where(by_y, 1.0, 0.0)
    return (slots[0].astype(F32) * core + slots[1].astype(F32) * y).astype(BF)


def pick_next(net, slots):
    q = quarter(net)
    return choose(slots, q == 1, q % 2 == 0)


def pick_prev(net, slots):
    q = quarter(net)
    return choose(slots, q == 2, q % 2 == 1)


ROW_BIASES = ("c1b", "c2b", "n1g", "n1b", "oub", "n2g", "n2b", "dnb")


ORDERS = dict(
    down=("c-x-y-w-z", "c-zy-w-x"),
    up=("c-xy-wz", "c-zy-x-w"),
    out=("c-zy-wx",),
    qkv=("c-y-z-x-w", "c-xz-yw", "c-z-x-y-w"),
    c2=("c-z-xy-w", "c-yx-z-w", "c-x-zy-w"),
    c1=("c-y-xz-w",),
    vec=("c-w-x-y-z",),
)
SCHEDULE = dict(
    ff2=("down0", "up0"),
    ffo=("down0", "down1", "up0", "up1"),
    out=("down1", "up1", "out0"),
    pull1=("out0",),
    pull2=("down0",),
    pull4=("up0",),
    pull6=("down1", "up1", "out0"),
    pull7=("down0", "up0"),
    pull8=("up1", "out0"),
    pull10=("down1",),
    pull11=("up0", "up1", "out0"),
    pull12=("down0", "down1"),
    pull13=("up0", "up1", "out0"),
    pull14=("down0", "down1"),
    pull15=("up0", "up1", "out0"),
    home=("down0",),
    qkvw1=("down1", "up1", "qkv1"),
    qkvw2=("qkv2",),
    qkvw0=("down0", "qkv0"),
    norm=("up1", "qkv1"),
    c2=("down1", "qkv0", "qkv2"),
    c2w0=("c20",),
    c2w1=("c21",),
    c2w2=("c22",),
    first=("down0", "down1", "qkv1", "c20", "c21", "c22"),
    c1=("qkv0", "qkv2"),
    c1w=("down0", "c10", "vec"),
    mel=("qkv0", "qkv1", "qkv2", "c20", "c21", "c10", "vec"),
    end=(
        "c22", "qkv1", "qkv0", "c21", "vec", "qkv2", "c20", "c22", "qkv0", "qkv1", "c10", "c21",
        "vec", "qkv2", "c20", "qkv1", "c22", "qkv0", "vec", "c10", "c21", "qkv2", "c20", "c22",
        "qkv0", "c10", "vec", "c21", "qkv2", "c20", "c22", "c10", "qkv0", "c21", "qkv2", "qkv0",
        "c10", "c20", "c22", "c21", "qkv2", "c10", "c20", "c22",
    ),
)


def orders(name, bits):
    dims = dict(c=["c"], y=["y"], x=[0], z=list(range(1, min(2, bits))), w=list(range(2, min(3, bits))))
    found = []
    for spec in ORDERS[name]:
        groups = [tuple(dim for ch in group for dim in dims[ch]) for group in spec.split("-")]
        found.append([group for group in groups if group] + [(dim,) for dim in range(3, bits)])
    return found


def partners(bits):
    found = [("c",), ("y",), ("c", "y")] + [(dim,) for dim in range(bits)]
    for name in ORDERS:
        for order in orders(name, bits):
            for dims in order:
                found += [one for one in subsets(dims) if set(one) not in [set(x) for x in found]]
    return found


def layer(r, bits):
    T, D = r.stream.shape
    half, F2 = D // 2, r.down_l.shape[0]
    side = F2 // D
    mels, span = r.w1.shape[1], 4 * T
    net = Net(r, bits)
    c, m = net.c, net.m
    sub = c + m - 2 * c * m
    rows_of_mine = rows16(sub * T, T)

    r.melbuf[...] = jnp.zeros_like(r.melbuf)
    mel_own = net.here(r.mel.at[0], r.melbuf.at[0:mels, 128 : 128 + span])
    qkv_own = net.here(r.wqkv_l, r.wqkv.at[m])
    w2_own = net.here(r.w2_l, r.w2)
    own = [
        net.here(r.wo_l.at[0 : D // 4], r.wo.at[rows16(m * (D // 4), D // 4)]),
        net.here(r.wo_l.at[D // 4 : half], r.wo.at[rows16(half + m * (D // 4), D // 4)]),
        net.here(r.up_l, r.up.at[m]),
        net.here(r.down_l, r.down.at[rows16(m * F2, F2)]),
        net.here(r.cot.at[0, rows_of_mine], r.bg),
    ]
    r.vec_mine[...] = jnp.zeros_like(r.vec_mine)
    own_lanes = pl.ds(pl.multiple_of(m * half, 128), half)
    r.vec_mine[0:2, own_lanes] = r.qkvb[...].astype(F32)
    for k in range(side):
        r.vec_mine[pl.ds(2 + m * side + k, 1), :] = r.upb[k * D : (k + 1) * D].astype(F32).reshape(1, D)
    for k, n in enumerate(ROW_BIASES):
        r.vecs[k : k + 1, :] = getattr(r, n)[...].astype(F32).reshape(1, D)
    net.greet(partners(bits))
    vec_copy = net.send(r.vec_mine, r.vec_got, "y")
    mel_own.wait()
    src = pl.ds(pl.multiple_of(128 + (1 - c) * (span - 128), 128), 128)
    dst = pl.ds(pl.multiple_of(c * (span + 128), 128), 128)
    mel_rim = net.send(r.melbuf.at[0:mels, src], r.melbuf.at[0:mels, dst], "c")
    p = 4 * c + 2 * net.bit(0) + net.bit(1) if bits > 1 else 2 * c + net.bit(0)
    cuts = 8 if bits > 1 else 4

    def pass_on(of, at, count, dim):
        def cut(n, base):
            return rows16(base + at * (n // cuts), count * (n // cuts))

        wo = rows16(c * half + of * (D // 4) + (at - c * (cuts // 2)) * (half // cuts), count * (half // cuts))
        parts = [r.wo.at[wo], r.up.at[of, cut(D, 0)], r.down.at[cut(F2, of * F2)]]
        return [net.copy(x, x, dim) for x in parts]

    def pass_qkv(of, at, count, dim):
        rows = r.wqkv.at[of, :, rows16(at * (D // 4), count * (D // 4))]
        return net.copy(rows, rows, dim)

    two = 2 if bits > 1 else 1
    qkv_y = pass_qkv(m, 2 * c + net.bit(0), 1, "y")
    qkv_x = pass_qkv(1 - m, 2 * c + net.bit(0), 1, 0)
    qkv_c = pass_qkv(1 - m, 2 * c, 2, "c")
    ff_y = pass_on(m, p, 1, "y")
    ff_z = pass_on(1 - m, p, 1, 1) if bits > 1 else []
    ff_x = pass_on(1 - m, (p // two) * two, two, 0)
    ff_c = pass_on(1 - m, c * (cuts // 2), cuts // 2, "c")
    qkv_own.wait()
    qkv_y.start()
    wait_all(own)
    r.small[...] = jnp.zeros_like(r.small)
    stage_mel_rows(r, sub, mel_rim.wait)
    start_all(ff_y)
    stage_first(r, jnp.logical_and(c == 0, m == 0))
    stage_odd(r)
    qkv_y.wait()
    qkv_x.start()
    w2_own.wait()
    stage_second(r, quarter(net))
    wait_all(ff_y)
    start_all(ff_z)
    vec_copy.wait()
    r.vecs[8:16, :] = r.vec_mine[...] + r.vec_got[...]

    def block(slot, part, h):
        return r.kv.at[rows16((3 * slot + part) * half + h * (half // 2), half // 2)]

    def project(h):
        far, near = [], []
        for part in (1, 2, 0):
            stage_qkv(r, part, h)
            if part:
                far.append(net.send(block(3 + c, part, h), block(0, part, h), "y"))
                far.append(net.send(block(4 - c, part, h), block(1, part, h), "c", "y"))
            near.append(net.send(block(4 - c, part, h), block(2, part, h), "c"))
        return far, near

    far_own, near_own = project(m)
    qkv_x.wait()
    qkv_c.start()
    stage_mask(r, sub)
    add_small(r, DNB, col(r.bg[...].astype(F32)))
    r.normedt[...] = r.normed[...].astype(F32).T.astype(BF)
    wait_all(near_own)
    heads = half // HEAD
    far_other = [
        net.copy(block(own, part, 1 - m), block(to, part, 1 - m), *dims)
        for part in (1, 2)
        for own, to, dims in ((3 + c, 0, ("y",)), (4 - c, 1, ("c", "y")))
    ]
    near_other = [net.copy(block(4 - c, part, 1 - m), block(2, part, 1 - m), "c") for part in range(3)]

    def project_other():
        qkv_c.wait()
        stage_qkv(r, 1, 1 - m)
        start_all(far_other[0:2])
        stage_qkv(r, 2, 1 - m)
        start_all(far_other[2:4])
        stage_qkv(r, 0, 1 - m)
        start_all(near_other)

    hooks = {
        heads - 1: [project_other],
        heads: [lambda: wait_all(near_other), lambda: wait_all(ff_z), lambda: start_all(ff_x)],
        2 * heads: [lambda: wait_all(far_own)],
        5 * heads // 2: [lambda: wait_all(ff_x), lambda: start_all(ff_c)],
        3 * heads: [lambda: wait_all(far_other)],
    }
    attend(r, c, m, hooks)
    attend_end(r, 1)
    mix_c = net.send(r.mixb.at[half:D], r.mix_got, "c")
    attend_end(r, 0)
    stage_mid(r, c, mix_c.wait, lambda: wait_all(ff_c))

    def summed(n, part, rows, halves):
        views = [
            getattr(r, "g_" + n).at[part * rows * halves : (part + 1) * rows * halves],
            getattr(r, "got_%s%d" % (n, part)),
            getattr(r, "done_" + n).at[part * rows : (part + 1) * rows],
        ]
        return bucket_sum(net, *views, halves, orders(n, bits)[part])

    tracks = {}
    for n, rows, halves, parts in (
        ("down", D, 2, side),
        ("up", D, 2, side),
        ("out", half, 2, 1),
        ("qkv", half, 2, 3),
        ("c2", D, 1, 3),
        ("c1", r.g_c1.shape[0], 1, 1),
    ):
        for part in range(parts):
            tracks["%s%d" % (n, part)] = summed(n, part, rows, halves)
    tracks["vec"] = small_sum(net, r.small, r.got_small, orders("vec", bits)[0])

    def acts_at(name):
        return [act for n in SCHEDULE.get(name, ()) if n in tracks for act in tracks[n].take()]

    def point(name):
        for act in acts_at(name):
            act()

    hooks = {}
    for step in range(2 * side):
        if step and step % 2 == 0:
            ready("down%d" % (step // 2 - 1), "up%d" % (step // 2 - 1))
        hooks[step] = acts_at("ff%d" % step)
    stage_ff(r, hooks)
    ready("down%d" % (side - 1), "up%d" % (side - 1))
    point("ffo")
    stage_mid_pull(r)
    stage_do(r, c, False)
    do_c = net.send(r.dot_out, r.dot.at[half:D], "c")
    point("mid")
    stage_out_weights(r, c)
    ready("out0")
    point("out")
    stage_do(r, c, True)
    stage_diag(r, 0)
    do_c.wait()
    stage_diag(r, 1)
    enc = [
        net.copy(r.enc, r.enc_got, "y"),
        pltpu.make_async_copy(r.enc, r.enc_o.at[rows_of_mine], r.own.at[39]),
    ]

    both = half * 2
    home_y = net.copy(r.dkv.at[0:both], r.from_y, "y")
    home_d = net.copy(r.dkv.at[both : 2 * both], r.from_d, "c", "y")
    home_c = net.copy(r.dkv.at[2 * both : 3 * both], r.from_c.at[half:], "c")
    hooks = {}

    def at_step(step, *acts):
        hooks.setdefault(step * heads // 4, []).extend(acts)

    at_step(4, home_y.start)
    at_step(8, home_d.start)
    at_step(11, lambda: start_all(enc))
    at_step(12, home_c.start)
    for step in range(16):
        at_step(step, *acts_at("pull%d" % step))
    attend_pull(r, c, hooks)
    r.dq_out[...] = (r.dqt[half:D, :] * HEAD**-0.5).astype(BF)
    dq_c = net.send(r.dq_out, r.from_c.at[0:half], "c")
    r.dsum[rows16(c * half, half), :] = (r.dqt[0:half, :] * HEAD**-0.5).astype(BF)
    point("home")
    home_y.wait()
    home_d.wait()
    home_c.wait()

    def total(i, carry):
        for part in range(2):
            rows = rows16(part * half + i * 32, 32)
            mine = r.dkv[rows16(3 * both + part * half + i * 32, 32), :].astype(F32) + r.from_y[rows, :].astype(F32)
            r.dsum[rows16((1 + part) * D + c * half + i * 32, 32), :] = mine.astype(BF)
            other = r.from_c[rows16((1 + part) * half + i * 32, 32), :].astype(F32) + r.from_d[rows, :].astype(F32)
            r.dsum[rows16((1 + part) * D + (1 - c) * half + i * 32, 32), :] = other.astype(BF)
        return carry

    lax.fori_loop(0, half // 32, total, 0)
    dq_c.wait()
    r.dsum[rows16((1 - c) * half, half), :] = r.from_c[0:half, :]

    for part in (1, 2, 0):
        stage_qkv_weights(r, part)
        ready("qkv%d" % part)
        point("qkvw%d" % part)
    stage_qkv_pull(r)
    point("norm")
    stage_norm_pull(r)
    rim = [net.send(r.sg.at[0:16], r.slots.at[0, i], dim) for i, dim in enumerate(("c", "y"))]
    point("c2")
    for part in range(3):
        stage_conv2_weights(r, part)
        ready("c2%d" % part)
        point("c2w%d" % part)
    wait_all(rim)
    stage_conv2_pull(r, pick_next(net, r.slots.at[0]))
    point("first")
    stage_first_pull(r)
    rim = [net.send(r.fe.at[0:16], r.slots.at[1, i], dim) for i, dim in enumerate(("c", "y"))]
    rim += [net.send(r.fo.at[T - 16 : T], r.slots.at[2, i], dim) for i, dim in enumerate(("c", "y"))]
    point("c1")
    stage_conv1_weights(r)
    ready("c10", "vec")
    point("c1w")
    wait_all(rim)
    stage_mel(r, pick_next(net, r.slots.at[1]), pick_prev(net, r.slots.at[2]))
    rows_of_yours = rows16((1 - sub) * T, T)
    mel_y = net.send(r.melg, r.melg_got, "y")
    point("mel")
    wait_all(enc)
    ends = [
        net.here(r.enc_got, r.enc_o.at[rows_of_yours]),
        net.here(r.melg, r.mel_o.at[rows_of_mine]),
    ]
    point("end")
    drain(*tracks.values())

    ends.append(net.here(r.done_down, r.down_o))
    for j in range(side):
        ends.append(net.here(r.done_up.at[j * D : (j + 1) * D], r.up_o.at[:, j * D : (j + 1) * D]))
    ends.append(net.here(r.done_out, r.out_o))
    for part in range(3):
        for j in range(2):
            ends.append(
                net.here(
                    r.done_qkv.at[part * half : (part + 1) * half, j * half : (j + 1) * half],
                    r.qkv_o.at[part, j * half : (j + 1) * half],
                )
            )
    ends.append(net.here(r.done_c2, r.c2_o))
    ends.append(net.here(r.done_c1, r.c1_o))
    ends.append(net.here(r.small, r.small_o))
    mel_y.wait()
    ends.append(net.here(r.melg_got, r.mel_o.at[rows_of_yours]))
    wait_all(ends)


def run_layer(bits, near, far, outs, T, D, F2, lanes):
    half, H = D // 2, D // HEAD
    td, dt = (T, D), (D, T)
    buckets = dict(down=(D, 2, F2 // D), up=(D, 2, F2 // D), out=(half, 2, 1), qkv=(half, 2, 3), c2=(D, 1, 3), c1=(lanes, 1, 1))
    scratch = dict(
        melbuf=((128, 4 * T + 256), BF),
        mele=((T + 24, 128), F32),
        melo=((T + 24, 128), F32),
        xe=((T, 384), BF),
        xo=((T, 384), BF),
        w1p=((384, D), BF),
        w2=((3, D, D), BF),
        bg=(td, BF),
        wqkv=((2, 3, D, half), BF),
        wo=((D, D), BF),
        up=((2, D, F2), BF),
        down=((2 * F2, D), BF),
        vecs=((16, D), F32),
        vec_mine=((8, D), F32),
        vec_got=((8, D), F32),
        stream=(td, F32),
        he=(td, BF),
        ho=(td, BF),
        hp=(td, BF),
        dge=(td, F32),
        dgo=(td, F32),
        dg2=(td, F32),
        normed=(td, BF),
        kv=((15 * half, T), BF),
        mixt=(dt, F32),
        mixb=(dt, BF),
        normedt=(dt, BF),
        mix_got=((half, T), BF),
        dot=(dt, BF),
        dot_out=((half, T), BF),
        top=((H, 1, T), F32),
        total=((H, 1, T), F32),
        diag=((H, 1, T), F32),
        tmp=(td, F32),
        tmp2=(td, F32),
        shift=((T + 16, D), F32),
        wide=((T + 16, 128), F32),
        mid=(td, F32),
        ntwo=(td, BF),
        act=(td, BF),
        ing=(td, BF),
        ffo=(td, F32),
        ntg=(td, F32),
        attg=(td, BF),
        dqt=(dt, F32),
        dq_out=((half, T), BF),
        pb=((T, 2 * T), BF),
        ds=((T, 2 * T), BF),
        dkv=((8 * half, T), BF),
        from_y=((2 * half, T), BF),
        from_d=((2 * half, T), BF),
        from_c=((3 * half, T), BF),
        dsum=((3 * D, T), BF),
        enc_got=(td, BF),
        melg=((T, 256), BF),
        melg_got=((T, 256), BF),
        small=((16, D), F32),
        got_small=((sum(len(subsets(dims)) for dims in orders("vec", bits)[0]), 16, D), F32),
        slots=((3, 2, 16, D), BF),
    )
    alias = T == D
    for n, (rows, halves, parts) in buckets.items():
        if n not in ("qkv", "c2"):
            scratch["g_" + n] = ((rows * halves * parts, D), BF)
        for part in range(parts):
            need = sum_plan(rows, halves, orders(n, bits)[part])[1]
            scratch["got_%s%d" % (n, part)] = ((need, D), BF)
        scratch["done_" + n] = ((rows * parts, D), BF)
    if not alias:
        scratch.update(g_qkv=((6 * half, D), BF), g_c2=((6 * half, D), BF))
    names = list(near) + list(far) + list(outs) + list(scratch) + ["send", "recv", "own"]

    def kernel(*refs):
        r = Box()
        for n, ref in zip(names, refs):
            setattr(r, n, ref)
        r.odd, r.smg, r.sg, r.fe, r.fo, r.enc = r.shift, r.mid, r.ntwo, r.act, r.ing, r.bg
        if alias:
            r.g_qkv, r.g_c2 = r.kv.at[0 : 6 * half], r.kv.at[6 * half : 12 * half]
        layer(r, bits)

    vmem, anywhere = pl.BlockSpec(memory_space=pltpu.VMEM), pl.BlockSpec(memory_space=pl.ANY)
    got = pl.pallas_call(
        kernel,
        name="layer",
        out_shape=[jax.ShapeDtypeStruct(*o) for o in outs.values()],
        in_specs=[vmem] * len(near) + [anywhere] * len(far),
        out_specs=[anywhere] * len(outs),
        scratch_shapes=[pltpu.VMEM(*s) for s in scratch.values()]
        + [pltpu.SemaphoreType.DMA((256,)), pltpu.SemaphoreType.DMA((256,)), pltpu.SemaphoreType.DMA((40,))],
        compiler_params=pltpu.CompilerParams(
            vmem_limit_bytes=VMEM_LIMIT, collective_id=1, has_side_effects=True
        ),
    )(*near.values(), *far.values())
    return dict(zip(outs, got))


def run_finish(got, mels, side):
    T2, D = got["enc_o"].shape
    half = D // 2
    ins = list(got)
    outs = dict(
        enc=((1, T2, D), BF),
        mel=((1, mels, 2 * T2), F32),
        c1=((3, mels, D), F32),
        c2=((3, D, D), F32),
        qkv=((3, D, half), F32),
        qkvb=((2, half), F32),
        out=((half, D), F32),
        up=((D, side * D), F32),
        upb=((side * D,), F32),
        down=((side * D, D), F32),
    )
    outs.update({n: ((D,), F32) for n in ROW_BIASES})

    def kernel(*refs):
        r = Box()
        for n, ref in zip(ins + list(outs), refs):
            setattr(r, n, ref)
        m = lax.axis_index("mp")

        def cast(src, dst):
            def one(rows):
                dst[rows, :] = src[rows, :].astype(dst.dtype)

            rows_loop(src.shape[0], 256, one)

        cast(r.enc_o, r.enc.at[0])
        cast(r.down_o, r.down)
        cast(r.up_o, r.up)
        cast(r.out_o, r.out)
        for o in range(3):
            cast(r.qkv_o.at[o], r.qkv.at[o])
            cast(r.c2_o.at[o * D : (o + 1) * D], r.c2.at[o])
            r.c1[o] = r.c1_o[o * mels : (o + 1) * mels, :].astype(F32)
        row = lax.broadcasted_iota(jnp.int32, (128, 256), 0)
        lane = lax.broadcasted_iota(jnp.int32, (128, 256), 1)
        even = jnp.where(lane == 2 * row, 1.0, 0.0).astype(BF)
        odd = jnp.where(lane == 2 * row + 1, 1.0, 0.0).astype(BF)
        for k in range(T2 // 128):
            rows = slice(k * 128, (k + 1) * 128)
            value = tn(r.mel_o[rows, 0:128], even) + tn(r.mel_o[rows, 128:256], odd)
            r.mel[0, :, k * 256 : (k + 1) * 256] = value[0:mels, :]
        for k, n in enumerate(ROW_BIASES):
            getattr(r, n)[...] = r.small_o[k : k + 1, :].reshape(D)
        r.qkvb[...] = r.small_o[QB : QB + 2, pl.ds(pl.multiple_of(m * half, 128), half)]
        for k in range(side):
            r.upb[k * D : (k + 1) * D] = r.small_o[pl.ds(UPB + m * side + k, 1), :].reshape(D)

    vmem = pl.BlockSpec(memory_space=pltpu.VMEM)
    done = pl.pallas_call(
        kernel,
        name="finish",
        out_shape=[jax.ShapeDtypeStruct(*o) for o in outs.values()],
        in_specs=[vmem] * len(ins),
        out_specs=[vmem] * len(outs),
        compiler_params=pltpu.CompilerParams(vmem_limit_bytes=VMEM_LIMIT),
    )(*got.values())
    return dict(zip(outs, done))


def sine_tables(frames, channels, fine):
    half_width = channels // 2
    rate = np.exp(-(math.log(10000.0) / (half_width - 1)) * np.arange(half_width))
    small = np.arange(fine)[:, None] * rate[None, :]
    large = np.arange(0, frames, fine)[:, None] * rate[None, :]
    table = dict(fine_s=np.sin(small), fine_c=np.cos(small), coarse_s=np.sin(large), coarse_c=np.cos(large))
    return {n: jnp.asarray(t, F32) for n, t in table.items()}


def on_device(
    mel_input,
    conv1_weight,
    conv1_bias,
    conv2_weight,
    conv2_bias,
    norm1_gain,
    norm1_bias,
    qkv_weight,
    qkv_bias,
    out_weight,
    out_bias,
    norm2_gain,
    norm2_bias,
    up_weight,
    up_bias,
    down_weight,
    down_bias,
    cotangent,
    speech_mask,
):
    mels = mel_input.shape[1]
    T, D = cotangent.shape[1] // 2, cotangent.shape[2]
    F2 = up_weight.shape[1]
    side, half = F2 // D, D // 2
    bits = (lax.axis_size("dp") - 1).bit_length()
    lanes = -(-3 * mels // 128) * 128
    near = dict(
        w1=conv1_weight,
        mask=speech_mask,
        qkvb=qkv_bias,
        upb=up_bias,
        c1b=conv1_bias,
        c2b=conv2_bias,
        n1g=norm1_gain,
        n1b=norm1_bias,
        oub=out_bias,
        n2g=norm2_gain,
        n2b=norm2_bias,
        dnb=down_bias,
    )
    near.update(sine_tables(4 * T, D, 32))
    got = run_layer(
        bits,
        near,
        dict(
            mel=mel_input,
            cot=cotangent,
            w2_l=conv2_weight,
            wqkv_l=qkv_weight,
            wo_l=out_weight,
            up_l=up_weight,
            down_l=down_weight,
        ),
        dict(
            enc_o=((2 * T, D), BF),
            mel_o=((2 * T, 256), BF),
            down_o=((F2, D), BF),
            up_o=((D, F2), BF),
            out_o=((half, D), BF),
            qkv_o=((3, D, half), BF),
            c2_o=((3 * D, D), BF),
            c1_o=((lanes, D), BF),
            small_o=((16, D), F32),
        ),
        T,
        D,
        F2,
        lanes,
    )
    done = run_finish(got, mels, side)
    names = ("enc", "mel", "c1", "c1b", "c2", "c2b", "n1g", "n1b", "qkv", "qkvb")
    names += ("out", "oub", "n2g", "n2b", "up", "upb", "down", "dnb")
    return tuple(done[n] for n in names)


def solution(mesh):
    placed = (
        P("dp", None, "seq"),
        P(),
        P(),
        P(),
        P(),
        P(),
        P(),
        P(None, None, "mp"),
        P(None, "mp"),
        P("mp", None),
        P(),
        P(),
        P(),
        P(None, "mp"),
        P("mp"),
        P("mp", None),
        P(),
        P("dp", "seq", None),
        P("dp", "seq"),
    )
    return jax.shard_map(
        on_device,
        mesh=mesh,
        in_specs=placed,
        out_specs=(
            P("dp", "seq", None),
            P("dp", None, "seq"),
            P(),
            P(),
            P(),
            P(),
            P(),
            P(),
            P(None, None, "mp"),
            P(None, "mp"),
            P("mp", None),
            P(),
            P(),
            P(),
            P(None, "mp"),
            P("mp"),
            P("mp", None),
            P(),
        ),
        check_vma=False,
    )
```

```python
import functools
import math

import jax
import jax.numpy as jnp
import numpy as np
from jax import lax
from jax.experimental import pallas as pl
from jax.experimental.pallas import tpu as pltpu
from jax.sharding import PartitionSpec as P

HEAD = 64
BF = jnp.bfloat16
F32 = jnp.float32
MESH = pl.DeviceIdType.MESH
VMEM_LIMIT = 61 * 1024 * 1024
C1B, C2B, N1G, N1B, OUB, N2G, N2B, DNB, QB, VB, UPB = range(11)


class Box:
    pass


def dot(a, b, ca, cb):
    return lax.dot_general(a, b, (((ca,), (cb,)), ((), ())), preferred_element_type=F32)


def nn(a, b):
    return dot(a, b, 1, 0)


def nt(a, b):
    return dot(a, b, 1, 1)


def tn(a, b):
    return dot(a, b, 0, 0)


def rows_loop(total, step, body, unroll=1):
    step = min(step, total)

    def one(i, carry):
        body(pl.ds(pl.multiple_of(i * step, step), step))
        return carry

    lax.fori_loop(0, total // step, one, 0, unroll=unroll)


def gelu_parts(v):
    t = 1.0 / (1.0 + (0.3275911 / math.sqrt(2.0)) * jnp.abs(v))
    e = jnp.exp(-0.5 * v * v)
    poly = 1.061405429 * t - 1.453152027
    poly = poly * t + 1.421413741
    poly = poly * t - 0.284496736
    poly = poly * t + 0.254829592
    tail = (0.5 * t) * poly * e
    return jnp.where(v >= 0, 1.0 - tail, tail), e * (1.0 / math.sqrt(2.0 * math.pi))


def gelu_both(v):
    cdf, pdf = gelu_parts(v)
    return v * cdf, cdf + v * pdf


def normal(x):
    center = x - jnp.mean(x, axis=-1, keepdims=True)
    spread = jnp.mean(center * center, axis=-1, keepdims=True)
    inv = lax.rsqrt(spread + 1e-05)
    return center * inv, inv


def normal_pull(gy, hat, inv):
    return inv * (
        gy
        - jnp.mean(gy, axis=-1, keepdims=True)
        - hat * jnp.mean(gy * hat, axis=-1, keepdims=True)
    )


def vec(r, i):
    return r.vecs[i : i + 1, :]


def add_small(r, i, value):
    r.small[i : i + 1, :] += value


def col(value):
    return jnp.sum(value, axis=0, keepdims=True)


def stage_mel_rows(r, sub, rim_came):
    T, D = r.stream.shape
    row = lax.broadcasted_iota(jnp.int32, (256, 256), 0)
    lane = lax.broadcasted_iota(jnp.int32, (256, 256), 1)
    pick = jnp.where(lane == 2 * (row % 128) + row // 128, 1.0, 0.0).astype(BF)
    base = sub * 2 * T

    def lanes(start, size):
        return r.melbuf[:, pl.ds(pl.multiple_of(base + start, 128), size)]

    row = lax.broadcasted_iota(jnp.int32, (16, 128), 0)
    lane = lax.broadcasted_iota(jnp.int32, (16, 128), 1)

    def select(at, to):
        return jnp.where(jnp.logical_and(row == to, lane == at), 1.0, 0.0).astype(BF)

    for k in range(T // 128):
        both = nt(pick, lanes(128 + 256 * k, 256))
        r.mele[8 + 128 * k : 136 + 128 * k, :] = both[0:128, :]
        r.melo[8 + 128 * k : 136 + 128 * k, :] = both[128:256, :]
    rim_came()
    before, after = lanes(0, 128), lanes(128 + 2 * T, 128)
    r.mele[0:8, :] = nt(select(126, 7), before)[0:8, :]
    r.melo[0:8, :] = nt(select(127, 7), before)[0:8, :]
    r.mele[T + 8 : T + 16, :] = nt(select(0, 0), after)[0:8, :]


def three(a, b, c):
    return jnp.concatenate([a, b, c], axis=1).astype(BF)


def stage_first(r, first):
    T, D = r.stream.shape
    for o in range(3):
        r.w1p[128 * o : 128 * o + r.w1.shape[1], :] = r.w1[o]
        r.w1p[128 * o + r.w1.shape[1] : 128 * (o + 1), :] = jnp.zeros((128 - r.w1.shape[1], D), BF)
    w1 = r.w1p[...]
    edge = nn(three(r.mele[0:16, :], r.melo[0:16, :], r.mele[1:17, :]), w1) + vec(r, C1B)
    edge = gelu_both(edge)[0] * jnp.where(first, 0.0, 1.0)
    r.odd[0:8, :] = edge[0:8, :]
    r.xe[...] = three(r.melo[7 : 7 + T, :], r.mele[8 : 8 + T, :], r.melo[8 : 8 + T, :])
    r.xo[...] = three(r.mele[8 : 8 + T, :], r.melo[8 : 8 + T, :], r.mele[9 : 9 + T, :])
    r.tmp[...] = nn(r.xe[...], w1)

    def even(rows):
        value, slope = gelu_both(r.tmp[rows, :] + vec(r, C1B))
        r.he[rows, :] = value.astype(BF)
        r.dge[rows, :] = slope

    rows_loop(T, 32, even)


def stage_odd(r):
    T, D = r.stream.shape
    r.tmp[...] = nn(r.xo[...], r.w1p[...])

    def odd(rows):
        value, slope = gelu_both(r.tmp[rows, :] + vec(r, C1B))
        r.ho[rows, :] = value.astype(BF)
        r.odd[pl.ds(pl.multiple_of(rows.start + 8, 8), rows.size), :] = value
        r.dgo[rows, :] = slope

    rows_loop(T, 32, odd)


def stage_second(r, place):
    T, D = r.stream.shape
    r.hp[...] = r.odd[7 : 7 + T, :].astype(BF)
    r.tmp[...] = nn(r.hp[...], r.w2[0]) + nn(r.he[...], r.w2[1]) + nn(r.ho[...], r.w2[2])
    fine = r.fine_s.shape[0]

    def second(rows):
        value, slope = gelu_both(r.tmp[rows, :] + vec(r, C2B))
        at = place * (T // fine) + rows.start // fine
        s0, c0 = r.coarse_s[pl.ds(at, 1), :], r.coarse_c[pl.ds(at, 1), :]
        s1, c1 = r.fine_s[...], r.fine_c[...]
        stream = value + jnp.concatenate([s0 * c1 + c0 * s1, c0 * c1 - s0 * s1], axis=1)
        r.dg2[rows, :] = slope
        r.stream[rows, :] = stream
        r.normed[rows, :] = (normal(stream)[0] * vec(r, N1G) + vec(r, N1B)).astype(BF)

    rows_loop(T, fine, second)


def stage_mask(r, sub):
    T, D = r.stream.shape
    row = r.mask[0:1, pl.ds(pl.multiple_of(sub * T, 128), T)].astype(F32)
    r.wide[0:T, :] = jnp.broadcast_to(row, (128, T)).T

    def one(rows):
        keep = r.wide[rows, :]
        keep = jnp.concatenate([keep] * (D // 128), axis=1)
        r.bg[rows, :] = (r.bg[rows, :].astype(F32) * keep).astype(BF)

    rows_loop(T, 32, one)


def stage_qkv(r, part, h):
    T, D = r.stream.shape
    half, qr = D // 2, D // 4
    bias, scale = ((QB, HEAD**-0.5), (None, 1.0), (VB, 1.0))[part]
    value = nn(r.normed[...], r.wqkv[h, part])
    if bias is not None:
        value = value + r.vecs[bias : bias + 1, pl.ds(pl.multiple_of(h * half, half), half)]
    value = (value.astype(BF).astype(F32) * scale).T.astype(BF)
    for k in range(2):
        r.kv[rows16((3 * (3 + k) + part) * half + h * qr, qr), :] = value[k * qr : (k + 1) * qr, :]


def at_head(start, h):
    return pl.ds(pl.multiple_of(start + h * HEAD, HEAD), HEAD)


def head_loop(steps, hooks, body):
    def one(step, carry):
        for at, todo in hooks.items():
            if not todo:
                continue

            @pl.when(step == at)
            def _(todo=todo):
                for act in todo:
                    act()

        body(step)
        return carry

    lax.fori_loop(0, steps, one, 0)


def attend(r, c, m, hooks):
    S, T = r.kv.shape[0] // 15, r.kv.shape[1]
    heads = S // HEAD
    r.top[...] = jnp.full(r.top.shape, -jnp.inf, F32)
    r.total[...] = jnp.zeros(r.total.shape, F32)
    r.mixt[...] = jnp.zeros(r.mixt.shape, F32)

    def body(step):
        quarter, u, pair = step // heads, step % heads, heads // 2
        g = 2 * (quarter // 2) + u // pair
        h = (m + (1 - 2 * m) * ((quarter + 1) // 2 % 2)) * pair + u % pair
        own = (3 - g) // 3
        slot = own * (3 + c) + (1 - own) * ((g + 1) % 3)
        k = r.kv[at_head((3 * slot + 1) * S, h), :]
        v = r.kv[at_head((3 * slot + 2) * S, h), :]
        for i, home in enumerate((3 + c, 2)):
            q = r.kv[at_head(3 * home * S, h), :]
            s = tn(k, q)
            before = r.top[i * heads + h]
            top = jnp.maximum(before, jnp.max(s, axis=0, keepdims=True))
            p = jnp.exp(s - top)
            keep = jnp.exp(before - top)
            rows = at_head(i * S, h)
            r.top[i * heads + h] = top
            r.total[i * heads + h] = keep * r.total[i * heads + h] + jnp.sum(p, axis=0, keepdims=True)
            r.mixt[rows, :] = keep * r.mixt[rows, :] + nn(v, p.astype(BF))

    head_loop(4 * heads, hooks, body)


def attend_end(r, i):
    S = r.kv.shape[0] // 15
    heads = S // HEAD

    def one(h, carry):
        rows = at_head(i * S, h)
        total = r.total[i * heads + h]
        value = r.mixt[rows, :] * (1.0 / total)
        r.mixt[rows, :] = value
        r.mixb[rows, :] = value.astype(BF)
        r.top[i * heads + h] = r.top[i * heads + h] + jnp.log(total)
        return carry

    lax.fori_loop(0, heads, one, 0)


def stage_mid(r, c, mix_came, weights_came):
    T, D = r.stream.shape
    half = D // 2
    weights_came()
    r.tmp[...] = tn(r.mixb[0:half, :], r.wo[rows16(c * half, half), :])
    mix_came()
    r.tmp[...] += tn(r.mix_got[...], r.wo[rows16((1 - c) * half, half), :])

    def one(rows):
        mid = r.stream[rows, :] + r.tmp[rows, :] + vec(r, OUB)
        r.mid[rows, :] = mid
        r.ntwo[rows, :] = (normal(mid)[0] * vec(r, N2G) + vec(r, N2B)).astype(BF)

    rows_loop(T, 32, one)


def stage_ff(r, hooks):
    T, D = r.stream.shape
    side = r.up.shape[2] // D
    parts, width = 2 * side, D

    def chunk(t):
        into, at = t % 2, t // 2
        j = into * side + at
        up = r.up[into, :, pl.ds(pl.multiple_of(at * D, D), D)]
        down = r.down[pl.ds(pl.multiple_of(j * D, D), D), :]
        r.tmp[...] = nn(r.ntwo[...], up)
        r.tmp2[...] = nt(r.bg[...], down)
        bias = r.vecs[pl.ds(UPB + j, 1), :]

        def one(i, acc):
            rows = pl.ds(pl.multiple_of(i * 32, 32), 32)
            value, slope = gelu_both(r.tmp[rows, :] + bias)
            r.act[rows, :] = value.astype(BF)
            grad = (r.tmp2[rows, :] * slope).astype(BF)
            r.ing[rows, :] = grad
            return acc + col(grad.astype(F32))

        r.small[pl.ds(UPB + j, 1), :] = lax.fori_loop(0, T // 32, one, jnp.zeros((1, width), F32))
        act = r.act[...]
        ing = r.ing[...]
        out = nn(act, down)
        back = nt(ing, up)

        r.ffo[...] += out
        r.ntg[...] += back
        rows = pl.ds(pl.multiple_of(t * D, D), D)
        r.g_down[rows, :] = tn(act, r.bg[...]).astype(BF)
        r.g_up[rows, :] = tn(r.ntwo[...], ing).astype(BF)

    r.ffo[...] = jnp.zeros_like(r.ffo)
    r.ntg[...] = jnp.zeros_like(r.ntg)
    head_loop(parts, hooks, chunk)


def stage_mid_pull(r):
    T, D = r.stream.shape

    def one(i, accs):
        rows = pl.ds(pl.multiple_of(i * 32, 32), 32)
        mid = r.mid[rows, :]
        enc = (mid + r.ffo[rows, :] + vec(r, DNB)).astype(BF)
        hat, inv = normal(mid)
        grad = r.ntg[rows, :]
        smg = r.bg[rows, :].astype(F32) + normal_pull(grad * vec(r, N2G), hat, inv)
        r.enc[rows, :] = enc
        r.smg[rows, :] = smg
        attg = smg.astype(BF)
        r.attg[rows, :] = attg
        return accs[0] + col(grad * hat), accs[1] + col(grad), accs[2] + col(attg.astype(F32))

    zero = jnp.zeros((1, D), F32)
    gain, bias, out_bias = lax.fori_loop(0, T // 32, one, (zero, zero, zero))
    add_small(r, N2G, gain)
    add_small(r, N2B, bias)
    add_small(r, OUB, out_bias)


def stage_do(r, c, own):
    half = r.attg.shape[1] // 2
    k = c if own else 1 - c
    value = nt(r.wo[rows16(k * half, half), :], r.attg[...]).astype(BF)
    if own:
        r.dot[0:half, :] = value
    else:
        r.dot_out[...] = value


def stage_out_weights(r, c):
    D = r.attg.shape[1]
    half, qr = D // 2, D // 4
    for k, mix in ((c, r.mixb[0:half, :]), (1 - c, r.mix_got[...])):
        value = nn(mix, r.attg[...]).astype(BF)
        for h in range(2):
            r.g_out[rows16(h * half + k * qr, qr), :] = value[h * qr : (h + 1) * qr, :]


def stage_diag(r, i):
    S = r.kv.shape[0] // 15
    heads = S // HEAD

    def one(h, carry):
        rows = at_head(i * S, h)
        value = r.dot[rows, :].astype(F32) * r.mixt[rows, :]
        r.diag[i * heads + h] = jnp.sum(value, axis=0, keepdims=True)
        return carry

    lax.fori_loop(0, heads, one, 0)


def attend_pull(r, c, hooks):
    S, T = r.kv.shape[0] // 15, r.kv.shape[1]
    heads = S // HEAD
    r.dqt[...] = jnp.zeros(r.dqt.shape, F32)

    def body(step):
        g, h = step // heads, step % heads
        slot = g + (g // 3) * c
        k = r.kv[at_head((3 * slot + 1) * S, h), :]
        v = r.kv[at_head((3 * slot + 2) * S, h), :]
        qs = [r.kv[at_head(3 * home * S, h), :] for home in (3 + c, 2)]
        dos = [r.dot[at_head(i * S, h), :] for i in range(2)]
        for i in range(2):
            top, diag = r.top[i * heads + h], r.diag[i * heads + h]
            for at in range(0, T, 128):
                rows, cols = slice(at, at + 128), slice(i * T, (i + 1) * T)
                p = jnp.exp(tn(k[:, rows], qs[i]) - top)
                r.pb[rows, cols] = p.astype(BF)
                r.ds[rows, cols] = (p * (tn(v[:, rows], dos[i]) - diag)).astype(BF)
        both = [jnp.concatenate(one, axis=1) for one in (qs, dos)]
        r.dkv[at_head(2 * g * S, h), :] = nt(both[0], r.ds[...]).astype(BF)
        r.dkv[at_head((2 * g + 1) * S, h), :] = nt(both[1], r.pb[...]).astype(BF)
        dq = nn(k, r.ds[...])
        for i in range(2):
            r.dqt[at_head(i * S, h), :] += dq[:, i * T : (i + 1) * T]

    head_loop(4 * heads, hooks, body)


def piece_of(r, part, h):
    D, qr = r.attg.shape[1], r.attg.shape[1] // 4
    at = part * D + h * qr
    return jnp.concatenate([r.dsum[at : at + qr, :], r.dsum[at + 2 * qr : at + 3 * qr, :]], axis=0)


def stage_qkv_weights(r, part):
    T, D = r.stream.shape
    half = D // 2
    ones = jnp.ones((8, T), BF)
    for h in range(2):
        piece = piece_of(r, part, h)
        if part != 1:
            row = QB if part == 0 else VB
            r.small[row : row + 1, h * half : (h + 1) * half] = nt(ones, piece)[0:1, :]
        grad = nt(r.normedt[...], piece).astype(BF)
        at = (2 * part + h) * half
        r.g_qkv[at : at + half, 0:half] = grad[0:half, :]
        r.g_qkv[at : at + half, half:D] = grad[half:D, :]


def stage_qkv_pull(r, queries_came):
    T, D = r.stream.shape
    total = None
    for part in (1, 2, 0):
        if part == 0:
            queries_came()
        for h in range(2):
            back = nn(r.wqkv[h, part], piece_of(r, part, h))
            total = back if total is None else total + back
    r.tmp[...] = total.T


def stage_norm_pull(r):
    T, D = r.stream.shape

    def one(i, accs):
        rows = pl.ds(pl.multiple_of(i * 32, 32), 32)
        hat, inv = normal(r.stream[rows, :])
        grad = r.tmp[rows, :]
        back = r.smg[rows, :] + normal_pull(grad * vec(r, N1G), hat, inv)
        sg = (back * r.dg2[rows, :]).astype(BF)
        r.sg[rows, :] = sg
        return accs[0] + col(grad * hat), accs[1] + col(grad), accs[2] + col(sg.astype(F32))

    zero = jnp.zeros((1, D), F32)
    gain, bias, c2b = lax.fori_loop(0, T // 32, one, (zero, zero, zero))
    add_small(r, N1G, gain)
    add_small(r, N1B, bias)
    add_small(r, C2B, c2b)


def stage_conv2_pull(r, next_row):
    T, D = r.stream.shape
    sg = r.sg[...]
    r.shift[0:T, :] = nt(sg, r.w2[0])
    r.tmp[...] = nt(sg, r.w2[1])
    r.shift[T : T + 16, :] = nt(next_row(), r.w2[0])
    r.tmp2[...] = nt(sg, r.w2[2]) + r.shift[1 : T + 1, :]


def stage_first_pull(r):
    T, D = r.stream.shape

    def one(i, acc):
        rows = pl.ds(pl.multiple_of(i * 32, 32), 32)
        even = (r.tmp[rows, :] * r.dge[rows, :]).astype(BF)
        odd = (r.tmp2[rows, :] * r.dgo[rows, :]).astype(BF)
        r.fe[rows, :] = even
        r.fo[rows, :] = odd
        return acc + col(even.astype(F32)) + col(odd.astype(F32))

    add_small(r, C1B, lax.fori_loop(0, T // 32, one, jnp.zeros((1, D), F32)))


def stage_conv2_weights(r, i):
    D = r.stream.shape[1]
    tap = (r.hp, r.he, r.ho)[i]
    r.g_c2[i * D : (i + 1) * D, :] = tn(tap[...], r.sg[...]).astype(BF)


def stage_conv1_weights(r):
    value = (tn(r.xe[...], r.fe[...]) + tn(r.xo[...], r.fo[...])).astype(BF)
    mels = r.w1.shape[1]
    for o in range(3):
        r.g_c1[mels * o : mels * (o + 1), :] = value[128 * o : 128 * o + mels, :]
    r.g_c1[3 * mels :, :] = jnp.zeros((r.g_c1.shape[0] - 3 * mels, r.g_c1.shape[1]), BF)


def stage_mel(r, next_row, prev_row):
    T, D = r.stream.shape
    fe, fo = r.fe[...], r.fo[...]
    w = [r.w1p[128 * o : 128 * (o + 1), :] for o in range(3)]
    r.wide[16 : 16 + T, :] = nt(fo, w[2])
    r.wide[0:16, :] = nt(prev_row, w[2])
    r.melg[:, 0:128] = (nt(fe, w[1]) + nt(fo, w[0]) + r.wide[15 : 15 + T, :]).astype(BF)
    r.wide[0:T, :] = nt(fe, w[0])
    r.wide[T : T + 16, :] = nt(next_row, w[0])
    r.melg[:, 128:256] = (nt(fe, w[2]) + nt(fo, w[1]) + r.wide[1 : 1 + T, :]).astype(BF)


class Net:
    def __init__(self, r, bits):
        self.r, self.bits, self.used, self.used_here = r, bits, 0, 0
        self.d, self.c, self.m = (lax.axis_index(n) for n in ("dp", "seq", "mp"))

    def bit(self, dim):
        if dim == "c":
            return self.c
        if dim == "y":
            return self.m
        return (self.d // (1 << dim)) % 2

    def peer(self, dims):
        d = self.d
        for k in dims:
            if k not in ("c", "y"):
                d = d + (1 << k) - 2 * (1 << k) * self.bit(k)
        return (
            d,
            1 - self.c if "c" in dims else self.c,
            1 - self.m if "y" in dims else self.m,
        )

    def greet(self, partners):
        barrier = pltpu.get_barrier_semaphore()
        for dims in partners:
            pl.semaphore_signal(barrier, inc=1, device_id=self.peer(dims), device_id_type=MESH)
        pl.semaphore_wait(barrier, len(partners))

    def copy(self, src, dst, *dims):
        i = self.used
        self.used += 1
        return pltpu.make_async_remote_copy(
            src_ref=src,
            dst_ref=dst,
            send_sem=self.r.send.at[i],
            recv_sem=self.r.recv.at[i],
            device_id=self.peer(dims),
            device_id_type=MESH,
        )

    def send(self, src, dst, *dims):
        copy = self.copy(src, dst, *dims)
        copy.start()
        return copy

    def here_later(self, src, dst):
        i = self.used_here
        self.used_here += 1
        return pltpu.make_async_copy(src, dst, self.r.own.at[i])

    def here(self, src, dst):
        copy = self.here_later(src, dst)
        copy.start()
        return copy


def start_all(copies):
    for copy in copies:
        copy.start()


def wait_all(copies):
    for copy in copies:
        copy.wait()


def rows16(start, size):
    return pl.ds(pl.multiple_of(start, 16), size)


def subsets(dims):
    found = [()]
    for dim in dims:
        found += [one + (dim,) for one in found]
    return found[1:]


def sum_plan(rows, halves, order):
    steps, need = [], 0
    for dims in order:
        by_half = halves == 2 and "y" in dims
        cutting = [dim for dim in dims if not (by_half and dim == "y")]
        if rows % (16 << len(cutting)):
            cutting = []
        rows >>= len(cutting)
        if by_half:
            halves = 1
        steps.append((dims, cutting, rows, halves, by_half))
        need += rows * halves * len(subsets(dims))
    return steps, need


class Track:
    def __init__(self, acts):
        self.acts = list(acts)

    def take(self):
        return [self.acts.pop(0)] if self.acts else []

    def then(self, more):
        last = self.acts.pop()

        def act():
            last()
            more()

        self.acts.append(act)


def bucket_sum(net, g, got, done, halves, order):
    R = g.shape[0] // halves
    lo, rows, at, bases = 0, R, 0, [h * R for h in range(halves)]
    acts, back, end = [], [], None

    def start_after(end, copies):
        def act():
            if end is not None:
                end()
            for copy in copies:
                copy.start()

        return act

    def adder(copies, places, n):
        step = 64 if n % 64 == 0 else 32 if n % 32 == 0 else 16

        def end():
            wait_all(copies)
            for to, ofs in places:

                def add(k, carry, to=to, ofs=ofs):
                    mine = rows16(to + k * step, step)
                    value = g[mine, :].astype(F32)
                    for of in ofs:
                        value = value + got[rows16(of + k * step, step), :].astype(F32)
                    g[mine, :] = value.astype(BF)
                    return carry

                lax.fori_loop(0, n // step, add, 0)

        return end

    for dims, cutting, n, _, by_half in sum_plan(R, halves, order)[0]:

        def part_of(other):
            start = lo
            for i, dim in enumerate(reversed(cutting)):
                b = net.bit(dim)
                start = start + (1 - b if dim in other else b) * (n << i)
            return start

        keep = part_of(())
        if by_half:
            bases = [net.m * R]
        copies, ofs = [], [[] for _ in bases]
        for other in subsets(dims):
            sources = [(1 - net.m) * R] if by_half and "y" in other else bases
            for i, base in enumerate(sources):
                src = g.at[rows16(base + part_of(other), n)]
                copies.append(net.copy(src, got.at[rows16(at, n)], *other))
                ofs[i].append(at)
                at += n
        acts.append(start_after(end, copies))
        end = adder(copies, [(base + keep, of) for base, of in zip(bases, ofs)], n)
        if cutting:
            back.append((cutting, n, lo))
        lo, rows = keep, n

    def settle(end=end, lo=lo, base=bases[0], rows=rows):
        end()
        for k in range(rows // 16):
            done[rows16(lo + 16 * k, 16), :] = g[rows16(base + lo + 16 * k, 16), :]

    end = settle
    for cutting, n, before in reversed(back):
        part = rows16(lo, n)
        copies = [net.copy(done.at[part], done.at[part], *other) for other in subsets(cutting)]
        acts.append(start_after(end, copies))
        end = functools.partial(wait_all, copies)
        lo = before
    return Track(acts + [end])


def small_sum(net, value, slots, order):
    acts, end, at = [], None, 0
    for dims in order:
        copies = [net.copy(value, slots.at[at + i], *other) for i, other in enumerate(subsets(dims))]

        def act(end=end, copies=copies):
            if end is not None:
                end()
            start_all(copies)

        def end(copies=copies, at=at):
            wait_all(copies)
            total = value[...]
            for i in range(len(copies)):
                total = total + slots[at + i]
            value[...] = total

        at += len(copies)
        acts.append(act)
    return Track(acts + [end])


def ready(*names):
    pass


def advance(*sums):
    for one in sums:
        for act in one.take():
            act()


def drain(*sums):
    while any(one.acts for one in sums):
        advance(*sums)


def quarter(net):
    return 2 * net.c + net.c + net.m - 2 * net.c * net.m


def choose(slots, by_core, by_y):
    core = jnp.where(by_core, 1.0, 0.0)
    y = jnp.where(by_y, 1.0, 0.0)
    return (slots[0].astype(F32) * core + slots[1].astype(F32) * y).astype(BF)


def pick_next(net, slots):
    q = quarter(net)
    return choose(slots, q == 1, q % 2 == 0)


def pick_prev(net, slots):
    q = quarter(net)
    return choose(slots, q == 2, q % 2 == 1)


ROW_BIASES = ("c1b", "c2b", "n1g", "n1b", "oub", "n2g", "n2b", "dnb")


ORDERS = dict(
    down=("c-yx-zw", "c-xz-wy"),
    up=("c-z-x-y-w", "c-xz-w-y"),
    out=("c-zx-y-w",),
    qkv=("c-z-x-y-w", "c-xy-w-z", "c-z-x-y-w"),
    c2=("c-z-xy-w", "c-yx-w-z", "c-xy-w-z"),
    c1=("cy-xz-w",),
    vec=("z-w-c-x-y",),
)
SCHEDULE = dict(
    ff2=("down0", "up0"),
    ffo=("down0", "down1", "up0", "up1"),
    out=("down1", "up1", "out0"),
    pull1=("out0",),
    pull2=("down0", "up0"),
    pull6=("out0",),
    pull7=("down0", "down1", "up0", "up1"),
    pull8=("out0",),
    pull10=("up0",),
    pull11=("out0",),
    pull12=("down0", "down1", "up0", "up1"),
    pull13=("out0",),
    pull14=("down0", "down1", "up0", "up1"),
    pull15=("out0",),
    home=("down0",),
    qkvw1=("down1", "up0", "up1", "out0", "qkv1"),
    qkvw2=("qkv2",),
    c2=("down1", "qkv1", "qkv2"),
    c2w0=("c20",),
    c2w1=("c21",),
    c2w2=("up1", "c22"),
    qkvw0=("qkv0",),
    first=("up0", "c20", "c21"),
    c1=("up1", "qkv0", "qkv1", "qkv2", "c22"),
    c1w=("up0", "c10", "vec"),
    mel=("qkv1", "qkv2", "c20", "c21"),
    end=(
        "vec", "qkv0", "c22", "qkv1", "c10", "c21", "qkv2", "c20", "vec", "qkv0", "qkv1", "c10",
        "c22", "c21", "vec", "qkv2", "c20", "qkv0", "vec", "qkv1", "c10", "c22", "c21", "qkv2",
        "c20", "qkv0", "vec", "c10", "c22", "c21", "qkv0", "qkv1", "qkv2", "c20", "c22", "qkv1",
        "qkv0", "c10", "qkv2", "c21", "c20", "qkv0", "c22", "qkv2", "c21", "c20", "qkv0", "c22",
    ),
)


def orders(name, bits):
    dims = dict(c=["c"], y=["y"], x=[0], z=list(range(1, min(2, bits))), w=list(range(2, min(3, bits))))
    found = []
    for spec in ORDERS[name]:
        groups = [tuple(dim for ch in group for dim in dims[ch]) for group in spec.split("-")]
        found.append([group for group in groups if group] + [(dim,) for dim in range(3, bits)])
    return found


def partners(bits):
    found = [("c",), ("y",), ("c", "y")] + [(dim,) for dim in range(bits)]
    for name in ORDERS:
        for order in orders(name, bits):
            for dims in order:
                found += [one for one in subsets(dims) if set(one) not in [set(x) for x in found]]
    return found


def layer(r, bits):
    T, D = r.stream.shape
    half, F2 = D // 2, r.down_l.shape[0]
    side = F2 // D
    mels, span = r.w1.shape[1], 4 * T
    net = Net(r, bits)
    c, m = net.c, net.m
    sub = c + m - 2 * c * m
    rows_of_mine = rows16(sub * T, T)

    r.melbuf[...] = jnp.zeros_like(r.melbuf)
    mel_own = net.here(r.mel.at[0], r.melbuf.at[0:mels, 128 : 128 + span])
    qkv_own = net.here(r.wqkv_l, r.wqkv.at[m])
    w2_own = net.here(r.w2_l, r.w2)
    own = [
        net.here(r.wo_l.at[0 : D // 4], r.wo.at[rows16(m * (D // 4), D // 4)]),
        net.here(r.wo_l.at[D // 4 : half], r.wo.at[rows16(half + m * (D // 4), D // 4)]),
        net.here(r.up_l, r.up.at[m]),
        net.here(r.down_l, r.down.at[rows16(m * F2, F2)]),
        net.here(r.cot.at[0, rows_of_mine], r.bg),
    ]
    r.vec_mine[...] = jnp.zeros_like(r.vec_mine)
    own_lanes = pl.ds(pl.multiple_of(m * half, 128), half)
    r.vec_mine[0:2, own_lanes] = r.qkvb[...].astype(F32)
    for k in range(side):
        r.vec_mine[pl.ds(2 + m * side + k, 1), :] = r.upb[k * D : (k + 1) * D].astype(F32).reshape(1, D)
    for k, n in enumerate(ROW_BIASES):
        r.vecs[k : k + 1, :] = getattr(r, n)[...].astype(F32).reshape(1, D)
    net.greet(partners(bits))
    vec_copy = net.send(r.vec_mine, r.vec_got, "y")
    mel_own.wait()
    src = pl.ds(pl.multiple_of(128 + (1 - c) * (span - 128), 128), 128)
    dst = pl.ds(pl.multiple_of(c * (span + 128), 128), 128)
    mel_rim = net.send(r.melbuf.at[0:mels, src], r.melbuf.at[0:mels, dst], "c")
    p = 4 * c + 2 * net.bit(0) + net.bit(1) if bits > 1 else 2 * c + net.bit(0)
    cuts = 8 if bits > 1 else 4

    def pass_on(of, at, count, dim):
        def cut(n, base):
            return rows16(base + at * (n // cuts), count * (n // cuts))

        wo = rows16(c * half + of * (D // 4) + (at - c * (cuts // 2)) * (half // cuts), count * (half // cuts))
        parts = [r.wo.at[wo], r.up.at[of, cut(D, 0)], r.down.at[cut(F2, of * F2)]]
        return [net.copy(x, x, dim) for x in parts]

    def pass_qkv(of, at, count, dim):
        rows = r.wqkv.at[of, :, rows16(at * (D // 4), count * (D // 4))]
        return net.copy(rows, rows, dim)

    two = 2 if bits > 1 else 1
    qkv_y = pass_qkv(m, 2 * c + net.bit(0), 1, "y")
    qkv_x = pass_qkv(1 - m, 2 * c + net.bit(0), 1, 0)
    qkv_c = pass_qkv(1 - m, 2 * c, 2, "c")
    ff_y = pass_on(m, p, 1, "y")
    ff_z = pass_on(1 - m, p, 1, 1) if bits > 1 else []
    ff_x = pass_on(1 - m, (p // two) * two, two, 0)
    ff_c = pass_on(1 - m, c * (cuts // 2), cuts // 2, "c")
    qkv_own.wait()
    qkv_y.start()
    wait_all(own)
    r.small[...] = jnp.zeros_like(r.small)
    stage_mel_rows(r, sub, mel_rim.wait)
    stage_first(r, jnp.logical_and(c == 0, m == 0))
    qkv_y.wait()
    qkv_x.start()
    start_all(ff_y)
    stage_odd(r)
    w2_own.wait()
    stage_second(r, quarter(net))
    vec_copy.wait()
    r.vecs[8:16, :] = r.vec_mine[...] + r.vec_got[...]
    qkv_x.wait()
    qkv_c.start()
    wait_all(ff_y)
    start_all(ff_z)

    def block(slot, part, h):
        return r.kv.at[rows16((3 * slot + part) * half + h * (half // 2), half // 2)]

    def project(h):
        far, near = [], []
        for part in (1, 2, 0):
            stage_qkv(r, part, h)
            if part:
                far.append(net.send(block(3 + c, part, h), block(0, part, h), "y"))
                far.append(net.send(block(4 - c, part, h), block(1, part, h), "c", "y"))
            near.append(net.send(block(4 - c, part, h), block(2, part, h), "c"))
        return far, near

    far_own, near_own = project(m)
    stage_mask(r, sub)
    add_small(r, DNB, col(r.bg[...].astype(F32)))
    r.normedt[...] = r.normed[...].astype(F32).T.astype(BF)
    qkv_c.wait()
    far_other, near_other = project(1 - m)
    wait_all(near_own)
    heads = half // HEAD
    hooks = {
        heads: [lambda: wait_all(near_other), lambda: wait_all(ff_z), lambda: start_all(ff_x)],
        2 * heads: [lambda: wait_all(far_own)],
        3 * heads: [lambda: wait_all(far_other), lambda: wait_all(ff_x), lambda: start_all(ff_c)],
    }
    attend(r, c, m, hooks)
    attend_end(r, 1)
    mix_c = net.send(r.mixb.at[half:D], r.mix_got, "c")
    attend_end(r, 0)
    stage_mid(r, c, mix_c.wait, lambda: wait_all(ff_c))

    def summed(n, part, rows, halves):
        views = [
            getattr(r, "g_" + n).at[part * rows * halves : (part + 1) * rows * halves],
            getattr(r, "got_%s%d" % (n, part)),
            getattr(r, "done_" + n).at[part * rows : (part + 1) * rows],
        ]
        return bucket_sum(net, *views, halves, orders(n, bits)[part])

    def leave(n, part):
        done = getattr(r, "done_" + n)
        size = half if n == "qkv" else D
        rows = done if n in ("out", "c1") else done.at[part * size : (part + 1) * size]
        if n == "qkv":
            pairs = [(rows.at[:, j * half : (j + 1) * half], r.qkv_o.at[part, j * half : (j + 1) * half]) for j in range(2)]
        elif n == "up":
            pairs = [(rows, r.up_o.at[:, part * D : (part + 1) * D])]
        elif n in ("down", "c2"):
            pairs = [(rows, getattr(r, n + "_o").at[part * D : (part + 1) * D])]
        else:
            pairs = [(done, getattr(r, n + "_o"))]
        return [net.here_later(src, dst) for src, dst in pairs]

    tracks, leaving = {}, {}
    for n, rows, halves, parts in (
        ("down", D, 2, side),
        ("up", D, 2, side),
        ("out", half, 2, 1),
        ("qkv", half, 2, 3),
        ("c2", D, 1, 3),
        ("c1", r.g_c1.shape[0], 1, 1),
    ):
        for part in range(parts):
            name = "%s%d" % (n, part)
            tracks[name] = summed(n, part, rows, halves)
            leaving[name] = leave(n, part)
            tracks[name].then(functools.partial(start_all, leaving[name]))
    tracks["vec"] = small_sum(net, r.small, r.got_small, orders("vec", bits)[0])

    def acts_at(name):
        return [act for n in SCHEDULE.get(name, ()) if n in tracks for act in tracks[n].take()]

    def point(name):
        for act in acts_at(name):
            act()

    hooks = {}
    for step in range(2 * side):
        if step and step % 2 == 0:
            ready("down%d" % (step // 2 - 1), "up%d" % (step // 2 - 1))
        hooks[step] = acts_at("ff%d" % step)
    stage_ff(r, hooks)
    ready("down%d" % (side - 1), "up%d" % (side - 1))
    point("ffo")
    stage_mid_pull(r)
    enc = [
        net.copy(r.enc, r.enc_got, "y"),
        pltpu.make_async_copy(r.enc, r.enc_o.at[rows_of_mine], r.own.at[39]),
    ]
    start_all(enc)
    stage_do(r, c, False)
    do_c = net.send(r.dot_out, r.dot.at[half:D], "c")
    point("mid")
    stage_out_weights(r, c)
    ready("out0")
    point("out")
    stage_do(r, c, True)
    stage_diag(r, 0)
    do_c.wait()
    stage_diag(r, 1)
    both = half * 2
    home_y = net.copy(r.dkv.at[0:both], r.from_y, "y")
    home_d = net.copy(r.dkv.at[both : 2 * both], r.from_d, "c", "y")
    home_c = net.copy(r.dkv.at[2 * both : 3 * both], r.from_c.at[half:], "c")
    hooks = {}

    def at_step(step, *acts):
        hooks.setdefault(step * heads // 4, []).extend(acts)

    at_step(4, home_y.start)
    at_step(8, home_d.start)
    at_step(12, home_c.start)
    for step in range(16):
        at_step(step, *acts_at("pull%d" % step))
    attend_pull(r, c, hooks)
    r.dq_out[...] = (r.dqt[half:D, :] * HEAD**-0.5).astype(BF)
    dq_c = net.send(r.dq_out, r.from_c.at[0:half], "c")
    r.dsum[rows16(c * half, half), :] = (r.dqt[0:half, :] * HEAD**-0.5).astype(BF)
    point("home")
    home_y.wait()
    home_d.wait()
    home_c.wait()

    def total(i, carry):
        for part in range(2):
            rows = rows16(part * half + i * 32, 32)
            mine = r.dkv[rows16(3 * both + part * half + i * 32, 32), :].astype(F32) + r.from_y[rows, :].astype(F32)
            r.dsum[rows16((1 + part) * D + c * half + i * 32, 32), :] = mine.astype(BF)
            other = r.from_c[rows16((1 + part) * half + i * 32, 32), :].astype(F32) + r.from_d[rows, :].astype(F32)
            r.dsum[rows16((1 + part) * D + (1 - c) * half + i * 32, 32), :] = other.astype(BF)
        return carry

    lax.fori_loop(0, half // 32, total, 0)

    def queries_came():
        dq_c.wait()
        r.dsum[rows16((1 - c) * half, half), :] = r.from_c[0:half, :]

    for part in (1, 2):
        stage_qkv_weights(r, part)
        ready("qkv%d" % part)
        point("qkvw%d" % part)
    stage_qkv_pull(r, queries_came)
    point("norm")
    stage_norm_pull(r)
    rim = [net.send(r.sg.at[0:16], r.slots.at[0, i], dim) for i, dim in enumerate(("c", "y"))]
    point("c2")
    for part in range(3):
        stage_conv2_weights(r, part)
        ready("c2%d" % part)
        point("c2w%d" % part)
    stage_qkv_weights(r, 0)
    ready("qkv0")
    point("qkvw0")

    def next_row():
        wait_all(rim)
        return pick_next(net, r.slots.at[0])

    stage_conv2_pull(r, next_row)
    point("first")
    stage_first_pull(r)
    rim = [net.send(r.fe.at[0:16], r.slots.at[1, i], dim) for i, dim in enumerate(("c", "y"))]
    rim += [net.send(r.fo.at[T - 16 : T], r.slots.at[2, i], dim) for i, dim in enumerate(("c", "y"))]
    point("c1")
    stage_conv1_weights(r)
    ready("c10", "vec")
    point("c1w")
    wait_all(rim)
    stage_mel(r, pick_next(net, r.slots.at[1]), pick_prev(net, r.slots.at[2]))
    rows_of_yours = rows16((1 - sub) * T, T)
    mel_y = net.send(r.melg, r.melg_got, "y")
    point("mel")
    wait_all(enc)
    ends = [
        net.here(r.enc_got, r.enc_o.at[rows_of_yours]),
        net.here(r.melg, r.mel_o.at[rows_of_mine]),
    ]
    point("end")
    drain(*tracks.values())
    mel_y.wait()
    ends.append(net.here(r.melg_got, r.mel_o.at[rows_of_yours]))
    ends.append(net.here(r.small, r.small_o))
    wait_all(ends)
    for copies in leaving.values():
        wait_all(copies)


def run_layer(bits, near, far, outs, T, D, F2, lanes):
    half, H = D // 2, D // HEAD
    td, dt = (T, D), (D, T)
    buckets = dict(down=(D, 2, F2 // D), up=(D, 2, F2 // D), out=(half, 2, 1), qkv=(half, 2, 3), c2=(D, 1, 3), c1=(lanes, 1, 1))
    scratch = dict(
        melbuf=((128, 4 * T + 256), BF),
        mele=((T + 24, 128), F32),
        melo=((T + 24, 128), F32),
        xe=((T, 384), BF),
        xo=((T, 384), BF),
        w1p=((384, D), BF),
        w2=((3, D, D), BF),
        bg=(td, BF),
        wqkv=((2, 3, D, half), BF),
        wo=((D, D), BF),
        up=((2, D, F2), BF),
        down=((2 * F2, D), BF),
        vecs=((16, D), F32),
        vec_mine=((8, D), F32),
        vec_got=((8, D), F32),
        stream=(td, F32),
        he=(td, BF),
        ho=(td, BF),
        hp=(td, BF),
        dge=(td, F32),
        dgo=(td, F32),
        dg2=(td, F32),
        normed=(td, BF),
        kv=((15 * half, T), BF),
        mixt=(dt, F32),
        mixb=(dt, BF),
        normedt=(dt, BF),
        mix_got=((half, T), BF),
        dot=(dt, BF),
        dot_out=((half, T), BF),
        top=((H, 1, T), F32),
        total=((H, 1, T), F32),
        diag=((H, 1, T), F32),
        tmp=(td, F32),
        tmp2=(td, F32),
        shift=((T + 16, D), F32),
        wide=((T + 16, 128), F32),
        mid=(td, F32),
        ntwo=(td, BF),
        act=(td, BF),
        ing=(td, BF),
        ffo=(td, F32),
        ntg=(td, F32),
        attg=(td, BF),
        dqt=(dt, F32),
        dq_out=((half, T), BF),
        pb=((T, 2 * T), BF),
        ds=((T, 2 * T), BF),
        dkv=((8 * half, T), BF),
        from_y=((2 * half, T), BF),
        from_d=((2 * half, T), BF),
        from_c=((3 * half, T), BF),
        dsum=((3 * D, T), BF),
        enc_got=(td, BF),
        melg=((T, 256), BF),
        melg_got=((T, 256), BF),
        small=((16, D), F32),
        got_small=((sum(len(subsets(dims)) for dims in orders("vec", bits)[0]), 16, D), F32),
        slots=((3, 2, 16, D), BF),
    )
    alias = T == D
    for n, (rows, halves, parts) in buckets.items():
        if n not in ("qkv", "c2"):
            scratch["g_" + n] = ((rows * halves * parts, D), BF)
        for part in range(parts):
            need = sum_plan(rows, halves, orders(n, bits)[part])[1]
            scratch["got_%s%d" % (n, part)] = ((need, D), BF)
        scratch["done_" + n] = ((rows * parts, D), BF)
    if not alias:
        scratch.update(g_qkv=((6 * half, D), BF), g_c2=((6 * half, D), BF))
    names = list(near) + list(far) + list(outs) + list(scratch) + ["send", "recv", "own"]

    def kernel(*refs):
        r = Box()
        for n, ref in zip(names, refs):
            setattr(r, n, ref)
        r.odd, r.smg, r.sg, r.fe, r.fo, r.enc = r.shift, r.mid, r.ntwo, r.act, r.ing, r.bg
        if alias:
            r.g_qkv, r.g_c2 = r.kv.at[0 : 6 * half], r.kv.at[6 * half : 12 * half]
        layer(r, bits)

    vmem, anywhere = pl.BlockSpec(memory_space=pltpu.VMEM), pl.BlockSpec(memory_space=pl.ANY)
    got = pl.pallas_call(
        kernel,
        name="layer",
        out_shape=[jax.ShapeDtypeStruct(*o) for o in outs.values()],
        in_specs=[vmem] * len(near) + [anywhere] * len(far),
        out_specs=[anywhere] * len(outs),
        scratch_shapes=[pltpu.VMEM(*s) for s in scratch.values()]
        + [pltpu.SemaphoreType.DMA((256,)), pltpu.SemaphoreType.DMA((256,)), pltpu.SemaphoreType.DMA((40,))],
        compiler_params=pltpu.CompilerParams(
            vmem_limit_bytes=VMEM_LIMIT, collective_id=1, has_side_effects=True
        ),
    )(*near.values(), *far.values())
    return dict(zip(outs, got))


def run_finish(got, mels, side):
    T2, D = got["enc_o"].shape
    half = D // 2
    ins = list(got)
    outs = dict(
        enc=((1, T2, D), BF),
        mel=((1, mels, 2 * T2), F32),
        c1=((3, mels, D), F32),
        c2=((3, D, D), F32),
        qkv=((3, D, half), F32),
        qkvb=((2, half), F32),
        out=((half, D), F32),
        up=((D, side * D), F32),
        upb=((side * D,), F32),
        down=((side * D, D), F32),
    )
    outs.update({n: ((D,), F32) for n in ROW_BIASES})

    big = ("mel", "c1", "c2", "qkv", "out", "up", "down")
    names = ins + list(outs) + ["in_" + n for n in ins] + ["out_" + n for n in big] + ["came", "went"]

    def kernel(*refs):
        r = Box()
        for n, ref in zip(names, refs):
            setattr(r, n, ref)
        m = lax.axis_index("mp")
        order = ["small_o", "enc_o", "down_o", "up_o", "qkv_o", "c2_o", "mel_o", "out_o", "c1_o"]
        loads = {}
        for k, n in enumerate(order):
            loads[n] = pltpu.make_async_copy(getattr(r, n), getattr(r, "in_" + n), r.came.at[k])
            loads[n].start()
        went = []

        def leave(n):
            copy = pltpu.make_async_copy(getattr(r, "out_" + n), getattr(r, n), r.went.at[len(went)])
            copy.start()
            went.append(copy)

        def cast(src, dst):
            def one(rows):
                dst[rows, :] = src[rows, :].astype(dst.dtype)

            rows_loop(src.shape[0], 256, one)

        loads["small_o"].wait()
        for k, n in enumerate(ROW_BIASES):
            getattr(r, n)[...] = r.in_small_o[k : k + 1, :].reshape(D)
        r.qkvb[...] = r.in_small_o[QB : QB + 2, pl.ds(pl.multiple_of(m * half, 128), half)]
        for k in range(side):
            r.upb[k * D : (k + 1) * D] = r.in_small_o[pl.ds(UPB + m * side + k, 1), :].reshape(D)
        loads["enc_o"].wait()
        copy = pltpu.make_async_copy(r.in_enc_o, r.enc.at[0], r.went.at[len(big)])
        copy.start()
        for n in ("down", "up"):
            loads[n + "_o"].wait()
            cast(getattr(r, "in_" + n + "_o"), getattr(r, "out_" + n))
            leave(n)
        loads["qkv_o"].wait()
        for o in range(3):
            cast(r.in_qkv_o.at[o], r.out_qkv.at[o])
        leave("qkv")
        loads["c2_o"].wait()
        for o in range(3):
            cast(r.in_c2_o.at[o * D : (o + 1) * D], r.out_c2.at[o])
        leave("c2")
        row = lax.broadcasted_iota(jnp.int32, (128, 256), 0)
        lane = lax.broadcasted_iota(jnp.int32, (128, 256), 1)
        even = jnp.where(lane == 2 * row, 1.0, 0.0).astype(BF)
        odd = jnp.where(lane == 2 * row + 1, 1.0, 0.0).astype(BF)
        loads["mel_o"].wait()
        for k in range(T2 // 128):
            rows = slice(k * 128, (k + 1) * 128)
            value = tn(r.in_mel_o[rows, 0:128], even) + tn(r.in_mel_o[rows, 128:256], odd)
            r.out_mel[0, :, k * 256 : (k + 1) * 256] = value[0:mels, :]
        leave("mel")
        loads["out_o"].wait()
        cast(r.in_out_o, r.out_out)
        leave("out")
        loads["c1_o"].wait()
        for o in range(3):
            r.out_c1[o] = r.in_c1_o[o * mels : (o + 1) * mels, :].astype(F32)
        leave("c1")
        copy.wait()
        wait_all(went)

    vmem, anywhere = pl.BlockSpec(memory_space=pltpu.VMEM), pl.BlockSpec(memory_space=pl.ANY)
    done = pl.pallas_call(
        kernel,
        name="finish",
        out_shape=[jax.ShapeDtypeStruct(*o) for o in outs.values()],
        in_specs=[anywhere] * len(ins),
        out_specs=[anywhere if n in big + ("enc",) else vmem for n in outs],
        scratch_shapes=[pltpu.VMEM(got[n].shape, got[n].dtype) for n in ins]
        + [pltpu.VMEM(*outs[n]) for n in big]
        + [pltpu.SemaphoreType.DMA((len(ins),)), pltpu.SemaphoreType.DMA((len(big) + 1,))],
        compiler_params=pltpu.CompilerParams(vmem_limit_bytes=VMEM_LIMIT),
    )(*got.values())
    return dict(zip(outs, done))


def sine_tables(frames, channels, fine):
    half_width = channels // 2
    rate = np.exp(-(math.log(10000.0) / (half_width - 1)) * np.arange(half_width))
    small = np.arange(fine)[:, None] * rate[None, :]
    large = np.arange(0, frames, fine)[:, None] * rate[None, :]
    table = dict(fine_s=np.sin(small), fine_c=np.cos(small), coarse_s=np.sin(large), coarse_c=np.cos(large))
    return {n: jnp.asarray(t, F32) for n, t in table.items()}


def on_device(
    mel_input,
    conv1_weight,
    conv1_bias,
    conv2_weight,
    conv2_bias,
    norm1_gain,
    norm1_bias,
    qkv_weight,
    qkv_bias,
    out_weight,
    out_bias,
    norm2_gain,
    norm2_bias,
    up_weight,
    up_bias,
    down_weight,
    down_bias,
    cotangent,
    speech_mask,
):
    mels = mel_input.shape[1]
    T, D = cotangent.shape[1] // 2, cotangent.shape[2]
    F2 = up_weight.shape[1]
    side, half = F2 // D, D // 2
    bits = (lax.axis_size("dp") - 1).bit_length()
    lanes = -(-3 * mels // 128) * 128
    near = dict(
        w1=conv1_weight,
        mask=speech_mask,
        qkvb=qkv_bias,
        upb=up_bias,
        c1b=conv1_bias,
        c2b=conv2_bias,
        n1g=norm1_gain,
        n1b=norm1_bias,
        oub=out_bias,
        n2g=norm2_gain,
        n2b=norm2_bias,
        dnb=down_bias,
    )
    near.update(sine_tables(4 * T, D, 32))
    got = run_layer(
        bits,
        near,
        dict(
            mel=mel_input,
            cot=cotangent,
            w2_l=conv2_weight,
            wqkv_l=qkv_weight,
            wo_l=out_weight,
            up_l=up_weight,
            down_l=down_weight,
        ),
        dict(
            enc_o=((2 * T, D), BF),
            mel_o=((2 * T, 256), BF),
            down_o=((F2, D), BF),
            up_o=((D, F2), BF),
            out_o=((half, D), BF),
            qkv_o=((3, D, half), BF),
            c2_o=((3 * D, D), BF),
            c1_o=((lanes, D), BF),
            small_o=((16, D), F32),
        ),
        T,
        D,
        F2,
        lanes,
    )
    done = run_finish(got, mels, side)
    names = ("enc", "mel", "c1", "c1b", "c2", "c2b", "n1g", "n1b", "qkv", "qkvb")
    names += ("out", "oub", "n2g", "n2b", "up", "upb", "down", "dnb")
    return tuple(done[n] for n in names)


def solution(mesh):
    placed = (
        P("dp", None, "seq"),
        P(),
        P(),
        P(),
        P(),
        P(),
        P(),
        P(None, None, "mp"),
        P(None, "mp"),
        P("mp", None),
        P(),
        P(),
        P(),
        P(None, "mp"),
        P("mp"),
        P("mp", None),
        P(),
        P("dp", "seq", None),
        P("dp", "seq"),
    )
    return jax.shard_map(
        on_device,
        mesh=mesh,
        in_specs=placed,
        out_specs=(
            P("dp", "seq", None),
            P("dp", None, "seq"),
            P(),
            P(),
            P(),
            P(),
            P(),
            P(),
            P(None, None, "mp"),
            P(None, "mp"),
            P("mp", None),
            P(),
            P(),
            P(),
            P(None, "mp"),
            P("mp"),
            P("mp", None),
            P(),
        ),
        check_vma=False,
    )
```

```python
import functools
import math

import jax
import jax.numpy as jnp
import numpy as np
from jax import lax
from jax.experimental import pallas as pl
from jax.experimental.pallas import tpu as pltpu
from jax.sharding import PartitionSpec as P

HEAD = 64
BF = jnp.bfloat16
F32 = jnp.float32
MESH = pl.DeviceIdType.MESH
VMEM_LIMIT = 62 * 1024 * 1024
C1B, C2B, N1G, N1B, OUB, N2G, N2B, DNB, QB, VB, UPB = range(11)


class Box:
    pass


def dot(a, b, ca, cb):
    return lax.dot_general(a, b, (((ca,), (cb,)), ((), ())), preferred_element_type=F32)


def nn(a, b):
    return dot(a, b, 1, 0)


def nt(a, b):
    return dot(a, b, 1, 1)


def tn(a, b):
    return dot(a, b, 0, 0)


def flip(value):
    return value.astype(F32).T.astype(BF)


def rows_loop(total, step, body, unroll=2):
    step = min(step, total)

    def one(i, carry):
        body(pl.ds(pl.multiple_of(i * step, step), step))
        return carry

    lax.fori_loop(0, total // step, one, 0, unroll=min(unroll, total // step))


def gelu_parts(v):
    t = 1.0 / (1.0 + (0.3275911 / math.sqrt(2.0)) * jnp.abs(v))
    e = jnp.exp(-0.5 * v * v)
    poly = 1.061405429 * t - 1.453152027
    poly = poly * t + 1.421413741
    poly = poly * t - 0.284496736
    poly = poly * t + 0.254829592
    tail = (0.5 * t) * poly * e
    return jnp.where(v >= 0, 1.0 - tail, tail), e * (1.0 / math.sqrt(2.0 * math.pi))


def gelu_both(v):
    cdf, pdf = gelu_parts(v)
    return v * cdf, cdf + v * pdf


def normal(x):
    center = x - jnp.mean(x, axis=-1, keepdims=True)
    spread = jnp.mean(center * center, axis=-1, keepdims=True)
    inv = lax.rsqrt(spread + 1e-05)
    return center * inv, inv


def normal_pull(gy, hat, inv):
    return inv * (
        gy
        - jnp.mean(gy, axis=-1, keepdims=True)
        - hat * jnp.mean(gy * hat, axis=-1, keepdims=True)
    )


def vec(r, i):
    return r.vecs[i : i + 1, :]


def add_small(r, i, value):
    r.small[i : i + 1, :] += value


def col(value):
    return jnp.sum(value, axis=0, keepdims=True)


def stage_mel_rows(r, sub, rim_came):
    T, D = r.stream.shape
    row = lax.broadcasted_iota(jnp.int32, (256, 256), 0)
    lane = lax.broadcasted_iota(jnp.int32, (256, 256), 1)
    pick = jnp.where(lane == 2 * (row % 128) + row // 128, 1.0, 0.0).astype(BF)
    base = sub * 2 * T

    def lanes(start, size):
        return r.melbuf[:, pl.ds(pl.multiple_of(base + start, 128), size)]

    row = lax.broadcasted_iota(jnp.int32, (16, 128), 0)
    lane = lax.broadcasted_iota(jnp.int32, (16, 128), 1)

    def select(at, to):
        return jnp.where(jnp.logical_and(row == to, lane == at), 1.0, 0.0).astype(BF)

    for k in range(T // 128):
        both = nt(pick, lanes(128 + 256 * k, 256))
        r.mele[8 + 128 * k : 136 + 128 * k, :] = both[0:128, :]
        r.melo[8 + 128 * k : 136 + 128 * k, :] = both[128:256, :]
    rim_came()
    before, after = lanes(0, 128), lanes(128 + 2 * T, 128)
    r.mele[0:8, :] = nt(select(126, 7), before)[0:8, :]
    r.melo[0:8, :] = nt(select(127, 7), before)[0:8, :]
    r.mele[T + 8 : T + 16, :] = nt(select(0, 0), after)[0:8, :]


def three(a, b, c):
    return jnp.concatenate([a, b, c], axis=1).astype(BF)


def stage_first(r, first):
    T, D = r.stream.shape
    for o in range(3):
        r.w1p[128 * o : 128 * o + r.w1.shape[1], :] = r.w1[o]
        r.w1p[128 * o + r.w1.shape[1] : 128 * (o + 1), :] = jnp.zeros((128 - r.w1.shape[1], D), BF)
    w1 = r.w1p[...]
    edge = nn(three(r.mele[0:16, :], r.melo[0:16, :], r.mele[1:17, :]), w1) + vec(r, C1B)
    edge = gelu_both(edge)[0] * jnp.where(first, 0.0, 1.0)
    r.odd[0:8, :] = edge[0:8, :]
    r.xe[...] = three(r.melo[7 : 7 + T, :], r.mele[8 : 8 + T, :], r.melo[8 : 8 + T, :])
    r.xo[...] = three(r.mele[8 : 8 + T, :], r.melo[8 : 8 + T, :], r.mele[9 : 9 + T, :])
    r.tmp[...] = nn(r.xe[...], w1)

    def even(rows):
        value, slope = gelu_both(r.tmp[rows, :] + vec(r, C1B))
        r.he[rows, :] = value.astype(BF)
        r.dge[rows, :] = slope

    rows_loop(T, 32, even)


def stage_odd(r):
    T, D = r.stream.shape
    r.tmp[...] = nn(r.xo[...], r.w1p[...])

    def odd(rows):
        value, slope = gelu_both(r.tmp[rows, :] + vec(r, C1B))
        r.ho[rows, :] = value.astype(BF)
        r.odd[pl.ds(pl.multiple_of(rows.start + 8, 8), rows.size), :] = value
        r.dgo[rows, :] = slope

    rows_loop(T, 32, odd)


def stage_second(r, place):
    T, D = r.stream.shape
    r.hp[...] = r.odd[7 : 7 + T, :].astype(BF)
    r.tmp[...] = nn(r.hp[...], r.w2[0]) + nn(r.he[...], r.w2[1]) + nn(r.ho[...], r.w2[2])
    fine = r.fine_s.shape[0]

    def second(rows):
        value, slope = gelu_both(r.tmp[rows, :] + vec(r, C2B))
        at = place * (T // fine) + rows.start // fine
        s0, c0 = r.coarse_s[pl.ds(at, 1), :], r.coarse_c[pl.ds(at, 1), :]
        s1, c1 = r.fine_s[...], r.fine_c[...]
        stream = value + jnp.concatenate([s0 * c1 + c0 * s1, c0 * c1 - s0 * s1], axis=1)
        r.dg2[rows, :] = slope
        r.stream[rows, :] = stream
        r.normed[rows, :] = (normal(stream)[0] * vec(r, N1G) + vec(r, N1B)).astype(BF)

    rows_loop(T, fine, second)


def stage_mask(r, sub):
    T, D = r.stream.shape
    row = r.mask[0:1, pl.ds(pl.multiple_of(sub * T, 128), T)].astype(F32)
    r.wide[0:T, :] = jnp.broadcast_to(row, (128, T)).T

    def one(rows):
        keep = r.wide[rows, :]
        keep = jnp.concatenate([keep] * (D // 128), axis=1)
        r.bg[rows, :] = (r.bg[rows, :].astype(F32) * keep).astype(BF)

    rows_loop(T, 32, one)


def stage_qkv(r, part, h):
    T, D = r.stream.shape
    half, qr = D // 2, D // 4
    bias, scale = ((QB, HEAD**-0.5), (None, 1.0), (VB, 1.0))[part]
    value = nn(r.normed[...], r.wqkv[h, part])
    if bias is not None:
        value = value + r.vecs[bias : bias + 1, pl.ds(pl.multiple_of(h * half, half), half)]
    value = (value.astype(BF).astype(F32) * scale).T.astype(BF)
    for k in range(2):
        r.kv[rows16((3 * (3 + k) + part) * half + h * qr, qr), :] = value[k * qr : (k + 1) * qr, :]


def at_head(start, h):
    return pl.ds(pl.multiple_of(start + h * HEAD, HEAD), HEAD)


def head_loop(steps, hooks, body):
    def one(step, carry):
        for at, todo in hooks.items():
            if not todo:
                continue

            @pl.when(step == at)
            def _(todo=todo):
                for act in todo:
                    act()

        body(step)
        return carry

    lax.fori_loop(0, steps, one, 0)


def attend(r, c, m, hooks):
    S, T = r.kv.shape[0] // 15, r.kv.shape[1]
    heads = S // HEAD
    r.top[...] = jnp.full(r.top.shape, -jnp.inf, F32)
    r.total[...] = jnp.zeros(r.total.shape, F32)
    r.mixt[...] = jnp.zeros(r.mixt.shape, F32)

    def body(step):
        quarter, u, pair = step // heads, step % heads, heads // 2
        g = 2 * (quarter // 2) + u // pair
        h = (m + (1 - 2 * m) * ((quarter + 1) // 2 % 2)) * pair + u % pair
        own = (3 - g) // 3
        slot = own * (3 + c) + (1 - own) * ((g + 1) % 3)
        k = r.kv[at_head((3 * slot + 1) * S, h), :]
        v = r.kv[at_head((3 * slot + 2) * S, h), :]
        for i, home in enumerate((3 + c, 2)):
            q = r.kv[at_head(3 * home * S, h), :]
            s = tn(k, q)
            before = r.top[i * heads + h]
            top = jnp.maximum(before, jnp.max(s, axis=0, keepdims=True))
            p = jnp.exp(s - top)
            keep = jnp.exp(before - top)
            rows = at_head(i * S, h)
            r.top[i * heads + h] = top
            r.total[i * heads + h] = keep * r.total[i * heads + h] + jnp.sum(p, axis=0, keepdims=True)
            r.mixt[rows, :] = keep * r.mixt[rows, :] + nn(v, p.astype(BF))

    head_loop(4 * heads, hooks, body)


def attend_end(r, i):
    S = r.kv.shape[0] // 15
    heads = S // HEAD

    def one(h, carry):
        rows = at_head(i * S, h)
        total = r.total[i * heads + h]
        value = r.mixt[rows, :] * (1.0 / total)
        r.mixt[rows, :] = value
        r.mixb[rows, :] = value.astype(BF)
        r.top[i * heads + h] = r.top[i * heads + h] + jnp.log(total)
        return carry

    lax.fori_loop(0, heads, one, 0)


def stage_mid(r, c, mix_came, weights_came):
    T, D = r.stream.shape
    half = D // 2
    weights_came()
    r.tmp[...] = tn(r.mixb[0:half, :], r.wo[rows16(c * half, half), :])
    mix_came()
    r.tmp[...] += tn(r.mix_got[...], r.wo[rows16((1 - c) * half, half), :])

    def one(rows):
        mid = r.stream[rows, :] + r.tmp[rows, :] + vec(r, OUB)
        r.mid[rows, :] = mid
        r.ntwo[rows, :] = (normal(mid)[0] * vec(r, N2G) + vec(r, N2B)).astype(BF)

    rows_loop(T, 32, one)


def stage_ff(r, hooks):
    T, D = r.stream.shape
    side = r.up.shape[2] // D
    parts, width = 2 * side, D

    def chunk(t):
        into, at = t % 2, t // 2
        j = into * side + at
        up = r.up[into, :, pl.ds(pl.multiple_of(at * D, D), D)]
        down = r.down[pl.ds(pl.multiple_of(j * D, D), D), :]
        r.tmp[...] = nn(r.ntwo[...], up)
        r.tmp2[...] = nt(r.bg[...], down)
        bias = r.vecs[pl.ds(UPB + j, 1), :]

        def one(i, acc):
            rows = pl.ds(pl.multiple_of(i * 32, 32), 32)
            value, slope = gelu_both(r.tmp[rows, :] + bias)
            r.act[rows, :] = value.astype(BF)
            grad = (r.tmp2[rows, :] * slope).astype(BF)
            r.ing[rows, :] = grad
            return acc + col(grad.astype(F32))

        r.small[pl.ds(UPB + j, 1), :] = lax.fori_loop(0, T // 32, one, jnp.zeros((1, width), F32), unroll=2)
        act = r.act[...]
        ing = r.ing[...]
        out = nn(act, down)
        back = nt(ing, up)

        r.ffo[...] += out
        r.ntg[...] += back
        rows = pl.ds(pl.multiple_of(t * D, D), D)
        r.g_down[rows, :] = tn(act, r.bg[...]).astype(BF)
        r.g_up[rows, :] = nn(r.ntwot[...], ing).astype(BF)

    r.ntwot[...] = flip(r.ntwo[...])
    r.ffo[...] = jnp.zeros_like(r.ffo)
    r.ntg[...] = jnp.zeros_like(r.ntg)
    head_loop(parts, hooks, chunk)


def stage_mid_pull(r):
    T, D = r.stream.shape

    def one(i, accs):
        rows = pl.ds(pl.multiple_of(i * 32, 32), 32)
        mid = r.mid[rows, :]
        enc = (mid + r.ffo[rows, :] + vec(r, DNB)).astype(BF)
        hat, inv = normal(mid)
        grad = r.ntg[rows, :]
        smg = r.bg[rows, :].astype(F32) + normal_pull(grad * vec(r, N2G), hat, inv)
        r.enc[rows, :] = enc
        r.smg[rows, :] = smg
        attg = smg.astype(BF)
        r.attg[rows, :] = attg
        return accs[0] + col(grad * hat), accs[1] + col(grad), accs[2] + col(attg.astype(F32))

    zero = jnp.zeros((1, D), F32)
    gain, bias, out_bias = lax.fori_loop(0, T // 32, one, (zero, zero, zero), unroll=2)
    add_small(r, N2G, gain)
    add_small(r, N2B, bias)
    add_small(r, OUB, out_bias)


def stage_do(r, c, own):
    half = r.attg.shape[1] // 2
    k = c if own else 1 - c
    value = nt(r.wo[rows16(k * half, half), :], r.attg[...]).astype(BF)
    if own:
        r.dot[0:half, :] = value
    else:
        r.dot_out[...] = value


def stage_out_weights(r, c):
    D = r.attg.shape[1]
    half, qr = D // 2, D // 4
    for k, mix in ((c, r.mixb[0:half, :]), (1 - c, r.mix_got[...])):
        value = nn(mix, r.attg[...]).astype(BF)
        for h in range(2):
            r.g_out[rows16(h * half + k * qr, qr), :] = value[h * qr : (h + 1) * qr, :]


def stage_diag(r, i):
    S = r.kv.shape[0] // 15
    heads = S // HEAD

    def one(h, carry):
        rows = at_head(i * S, h)
        value = r.dot[rows, :].astype(F32) * r.mixt[rows, :]
        r.diag[i * heads + h] = jnp.sum(value, axis=0, keepdims=True)
        return carry

    lax.fori_loop(0, heads, one, 0)


def attend_pull(r, c, hooks):
    S, T = r.kv.shape[0] // 15, r.kv.shape[1]
    heads = S // HEAD
    r.dqt[...] = jnp.zeros(r.dqt.shape, F32)

    def body(step):
        g, h = step // heads, step % heads
        slot = g + (g // 3) * c
        k = r.kv[at_head((3 * slot + 1) * S, h), :]
        v = r.kv[at_head((3 * slot + 2) * S, h), :]
        qs = [r.kv[at_head(3 * home * S, h), :] for home in (3 + c, 2)]
        dos = [r.dot[at_head(i * S, h), :] for i in range(2)]
        for i in range(2):
            top, diag = r.top[i * heads + h], r.diag[i * heads + h]
            for at in range(0, T, 128):
                rows, cols = slice(at, at + 128), slice(i * T, (i + 1) * T)
                p = jnp.exp(tn(k[:, rows], qs[i]) - top)
                r.pb[rows, cols] = p.astype(BF)
                r.ds[rows, cols] = (p * (tn(v[:, rows], dos[i]) - diag)).astype(BF)
        both = [jnp.concatenate(one, axis=1) for one in (qs, dos)]
        r.dkv[at_head(2 * g * S, h), :] = nt(both[0], r.ds[...]).astype(BF)
        r.dkv[at_head((2 * g + 1) * S, h), :] = nt(both[1], r.pb[...]).astype(BF)
        dq = nn(k, r.ds[...])
        for i in range(2):
            r.dqt[at_head(i * S, h), :] += dq[:, i * T : (i + 1) * T]

    head_loop(4 * heads, hooks, body)


def piece_of(r, part, h):
    D, qr = r.attg.shape[1], r.attg.shape[1] // 4
    at = part * D + h * qr
    return jnp.concatenate([r.dsum[at : at + qr, :], r.dsum[at + 2 * qr : at + 3 * qr, :]], axis=0)


def stage_qkv_weights(r, part):
    T, D = r.stream.shape
    half = D // 2
    ones = jnp.ones((8, T), BF)
    for h in range(2):
        piece = piece_of(r, part, h)
        if part != 1:
            row = QB if part == 0 else VB
            r.small[row : row + 1, h * half : (h + 1) * half] = nt(ones, piece)[0:1, :]
        grad = nt(r.normedt[...], piece).astype(BF)
        at = (2 * part + h) * half
        r.g_qkv[at : at + half, 0:half] = grad[0:half, :]
        r.g_qkv[at : at + half, half:D] = grad[half:D, :]


def stage_qkv_pull(r, queries_came):
    T, D = r.stream.shape
    total = None
    for part in (1, 2, 0):
        if part == 0:
            queries_came()
        for h in range(2):
            back = nn(r.wqkv[h, part], piece_of(r, part, h))
            total = back if total is None else total + back
    r.tmp[...] = total.T


def stage_norm_pull(r):
    T, D = r.stream.shape

    def one(i, accs):
        rows = pl.ds(pl.multiple_of(i * 32, 32), 32)
        hat, inv = normal(r.stream[rows, :])
        grad = r.tmp[rows, :]
        back = r.smg[rows, :] + normal_pull(grad * vec(r, N1G), hat, inv)
        sg = (back * r.dg2[rows, :]).astype(BF)
        r.sg[rows, :] = sg
        return accs[0] + col(grad * hat), accs[1] + col(grad), accs[2] + col(sg.astype(F32))

    zero = jnp.zeros((1, D), F32)
    gain, bias, c2b = lax.fori_loop(0, T // 32, one, (zero, zero, zero), unroll=2)
    add_small(r, N1G, gain)
    add_small(r, N1B, bias)
    add_small(r, C2B, c2b)


def stage_conv2_pull(r, next_row):
    T, D = r.stream.shape
    sg = r.sg[...]
    r.shift[0:T, :] = nt(sg, r.w2[0])
    r.tmp[...] = nt(sg, r.w2[1])
    r.shift[T : T + 16, :] = nt(next_row(), r.w2[0])
    r.tmp2[...] = nt(sg, r.w2[2]) + r.shift[1 : T + 1, :]


def stage_first_pull(r):
    T, D = r.stream.shape

    def one(i, acc):
        rows = pl.ds(pl.multiple_of(i * 32, 32), 32)
        even = (r.tmp[rows, :] * r.dge[rows, :]).astype(BF)
        odd = (r.tmp2[rows, :] * r.dgo[rows, :]).astype(BF)
        r.fe[rows, :] = even
        r.fo[rows, :] = odd
        return acc + col(even.astype(F32)) + col(odd.astype(F32))

    add_small(r, C1B, lax.fori_loop(0, T // 32, one, jnp.zeros((1, D), F32), unroll=2))


def stage_conv2_weights(r, i):
    D = r.stream.shape[1]
    r.g_c2[i * D : (i + 1) * D, :] = nn(r.tapt[i][...], r.sg[...]).astype(BF)


def stage_conv1_weights(r):
    value = (tn(r.xe[...], r.fe[...]) + tn(r.xo[...], r.fo[...])).astype(BF)
    mels = r.w1.shape[1]
    for o in range(3):
        r.g_c1[mels * o : mels * (o + 1), :] = value[128 * o : 128 * o + mels, :]
    r.g_c1[3 * mels :, :] = jnp.zeros((r.g_c1.shape[0] - 3 * mels, r.g_c1.shape[1]), BF)


def stage_mel(r, next_row, prev_row):
    T, D = r.stream.shape
    fe, fo = r.fe[...], r.fo[...]
    w = [r.w1p[128 * o : 128 * (o + 1), :] for o in range(3)]
    r.wide[16 : 16 + T, :] = nt(fo, w[2])
    r.wide[0:16, :] = nt(prev_row, w[2])
    r.melg[:, 0:128] = (nt(fe, w[1]) + nt(fo, w[0]) + r.wide[15 : 15 + T, :]).astype(BF)
    r.wide[0:T, :] = nt(fe, w[0])
    r.wide[T : T + 16, :] = nt(next_row, w[0])
    r.melg[:, 128:256] = (nt(fe, w[2]) + nt(fo, w[1]) + r.wide[1 : 1 + T, :]).astype(BF)


class Net:
    def __init__(self, r, bits):
        self.r, self.bits, self.used, self.used_here = r, bits, 0, 0
        self.d, self.c, self.m = (lax.axis_index(n) for n in ("dp", "seq", "mp"))

    def bit(self, dim):
        if dim == "c":
            return self.c
        if dim == "y":
            return self.m
        return (self.d // (1 << dim)) % 2

    def peer(self, dims):
        d = self.d
        for k in dims:
            if k not in ("c", "y"):
                d = d + (1 << k) - 2 * (1 << k) * self.bit(k)
        return (
            d,
            1 - self.c if "c" in dims else self.c,
            1 - self.m if "y" in dims else self.m,
        )

    def greet(self, partners):
        barrier = pltpu.get_barrier_semaphore()
        for dims in partners:
            pl.semaphore_signal(barrier, inc=1, device_id=self.peer(dims), device_id_type=MESH)
        pl.semaphore_wait(barrier, len(partners))

    def copy(self, src, dst, *dims):
        i = self.used
        self.used += 1
        return pltpu.make_async_remote_copy(
            src_ref=src,
            dst_ref=dst,
            send_sem=self.r.send.at[i],
            recv_sem=self.r.recv.at[i],
            device_id=self.peer(dims),
            device_id_type=MESH,
        )

    def send(self, src, dst, *dims):
        copy = self.copy(src, dst, *dims)
        copy.start()
        return copy

    def here_later(self, src, dst):
        i = self.used_here
        self.used_here += 1
        return pltpu.make_async_copy(src, dst, self.r.own.at[i])

    def here(self, src, dst):
        copy = self.here_later(src, dst)
        copy.start()
        return copy


def start_all(copies):
    for copy in copies:
        copy.start()


def wait_all(copies):
    for copy in copies:
        copy.wait()


def rows16(start, size):
    return pl.ds(pl.multiple_of(start, 16), size)


def subsets(dims):
    found = [()]
    for dim in dims:
        found += [one + (dim,) for one in found]
    return found[1:]


def sum_plan(rows, halves, order):
    steps, need = [], 0
    for dims in order:
        by_half = halves == 2 and "y" in dims
        cutting = [dim for dim in dims if not (by_half and dim == "y")]
        if rows % (16 << len(cutting)):
            cutting = []
        rows >>= len(cutting)
        if by_half:
            halves = 1
        steps.append((dims, cutting, rows, halves, by_half))
        need += rows * halves * len(subsets(dims))
    return steps, need


class Track:
    def __init__(self, acts):
        self.acts = list(acts)

    def take(self):
        return [self.acts.pop(0)] if self.acts else []

    def then(self, more):
        last = self.acts.pop()

        def act():
            last()
            more()

        self.acts.append(act)


def bucket_sum(net, g, got, done, halves, order):
    R = g.shape[0] // halves
    lo, rows, at, bases = 0, R, 0, [h * R for h in range(halves)]
    acts, back, end = [], [], None

    def start_after(end, copies):
        def act():
            if end is not None:
                end()
            for copy in copies:
                copy.start()

        return act

    def adder(copies, places, n):
        step = 64 if n % 64 == 0 else 32 if n % 32 == 0 else 16

        def end():
            wait_all(copies)
            for to, ofs in places:

                def add(k, carry, to=to, ofs=ofs):
                    mine = rows16(to + k * step, step)
                    value = g[mine, :].astype(F32)
                    for of in ofs:
                        value = value + got[rows16(of + k * step, step), :].astype(F32)
                    g[mine, :] = value.astype(BF)
                    return carry

                lax.fori_loop(0, n // step, add, 0)

        return end

    for dims, cutting, n, _, by_half in sum_plan(R, halves, order)[0]:

        def part_of(other):
            start = lo
            for i, dim in enumerate(reversed(cutting)):
                b = net.bit(dim)
                start = start + (1 - b if dim in other else b) * (n << i)
            return start

        keep = part_of(())
        if by_half:
            bases = [net.m * R]
        copies, ofs = [], [[] for _ in bases]
        for other in subsets(dims):
            sources = [(1 - net.m) * R] if by_half and "y" in other else bases
            for i, base in enumerate(sources):
                src = g.at[rows16(base + part_of(other), n)]
                copies.append(net.copy(src, got.at[rows16(at, n)], *other))
                ofs[i].append(at)
                at += n
        acts.append(start_after(end, copies))
        end = adder(copies, [(base + keep, of) for base, of in zip(bases, ofs)], n)
        if cutting:
            back.append((cutting, n, lo))
        lo, rows = keep, n

    def settle(end=end, lo=lo, base=bases[0], rows=rows):
        end()
        for k in range(rows // 16):
            done[rows16(lo + 16 * k, 16), :] = g[rows16(base + lo + 16 * k, 16), :]

    end = settle
    for cutting, n, before in reversed(back):
        part = rows16(lo, n)
        copies = [net.copy(done.at[part], done.at[part], *other) for other in subsets(cutting)]
        acts.append(start_after(end, copies))
        end = functools.partial(wait_all, copies)
        lo = before
    return Track(acts + [end])


def small_sum(net, value, slots, order):
    acts, end, at = [], None, 0
    for dims in order:
        copies = [net.copy(value, slots.at[at + i], *other) for i, other in enumerate(subsets(dims))]

        def act(end=end, copies=copies):
            if end is not None:
                end()
            start_all(copies)

        def end(copies=copies, at=at):
            wait_all(copies)
            total = value[...]
            for i in range(len(copies)):
                total = total + slots[at + i]
            value[...] = total

        at += len(copies)
        acts.append(act)
    return Track(acts + [end])


def ready(*names):
    pass


def advance(*sums):
    for one in sums:
        for act in one.take():
            act()


def drain(*sums):
    while any(one.acts for one in sums):
        advance(*sums)


def quarter(net):
    return 2 * net.c + net.c + net.m - 2 * net.c * net.m


def choose(slots, by_core, by_y):
    core = jnp.where(by_core, 1.0, 0.0)
    y = jnp.where(by_y, 1.0, 0.0)
    return (slots[0].astype(F32) * core + slots[1].astype(F32) * y).astype(BF)


def pick_next(net, slots):
    q = quarter(net)
    return choose(slots, q == 1, q % 2 == 0)


def pick_prev(net, slots):
    q = quarter(net)
    return choose(slots, q == 2, q % 2 == 1)


ROW_BIASES = ("c1b", "c2b", "n1g", "n1b", "oub", "n2g", "n2b", "dnb")


ORDERS = dict(
    down=("c-xy-z-w", "c-zx-yw"),
    up=("c-xz-w-y", "c-zx-y-w"),
    out=("c-yw-xz",),
    qkv=("c-z-xy-w", "c-z-w-y-x", "x-c-z-y-w"),
    c2=("c-z-xy-w", "c-xy-z-w", "c-yx-w-z"),
    c1=("cy-xz-w",),
    vec=("c-w-xy-z",),
)
TRACKS = (
    ("down", 0), ("down", 1), ("up", 0), ("up", 1), ("out", 0), ("qkv", 0), ("qkv", 1), ("qkv", 2),
    ("c2", 0), ("c2", 1), ("c2", 2), ("c1", 0), ("vec", 0),
)
SCHEDULE = dict(
    ff2=(0, 2),
    ffo=(0, 1, 2, 3),
    out=(1, 3, 4),
    pull1=(4,),
    pull3=(2,),
    pull6=(0, 1),
    pull7=(2, 3, 4),
    pull8=(1,),
    pull9=(0, 2, 4),
    pull10=(1, 3),
    pull11=(0, 2, 4),
    pull12=(3,),
    pull14=(0, 1),
    pull15=(2, 3, 4),
    home=(0, 1),
    qkvw1=(2, 4, 6),
    qkvw2=(3, 7),
    c2=(0, 3, 6),
    c2w0=(8,),
    c2w1=(9,),
    c2w2=(10,),
    qkvw0=(5,),
    first=(0, 7, 8, 9, 10),
    c1=(5, 6, 7),
    c1w=(11, 12),
    mel=(8, 12),
    end=(
        9, 10, 6, 7, 11, 5, 8, 12, 9, 11, 10, 6, 7, 5, 8, 9, 12, 6, 11, 10, 7, 5, 8, 9, 6, 12,
        11, 10, 7, 5, 8, 9, 6, 5, 10, 7, 11, 7, 9, 6, 8, 5, 10, 9, 6, 5, 8, 7, 10,
    ),
)


def orders(name, bits):
    dims = dict(c=["c"], y=["y"], x=[0], z=list(range(1, min(2, bits))), w=list(range(2, min(3, bits))))
    found = []
    for spec in ORDERS[name]:
        groups = [tuple(dim for ch in group for dim in dims[ch]) for group in spec.split("-")]
        found.append([group for group in groups if group] + [(dim,) for dim in range(3, bits)])
    return found


def partners(bits):
    found = [("c",), ("y",), ("c", "y")] + [(dim,) for dim in range(bits)]
    for name in ORDERS:
        for order in orders(name, bits):
            for dims in order:
                found += [one for one in subsets(dims) if set(one) not in [set(x) for x in found]]
    return found


def layer(r, bits):
    T, D = r.stream.shape
    half, F2 = D // 2, r.down_l.shape[0]
    side = F2 // D
    mels, span = r.w1.shape[1], 4 * T
    net = Net(r, bits)
    c, m = net.c, net.m
    sub = c + m - 2 * c * m
    rows_of_mine = rows16(sub * T, T)

    r.melbuf[...] = jnp.zeros_like(r.melbuf)
    mel_own = net.here(r.mel.at[0], r.melbuf.at[0:mels, 128 : 128 + span])
    qkv_own = net.here(r.wqkv_l, r.wqkv.at[m])
    w2_own = net.here(r.w2_l, r.w2)
    own = [
        net.here(r.wo_l.at[0 : D // 4], r.wo.at[rows16(m * (D // 4), D // 4)]),
        net.here(r.wo_l.at[D // 4 : half], r.wo.at[rows16(half + m * (D // 4), D // 4)]),
        net.here(r.up_l, r.up.at[m]),
        net.here(r.down_l, r.down.at[rows16(m * F2, F2)]),
        net.here(r.cot.at[0, rows_of_mine], r.bg),
    ]
    r.vec_mine[...] = jnp.zeros_like(r.vec_mine)
    own_lanes = pl.ds(pl.multiple_of(m * half, 128), half)
    r.vec_mine[0:2, own_lanes] = r.qkvb[...].astype(F32)
    for k in range(side):
        r.vec_mine[pl.ds(2 + m * side + k, 1), :] = r.upb[k * D : (k + 1) * D].astype(F32).reshape(1, D)
    for k, n in enumerate(ROW_BIASES):
        r.vecs[k : k + 1, :] = getattr(r, n)[...].astype(F32).reshape(1, D)
    net.greet(partners(bits))
    vec_copy = net.send(r.vec_mine, r.vec_got, "y")
    mel_own.wait()
    src = pl.ds(pl.multiple_of(128 + (1 - c) * (span - 128), 128), 128)
    dst = pl.ds(pl.multiple_of(c * (span + 128), 128), 128)
    mel_rim = net.send(r.melbuf.at[0:mels, src], r.melbuf.at[0:mels, dst], "c")
    p = 4 * c + 2 * net.bit(0) + net.bit(1) if bits > 1 else 2 * c + net.bit(0)
    cuts = 8 if bits > 1 else 4

    def pass_on(of, at, count, dim):
        def cut(n, base):
            return rows16(base + at * (n // cuts), count * (n // cuts))

        wo = rows16(c * half + of * (D // 4) + (at - c * (cuts // 2)) * (half // cuts), count * (half // cuts))
        parts = [r.wo.at[wo], r.up.at[of, cut(D, 0)], r.down.at[cut(F2, of * F2)]]
        return [net.copy(x, x, dim) for x in parts]

    def pass_qkv(of, at, count, dim):
        rows = r.wqkv.at[of, :, rows16(at * (D // 4), count * (D // 4))]
        return net.copy(rows, rows, dim)

    two = 2 if bits > 1 else 1
    qkv_y = pass_qkv(m, 2 * c + net.bit(0), 1, "y")
    qkv_x = pass_qkv(1 - m, 2 * c + net.bit(0), 1, 0)
    qkv_c = pass_qkv(1 - m, 2 * c, 2, "c")
    ff_y = pass_on(m, p, 1, "y")
    ff_z = pass_on(1 - m, p, 1, 1) if bits > 1 else []
    ff_x = pass_on(1 - m, (p // two) * two, two, 0)
    ff_c = pass_on(1 - m, c * (cuts // 2), cuts // 2, "c")
    qkv_own.wait()
    qkv_y.start()
    wait_all(own)
    r.small[...] = jnp.zeros_like(r.small)
    stage_mel_rows(r, sub, mel_rim.wait)
    stage_first(r, jnp.logical_and(c == 0, m == 0))
    qkv_y.wait()
    qkv_x.start()
    start_all(ff_y)
    stage_odd(r)
    w2_own.wait()
    stage_second(r, quarter(net))
    vec_copy.wait()
    r.vecs[8:16, :] = r.vec_mine[...] + r.vec_got[...]
    qkv_x.wait()
    qkv_c.start()
    wait_all(ff_y)
    start_all(ff_z)

    def block(slot, part, h):
        return r.kv.at[rows16((3 * slot + part) * half + h * (half // 2), half // 2)]

    def project(h):
        far, near = [], []
        for part in (1, 2, 0):
            stage_qkv(r, part, h)
            if part:
                far.append(net.send(block(3 + c, part, h), block(0, part, h), "y"))
                far.append(net.send(block(4 - c, part, h), block(1, part, h), "c", "y"))
            near.append(net.send(block(4 - c, part, h), block(2, part, h), "c"))
        return far, near

    far_own, near_own = project(m)
    stage_mask(r, sub)
    add_small(r, DNB, col(r.bg[...].astype(F32)))
    r.normedt[...] = flip(r.normed[...])
    qkv_c.wait()
    far_other, near_other = project(1 - m)
    wait_all(near_own)
    heads = half // HEAD

    def flip_taps():
        for tap, to in zip((r.hp, r.he, r.ho), r.tapt):
            to[...] = flip(tap[...])

    hooks = {
        heads: [lambda: wait_all(near_other), lambda: wait_all(ff_z), lambda: start_all(ff_x)],
        2 * heads - 1: [flip_taps],
        2 * heads: [lambda: wait_all(far_own)],
        3 * heads: [lambda: wait_all(far_other), lambda: wait_all(ff_x), lambda: start_all(ff_c)],
    }
    attend(r, c, m, hooks)
    attend_end(r, 1)
    mix_c = net.send(r.mixb.at[half:D], r.mix_got, "c")
    attend_end(r, 0)
    stage_mid(r, c, mix_c.wait, lambda: wait_all(ff_c))

    def summed(n, part, rows, halves):
        views = [
            getattr(r, "g_" + n).at[part * rows * halves : (part + 1) * rows * halves],
            getattr(r, "got_%s%d" % (n, part)),
            getattr(r, "done_" + n).at[part * rows : (part + 1) * rows],
        ]
        return bucket_sum(net, *views, halves, orders(n, bits)[part])

    def leave(n, part):
        done = getattr(r, "done_" + n)
        size = half if n == "qkv" else D
        rows = done if n in ("out", "c1") else done.at[part * size : (part + 1) * size]
        if n == "qkv":
            pairs = [(rows.at[:, j * half : (j + 1) * half], r.qkv_o.at[part, j * half : (j + 1) * half]) for j in range(2)]
        elif n == "up":
            pairs = [(rows, r.up_o.at[:, part * D : (part + 1) * D])]
        elif n in ("down", "c2"):
            pairs = [(rows, getattr(r, n + "_o").at[part * D : (part + 1) * D])]
        else:
            pairs = [(done, getattr(r, n + "_o"))]
        return [net.here_later(src, dst) for src, dst in pairs]

    tracks, leaving = {}, {}
    for n, rows, halves, parts in (
        ("down", D, 2, side),
        ("up", D, 2, side),
        ("out", half, 2, 1),
        ("qkv", half, 2, 3),
        ("c2", D, 1, 3),
        ("c1", r.g_c1.shape[0], 1, 1),
    ):
        for part in range(parts):
            name = "%s%d" % (n, part)
            tracks[name] = summed(n, part, rows, halves)
            leaving[name] = leave(n, part)
            tracks[name].then(functools.partial(start_all, leaving[name]))
    tracks["vec0"] = small_sum(net, r.small, r.got_small, orders("vec", bits)[0])

    def acts_at(name):
        names = ["%s%d" % TRACKS[k] for k in SCHEDULE.get(name, ())]
        return [act for n in names if n in tracks for act in tracks[n].take()]

    def point(name):
        for act in acts_at(name):
            act()

    hooks = {}
    for step in range(2 * side):
        if step and step % 2 == 0:
            ready("down%d" % (step // 2 - 1), "up%d" % (step // 2 - 1))
        hooks[step] = acts_at("ff%d" % step)
    stage_ff(r, hooks)
    ready("down%d" % (side - 1), "up%d" % (side - 1))
    point("ffo")
    stage_mid_pull(r)
    enc = [
        net.copy(r.enc, r.enc_got, "y"),
        pltpu.make_async_copy(r.enc, r.enc_o.at[rows_of_mine], r.own.at[39]),
    ]
    start_all(enc)
    stage_do(r, c, False)
    do_c = net.send(r.dot_out, r.dot.at[half:D], "c")
    point("mid")
    stage_out_weights(r, c)
    ready("out0")
    point("out")
    stage_do(r, c, True)
    stage_diag(r, 0)
    do_c.wait()
    stage_diag(r, 1)
    both = half * 2
    home_y = net.copy(r.dkv.at[0:both], r.from_y, "y")
    home_d = net.copy(r.dkv.at[both : 2 * both], r.from_d, "c", "y")
    home_c = net.copy(r.dkv.at[2 * both : 3 * both], r.from_c.at[half:], "c")
    hooks = {}

    def at_step(step, *acts):
        hooks.setdefault(step * heads // 4, []).extend(acts)

    at_step(4, home_y.start)
    at_step(8, home_d.start)
    at_step(12, home_c.start)
    for step in range(16):
        at_step(step, *acts_at("pull%d" % step))
    attend_pull(r, c, hooks)
    r.dq_out[...] = (r.dqt[half:D, :] * HEAD**-0.5).astype(BF)
    dq_c = net.send(r.dq_out, r.from_c.at[0:half], "c")
    r.dsum[rows16(c * half, half), :] = (r.dqt[0:half, :] * HEAD**-0.5).astype(BF)
    point("home")
    home_y.wait()
    home_d.wait()
    home_c.wait()

    def total(i, carry):
        for part in range(2):
            rows = rows16(part * half + i * 32, 32)
            mine = r.dkv[rows16(3 * both + part * half + i * 32, 32), :].astype(F32) + r.from_y[rows, :].astype(F32)
            r.dsum[rows16((1 + part) * D + c * half + i * 32, 32), :] = mine.astype(BF)
            other = r.from_c[rows16((1 + part) * half + i * 32, 32), :].astype(F32) + r.from_d[rows, :].astype(F32)
            r.dsum[rows16((1 + part) * D + (1 - c) * half + i * 32, 32), :] = other.astype(BF)
        return carry

    lax.fori_loop(0, half // 32, total, 0)

    def queries_came():
        dq_c.wait()
        r.dsum[rows16((1 - c) * half, half), :] = r.from_c[0:half, :]

    for part in (1, 2):
        stage_qkv_weights(r, part)
        ready("qkv%d" % part)
        point("qkvw%d" % part)
    stage_qkv_pull(r, queries_came)
    point("norm")
    stage_norm_pull(r)
    rim = [net.send(r.sg.at[0:16], r.slots.at[0, i], dim) for i, dim in enumerate(("c", "y"))]
    point("c2")
    for part in range(3):
        stage_conv2_weights(r, part)
        ready("c2%d" % part)
        point("c2w%d" % part)
    stage_qkv_weights(r, 0)
    ready("qkv0")
    point("qkvw0")

    def next_row():
        wait_all(rim)
        return pick_next(net, r.slots.at[0])

    stage_conv2_pull(r, next_row)
    point("first")
    stage_first_pull(r)
    rim = [net.send(r.fe.at[0:16], r.slots.at[1, i], dim) for i, dim in enumerate(("c", "y"))]
    rim += [net.send(r.fo.at[T - 16 : T], r.slots.at[2, i], dim) for i, dim in enumerate(("c", "y"))]
    point("c1")
    stage_conv1_weights(r)
    ready("c10", "vec0")
    point("c1w")
    wait_all(rim)
    stage_mel(r, pick_next(net, r.slots.at[1]), pick_prev(net, r.slots.at[2]))
    rows_of_yours = rows16((1 - sub) * T, T)
    mel_y = net.send(r.melg, r.melg_got, "y")
    point("mel")
    wait_all(enc)
    ends = [
        net.here(r.enc_got, r.enc_o.at[rows_of_yours]),
        net.here(r.melg, r.mel_o.at[rows_of_mine]),
    ]
    point("end")
    drain(*tracks.values())
    mel_y.wait()
    ends.append(net.here(r.melg_got, r.mel_o.at[rows_of_yours]))
    ends.append(net.here(r.small, r.small_o))
    wait_all(ends)
    for copies in leaving.values():
        wait_all(copies)


def run_layer(bits, near, far, outs, T, D, F2, lanes):
    half, H = D // 2, D // HEAD
    td, dt = (T, D), (D, T)
    buckets = dict(down=(D, 2, F2 // D), up=(D, 2, F2 // D), out=(half, 2, 1), qkv=(half, 2, 3), c2=(D, 1, 3), c1=(lanes, 1, 1))
    scratch = dict(
        melbuf=((128, 4 * T + 256), BF),
        mele=((T + 24, 128), F32),
        melo=((T + 24, 128), F32),
        xe=((T, 384), BF),
        xo=((T, 384), BF),
        w1p=((384, D), BF),
        w2=((3, D, D), BF),
        bg=(td, BF),
        wqkv=((2, 3, D, half), BF),
        wo=((D, D), BF),
        up=((2, D, F2), BF),
        down=((2 * F2, D), BF),
        vecs=((16, D), F32),
        vec_mine=((8, D), F32),
        vec_got=((8, D), F32),
        stream=(td, F32),
        he=(td, BF),
        ho=(td, BF),
        hp=(td, BF),
        dge=(td, F32),
        dgo=(td, F32),
        dg2=(td, F32),
        normed=(td, BF),
        kv=((15 * half, T), BF),
        mixt=(dt, F32),
        mixb=(dt, BF),
        normedt=(dt, BF),
        ntwot=(dt, BF),
        mix_got=((half, T), BF),
        dot=(dt, BF),
        dot_out=((half, T), BF),
        top=((H, 1, T), F32),
        total=((H, 1, T), F32),
        diag=((H, 1, T), F32),
        tmp=(td, F32),
        tmp2=(td, F32),
        shift=((T + 16, D), F32),
        wide=((T + 16, 128), F32),
        mid=(td, F32),
        ntwo=(td, BF),
        act=(td, BF),
        ing=(td, BF),
        ffo=(td, F32),
        ntg=(td, F32),
        attg=(td, BF),
        dqt=(dt, F32),
        dq_out=((half, T), BF),
        pb=((T, 2 * T), BF),
        ds=((T, 2 * T), BF),
        dkv=((8 * half, T), BF),
        from_y=((2 * half, T), BF),
        from_d=((2 * half, T), BF),
        from_c=((3 * half, T), BF),
        dsum=((3 * D, T), BF),
        enc_got=(td, BF),
        melg=((T, 256), BF),
        melg_got=((T, 256), BF),
        small=((16, D), F32),
        got_small=((sum(len(subsets(dims)) for dims in orders("vec", bits)[0]), 16, D), F32),
        slots=((3, 2, 16, D), BF),
    )
    alias = T == D
    for n, (rows, halves, parts) in buckets.items():
        if n not in ("qkv", "c2"):
            scratch["g_" + n] = ((rows * halves * parts, D), BF)
        for part in range(parts):
            need = sum_plan(rows, halves, orders(n, bits)[part])[1]
            scratch["got_%s%d" % (n, part)] = ((need, D), BF)
        scratch["done_" + n] = ((rows * parts, D), BF)
    if not alias:
        scratch.update({"tapt%d" % i: (dt, BF) for i in range(3)})
        scratch.update(g_qkv=((6 * half, D), BF), g_c2=((6 * half, D), BF))
    names = list(near) + list(far) + list(outs) + list(scratch) + ["send", "recv", "own"]

    def kernel(*refs):
        r = Box()
        for n, ref in zip(names, refs):
            setattr(r, n, ref)
        r.odd, r.smg, r.sg, r.fe, r.fo, r.enc = r.shift, r.mid, r.ntwo, r.act, r.ing, r.bg
        r.tapt = (r.hp, r.he, r.ho) if alias else (r.tapt0, r.tapt1, r.tapt2)
        if alias:
            r.g_qkv, r.g_c2 = r.kv.at[0 : 6 * half], r.kv.at[6 * half : 12 * half]
        layer(r, bits)

    vmem, anywhere = pl.BlockSpec(memory_space=pltpu.VMEM), pl.BlockSpec(memory_space=pl.ANY)
    got = pl.pallas_call(
        kernel,
        name="layer",
        out_shape=[jax.ShapeDtypeStruct(*o) for o in outs.values()],
        in_specs=[vmem] * len(near) + [anywhere] * len(far),
        out_specs=[anywhere] * len(outs),
        scratch_shapes=[pltpu.VMEM(*s) for s in scratch.values()]
        + [pltpu.SemaphoreType.DMA((256,)), pltpu.SemaphoreType.DMA((256,)), pltpu.SemaphoreType.DMA((40,))],
        compiler_params=pltpu.CompilerParams(
            vmem_limit_bytes=VMEM_LIMIT, collective_id=1, has_side_effects=True
        ),
    )(*near.values(), *far.values())
    return dict(zip(outs, got))


def run_finish(got, mels, side):
    T2, D = got["enc_o"].shape
    half = D // 2
    ins = list(got)
    outs = dict(
        enc=((1, T2, D), BF),
        mel=((1, mels, 2 * T2), F32),
        c1=((3, mels, D), F32),
        c2=((3, D, D), F32),
        qkv=((3, D, half), F32),
        qkvb=((2, half), F32),
        out=((half, D), F32),
        up=((D, side * D), F32),
        upb=((side * D,), F32),
        down=((side * D, D), F32),
    )
    outs.update({n: ((D,), F32) for n in ROW_BIASES})

    big = ("mel", "c1", "c2", "qkv", "out", "up", "down")
    names = ins + list(outs) + ["in_" + n for n in ins] + ["out_" + n for n in big] + ["came", "went"]

    def kernel(*refs):
        r = Box()
        for n, ref in zip(names, refs):
            setattr(r, n, ref)
        m = lax.axis_index("mp")
        order = ["small_o", "enc_o", "down_o", "up_o", "qkv_o", "c2_o", "mel_o", "out_o", "c1_o"]
        loads = {}
        for k, n in enumerate(order):
            loads[n] = pltpu.make_async_copy(getattr(r, n), getattr(r, "in_" + n), r.came.at[k])
            loads[n].start()
        went = []

        def leave(n):
            copy = pltpu.make_async_copy(getattr(r, "out_" + n), getattr(r, n), r.went.at[len(went)])
            copy.start()
            went.append(copy)

        def cast(src, dst):
            def one(rows):
                dst[rows, :] = src[rows, :].astype(dst.dtype)

            rows_loop(src.shape[0], 256, one)

        loads["small_o"].wait()
        for k, n in enumerate(ROW_BIASES):
            getattr(r, n)[...] = r.in_small_o[k : k + 1, :].reshape(D)
        r.qkvb[...] = r.in_small_o[QB : QB + 2, pl.ds(pl.multiple_of(m * half, 128), half)]
        for k in range(side):
            r.upb[k * D : (k + 1) * D] = r.in_small_o[pl.ds(UPB + m * side + k, 1), :].reshape(D)
        loads["enc_o"].wait()
        copy = pltpu.make_async_copy(r.in_enc_o, r.enc.at[0], r.went.at[len(big)])
        copy.start()
        for n in ("down", "up"):
            loads[n + "_o"].wait()
            cast(getattr(r, "in_" + n + "_o"), getattr(r, "out_" + n))
            leave(n)
        loads["qkv_o"].wait()
        for o in range(3):
            cast(r.in_qkv_o.at[o], r.out_qkv.at[o])
        leave("qkv")
        loads["c2_o"].wait()
        for o in range(3):
            cast(r.in_c2_o.at[o * D : (o + 1) * D], r.out_c2.at[o])
        leave("c2")
        row = lax.broadcasted_iota(jnp.int32, (128, 256), 0)
        lane = lax.broadcasted_iota(jnp.int32, (128, 256), 1)
        even = jnp.where(lane == 2 * row, 1.0, 0.0).astype(BF)
        odd = jnp.where(lane == 2 * row + 1, 1.0, 0.0).astype(BF)
        loads["mel_o"].wait()
        for k in range(T2 // 128):
            rows = slice(k * 128, (k + 1) * 128)
            value = tn(r.in_mel_o[rows, 0:128], even) + tn(r.in_mel_o[rows, 128:256], odd)
            r.out_mel[0, :, k * 256 : (k + 1) * 256] = value[0:mels, :]
        leave("mel")
        loads["out_o"].wait()
        cast(r.in_out_o, r.out_out)
        leave("out")
        loads["c1_o"].wait()
        for o in range(3):
            r.out_c1[o] = r.in_c1_o[o * mels : (o + 1) * mels, :].astype(F32)
        leave("c1")
        copy.wait()
        wait_all(went)

    vmem, anywhere = pl.BlockSpec(memory_space=pltpu.VMEM), pl.BlockSpec(memory_space=pl.ANY)
    done = pl.pallas_call(
        kernel,
        name="finish",
        out_shape=[jax.ShapeDtypeStruct(*o) for o in outs.values()],
        in_specs=[anywhere] * len(ins),
        out_specs=[anywhere if n in big + ("enc",) else vmem for n in outs],
        scratch_shapes=[pltpu.VMEM(got[n].shape, got[n].dtype) for n in ins]
        + [pltpu.VMEM(*outs[n]) for n in big]
        + [pltpu.SemaphoreType.DMA((len(ins),)), pltpu.SemaphoreType.DMA((len(big) + 1,))],
        compiler_params=pltpu.CompilerParams(vmem_limit_bytes=VMEM_LIMIT),
    )(*got.values())
    return dict(zip(outs, done))


def sine_tables(frames, channels, fine):
    half_width = channels // 2
    rate = np.exp(-(math.log(10000.0) / (half_width - 1)) * np.arange(half_width))
    small = np.arange(fine)[:, None] * rate[None, :]
    large = np.arange(0, frames, fine)[:, None] * rate[None, :]
    table = dict(fine_s=np.sin(small), fine_c=np.cos(small), coarse_s=np.sin(large), coarse_c=np.cos(large))
    return {n: jnp.asarray(t, F32) for n, t in table.items()}


def on_device(
    mel_input,
    conv1_weight,
    conv1_bias,
    conv2_weight,
    conv2_bias,
    norm1_gain,
    norm1_bias,
    qkv_weight,
    qkv_bias,
    out_weight,
    out_bias,
    norm2_gain,
    norm2_bias,
    up_weight,
    up_bias,
    down_weight,
    down_bias,
    cotangent,
    speech_mask,
):
    mels = mel_input.shape[1]
    T, D = cotangent.shape[1] // 2, cotangent.shape[2]
    F2 = up_weight.shape[1]
    side, half = F2 // D, D // 2
    bits = (lax.axis_size("dp") - 1).bit_length()
    lanes = -(-3 * mels // 128) * 128
    near = dict(
        w1=conv1_weight,
        mask=speech_mask,
        qkvb=qkv_bias,
        upb=up_bias,
        c1b=conv1_bias,
        c2b=conv2_bias,
        n1g=norm1_gain,
        n1b=norm1_bias,
        oub=out_bias,
        n2g=norm2_gain,
        n2b=norm2_bias,
        dnb=down_bias,
    )
    near.update(sine_tables(4 * T, D, 32))
    got = run_layer(
        bits,
        near,
        dict(
            mel=mel_input,
            cot=cotangent,
            w2_l=conv2_weight,
            wqkv_l=qkv_weight,
            wo_l=out_weight,
            up_l=up_weight,
            down_l=down_weight,
        ),
        dict(
            enc_o=((2 * T, D), BF),
            mel_o=((2 * T, 256), BF),
            down_o=((F2, D), BF),
            up_o=((D, F2), BF),
            out_o=((half, D), BF),
            qkv_o=((3, D, half), BF),
            c2_o=((3 * D, D), BF),
            c1_o=((lanes, D), BF),
            small_o=((16, D), F32),
        ),
        T,
        D,
        F2,
        lanes,
    )
    done = run_finish(got, mels, side)
    names = ("enc", "mel", "c1", "c1b", "c2", "c2b", "n1g", "n1b", "qkv", "qkvb")
    names += ("out", "oub", "n2g", "n2b", "up", "upb", "down", "dnb")
    return tuple(done[n] for n in names)


def solution(mesh):
    placed = (
        P("dp", None, "seq"),
        P(),
        P(),
        P(),
        P(),
        P(),
        P(),
        P(None, None, "mp"),
        P(None, "mp"),
        P("mp", None),
        P(),
        P(),
        P(),
        P(None, "mp"),
        P("mp"),
        P("mp", None),
        P(),
        P("dp", "seq", None),
        P("dp", "seq"),
    )
    return jax.shard_map(
        on_device,
        mesh=mesh,
        in_specs=placed,
        out_specs=(
            P("dp", "seq", None),
            P("dp", None, "seq"),
            P(),
            P(),
            P(),
            P(),
            P(),
            P(),
            P(None, None, "mp"),
            P(None, "mp"),
            P("mp", None),
            P(),
            P(),
            P(),
            P(None, "mp"),
            P("mp"),
            P("mp", None),
            P(),
        ),
        check_vma=False,
    )
```

```python
import functools
import math

import jax
import jax.numpy as jnp
import numpy as np
from jax import lax
from jax.experimental import pallas as pl
from jax.experimental.pallas import tpu as pltpu
from jax.sharding import PartitionSpec as P

HEAD = 64
BF = jnp.bfloat16
F32 = jnp.float32
MESH = pl.DeviceIdType.MESH
VMEM_LIMIT = 62 * 1024 * 1024
C1B, C2B, N1G, N1B, OUB, N2G, N2B, DNB, QB, VB, UPB = range(11)


class Box:
    pass


def dot(a, b, ca, cb):
    return lax.dot_general(a, b, (((ca,), (cb,)), ((), ())), preferred_element_type=F32)


def nn(a, b):
    return dot(a, b, 1, 0)


def nt(a, b):
    return dot(a, b, 1, 1)


def tn(a, b):
    return dot(a, b, 0, 0)


def flip(value):
    return value.astype(F32).T.astype(BF)


def rows_loop(total, step, body, unroll=1):
    step = min(step, total)

    def one(i, carry):
        body(pl.ds(pl.multiple_of(i * step, step), step))
        return carry

    lax.fori_loop(0, total // step, one, 0, unroll=min(unroll, total // step))


def gelu_parts(v):
    t = 1.0 / (1.0 + (0.3275911 / math.sqrt(2.0)) * jnp.abs(v))
    e = jnp.exp(-0.5 * v * v)
    poly = 1.061405429 * t - 1.453152027
    poly = poly * t + 1.421413741
    poly = poly * t - 0.284496736
    poly = poly * t + 0.254829592
    tail = (0.5 * t) * poly * e
    return jnp.where(v >= 0, 1.0 - tail, tail), e * (1.0 / math.sqrt(2.0 * math.pi))


def gelu_both(v):
    cdf, pdf = gelu_parts(v)
    return v * cdf, cdf + v * pdf


def normal(x):
    center = x - jnp.mean(x, axis=-1, keepdims=True)
    spread = jnp.mean(center * center, axis=-1, keepdims=True)
    inv = lax.rsqrt(spread + 1e-05)
    return center * inv, inv


def normal_pull(gy, hat, inv):
    return inv * (
        gy
        - jnp.mean(gy, axis=-1, keepdims=True)
        - hat * jnp.mean(gy * hat, axis=-1, keepdims=True)
    )


def vec(r, i):
    return r.vecs[i : i + 1, :]


def add_small(r, i, value):
    r.small[i : i + 1, :] += value


def col(value):
    return jnp.sum(value, axis=0, keepdims=True)


def stage_mel_rows(r, sub, rim_came):
    T, D = r.stream.shape
    row = lax.broadcasted_iota(jnp.int32, (256, 256), 0)
    lane = lax.broadcasted_iota(jnp.int32, (256, 256), 1)
    pick = jnp.where(lane == 2 * (row % 128) + row // 128, 1.0, 0.0).astype(BF)
    base = sub * 2 * T

    def lanes(start, size):
        return r.melbuf[:, pl.ds(pl.multiple_of(base + start, 128), size)]

    row = lax.broadcasted_iota(jnp.int32, (16, 128), 0)
    lane = lax.broadcasted_iota(jnp.int32, (16, 128), 1)

    def select(at, to):
        return jnp.where(jnp.logical_and(row == to, lane == at), 1.0, 0.0).astype(BF)

    for k in range(T // 128):
        both = nt(pick, lanes(128 + 256 * k, 256))
        r.mele[8 + 128 * k : 136 + 128 * k, :] = both[0:128, :]
        r.melo[8 + 128 * k : 136 + 128 * k, :] = both[128:256, :]
    rim_came()
    before, after = lanes(0, 128), lanes(128 + 2 * T, 128)
    r.mele[0:8, :] = nt(select(126, 7), before)[0:8, :]
    r.melo[0:8, :] = nt(select(127, 7), before)[0:8, :]
    r.mele[T + 8 : T + 16, :] = nt(select(0, 0), after)[0:8, :]


def three(a, b, c):
    return jnp.concatenate([a, b, c], axis=1).astype(BF)


def stage_first(r, first):
    T, D = r.stream.shape
    for o in range(3):
        r.w1p[128 * o : 128 * o + r.w1.shape[1], :] = r.w1[o]
        r.w1p[128 * o + r.w1.shape[1] : 128 * (o + 1), :] = jnp.zeros((128 - r.w1.shape[1], D), BF)
    w1 = r.w1p[...]
    edge = nn(three(r.mele[0:16, :], r.melo[0:16, :], r.mele[1:17, :]), w1) + vec(r, C1B)
    edge = gelu_both(edge)[0] * jnp.where(first, 0.0, 1.0)
    r.odd[0:8, :] = edge[0:8, :]
    r.xe[...] = three(r.melo[7 : 7 + T, :], r.mele[8 : 8 + T, :], r.melo[8 : 8 + T, :])
    r.xo[...] = three(r.mele[8 : 8 + T, :], r.melo[8 : 8 + T, :], r.mele[9 : 9 + T, :])
    r.tmp[...] = nn(r.xe[...], w1)

    def even(rows):
        value, slope = gelu_both(r.tmp[rows, :] + vec(r, C1B))
        r.he[rows, :] = value.astype(BF)
        r.dge[rows, :] = slope

    rows_loop(T, 32, even)


def stage_odd(r):
    T, D = r.stream.shape
    r.tmp[...] = nn(r.xo[...], r.w1p[...])

    def odd(rows):
        value, slope = gelu_both(r.tmp[rows, :] + vec(r, C1B))
        r.ho[rows, :] = value.astype(BF)
        r.odd[pl.ds(pl.multiple_of(rows.start + 8, 8), rows.size), :] = value
        r.dgo[rows, :] = slope

    rows_loop(T, 32, odd)


def stage_second(r, place):
    T, D = r.stream.shape
    r.hp[...] = r.odd[7 : 7 + T, :].astype(BF)
    r.tmp[...] = nn(r.hp[...], r.w2[0]) + nn(r.he[...], r.w2[1]) + nn(r.ho[...], r.w2[2])
    fine = r.fine_s.shape[0]

    def second(rows):
        value, slope = gelu_both(r.tmp[rows, :] + vec(r, C2B))
        at = place * (T // fine) + rows.start // fine
        s0, c0 = r.coarse_s[pl.ds(at, 1), :], r.coarse_c[pl.ds(at, 1), :]
        s1, c1 = r.fine_s[...], r.fine_c[...]
        stream = value + jnp.concatenate([s0 * c1 + c0 * s1, c0 * c1 - s0 * s1], axis=1)
        r.dg2[rows, :] = slope
        r.stream[rows, :] = stream
        r.normed[rows, :] = (normal(stream)[0] * vec(r, N1G) + vec(r, N1B)).astype(BF)

    rows_loop(T, fine, second)


def stage_mask(r, sub):
    T, D = r.stream.shape
    row = r.mask[0:1, pl.ds(pl.multiple_of(sub * T, 128), T)].astype(F32)
    r.wide[0:T, :] = jnp.broadcast_to(row, (128, T)).T

    def one(rows):
        keep = r.wide[rows, :]
        keep = jnp.concatenate([keep] * (D // 128), axis=1)
        r.bg[rows, :] = (r.bg[rows, :].astype(F32) * keep).astype(BF)

    rows_loop(T, 32, one)


def stage_qkv(r, part, h):
    T, D = r.stream.shape
    half, qr = D // 2, D // 4
    bias, scale = ((QB, HEAD**-0.5), (None, 1.0), (VB, 1.0))[part]
    value = nn(r.normed[...], r.wqkv[h, part])
    if bias is not None:
        value = value + r.vecs[bias : bias + 1, pl.ds(pl.multiple_of(h * half, half), half)]
    value = (value.astype(BF).astype(F32) * scale).T.astype(BF)
    for k in range(2):
        r.kv[rows16((3 * (3 + k) + part) * half + h * qr, qr), :] = value[k * qr : (k + 1) * qr, :]


def at_head(start, h):
    return pl.ds(pl.multiple_of(start + h * HEAD, HEAD), HEAD)


def head_loop(steps, hooks, body):
    def one(step, carry):
        for at, todo in hooks.items():
            if not todo:
                continue

            @pl.when(step == at)
            def _(todo=todo):
                for act in todo:
                    act()

        body(step)
        return carry

    lax.fori_loop(0, steps, one, 0)


def attend(r, c, m, hooks):
    S, T = r.kv.shape[0] // 15, r.kv.shape[1]
    heads = S // HEAD
    r.top[...] = jnp.full(r.top.shape, -jnp.inf, F32)
    r.total[...] = jnp.zeros(r.total.shape, F32)
    r.mixt[...] = jnp.zeros(r.mixt.shape, F32)

    def body(step):
        quarter, u, pair = step // heads, step % heads, heads // 2
        g = 2 * (quarter // 2) + u // pair
        h = (m + (1 - 2 * m) * ((quarter + 1) // 2 % 2)) * pair + u % pair
        own = (3 - g) // 3
        slot = own * (3 + c) + (1 - own) * ((g + 1) % 3)
        k = r.kv[at_head((3 * slot + 1) * S, h), :]
        v = r.kv[at_head((3 * slot + 2) * S, h), :]
        for i, home in enumerate((3 + c, 2)):
            q = r.kv[at_head(3 * home * S, h), :]
            s = tn(k, q)
            before = r.top[i * heads + h]
            top = jnp.maximum(before, jnp.max(s, axis=0, keepdims=True))
            p = jnp.exp(s - top)
            keep = jnp.exp(before - top)
            rows = at_head(i * S, h)
            r.top[i * heads + h] = top
            r.total[i * heads + h] = keep * r.total[i * heads + h] + jnp.sum(p, axis=0, keepdims=True)
            r.mixt[rows, :] = keep * r.mixt[rows, :] + nn(v, p.astype(BF))

    head_loop(4 * heads, hooks, body)


def attend_end(r, i):
    S = r.kv.shape[0] // 15
    heads = S // HEAD

    def one(h, carry):
        rows = at_head(i * S, h)
        total = r.total[i * heads + h]
        value = r.mixt[rows, :] * (1.0 / total)
        r.mixt[rows, :] = value
        r.mixb[rows, :] = value.astype(BF)
        r.top[i * heads + h] = r.top[i * heads + h] + jnp.log(total)
        return carry

    lax.fori_loop(0, heads, one, 0)


def stage_mid(r, c, mix_came, weights_came):
    T, D = r.stream.shape
    half = D // 2
    weights_came()
    r.tmp[...] = tn(r.mixb[0:half, :], r.wo[rows16(c * half, half), :])
    mix_came()
    r.tmp[...] += tn(r.mix_got[...], r.wo[rows16((1 - c) * half, half), :])

    def one(rows):
        mid = r.stream[rows, :] + r.tmp[rows, :] + vec(r, OUB)
        r.mid[rows, :] = mid
        r.ntwo[rows, :] = (normal(mid)[0] * vec(r, N2G) + vec(r, N2B)).astype(BF)

    rows_loop(T, 32, one)


def stage_ff(r, hooks):
    T, D = r.stream.shape
    side = r.up.shape[2] // D
    parts, width = 2 * side, D

    def chunk(t):
        into, at = t % 2, t // 2
        j = into * side + at
        up = r.up[into, :, pl.ds(pl.multiple_of(at * D, D), D)]
        down = r.down[pl.ds(pl.multiple_of(j * D, D), D), :]
        r.tmp[...] = nn(r.ntwo[...], up)
        r.tmp2[...] = nt(r.bg[...], down)
        bias = r.vecs[pl.ds(UPB + j, 1), :]

        def one(i, acc):
            rows = pl.ds(pl.multiple_of(i * 32, 32), 32)
            value, slope = gelu_both(r.tmp[rows, :] + bias)
            r.act[rows, :] = value.astype(BF)
            grad = (r.tmp2[rows, :] * slope).astype(BF)
            r.ing[rows, :] = grad
            return acc + col(grad.astype(F32))

        r.small[pl.ds(UPB + j, 1), :] = lax.fori_loop(0, T // 32, one, jnp.zeros((1, width), F32))
        act = r.act[...]
        ing = r.ing[...]
        out = nn(act, down)
        back = nt(ing, up)

        r.ffo[...] += out
        r.ntg[...] += back
        rows = pl.ds(pl.multiple_of(t * D, D), D)
        r.g_down[rows, :] = tn(act, r.bg[...]).astype(BF)
        r.g_up[rows, :] = nn(r.ntwot[...], ing).astype(BF)

    r.ntwot[...] = flip(r.ntwo[...])
    r.ffo[...] = jnp.zeros_like(r.ffo)
    r.ntg[...] = jnp.zeros_like(r.ntg)
    head_loop(parts, hooks, chunk)


def stage_mid_pull(r):
    T, D = r.stream.shape

    def one(i, accs):
        rows = pl.ds(pl.multiple_of(i * 32, 32), 32)
        mid = r.mid[rows, :]
        enc = (mid + r.ffo[rows, :] + vec(r, DNB)).astype(BF)
        hat, inv = normal(mid)
        grad = r.ntg[rows, :]
        smg = r.bg[rows, :].astype(F32) + normal_pull(grad * vec(r, N2G), hat, inv)
        r.enc[rows, :] = enc
        r.smg[rows, :] = smg
        attg = smg.astype(BF)
        r.attg[rows, :] = attg
        return accs[0] + col(grad * hat), accs[1] + col(grad), accs[2] + col(attg.astype(F32))

    zero = jnp.zeros((1, D), F32)
    gain, bias, out_bias = lax.fori_loop(0, T // 32, one, (zero, zero, zero))
    add_small(r, N2G, gain)
    add_small(r, N2B, bias)
    add_small(r, OUB, out_bias)


def stage_do(r, c, own):
    half = r.attg.shape[1] // 2
    k = c if own else 1 - c
    value = nt(r.wo[rows16(k * half, half), :], r.attg[...]).astype(BF)
    if own:
        r.dot[0:half, :] = value
    else:
        r.dot_out[...] = value


def stage_out_weights(r, c):
    D = r.attg.shape[1]
    half, qr = D // 2, D // 4
    for k, mix in ((c, r.mixb[0:half, :]), (1 - c, r.mix_got[...])):
        value = nn(mix, r.attg[...]).astype(BF)
        for h in range(2):
            r.g_out[rows16(h * half + k * qr, qr), :] = value[h * qr : (h + 1) * qr, :]


def stage_diag(r, i):
    S = r.kv.shape[0] // 15
    heads = S // HEAD

    def one(h, carry):
        rows = at_head(i * S, h)
        value = r.dot[rows, :].astype(F32) * r.mixt[rows, :]
        r.diag[i * heads + h] = jnp.sum(value, axis=0, keepdims=True)
        return carry

    lax.fori_loop(0, heads, one, 0)


def attend_pull(r, c, hooks):
    S, T = r.kv.shape[0] // 15, r.kv.shape[1]
    heads = S // HEAD
    r.dqt[...] = jnp.zeros(r.dqt.shape, F32)

    def body(step):
        g, h = step // heads, step % heads
        slot = g + (g // 3) * c
        k = r.kv[at_head((3 * slot + 1) * S, h), :]
        v = r.kv[at_head((3 * slot + 2) * S, h), :]
        qs = [r.kv[at_head(3 * home * S, h), :] for home in (3 + c, 2)]
        dos = [r.dot[at_head(i * S, h), :] for i in range(2)]
        for i in range(2):
            top, diag = r.top[i * heads + h], r.diag[i * heads + h]
            for at in range(0, T, 128):
                rows, cols = slice(at, at + 128), slice(i * T, (i + 1) * T)
                p = jnp.exp(tn(k[:, rows], qs[i]) - top)
                r.pb[rows, cols] = p.astype(BF)
                r.ds[rows, cols] = (p * (tn(v[:, rows], dos[i]) - diag)).astype(BF)
        pair = [pl.ds(pl.multiple_of(i * S + h // 2 * 128, 128), 128) for i in range(2)]
        for part, left, right in ((0, r.ds, r.qrow), (1, r.pb, r.dorow)):
            r.turn[128 * part : 128 * (part + 1), :] = sum(
                nn(left[:, i * T : (i + 1) * T], right[:, pair[i]]) for i in range(2)
            ).T
            value = r.turn[pl.ds(pl.multiple_of(128 * part + h % 2 * HEAD, HEAD), HEAD), :]
            r.dkv[at_head((2 * g + part) * S, h), :] = value.astype(BF)
        dq = nn(k, r.ds[...])
        for i in range(2):
            r.dqt[at_head(i * S, h), :] += dq[:, i * T : (i + 1) * T]

    head_loop(4 * heads, hooks, body)


def piece_of(r, part, h):
    D, qr = r.attg.shape[1], r.attg.shape[1] // 4
    at = part * D + h * qr
    return jnp.concatenate([r.dsum[at : at + qr, :], r.dsum[at + 2 * qr : at + 3 * qr, :]], axis=0)


def stage_qkv_weights(r, part):
    T, D = r.stream.shape
    half = D // 2
    ones = jnp.ones((8, T), BF)
    for h in range(2):
        piece = piece_of(r, part, h)
        if part != 1:
            row = QB if part == 0 else VB
            r.small[row : row + 1, h * half : (h + 1) * half] = nt(ones, piece)[0:1, :]
        grad = nt(r.normedt[...], piece).astype(BF)
        at = (2 * part + h) * half
        r.g_qkv[at : at + half, 0:half] = grad[0:half, :]
        r.g_qkv[at : at + half, half:D] = grad[half:D, :]


def stage_qkv_pull(r, queries_came):
    T, D = r.stream.shape
    total = None
    for part in (1, 2, 0):
        if part == 0:
            queries_came()
        for h in range(2):
            back = nn(r.wqkv[h, part], piece_of(r, part, h))
            total = back if total is None else total + back
    r.tmp[...] = total.T


def stage_norm_pull(r):
    T, D = r.stream.shape

    def one(i, accs):
        rows = pl.ds(pl.multiple_of(i * 32, 32), 32)
        hat, inv = normal(r.stream[rows, :])
        grad = r.tmp[rows, :]
        back = r.smg[rows, :] + normal_pull(grad * vec(r, N1G), hat, inv)
        sg = (back * r.dg2[rows, :]).astype(BF)
        r.sg[rows, :] = sg
        return accs[0] + col(grad * hat), accs[1] + col(grad), accs[2] + col(sg.astype(F32))

    zero = jnp.zeros((1, D), F32)
    gain, bias, c2b = lax.fori_loop(0, T // 32, one, (zero, zero, zero))
    add_small(r, N1G, gain)
    add_small(r, N1B, bias)
    add_small(r, C2B, c2b)


def stage_conv2_pull(r, next_row):
    T, D = r.stream.shape
    sg = r.sg[...]
    r.shift[0:T, :] = nt(sg, r.w2[0])
    r.tmp[...] = nt(sg, r.w2[1])
    r.shift[T : T + 16, :] = nt(next_row(), r.w2[0])
    r.tmp2[...] = nt(sg, r.w2[2]) + r.shift[1 : T + 1, :]


def stage_first_pull(r):
    T, D = r.stream.shape

    def one(i, acc):
        rows = pl.ds(pl.multiple_of(i * 32, 32), 32)
        even = (r.tmp[rows, :] * r.dge[rows, :]).astype(BF)
        odd = (r.tmp2[rows, :] * r.dgo[rows, :]).astype(BF)
        r.fe[rows, :] = even
        r.fo[rows, :] = odd
        return acc + col(even.astype(F32)) + col(odd.astype(F32))

    add_small(r, C1B, lax.fori_loop(0, T // 32, one, jnp.zeros((1, D), F32)))


def stage_conv2_weights(r, i):
    D = r.stream.shape[1]
    r.g_c2[i * D : (i + 1) * D, :] = nn(r.tapt[i][...], r.sg[...]).astype(BF)


def stage_conv1_weights(r):
    value = (tn(r.xe[...], r.fe[...]) + tn(r.xo[...], r.fo[...])).astype(BF)
    mels = r.w1.shape[1]
    for o in range(3):
        r.g_c1[mels * o : mels * (o + 1), :] = value[128 * o : 128 * o + mels, :]
    r.g_c1[3 * mels :, :] = jnp.zeros((r.g_c1.shape[0] - 3 * mels, r.g_c1.shape[1]), BF)


def stage_mel(r, next_row, prev_row):
    T, D = r.stream.shape
    fe, fo = r.fe[...], r.fo[...]
    w = [r.w1p[128 * o : 128 * (o + 1), :] for o in range(3)]
    r.wide[16 : 16 + T, :] = nt(fo, w[2])
    r.wide[0:16, :] = nt(prev_row, w[2])
    r.melg[:, 0:128] = (nt(fe, w[1]) + nt(fo, w[0]) + r.wide[15 : 15 + T, :]).astype(BF)
    r.wide[0:T, :] = nt(fe, w[0])
    r.wide[T : T + 16, :] = nt(next_row, w[0])
    r.melg[:, 128:256] = (nt(fe, w[2]) + nt(fo, w[1]) + r.wide[1 : 1 + T, :]).astype(BF)


class Net:
    def __init__(self, r, bits):
        self.r, self.bits, self.used, self.used_here = r, bits, 0, 0
        self.d, self.c, self.m = (lax.axis_index(n) for n in ("dp", "seq", "mp"))

    def bit(self, dim):
        if dim == "c":
            return self.c
        if dim == "y":
            return self.m
        return (self.d // (1 << dim)) % 2

    def peer(self, dims):
        d = self.d
        for k in dims:
            if k not in ("c", "y"):
                d = d + (1 << k) - 2 * (1 << k) * self.bit(k)
        return (
            d,
            1 - self.c if "c" in dims else self.c,
            1 - self.m if "y" in dims else self.m,
        )

    def greet(self, partners):
        barrier = pltpu.get_barrier_semaphore()
        for dims in partners:
            pl.semaphore_signal(barrier, inc=1, device_id=self.peer(dims), device_id_type=MESH)
        pl.semaphore_wait(barrier, len(partners))

    def copy(self, src, dst, *dims):
        i = self.used
        self.used += 1
        return pltpu.make_async_remote_copy(
            src_ref=src,
            dst_ref=dst,
            send_sem=self.r.send.at[i],
            recv_sem=self.r.recv.at[i],
            device_id=self.peer(dims),
            device_id_type=MESH,
        )

    def send(self, src, dst, *dims):
        copy = self.copy(src, dst, *dims)
        copy.start()
        return copy

    def here_later(self, src, dst):
        i = self.used_here
        self.used_here += 1
        return pltpu.make_async_copy(src, dst, self.r.own.at[i])

    def here(self, src, dst):
        copy = self.here_later(src, dst)
        copy.start()
        return copy


def start_all(copies):
    for copy in copies:
        copy.start()


def wait_all(copies):
    for copy in copies:
        copy.wait()


def rows16(start, size):
    return pl.ds(pl.multiple_of(start, 16), size)


def subsets(dims):
    found = [()]
    for dim in dims:
        found += [one + (dim,) for one in found]
    return found[1:]


def sum_plan(rows, halves, order):
    steps, need = [], 0
    for dims in order:
        by_half = halves == 2 and "y" in dims
        cutting = [dim for dim in dims if not (by_half and dim == "y")]
        if rows % (16 << len(cutting)):
            cutting = []
        rows >>= len(cutting)
        if by_half:
            halves = 1
        steps.append((dims, cutting, rows, halves, by_half))
        need += rows * halves * len(subsets(dims))
    return steps, need


class Track:
    def __init__(self, acts):
        self.acts = list(acts)

    def take(self):
        return [self.acts.pop(0)] if self.acts else []

    def then(self, more):
        last = self.acts.pop()

        def act():
            last()
            more()

        self.acts.append(act)


def bucket_sum(net, g, got, done, halves, order):
    R = g.shape[0] // halves
    lo, rows, at, bases = 0, R, 0, [h * R for h in range(halves)]
    acts, back, end = [], [], None

    def start_after(end, copies):
        def act():
            if end is not None:
                end()
            for copy in copies:
                copy.start()

        return act

    def adder(copies, places, n):
        step = 64 if n % 64 == 0 else 32 if n % 32 == 0 else 16

        def end():
            wait_all(copies)
            for to, ofs in places:

                def add(k, carry, to=to, ofs=ofs):
                    mine = rows16(to + k * step, step)
                    value = g[mine, :].astype(F32)
                    for of in ofs:
                        value = value + got[rows16(of + k * step, step), :].astype(F32)
                    g[mine, :] = value.astype(BF)
                    return carry

                lax.fori_loop(0, n // step, add, 0)

        return end

    for dims, cutting, n, _, by_half in sum_plan(R, halves, order)[0]:

        def part_of(other):
            start = lo
            for i, dim in enumerate(reversed(cutting)):
                b = net.bit(dim)
                start = start + (1 - b if dim in other else b) * (n << i)
            return start

        keep = part_of(())
        if by_half:
            bases = [net.m * R]
        copies, ofs = [], [[] for _ in bases]
        for other in subsets(dims):
            sources = [(1 - net.m) * R] if by_half and "y" in other else bases
            for i, base in enumerate(sources):
                src = g.at[rows16(base + part_of(other), n)]
                copies.append(net.copy(src, got.at[rows16(at, n)], *other))
                ofs[i].append(at)
                at += n
        acts.append(start_after(end, copies))
        end = adder(copies, [(base + keep, of) for base, of in zip(bases, ofs)], n)
        if cutting:
            back.append((cutting, n, lo))
        lo, rows = keep, n

    def settle(end=end, lo=lo, base=bases[0], rows=rows):
        end()
        for k in range(rows // 16):
            done[rows16(lo + 16 * k, 16), :] = g[rows16(base + lo + 16 * k, 16), :]

    end = settle
    for cutting, n, before in reversed(back):
        part = rows16(lo, n)
        copies = [net.copy(done.at[part], done.at[part], *other) for other in subsets(cutting)]
        acts.append(start_after(end, copies))
        end = functools.partial(wait_all, copies)
        lo = before
    return Track(acts + [end])


def small_sum(net, value, slots, order):
    acts, end, at = [], None, 0
    for dims in order:
        copies = [net.copy(value, slots.at[at + i], *other) for i, other in enumerate(subsets(dims))]

        def act(end=end, copies=copies):
            if end is not None:
                end()
            start_all(copies)

        def end(copies=copies, at=at):
            wait_all(copies)
            total = value[...]
            for i in range(len(copies)):
                total = total + slots[at + i]
            value[...] = total

        at += len(copies)
        acts.append(act)
    return Track(acts + [end])


def ready(*names):
    pass


def advance(*sums):
    for one in sums:
        for act in one.take():
            act()


def drain(*sums):
    while any(one.acts for one in sums):
        advance(*sums)


def quarter(net):
    return 2 * net.c + net.c + net.m - 2 * net.c * net.m


def choose(slots, by_core, by_y):
    core = jnp.where(by_core, 1.0, 0.0)
    y = jnp.where(by_y, 1.0, 0.0)
    return (slots[0].astype(F32) * core + slots[1].astype(F32) * y).astype(BF)


def pick_next(net, slots):
    q = quarter(net)
    return choose(slots, q == 1, q % 2 == 0)


def pick_prev(net, slots):
    q = quarter(net)
    return choose(slots, q == 2, q % 2 == 1)


ROW_BIASES = ("c1b", "c2b", "n1g", "n1b", "oub", "n2g", "n2b", "dnb")


ORDERS = dict(
    down=("c-y-z-xw", "c-x-z-y-w"),
    up=("c-w-x-zy", "c-xz-w-y"),
    out=("c-x-w-zy",),
    qkv=("c-w-yx-z", "c-y-z-w-x", "x-c-z-y-w"),
    c2=("c-z-yx-w", "c-xy-z-w", "c-xy-w-z"),
    c1=("cy-xz-w",),
    vec=("c-y-w-z-x",),
)
TRACKS = (
    ("down", 0), ("down", 1), ("up", 0), ("up", 1), ("out", 0), ("qkv", 0), ("qkv", 1), ("qkv", 2),
    ("c2", 0), ("c2", 1), ("c2", 2), ("c1", 0), ("vec", 0),
)
SCHEDULE = dict(
    ff2=(0, 2),
    ffo=(0, 1, 2, 3),
    out=(1, 3, 4),
    pull1=(4,),
    pull2=(0,),
    pull5=(2, 3),
    pull6=(0, 1, 4),
    pull7=(2, 3),
    pull10=(0, 3, 4),
    pull11=(1, 2),
    pull13=(0, 3, 4),
    pull14=(1, 2),
    pull15=(4,),
    qkvw1=(1, 2, 3, 6),
    qkvw2=(7,),
    norm=(0, 4),
    c2=(3, 6),
    c2w0=(1, 8),
    c2w1=(9,),
    c2w2=(0, 10),
    qkvw0=(5,),
    first=(8, 9),
    c1=(1, 2, 4, 5, 6, 7, 10),
    c1w=(11, 12),
    mel=(2, 4, 7, 8, 9, 12),
    end=(
        10, 1, 5, 6, 11, 7, 9, 8, 12, 1, 10, 11, 5, 7, 6, 9, 8, 10, 12, 11, 5, 6, 7, 9, 8, 10,
        11, 6, 5, 12, 7, 8, 9, 10, 5, 6, 12, 7, 11, 7, 8, 9, 10, 5, 6, 8, 7, 9, 10, 5, 6,
    ),
)


def orders(name, bits):
    dims = dict(c=["c"], y=["y"], x=[0], z=list(range(1, min(2, bits))), w=list(range(2, min(3, bits))))
    found = []
    for spec in ORDERS[name]:
        groups = [tuple(dim for ch in group for dim in dims[ch]) for group in spec.split("-")]
        found.append([group for group in groups if group] + [(dim,) for dim in range(3, bits)])
    return found


def partners(bits):
    found = [("c",), ("y",), ("c", "y")] + [(dim,) for dim in range(bits)]
    for name in ORDERS:
        for order in orders(name, bits):
            for dims in order:
                found += [one for one in subsets(dims) if set(one) not in [set(x) for x in found]]
    return found


def layer(r, bits):
    T, D = r.stream.shape
    half, F2 = D // 2, r.down_l.shape[0]
    side = F2 // D
    mels, span = r.w1.shape[1], 4 * T
    net = Net(r, bits)
    c, m = net.c, net.m
    sub = c + m - 2 * c * m
    rows_of_mine = rows16(sub * T, T)

    r.melbuf[...] = jnp.zeros_like(r.melbuf)
    mel_own = net.here(r.mel.at[0], r.melbuf.at[0:mels, 128 : 128 + span])
    qkv_own = net.here(r.wqkv_l, r.wqkv.at[m])
    w2_own = net.here(r.w2_l, r.w2)
    own = [
        net.here(r.wo_l.at[0 : D // 4], r.wo.at[rows16(m * (D // 4), D // 4)]),
        net.here(r.wo_l.at[D // 4 : half], r.wo.at[rows16(half + m * (D // 4), D // 4)]),
        net.here(r.up_l, r.up.at[m]),
        net.here(r.down_l, r.down.at[rows16(m * F2, F2)]),
        net.here(r.cot.at[0, rows_of_mine], r.bg),
    ]
    r.vec_mine[...] = jnp.zeros_like(r.vec_mine)
    own_lanes = pl.ds(pl.multiple_of(m * half, 128), half)
    r.vec_mine[0:2, own_lanes] = r.qkvb[...].astype(F32)
    for k in range(side):
        r.vec_mine[pl.ds(2 + m * side + k, 1), :] = r.upb[k * D : (k + 1) * D].astype(F32).reshape(1, D)
    for k, n in enumerate(ROW_BIASES):
        r.vecs[k : k + 1, :] = getattr(r, n)[...].astype(F32).reshape(1, D)
    net.greet(partners(bits))
    vec_copy = net.send(r.vec_mine, r.vec_got, "y")
    mel_own.wait()
    src = pl.ds(pl.multiple_of(128 + (1 - c) * (span - 128), 128), 128)
    dst = pl.ds(pl.multiple_of(c * (span + 128), 128), 128)
    mel_rim = net.send(r.melbuf.at[0:mels, src], r.melbuf.at[0:mels, dst], "c")
    p = 4 * c + 2 * net.bit(0) + net.bit(1) if bits > 1 else 2 * c + net.bit(0)
    cuts = 8 if bits > 1 else 4

    def pass_on(of, at, count, dim):
        def cut(n, base):
            return rows16(base + at * (n // cuts), count * (n // cuts))

        wo = rows16(c * half + of * (D // 4) + (at - c * (cuts // 2)) * (half // cuts), count * (half // cuts))
        parts = [r.wo.at[wo], r.up.at[of, cut(D, 0)], r.down.at[cut(F2, of * F2)]]
        return [net.copy(x, x, dim) for x in parts]

    def pass_qkv(of, at, count, dim):
        rows = r.wqkv.at[of, :, rows16(at * (D // 4), count * (D // 4))]
        return net.copy(rows, rows, dim)

    two = 2 if bits > 1 else 1
    qkv_y = pass_qkv(m, 2 * c + net.bit(0), 1, "y")
    qkv_x = pass_qkv(1 - m, 2 * c + net.bit(0), 1, 0)
    qkv_c = pass_qkv(1 - m, 2 * c, 2, "c")
    ff_y = pass_on(m, p, 1, "y")
    ff_z = pass_on(1 - m, p, 1, 1) if bits > 1 else []
    ff_x = pass_on(1 - m, (p // two) * two, two, 0)
    ff_c = pass_on(1 - m, c * (cuts // 2), cuts // 2, "c")
    qkv_own.wait()
    qkv_y.start()
    wait_all(own)
    r.small[...] = jnp.zeros_like(r.small)
    stage_mel_rows(r, sub, mel_rim.wait)
    stage_first(r, jnp.logical_and(c == 0, m == 0))
    qkv_y.wait()
    qkv_x.start()
    start_all(ff_y)
    stage_odd(r)
    w2_own.wait()
    stage_second(r, quarter(net))
    vec_copy.wait()
    r.vecs[8:16, :] = r.vec_mine[...] + r.vec_got[...]
    qkv_x.wait()
    qkv_c.start()
    wait_all(ff_y)
    start_all(ff_z)

    def block(slot, part, h):
        return r.kv.at[rows16((3 * slot + part) * half + h * (half // 2), half // 2)]

    def project(h):
        far, near = [], []
        for part in (1, 2, 0):
            stage_qkv(r, part, h)
            if part:
                far.append(net.send(block(3 + c, part, h), block(0, part, h), "y"))
                far.append(net.send(block(4 - c, part, h), block(1, part, h), "c", "y"))
            near.append(net.send(block(4 - c, part, h), block(2, part, h), "c"))
        return far, near

    far_own, near_own = project(m)
    stage_mask(r, sub)
    add_small(r, DNB, col(r.bg[...].astype(F32)))
    r.normedt[...] = flip(r.normed[...])
    qkv_c.wait()
    far_other, near_other = project(1 - m)
    wait_all(near_own)
    heads = half // HEAD

    def flip_taps():
        for tap, to in zip((r.hp, r.he, r.ho), r.tapt):
            to[...] = flip(tap[...])

    hooks = {
        heads: [lambda: wait_all(near_other), lambda: wait_all(ff_z), lambda: start_all(ff_x)],
        2 * heads - 1: [flip_taps],
        2 * heads: [lambda: wait_all(far_own)],
        3 * heads: [lambda: wait_all(far_other), lambda: wait_all(ff_x), lambda: start_all(ff_c)],
    }
    attend(r, c, m, hooks)
    attend_end(r, 1)
    mix_c = net.send(r.mixb.at[half:D], r.mix_got, "c")
    attend_end(r, 0)
    stage_mid(r, c, mix_c.wait, lambda: wait_all(ff_c))

    def summed(n, part, rows, halves):
        views = [
            getattr(r, "g_" + n).at[part * rows * halves : (part + 1) * rows * halves],
            getattr(r, "got_%s%d" % (n, part)),
            getattr(r, "done_" + n).at[part * rows : (part + 1) * rows],
        ]
        return bucket_sum(net, *views, halves, orders(n, bits)[part])

    def leave(n, part):
        done = getattr(r, "done_" + n)
        size = half if n == "qkv" else D
        rows = done if n in ("out", "c1") else done.at[part * size : (part + 1) * size]
        if n == "qkv":
            pairs = [(rows.at[:, j * half : (j + 1) * half], r.qkv_o.at[part, j * half : (j + 1) * half]) for j in range(2)]
        elif n == "up":
            pairs = [(rows, r.up_o.at[:, part * D : (part + 1) * D])]
        elif n in ("down", "c2"):
            pairs = [(rows, getattr(r, n + "_o").at[part * D : (part + 1) * D])]
        else:
            pairs = [(done, getattr(r, n + "_o"))]
        return [net.here_later(src, dst) for src, dst in pairs]

    tracks, leaving = {}, {}
    for n, rows, halves, parts in (
        ("down", D, 2, side),
        ("up", D, 2, side),
        ("out", half, 2, 1),
        ("qkv", half, 2, 3),
        ("c2", D, 1, 3),
        ("c1", r.g_c1.shape[0], 1, 1),
    ):
        for part in range(parts):
            name = "%s%d" % (n, part)
            tracks[name] = summed(n, part, rows, halves)
            leaving[name] = leave(n, part)
            tracks[name].then(functools.partial(start_all, leaving[name]))
    tracks["vec0"] = small_sum(net, r.small, r.got_small, orders("vec", bits)[0])

    def acts_at(name):
        names = ["%s%d" % TRACKS[k] for k in SCHEDULE.get(name, ())]
        return [act for n in names if n in tracks for act in tracks[n].take()]

    def point(name):
        for act in acts_at(name):
            act()

    hooks = {}
    for step in range(2 * side):
        if step and step % 2 == 0:
            ready("down%d" % (step // 2 - 1), "up%d" % (step // 2 - 1))
        hooks[step] = acts_at("ff%d" % step)
    stage_ff(r, hooks)
    ready("down%d" % (side - 1), "up%d" % (side - 1))
    point("ffo")
    stage_mid_pull(r)
    enc = [
        net.copy(r.enc, r.enc_got, "y"),
        pltpu.make_async_copy(r.enc, r.enc_o.at[rows_of_mine], r.own.at[39]),
    ]
    start_all(enc)
    stage_do(r, c, False)
    do_c = net.send(r.dot_out, r.dot.at[half:D], "c")
    point("mid")
    stage_out_weights(r, c)
    ready("out0")
    point("out")
    stage_do(r, c, True)
    stage_diag(r, 0)
    for i, home in enumerate((3 + c, 2)):
        r.qrow[:, i * half : (i + 1) * half] = flip(r.kv[rows16(3 * home * half, half), :])
    r.dorow[:, 0:half] = flip(r.dot[0:half, :])
    do_c.wait()
    r.dorow[:, half:D] = flip(r.dot[half:D, :])
    stage_diag(r, 1)
    both = half * 2
    home_y = net.copy(r.dkv.at[0:both], r.from_y, "y")
    home_d = net.copy(r.dkv.at[both : 2 * both], r.from_d, "c", "y")
    home_c = net.copy(r.dkv.at[2 * both : 3 * both], r.from_c.at[half:], "c")
    hooks = {}

    def at_step(step, *acts):
        hooks.setdefault(step * heads // 4, []).extend(acts)

    at_step(4, home_y.start)
    at_step(8, home_d.start)
    at_step(12, home_c.start)
    for step in range(16):
        at_step(step, *acts_at("pull%d" % step))
    attend_pull(r, c, hooks)
    r.dq_out[...] = (r.dqt[half:D, :] * HEAD**-0.5).astype(BF)
    dq_c = net.send(r.dq_out, r.from_c.at[0:half], "c")
    r.dsum[rows16(c * half, half), :] = (r.dqt[0:half, :] * HEAD**-0.5).astype(BF)
    point("home")
    home_y.wait()
    home_d.wait()
    home_c.wait()

    def total(i, carry):
        for part in range(2):
            rows = rows16(part * half + i * 32, 32)
            mine = r.dkv[rows16(3 * both + part * half + i * 32, 32), :].astype(F32) + r.from_y[rows, :].astype(F32)
            r.dsum[rows16((1 + part) * D + c * half + i * 32, 32), :] = mine.astype(BF)
            other = r.from_c[rows16((1 + part) * half + i * 32, 32), :].astype(F32) + r.from_d[rows, :].astype(F32)
            r.dsum[rows16((1 + part) * D + (1 - c) * half + i * 32, 32), :] = other.astype(BF)
        return carry

    lax.fori_loop(0, half // 32, total, 0)

    def queries_came():
        dq_c.wait()
        r.dsum[rows16((1 - c) * half, half), :] = r.from_c[0:half, :]

    for part in (1, 2):
        stage_qkv_weights(r, part)
        ready("qkv%d" % part)
        point("qkvw%d" % part)
    stage_qkv_pull(r, queries_came)
    point("norm")
    stage_norm_pull(r)
    rim = [net.send(r.sg.at[0:16], r.slots.at[0, i], dim) for i, dim in enumerate(("c", "y"))]
    point("c2")
    for part in range(3):
        stage_conv2_weights(r, part)
        ready("c2%d" % part)
        point("c2w%d" % part)
    stage_qkv_weights(r, 0)
    ready("qkv0")
    point("qkvw0")

    def next_row():
        wait_all(rim)
        return pick_next(net, r.slots.at[0])

    stage_conv2_pull(r, next_row)
    point("first")
    stage_first_pull(r)
    rim = [net.send(r.fe.at[0:16], r.slots.at[1, i], dim) for i, dim in enumerate(("c", "y"))]
    rim += [net.send(r.fo.at[T - 16 : T], r.slots.at[2, i], dim) for i, dim in enumerate(("c", "y"))]
    point("c1")
    stage_conv1_weights(r)
    ready("c10", "vec0")
    point("c1w")
    wait_all(rim)
    stage_mel(r, pick_next(net, r.slots.at[1]), pick_prev(net, r.slots.at[2]))
    rows_of_yours = rows16((1 - sub) * T, T)
    mel_y = net.send(r.melg, r.melg_got, "y")
    point("mel")
    wait_all(enc)
    ends = [
        net.here(r.enc_got, r.enc_o.at[rows_of_yours]),
        net.here(r.melg, r.mel_o.at[rows_of_mine]),
    ]
    point("end")
    drain(*tracks.values())
    mel_y.wait()
    ends.append(net.here(r.melg_got, r.mel_o.at[rows_of_yours]))
    ends.append(net.here(r.small, r.small_o))
    wait_all(ends)
    for copies in leaving.values():
        wait_all(copies)


def run_layer(bits, near, far, outs, T, D, F2, lanes):
    half, H = D // 2, D // HEAD
    td, dt = (T, D), (D, T)
    buckets = dict(down=(D, 2, F2 // D), up=(D, 2, F2 // D), out=(half, 2, 1), qkv=(half, 2, 3), c2=(D, 1, 3), c1=(lanes, 1, 1))
    scratch = dict(
        melbuf=((128, 4 * T + 256), BF),
        mele=((T + 24, 128), F32),
        melo=((T + 24, 128), F32),
        xe=((T, 384), BF),
        xo=((T, 384), BF),
        w1p=((384, D), BF),
        w2=((3, D, D), BF),
        bg=(td, BF),
        wqkv=((2, 3, D, half), BF),
        wo=((D, D), BF),
        up=((2, D, F2), BF),
        down=((2 * F2, D), BF),
        vecs=((16, D), F32),
        vec_mine=((8, D), F32),
        vec_got=((8, D), F32),
        stream=(td, F32),
        he=(td, BF),
        ho=(td, BF),
        hp=(td, BF),
        dge=(td, F32),
        dgo=(td, F32),
        dg2=(td, F32),
        normed=(td, BF),
        kv=((15 * half, T), BF),
        mixt=(dt, F32),
        mixb=(dt, BF),
        normedt=(dt, BF),
        ntwot=(dt, BF),
        mix_got=((half, T), BF),
        dot=(dt, BF),
        dot_out=((half, T), BF),
        top=((H, 1, T), F32),
        total=((H, 1, T), F32),
        diag=((H, 1, T), F32),
        tmp=(td, F32),
        tmp2=(td, F32),
        shift=((T + 16, D), F32),
        wide=((T + 16, 128), F32),
        mid=(td, F32),
        ntwo=(td, BF),
        act=(td, BF),
        ing=(td, BF),
        ffo=(td, F32),
        ntg=(td, F32),
        attg=(td, BF),
        dqt=(dt, F32),
        dq_out=((half, T), BF),
        pb=((T, 2 * T), BF),
        ds=((T, 2 * T), BF),
        dkv=((8 * half, T), BF),
        from_y=((2 * half, T), BF),
        from_d=((2 * half, T), BF),
        from_c=((3 * half, T), BF),
        dsum=((3 * D, T), BF),
        enc_got=(td, BF),
        melg=((T, 256), BF),
        melg_got=((T, 256), BF),
        small=((16, D), F32),
        got_small=((sum(len(subsets(dims)) for dims in orders("vec", bits)[0]), 16, D), F32),
        slots=((3, 2, 16, D), BF),
    )
    alias = T == D
    for n, (rows, halves, parts) in buckets.items():
        if n not in ("qkv", "c2"):
            scratch["g_" + n] = ((rows * halves * parts, D), BF)
        for part in range(parts):
            need = sum_plan(rows, halves, orders(n, bits)[part])[1]
            scratch["got_%s%d" % (n, part)] = ((need, D), BF)
        scratch["done_" + n] = ((rows * parts, D), BF)
    if not alias:
        scratch.update({"tapt%d" % i: (dt, BF) for i in range(3)})
        scratch["turn"] = ((256, T), F32)
        scratch.update(g_qkv=((6 * half, D), BF), g_c2=((6 * half, D), BF))
    names = list(near) + list(far) + list(outs) + list(scratch) + ["send", "recv", "own"]

    def kernel(*refs):
        r = Box()
        for n, ref in zip(names, refs):
            setattr(r, n, ref)
        r.odd, r.smg, r.sg, r.fe, r.fo, r.enc = r.shift, r.mid, r.ntwo, r.act, r.ing, r.bg
        r.qrow, r.dorow = r.act, r.ing
        if alias:
            r.turn = r.tmp.at[0:256]
        r.tapt = (r.hp, r.he, r.ho) if alias else (r.tapt0, r.tapt1, r.tapt2)
        if alias:
            r.g_qkv, r.g_c2 = r.kv.at[0 : 6 * half], r.kv.at[6 * half : 12 * half]
        layer(r, bits)

    vmem, anywhere = pl.BlockSpec(memory_space=pltpu.VMEM), pl.BlockSpec(memory_space=pl.ANY)
    got = pl.pallas_call(
        kernel,
        name="layer",
        out_shape=[jax.ShapeDtypeStruct(*o) for o in outs.values()],
        in_specs=[vmem] * len(near) + [anywhere] * len(far),
        out_specs=[anywhere] * len(outs),
        scratch_shapes=[pltpu.VMEM(*s) for s in scratch.values()]
        + [pltpu.SemaphoreType.DMA((256,)), pltpu.SemaphoreType.DMA((256,)), pltpu.SemaphoreType.DMA((40,))],
        compiler_params=pltpu.CompilerParams(
            vmem_limit_bytes=VMEM_LIMIT, collective_id=1, has_side_effects=True
        ),
    )(*near.values(), *far.values())
    return dict(zip(outs, got))


def run_finish(got, mels, side):
    T2, D = got["enc_o"].shape
    half = D // 2
    ins = list(got)
    outs = dict(
        enc=((1, T2, D), BF),
        mel=((1, mels, 2 * T2), F32),
        c1=((3, mels, D), F32),
        c2=((3, D, D), F32),
        qkv=((3, D, half), F32),
        qkvb=((2, half), F32),
        out=((half, D), F32),
        up=((D, side * D), F32),
        upb=((side * D,), F32),
        down=((side * D, D), F32),
    )
    outs.update({n: ((D,), F32) for n in ROW_BIASES})

    big = ("mel", "c1", "c2", "qkv", "out", "up", "down")
    names = ins + list(outs) + ["in_" + n for n in ins] + ["out_" + n for n in big] + ["came", "went"]

    def kernel(*refs):
        r = Box()
        for n, ref in zip(names, refs):
            setattr(r, n, ref)
        m = lax.axis_index("mp")
        order = ["small_o", "enc_o", "down_o", "up_o", "qkv_o", "c2_o", "mel_o", "out_o", "c1_o"]
        loads = {}
        for k, n in enumerate(order):
            loads[n] = pltpu.make_async_copy(getattr(r, n), getattr(r, "in_" + n), r.came.at[k])
            loads[n].start()
        went = []

        def leave(n):
            copy = pltpu.make_async_copy(getattr(r, "out_" + n), getattr(r, n), r.went.at[len(went)])
            copy.start()
            went.append(copy)

        def cast(src, dst):
            def one(rows):
                dst[rows, :] = src[rows, :].astype(dst.dtype)

            rows_loop(src.shape[0], 256, one)

        loads["small_o"].wait()
        for k, n in enumerate(ROW_BIASES):
            getattr(r, n)[...] = r.in_small_o[k : k + 1, :].reshape(D)
        r.qkvb[...] = r.in_small_o[QB : QB + 2, pl.ds(pl.multiple_of(m * half, 128), half)]
        for k in range(side):
            r.upb[k * D : (k + 1) * D] = r.in_small_o[pl.ds(UPB + m * side + k, 1), :].reshape(D)
        loads["enc_o"].wait()
        copy = pltpu.make_async_copy(r.in_enc_o, r.enc.at[0], r.went.at[len(big)])
        copy.start()
        for n in ("down", "up"):
            loads[n + "_o"].wait()
            cast(getattr(r, "in_" + n + "_o"), getattr(r, "out_" + n))
            leave(n)
        loads["qkv_o"].wait()
        for o in range(3):
            cast(r.in_qkv_o.at[o], r.out_qkv.at[o])
        leave("qkv")
        loads["c2_o"].wait()
        for o in range(3):
            cast(r.in_c2_o.at[o * D : (o + 1) * D], r.out_c2.at[o])
        leave("c2")
        row = lax.broadcasted_iota(jnp.int32, (128, 256), 0)
        lane = lax.broadcasted_iota(jnp.int32, (128, 256), 1)
        even = jnp.where(lane == 2 * row, 1.0, 0.0).astype(BF)
        odd = jnp.where(lane == 2 * row + 1, 1.0, 0.0).astype(BF)
        loads["mel_o"].wait()
        for k in range(T2 // 128):
            rows = slice(k * 128, (k + 1) * 128)
            value = tn(r.in_mel_o[rows, 0:128], even) + tn(r.in_mel_o[rows, 128:256], odd)
            r.out_mel[0, :, k * 256 : (k + 1) * 256] = value[0:mels, :]
        leave("mel")
        loads["out_o"].wait()
        cast(r.in_out_o, r.out_out)
        leave("out")
        loads["c1_o"].wait()
        for o in range(3):
            r.out_c1[o] = r.in_c1_o[o * mels : (o + 1) * mels, :].astype(F32)
        leave("c1")
        copy.wait()
        wait_all(went)

    vmem, anywhere = pl.BlockSpec(memory_space=pltpu.VMEM), pl.BlockSpec(memory_space=pl.ANY)
    done = pl.pallas_call(
        kernel,
        name="finish",
        out_shape=[jax.ShapeDtypeStruct(*o) for o in outs.values()],
        in_specs=[anywhere] * len(ins),
        out_specs=[anywhere if n in big + ("enc",) else vmem for n in outs],
        scratch_shapes=[pltpu.VMEM(got[n].shape, got[n].dtype) for n in ins]
        + [pltpu.VMEM(*outs[n]) for n in big]
        + [pltpu.SemaphoreType.DMA((len(ins),)), pltpu.SemaphoreType.DMA((len(big) + 1,))],
        compiler_params=pltpu.CompilerParams(vmem_limit_bytes=VMEM_LIMIT),
    )(*got.values())
    return dict(zip(outs, done))


def sine_tables(frames, channels, fine):
    half_width = channels // 2
    rate = np.exp(-(math.log(10000.0) / (half_width - 1)) * np.arange(half_width))
    small = np.arange(fine)[:, None] * rate[None, :]
    large = np.arange(0, frames, fine)[:, None] * rate[None, :]
    table = dict(fine_s=np.sin(small), fine_c=np.cos(small), coarse_s=np.sin(large), coarse_c=np.cos(large))
    return {n: jnp.asarray(t, F32) for n, t in table.items()}


def on_device(
    mel_input,
    conv1_weight,
    conv1_bias,
    conv2_weight,
    conv2_bias,
    norm1_gain,
    norm1_bias,
    qkv_weight,
    qkv_bias,
    out_weight,
    out_bias,
    norm2_gain,
    norm2_bias,
    up_weight,
    up_bias,
    down_weight,
    down_bias,
    cotangent,
    speech_mask,
):
    mels = mel_input.shape[1]
    T, D = cotangent.shape[1] // 2, cotangent.shape[2]
    F2 = up_weight.shape[1]
    side, half = F2 // D, D // 2
    bits = (lax.axis_size("dp") - 1).bit_length()
    lanes = -(-3 * mels // 128) * 128
    near = dict(
        w1=conv1_weight,
        mask=speech_mask,
        qkvb=qkv_bias,
        upb=up_bias,
        c1b=conv1_bias,
        c2b=conv2_bias,
        n1g=norm1_gain,
        n1b=norm1_bias,
        oub=out_bias,
        n2g=norm2_gain,
        n2b=norm2_bias,
        dnb=down_bias,
    )
    near.update(sine_tables(4 * T, D, 32))
    got = run_layer(
        bits,
        near,
        dict(
            mel=mel_input,
            cot=cotangent,
            w2_l=conv2_weight,
            wqkv_l=qkv_weight,
            wo_l=out_weight,
            up_l=up_weight,
            down_l=down_weight,
        ),
        dict(
            enc_o=((2 * T, D), BF),
            mel_o=((2 * T, 256), BF),
            down_o=((F2, D), BF),
            up_o=((D, F2), BF),
            out_o=((half, D), BF),
            qkv_o=((3, D, half), BF),
            c2_o=((3 * D, D), BF),
            c1_o=((lanes, D), BF),
            small_o=((16, D), F32),
        ),
        T,
        D,
        F2,
        lanes,
    )
    done = run_finish(got, mels, side)
    names = ("enc", "mel", "c1", "c1b", "c2", "c2b", "n1g", "n1b", "qkv", "qkvb")
    names += ("out", "oub", "n2g", "n2b", "up", "upb", "down", "dnb")
    return tuple(done[n] for n in names)


def solution(mesh):
    placed = (
        P("dp", None, "seq"),
        P(),
        P(),
        P(),
        P(),
        P(),
        P(),
        P(None, None, "mp"),
        P(None, "mp"),
        P("mp", None),
        P(),
        P(),
        P(),
        P(None, "mp"),
        P("mp"),
        P("mp", None),
        P(),
        P("dp", "seq", None),
        P("dp", "seq"),
    )
    return jax.shard_map(
        on_device,
        mesh=mesh,
        in_specs=placed,
        out_specs=(
            P("dp", "seq", None),
            P("dp", None, "seq"),
            P(),
            P(),
            P(),
            P(),
            P(),
            P(),
            P(None, None, "mp"),
            P(None, "mp"),
            P("mp", None),
            P(),
            P(),
            P(),
            P(None, "mp"),
            P("mp"),
            P("mp", None),
            P(),
        ),
        check_vma=False,
    )
```

```python
import functools
import math

import jax
import jax.numpy as jnp
import numpy as np
from jax import lax
from jax.experimental import pallas as pl
from jax.experimental.pallas import tpu as pltpu
from jax.sharding import PartitionSpec as P

HEAD = 64
BF = jnp.bfloat16
F32 = jnp.float32
MESH = pl.DeviceIdType.MESH
VMEM_LIMIT = 62 * 1024 * 1024
C1B, C2B, N1G, N1B, OUB, N2G, N2B, DNB, QB, VB, UPB = range(11)


class Box:
    pass


def dot(a, b, ca, cb):
    return lax.dot_general(a, b, (((ca,), (cb,)), ((), ())), preferred_element_type=F32)


def nn(a, b):
    return dot(a, b, 1, 0)


def nt(a, b):
    return dot(a, b, 1, 1)


def tn(a, b):
    return dot(a, b, 0, 0)


def flip(value):
    return value.astype(F32).T.astype(BF)


def rows_loop(total, step, body, unroll=1):
    step = min(step, total)

    def one(i, carry):
        body(pl.ds(pl.multiple_of(i * step, step), step))
        return carry

    lax.fori_loop(0, total // step, one, 0, unroll=min(unroll, total // step))


def gelu_parts(v):
    t = 1.0 / (1.0 + (0.3275911 / math.sqrt(2.0)) * jnp.abs(v))
    e = jnp.exp(-0.5 * v * v)
    poly = 1.061405429 * t - 1.453152027
    poly = poly * t + 1.421413741
    poly = poly * t - 0.284496736
    poly = poly * t + 0.254829592
    tail = (0.5 * t) * poly * e
    return jnp.where(v >= 0, 1.0 - tail, tail), e * (1.0 / math.sqrt(2.0 * math.pi))


def gelu_both(v):
    cdf, pdf = gelu_parts(v)
    return v * cdf, cdf + v * pdf


def normal(x):
    center = x - jnp.mean(x, axis=-1, keepdims=True)
    spread = jnp.mean(center * center, axis=-1, keepdims=True)
    inv = lax.rsqrt(spread + 1e-05)
    return center * inv, inv


def normal_pull(gy, hat, inv):
    return inv * (
        gy
        - jnp.mean(gy, axis=-1, keepdims=True)
        - hat * jnp.mean(gy * hat, axis=-1, keepdims=True)
    )


def vec(r, i):
    return r.vecs[i : i + 1, :]


def add_small(r, i, value):
    r.small[i : i + 1, :] += value


def col(value):
    return jnp.sum(value, axis=0, keepdims=True)


def stage_mel_rows(r, sub, rim_came):
    T, D = r.stream.shape
    row = lax.broadcasted_iota(jnp.int32, (256, 256), 0)
    lane = lax.broadcasted_iota(jnp.int32, (256, 256), 1)
    pick = jnp.where(lane == 2 * (row % 128) + row // 128, 1.0, 0.0).astype(BF)
    base = sub * 2 * T

    def lanes(start, size):
        return r.melbuf[:, pl.ds(pl.multiple_of(base + start, 128), size)]

    row = lax.broadcasted_iota(jnp.int32, (16, 128), 0)
    lane = lax.broadcasted_iota(jnp.int32, (16, 128), 1)

    def select(at, to):
        return jnp.where(jnp.logical_and(row == to, lane == at), 1.0, 0.0).astype(BF)

    for k in range(T // 128):
        both = nt(pick, lanes(128 + 256 * k, 256))
        r.mele[8 + 128 * k : 136 + 128 * k, :] = both[0:128, :]
        r.melo[8 + 128 * k : 136 + 128 * k, :] = both[128:256, :]
    rim_came()
    before, after = lanes(0, 128), lanes(128 + 2 * T, 128)
    r.mele[0:8, :] = nt(select(126, 7), before)[0:8, :]
    r.melo[0:8, :] = nt(select(127, 7), before)[0:8, :]
    r.mele[T + 8 : T + 16, :] = nt(select(0, 0), after)[0:8, :]


def three(a, b, c):
    return jnp.concatenate([a, b, c], axis=1).astype(BF)


def stage_first(r, first):
    T, D = r.stream.shape
    for o in range(3):
        r.w1p[128 * o : 128 * o + r.w1.shape[1], :] = r.w1[o]
        r.w1p[128 * o + r.w1.shape[1] : 128 * (o + 1), :] = jnp.zeros((128 - r.w1.shape[1], D), BF)
    w1 = r.w1p[...]
    edge = nn(three(r.mele[0:16, :], r.melo[0:16, :], r.mele[1:17, :]), w1) + vec(r, C1B)
    edge = gelu_both(edge)[0] * jnp.where(first, 0.0, 1.0)
    r.odd[0:8, :] = edge[0:8, :]
    r.xe[...] = three(r.melo[7 : 7 + T, :], r.mele[8 : 8 + T, :], r.melo[8 : 8 + T, :])
    r.xo[...] = three(r.mele[8 : 8 + T, :], r.melo[8 : 8 + T, :], r.mele[9 : 9 + T, :])
    r.tmp[...] = nn(r.xe[...], w1)

    def even(rows):
        value, slope = gelu_both(r.tmp[rows, :] + vec(r, C1B))
        r.he[rows, :] = value.astype(BF)
        r.dge[rows, :] = slope

    rows_loop(T, 32, even)


def stage_odd(r):
    T, D = r.stream.shape
    r.tmp[...] = nn(r.xo[...], r.w1p[...])

    def odd(rows):
        value, slope = gelu_both(r.tmp[rows, :] + vec(r, C1B))
        r.ho[rows, :] = value.astype(BF)
        r.odd[pl.ds(pl.multiple_of(rows.start + 8, 8), rows.size), :] = value
        r.dgo[rows, :] = slope

    rows_loop(T, 32, odd)


def stage_second(r, place):
    T, D = r.stream.shape
    r.hp[...] = r.odd[7 : 7 + T, :].astype(BF)
    r.tmp[...] = nn(r.hp[...], r.w2[0]) + nn(r.he[...], r.w2[1]) + nn(r.ho[...], r.w2[2])
    fine = r.fine_s.shape[0]

    def second(rows):
        value, slope = gelu_both(r.tmp[rows, :] + vec(r, C2B))
        at = place * (T // fine) + rows.start // fine
        s0, c0 = r.coarse_s[pl.ds(at, 1), :], r.coarse_c[pl.ds(at, 1), :]
        s1, c1 = r.fine_s[...], r.fine_c[...]
        stream = value + jnp.concatenate([s0 * c1 + c0 * s1, c0 * c1 - s0 * s1], axis=1)
        r.dg2[rows, :] = slope
        r.stream[rows, :] = stream
        r.normed[rows, :] = (normal(stream)[0] * vec(r, N1G) + vec(r, N1B)).astype(BF)

    rows_loop(T, fine, second)


def stage_mask(r, sub):
    T, D = r.stream.shape
    row = r.mask[0:1, pl.ds(pl.multiple_of(sub * T, 128), T)].astype(F32)
    r.wide[0:T, :] = jnp.broadcast_to(row, (128, T)).T

    def one(rows):
        keep = r.wide[rows, :]
        keep = jnp.concatenate([keep] * (D // 128), axis=1)
        r.bg[rows, :] = (r.bg[rows, :].astype(F32) * keep).astype(BF)

    rows_loop(T, 32, one)


def stage_qkv(r, part, h):
    T, D = r.stream.shape
    half, qr = D // 2, D // 4
    bias, scale = ((QB, HEAD**-0.5), (None, 1.0), (VB, 1.0))[part]
    value = nn(r.normed[...], r.wqkv[h, part])
    if bias is not None:
        value = value + r.vecs[bias : bias + 1, pl.ds(pl.multiple_of(h * half, half), half)]
    value = (value.astype(BF).astype(F32) * scale).T.astype(BF)
    for k in range(2):
        r.kv[rows16((3 * (3 + k) + part) * half + h * qr, qr), :] = value[k * qr : (k + 1) * qr, :]


def at_head(start, h):
    return pl.ds(pl.multiple_of(start + h * HEAD, HEAD), HEAD)


def head_loop(steps, hooks, body):
    def one(step, carry):
        for at, todo in hooks.items():
            if not todo:
                continue

            @pl.when(step == at)
            def _(todo=todo):
                for act in todo:
                    act()

        body(step)
        return carry

    lax.fori_loop(0, steps, one, 0)


def attend(r, c, m, hooks):
    S, T = r.kv.shape[0] // 15, r.kv.shape[1]
    heads = S // HEAD
    r.top[...] = jnp.full(r.top.shape, -jnp.inf, F32)
    r.total[...] = jnp.zeros(r.total.shape, F32)
    r.mixt[...] = jnp.zeros(r.mixt.shape, F32)

    def body(step):
        quarter, u, pair = step // heads, step % heads, heads // 2
        g = 2 * (quarter // 2) + u // pair
        h = (m + (1 - 2 * m) * ((quarter + 1) // 2 % 2)) * pair + u % pair
        own = (3 - g) // 3
        slot = own * (3 + c) + (1 - own) * ((g + 1) % 3)
        k = r.kv[at_head((3 * slot + 1) * S, h), :]
        v = r.kv[at_head((3 * slot + 2) * S, h), :]
        turned = flip(k)
        for i, home in enumerate((3 + c, 2)):
            rows, at = at_head(i * S, h), i * heads + h
            for start in range(0, T, 256):
                cols = slice(start, start + 256)
                s = nn(turned, r.kv[at_head(3 * home * S, h), cols])
                before = r.top[at, :, cols]
                top = jnp.maximum(before, jnp.max(s, axis=0, keepdims=True))
                p = jnp.exp(s - top)
                keep = jnp.exp(before - top)
                r.top[at, :, cols] = top
                r.total[at, :, cols] = keep * r.total[at, :, cols] + jnp.sum(p, axis=0, keepdims=True)
                r.mixt[rows, cols] = keep * r.mixt[rows, cols] + nn(v, p.astype(BF))

    head_loop(4 * heads, hooks, body)


def attend_end(r, i):
    S = r.kv.shape[0] // 15
    heads = S // HEAD

    def one(h, carry):
        rows = at_head(i * S, h)
        total = r.total[i * heads + h]
        value = r.mixt[rows, :] * (1.0 / total)
        r.mixt[rows, :] = value
        r.mixb[rows, :] = value.astype(BF)
        r.top[i * heads + h] = r.top[i * heads + h] + jnp.log(total)
        return carry

    lax.fori_loop(0, heads, one, 0)


def stage_mid(r, c, mix_came, weights_came):
    T, D = r.stream.shape
    half = D // 2
    weights_came()
    r.tmp[...] = tn(r.mixb[0:half, :], r.wo[rows16(c * half, half), :])
    mix_came()
    r.tmp[...] += tn(r.mix_got[...], r.wo[rows16((1 - c) * half, half), :])

    def one(rows):
        mid = r.stream[rows, :] + r.tmp[rows, :] + vec(r, OUB)
        r.mid[rows, :] = mid
        r.ntwo[rows, :] = (normal(mid)[0] * vec(r, N2G) + vec(r, N2B)).astype(BF)

    rows_loop(T, 32, one)


def stage_ff(r, hooks):
    T, D = r.stream.shape
    side = r.up.shape[2] // D
    parts, width = 2 * side, D

    def chunk(t):
        into, at = t % 2, t // 2
        j = into * side + at
        up = r.up[into, :, pl.ds(pl.multiple_of(at * D, D), D)]
        down = r.down[pl.ds(pl.multiple_of(j * D, D), D), :]
        r.tmp[...] = nn(r.ntwo[...], up)
        r.tmp2[...] = nt(r.bg[...], down)
        bias = r.vecs[pl.ds(UPB + j, 1), :]

        def one(i, acc):
            rows = pl.ds(pl.multiple_of(i * 32, 32), 32)
            value, slope = gelu_both(r.tmp[rows, :] + bias)
            r.act[rows, :] = value.astype(BF)
            grad = (r.tmp2[rows, :] * slope).astype(BF)
            r.ing[rows, :] = grad
            return acc + col(grad.astype(F32))

        r.small[pl.ds(UPB + j, 1), :] = lax.fori_loop(0, T // 32, one, jnp.zeros((1, width), F32))
        act = r.act[...]
        ing = r.ing[...]
        out = nn(act, down)
        back = nt(ing, up)

        r.ffo[...] += out
        r.ntg[...] += back
        rows = pl.ds(pl.multiple_of(t * D, D), D)
        r.g_down[rows, :] = tn(act, r.bg[...]).astype(BF)
        r.g_up[rows, :] = nn(r.ntwot[...], ing).astype(BF)

    r.ntwot[...] = flip(r.ntwo[...])
    r.ffo[...] = jnp.zeros_like(r.ffo)
    r.ntg[...] = jnp.zeros_like(r.ntg)
    head_loop(parts, hooks, chunk)


def stage_mid_pull(r):
    T, D = r.stream.shape

    def one(i, accs):
        rows = pl.ds(pl.multiple_of(i * 32, 32), 32)
        mid = r.mid[rows, :]
        enc = (mid + r.ffo[rows, :] + vec(r, DNB)).astype(BF)
        hat, inv = normal(mid)
        grad = r.ntg[rows, :]
        smg = r.bg[rows, :].astype(F32) + normal_pull(grad * vec(r, N2G), hat, inv)
        r.enc[rows, :] = enc
        r.smg[rows, :] = smg
        attg = smg.astype(BF)
        r.attg[rows, :] = attg
        return accs[0] + col(grad * hat), accs[1] + col(grad), accs[2] + col(attg.astype(F32))

    zero = jnp.zeros((1, D), F32)
    gain, bias, out_bias = lax.fori_loop(0, T // 32, one, (zero, zero, zero))
    add_small(r, N2G, gain)
    add_small(r, N2B, bias)
    add_small(r, OUB, out_bias)


def stage_do(r, c, own):
    half = r.attg.shape[1] // 2
    k = c if own else 1 - c
    value = nt(r.wo[rows16(k * half, half), :], r.attg[...]).astype(BF)
    if own:
        r.dot[0:half, :] = value
    else:
        r.dot_out[...] = value


def stage_out_weights(r, c):
    D = r.attg.shape[1]
    half, qr = D // 2, D // 4
    for k, mix in ((c, r.mixb[0:half, :]), (1 - c, r.mix_got[...])):
        value = nn(mix, r.attg[...]).astype(BF)
        for h in range(2):
            r.g_out[rows16(h * half + k * qr, qr), :] = value[h * qr : (h + 1) * qr, :]


def stage_diag(r, i):
    S = r.kv.shape[0] // 15
    heads = S // HEAD

    def one(h, carry):
        rows = at_head(i * S, h)
        value = r.dot[rows, :].astype(F32) * r.mixt[rows, :]
        r.diag[i * heads + h] = jnp.sum(value, axis=0, keepdims=True)
        return carry

    lax.fori_loop(0, heads, one, 0)


def attend_pull(r, c, hooks):
    S, T = r.kv.shape[0] // 15, r.kv.shape[1]
    heads = S // HEAD
    r.dqt[...] = jnp.zeros(r.dqt.shape, F32)

    def body(step):
        g, h = step // heads, step % heads
        slot = g + (g // 3) * c
        k = r.kv[at_head((3 * slot + 1) * S, h), :]
        v = r.kv[at_head((3 * slot + 2) * S, h), :]
        kt, vt = flip(k), flip(v)
        for i, home in enumerate((3 + c, 2)):
            at = i * heads + h
            for start in range(0, T, 256):
                cols, to = slice(start, start + 256), slice(i * T + start, i * T + start + 256)
                p = jnp.exp(nn(kt, r.kv[at_head(3 * home * S, h), cols]) - r.top[at, :, cols])
                r.pb[:, to] = p.astype(BF)
                dp = nn(vt, r.dot[at_head(i * S, h), cols])
                r.ds[:, to] = (p * (dp - r.diag[at, :, cols])).astype(BF)
        pair = [pl.ds(pl.multiple_of(i * S + h // 2 * 128, 128), 128) for i in range(2)]
        for part, left, right in ((0, r.ds, r.qrow), (1, r.pb, r.dorow)):
            r.turn[128 * part : 128 * (part + 1), :] = sum(
                nn(left[:, i * T : (i + 1) * T], right[:, pair[i]]) for i in range(2)
            ).T
            value = r.turn[pl.ds(pl.multiple_of(128 * part + h % 2 * HEAD, HEAD), HEAD), :]
            r.dkv[at_head((2 * g + part) * S, h), :] = value.astype(BF)
        dq = nn(k, r.ds[...])
        for i in range(2):
            r.dqt[at_head(i * S, h), :] += dq[:, i * T : (i + 1) * T]

    head_loop(4 * heads, hooks, body)


def piece_of(r, part, h):
    D, qr = r.attg.shape[1], r.attg.shape[1] // 4
    at = part * D + h * qr
    return jnp.concatenate([r.dsum[at : at + qr, :], r.dsum[at + 2 * qr : at + 3 * qr, :]], axis=0)


def stage_qkv_weights(r, part):
    T, D = r.stream.shape
    half = D // 2
    ones = jnp.ones((8, T), BF)
    for h in range(2):
        piece = piece_of(r, part, h)
        if part != 1:
            row = QB if part == 0 else VB
            r.small[row : row + 1, h * half : (h + 1) * half] = nt(ones, piece)[0:1, :]
        grad = nt(r.normedt[...], piece).astype(BF)
        at = (2 * part + h) * half
        r.g_qkv[at : at + half, 0:half] = grad[0:half, :]
        r.g_qkv[at : at + half, half:D] = grad[half:D, :]


def stage_qkv_pull(r, queries_came):
    T, D = r.stream.shape
    total = None
    for part in (1, 2, 0):
        if part == 0:
            queries_came()
        for h in range(2):
            back = nn(r.wqkv[h, part], piece_of(r, part, h))
            total = back if total is None else total + back
    r.tmp[...] = total.T


def stage_norm_pull(r):
    T, D = r.stream.shape

    def one(i, accs):
        rows = pl.ds(pl.multiple_of(i * 32, 32), 32)
        hat, inv = normal(r.stream[rows, :])
        grad = r.tmp[rows, :]
        back = r.smg[rows, :] + normal_pull(grad * vec(r, N1G), hat, inv)
        sg = (back * r.dg2[rows, :]).astype(BF)
        r.sg[rows, :] = sg
        return accs[0] + col(grad * hat), accs[1] + col(grad), accs[2] + col(sg.astype(F32))

    zero = jnp.zeros((1, D), F32)
    gain, bias, c2b = lax.fori_loop(0, T // 32, one, (zero, zero, zero))
    add_small(r, N1G, gain)
    add_small(r, N1B, bias)
    add_small(r, C2B, c2b)


def stage_conv2_pull(r, next_row):
    T, D = r.stream.shape
    sg = r.sg[...]
    r.shift[0:T, :] = nt(sg, r.w2[0])
    r.tmp[...] = nt(sg, r.w2[1])
    r.shift[T : T + 16, :] = nt(next_row(), r.w2[0])
    r.tmp2[...] = nt(sg, r.w2[2]) + r.shift[1 : T + 1, :]


def stage_first_pull(r):
    T, D = r.stream.shape

    def one(i, acc):
        rows = pl.ds(pl.multiple_of(i * 32, 32), 32)
        even = (r.tmp[rows, :] * r.dge[rows, :]).astype(BF)
        odd = (r.tmp2[rows, :] * r.dgo[rows, :]).astype(BF)
        r.fe[rows, :] = even
        r.fo[rows, :] = odd
        return acc + col(even.astype(F32)) + col(odd.astype(F32))

    add_small(r, C1B, lax.fori_loop(0, T // 32, one, jnp.zeros((1, D), F32)))


def stage_conv2_weights(r, i):
    D = r.stream.shape[1]
    r.g_c2[i * D : (i + 1) * D, :] = nn(r.tapt[i][...], r.sg[...]).astype(BF)


def stage_conv1_weights(r):
    value = (tn(r.xe[...], r.fe[...]) + tn(r.xo[...], r.fo[...])).astype(BF)
    mels = r.w1.shape[1]
    for o in range(3):
        r.g_c1[mels * o : mels * (o + 1), :] = value[128 * o : 128 * o + mels, :]
    r.g_c1[3 * mels :, :] = jnp.zeros((r.g_c1.shape[0] - 3 * mels, r.g_c1.shape[1]), BF)


def stage_mel(r, next_row, prev_row):
    T, D = r.stream.shape
    fe, fo = r.fe[...], r.fo[...]
    w = [r.w1p[128 * o : 128 * (o + 1), :] for o in range(3)]
    r.wide[16 : 16 + T, :] = nt(fo, w[2])
    r.wide[0:16, :] = nt(prev_row, w[2])
    r.melg[:, 0:128] = (nt(fe, w[1]) + nt(fo, w[0]) + r.wide[15 : 15 + T, :]).astype(BF)
    r.wide[0:T, :] = nt(fe, w[0])
    r.wide[T : T + 16, :] = nt(next_row, w[0])
    r.melg[:, 128:256] = (nt(fe, w[2]) + nt(fo, w[1]) + r.wide[1 : 1 + T, :]).astype(BF)


class Net:
    def __init__(self, r, bits):
        self.r, self.bits, self.used, self.used_here = r, bits, 0, 0
        self.d, self.c, self.m = (lax.axis_index(n) for n in ("dp", "seq", "mp"))

    def bit(self, dim):
        if dim == "c":
            return self.c
        if dim == "y":
            return self.m
        return (self.d // (1 << dim)) % 2

    def peer(self, dims):
        d = self.d
        for k in dims:
            if k not in ("c", "y"):
                d = d + (1 << k) - 2 * (1 << k) * self.bit(k)
        return (
            d,
            1 - self.c if "c" in dims else self.c,
            1 - self.m if "y" in dims else self.m,
        )

    def greet(self, partners):
        barrier = pltpu.get_barrier_semaphore()
        for dims in partners:
            pl.semaphore_signal(barrier, inc=1, device_id=self.peer(dims), device_id_type=MESH)
        pl.semaphore_wait(barrier, len(partners))

    def copy(self, src, dst, *dims):
        i = self.used
        self.used += 1
        return pltpu.make_async_remote_copy(
            src_ref=src,
            dst_ref=dst,
            send_sem=self.r.send.at[i],
            recv_sem=self.r.recv.at[i],
            device_id=self.peer(dims),
            device_id_type=MESH,
        )

    def send(self, src, dst, *dims):
        copy = self.copy(src, dst, *dims)
        copy.start()
        return copy

    def here_later(self, src, dst):
        i = self.used_here
        self.used_here += 1
        return pltpu.make_async_copy(src, dst, self.r.own.at[i])

    def here(self, src, dst):
        copy = self.here_later(src, dst)
        copy.start()
        return copy


def start_all(copies):
    for copy in copies:
        copy.start()


def wait_all(copies):
    for copy in copies:
        copy.wait()


def rows16(start, size):
    return pl.ds(pl.multiple_of(start, 16), size)


def subsets(dims):
    found = [()]
    for dim in dims:
        found += [one + (dim,) for one in found]
    return found[1:]


def sum_plan(rows, halves, order):
    steps, need = [], 0
    for dims in order:
        by_half = halves == 2 and "y" in dims
        cutting = [dim for dim in dims if not (by_half and dim == "y")]
        if rows % (16 << len(cutting)):
            cutting = []
        rows >>= len(cutting)
        if by_half:
            halves = 1
        steps.append((dims, cutting, rows, halves, by_half))
        need += rows * halves * len(subsets(dims))
    return steps, need


class Track:
    def __init__(self, acts):
        self.acts = list(acts)

    def take(self):
        return [self.acts.pop(0)] if self.acts else []

    def then(self, more):
        last = self.acts.pop()

        def act():
            last()
            more()

        self.acts.append(act)


def bucket_sum(net, g, got, done, halves, order):
    R = g.shape[0] // halves
    lo, rows, at, bases = 0, R, 0, [h * R for h in range(halves)]
    acts, back, end = [], [], None

    def start_after(end, copies):
        def act():
            if end is not None:
                end()
            for copy in copies:
                copy.start()

        return act

    def adder(copies, places, n):
        step = 64 if n % 64 == 0 else 32 if n % 32 == 0 else 16

        def end():
            wait_all(copies)
            for to, ofs in places:

                def add(k, carry, to=to, ofs=ofs):
                    mine = rows16(to + k * step, step)
                    value = g[mine, :].astype(F32)
                    for of in ofs:
                        value = value + got[rows16(of + k * step, step), :].astype(F32)
                    g[mine, :] = value.astype(BF)
                    return carry

                lax.fori_loop(0, n // step, add, 0)

        return end

    for dims, cutting, n, _, by_half in sum_plan(R, halves, order)[0]:

        def part_of(other):
            start = lo
            for i, dim in enumerate(reversed(cutting)):
                b = net.bit(dim)
                start = start + (1 - b if dim in other else b) * (n << i)
            return start

        keep = part_of(())
        if by_half:
            bases = [net.m * R]
        copies, ofs = [], [[] for _ in bases]
        for other in subsets(dims):
            sources = [(1 - net.m) * R] if by_half and "y" in other else bases
            for i, base in enumerate(sources):
                src = g.at[rows16(base + part_of(other), n)]
                copies.append(net.copy(src, got.at[rows16(at, n)], *other))
                ofs[i].append(at)
                at += n
        acts.append(start_after(end, copies))
        end = adder(copies, [(base + keep, of) for base, of in zip(bases, ofs)], n)
        if cutting:
            back.append((cutting, n, lo))
        lo, rows = keep, n

    def settle(end=end, lo=lo, base=bases[0], rows=rows):
        end()
        for k in range(rows // 16):
            done[rows16(lo + 16 * k, 16), :] = g[rows16(base + lo + 16 * k, 16), :]

    end = settle
    for cutting, n, before in reversed(back):
        part = rows16(lo, n)
        copies = [net.copy(done.at[part], done.at[part], *other) for other in subsets(cutting)]
        acts.append(start_after(end, copies))
        end = functools.partial(wait_all, copies)
        lo = before
    return Track(acts + [end])


def small_sum(net, value, slots, order):
    acts, end, at = [], None, 0
    for dims in order:
        copies = [net.copy(value, slots.at[at + i], *other) for i, other in enumerate(subsets(dims))]

        def act(end=end, copies=copies):
            if end is not None:
                end()
            start_all(copies)

        def end(copies=copies, at=at):
            wait_all(copies)
            total = value[...]
            for i in range(len(copies)):
                total = total + slots[at + i]
            value[...] = total

        at += len(copies)
        acts.append(act)
    return Track(acts + [end])


def ready(*names):
    pass


def advance(*sums):
    for one in sums:
        for act in one.take():
            act()


def drain(*sums):
    while any(one.acts for one in sums):
        advance(*sums)


def quarter(net):
    return 2 * net.c + net.c + net.m - 2 * net.c * net.m


def choose(slots, by_core, by_y):
    core = jnp.where(by_core, 1.0, 0.0)
    y = jnp.where(by_y, 1.0, 0.0)
    return (slots[0].astype(F32) * core + slots[1].astype(F32) * y).astype(BF)


def pick_next(net, slots):
    q = quarter(net)
    return choose(slots, q == 1, q % 2 == 0)


def pick_prev(net, slots):
    q = quarter(net)
    return choose(slots, q == 2, q % 2 == 1)


ROW_BIASES = ("c1b", "c2b", "n1g", "n1b", "oub", "n2g", "n2b", "dnb")


ORDERS = dict(
    down=("c-y-z-xw", "c-x-z-y-w"),
    up=("c-w-x-zy", "c-xz-w-y"),
    out=("c-x-w-zy",),
    qkv=("c-w-yx-z", "c-y-z-w-x", "x-c-z-y-w"),
    c2=("c-z-yx-w", "c-xy-z-w", "c-xy-w-z"),
    c1=("cy-xz-w",),
    vec=("c-y-w-z-x",),
)
TRACKS = (
    ("down", 0), ("down", 1), ("up", 0), ("up", 1), ("out", 0), ("qkv", 0), ("qkv", 1), ("qkv", 2),
    ("c2", 0), ("c2", 1), ("c2", 2), ("c1", 0), ("vec", 0),
)
SCHEDULE = dict(
    ff2=(0, 2),
    ffo=(0, 1, 2, 3),
    out=(1, 3, 4),
    pull1=(4,),
    pull2=(0,),
    pull5=(2, 3),
    pull6=(0, 1, 4),
    pull7=(2, 3),
    pull10=(0, 3, 4),
    pull11=(1, 2),
    pull13=(0, 3, 4),
    pull14=(1, 2),
    pull15=(4,),
    qkvw1=(1, 2, 3, 6),
    qkvw2=(7,),
    norm=(0, 4),
    c2=(3, 6),
    c2w0=(1, 8),
    c2w1=(9,),
    c2w2=(0, 10),
    qkvw0=(5,),
    first=(8, 9),
    c1=(1, 2, 4, 5, 6, 7, 10),
    c1w=(11, 12),
    mel=(2, 4, 7, 8, 9, 12),
    end=(
        10, 1, 5, 6, 11, 7, 9, 8, 12, 1, 10, 11, 5, 7, 6, 9, 8, 10, 12, 11, 5, 6, 7, 9, 8, 10,
        11, 6, 5, 12, 7, 8, 9, 10, 5, 6, 12, 7, 11, 7, 8, 9, 10, 5, 6, 8, 7, 9, 10, 5, 6,
    ),
)


def orders(name, bits):
    dims = dict(c=["c"], y=["y"], x=[0], z=list(range(1, min(2, bits))), w=list(range(2, min(3, bits))))
    found = []
    for spec in ORDERS[name]:
        groups = [tuple(dim for ch in group for dim in dims[ch]) for group in spec.split("-")]
        found.append([group for group in groups if group] + [(dim,) for dim in range(3, bits)])
    return found


def partners(bits):
    found = [("c",), ("y",), ("c", "y")] + [(dim,) for dim in range(bits)]
    for name in ORDERS:
        for order in orders(name, bits):
            for dims in order:
                found += [one for one in subsets(dims) if set(one) not in [set(x) for x in found]]
    return found


def layer(r, bits):
    T, D = r.stream.shape
    half, F2 = D // 2, r.down_l.shape[0]
    side = F2 // D
    mels, span = r.w1.shape[1], 4 * T
    net = Net(r, bits)
    c, m = net.c, net.m
    sub = c + m - 2 * c * m
    rows_of_mine = rows16(sub * T, T)

    r.melbuf[...] = jnp.zeros_like(r.melbuf)
    mel_own = net.here(r.mel.at[0], r.melbuf.at[0:mels, 128 : 128 + span])
    qkv_own = net.here(r.wqkv_l, r.wqkv.at[m])
    w2_own = net.here(r.w2_l, r.w2)
    own = [
        net.here(r.wo_l.at[0 : D // 4], r.wo.at[rows16(m * (D // 4), D // 4)]),
        net.here(r.wo_l.at[D // 4 : half], r.wo.at[rows16(half + m * (D // 4), D // 4)]),
        net.here(r.up_l, r.up.at[m]),
        net.here(r.down_l, r.down.at[rows16(m * F2, F2)]),
        net.here(r.cot.at[0, rows_of_mine], r.bg),
    ]
    r.vec_mine[...] = jnp.zeros_like(r.vec_mine)
    own_lanes = pl.ds(pl.multiple_of(m * half, 128), half)
    r.vec_mine[0:2, own_lanes] = r.qkvb[...].astype(F32)
    for k in range(side):
        r.vec_mine[pl.ds(2 + m * side + k, 1), :] = r.upb[k * D : (k + 1) * D].astype(F32).reshape(1, D)
    for k, n in enumerate(ROW_BIASES):
        r.vecs[k : k + 1, :] = getattr(r, n)[...].astype(F32).reshape(1, D)
    net.greet(partners(bits))
    vec_copy = net.send(r.vec_mine, r.vec_got, "y")
    mel_own.wait()
    src = pl.ds(pl.multiple_of(128 + (1 - c) * (span - 128), 128), 128)
    dst = pl.ds(pl.multiple_of(c * (span + 128), 128), 128)
    mel_rim = net.send(r.melbuf.at[0:mels, src], r.melbuf.at[0:mels, dst], "c")
    p = 4 * c + 2 * net.bit(0) + net.bit(1) if bits > 1 else 2 * c + net.bit(0)
    cuts = 8 if bits > 1 else 4

    def pass_on(of, at, count, dim):
        def cut(n, base):
            return rows16(base + at * (n // cuts), count * (n // cuts))

        wo = rows16(c * half + of * (D // 4) + (at - c * (cuts // 2)) * (half // cuts), count * (half // cuts))
        parts = [r.wo.at[wo], r.up.at[of, cut(D, 0)], r.down.at[cut(F2, of * F2)]]
        return [net.copy(x, x, dim) for x in parts]

    def pass_qkv(of, at, count, dim):
        rows = r.wqkv.at[of, :, rows16(at * (D // 4), count * (D // 4))]
        return net.copy(rows, rows, dim)

    two = 2 if bits > 1 else 1
    qkv_y = pass_qkv(m, 2 * c + net.bit(0), 1, "y")
    qkv_x = pass_qkv(1 - m, 2 * c + net.bit(0), 1, 0)
    qkv_c = pass_qkv(1 - m, 2 * c, 2, "c")
    ff_y = pass_on(m, p, 1, "y")
    ff_z = pass_on(1 - m, p, 1, 1) if bits > 1 else []
    ff_x = pass_on(1 - m, (p // two) * two, two, 0)
    ff_c = pass_on(1 - m, c * (cuts // 2), cuts // 2, "c")
    qkv_own.wait()
    qkv_y.start()
    wait_all(own)
    r.small[...] = jnp.zeros_like(r.small)
    stage_mel_rows(r, sub, mel_rim.wait)
    stage_first(r, jnp.logical_and(c == 0, m == 0))
    qkv_y.wait()
    qkv_x.start()
    start_all(ff_y)
    stage_odd(r)
    w2_own.wait()
    stage_second(r, quarter(net))
    vec_copy.wait()
    r.vecs[8:16, :] = r.vec_mine[...] + r.vec_got[...]
    qkv_x.wait()
    qkv_c.start()
    wait_all(ff_y)
    start_all(ff_z)

    def block(slot, part, h):
        return r.kv.at[rows16((3 * slot + part) * half + h * (half // 2), half // 2)]

    def project(h):
        far, near = [], []
        for part in (1, 2, 0):
            stage_qkv(r, part, h)
            if part:
                far.append(net.send(block(3 + c, part, h), block(0, part, h), "y"))
                far.append(net.send(block(4 - c, part, h), block(1, part, h), "c", "y"))
            near.append(net.send(block(4 - c, part, h), block(2, part, h), "c"))
        return far, near

    far_own, near_own = project(m)
    stage_mask(r, sub)
    add_small(r, DNB, col(r.bg[...].astype(F32)))
    r.normedt[...] = flip(r.normed[...])
    qkv_c.wait()
    far_other, near_other = project(1 - m)
    wait_all(near_own)
    heads = half // HEAD

    def flip_taps():
        for tap, to in zip((r.hp, r.he, r.ho), r.tapt):
            to[...] = flip(tap[...])

    hooks = {
        heads: [lambda: wait_all(near_other), lambda: wait_all(ff_z), lambda: start_all(ff_x)],
        2 * heads - 1: [flip_taps],
        2 * heads: [lambda: wait_all(far_own)],
        3 * heads: [lambda: wait_all(far_other), lambda: wait_all(ff_x), lambda: start_all(ff_c)],
    }
    attend(r, c, m, hooks)
    attend_end(r, 1)
    mix_c = net.send(r.mixb.at[half:D], r.mix_got, "c")
    attend_end(r, 0)
    stage_mid(r, c, mix_c.wait, lambda: wait_all(ff_c))

    def summed(n, part, rows, halves):
        views = [
            getattr(r, "g_" + n).at[part * rows * halves : (part + 1) * rows * halves],
            getattr(r, "got_%s%d" % (n, part)),
            getattr(r, "done_" + n).at[part * rows : (part + 1) * rows],
        ]
        return bucket_sum(net, *views, halves, orders(n, bits)[part])

    def leave(n, part):
        done = getattr(r, "done_" + n)
        size = half if n == "qkv" else D
        rows = done if n in ("out", "c1") else done.at[part * size : (part + 1) * size]
        if n == "qkv":
            pairs = [(rows.at[:, j * half : (j + 1) * half], r.qkv_o.at[part, j * half : (j + 1) * half]) for j in range(2)]
        elif n == "up":
            pairs = [(rows, r.up_o.at[:, part * D : (part + 1) * D])]
        elif n in ("down", "c2"):
            pairs = [(rows, getattr(r, n + "_o").at[part * D : (part + 1) * D])]
        else:
            pairs = [(done, getattr(r, n + "_o"))]
        return [net.here_later(src, dst) for src, dst in pairs]

    tracks, leaving = {}, {}
    for n, rows, halves, parts in (
        ("down", D, 2, side),
        ("up", D, 2, side),
        ("out", half, 2, 1),
        ("qkv", half, 2, 3),
        ("c2", D, 1, 3),
        ("c1", r.g_c1.shape[0], 1, 1),
    ):
        for part in range(parts):
            name = "%s%d" % (n, part)
            tracks[name] = summed(n, part, rows, halves)
            leaving[name] = leave(n, part)
            tracks[name].then(functools.partial(start_all, leaving[name]))
    tracks["vec0"] = small_sum(net, r.small, r.got_small, orders("vec", bits)[0])

    def acts_at(name):
        names = ["%s%d" % TRACKS[k] for k in SCHEDULE.get(name, ())]
        return [act for n in names if n in tracks for act in tracks[n].take()]

    def point(name):
        for act in acts_at(name):
            act()

    hooks = {}
    for step in range(2 * side):
        if step and step % 2 == 0:
            ready("down%d" % (step // 2 - 1), "up%d" % (step // 2 - 1))
        hooks[step] = acts_at("ff%d" % step)
    stage_ff(r, hooks)
    ready("down%d" % (side - 1), "up%d" % (side - 1))
    point("ffo")
    stage_mid_pull(r)
    enc = [
        net.copy(r.enc, r.enc_got, "y"),
        pltpu.make_async_copy(r.enc, r.enc_o.at[rows_of_mine], r.own.at[39]),
    ]
    start_all(enc)
    stage_do(r, c, False)
    do_c = net.send(r.dot_out, r.dot.at[half:D], "c")
    point("mid")
    stage_out_weights(r, c)
    ready("out0")
    point("out")
    stage_do(r, c, True)
    stage_diag(r, 0)
    for i, home in enumerate((3 + c, 2)):
        r.qrow[:, i * half : (i + 1) * half] = flip(r.kv[rows16(3 * home * half, half), :])
    r.dorow[:, 0:half] = flip(r.dot[0:half, :])
    do_c.wait()
    r.dorow[:, half:D] = flip(r.dot[half:D, :])
    stage_diag(r, 1)
    both = half * 2
    home_y = net.copy(r.dkv.at[0:both], r.from_y, "y")
    home_d = net.copy(r.dkv.at[both : 2 * both], r.from_d, "c", "y")
    home_c = net.copy(r.dkv.at[2 * both : 3 * both], r.from_c.at[half:], "c")
    hooks = {}

    def at_step(step, *acts):
        hooks.setdefault(step * heads // 4, []).extend(acts)

    at_step(4, home_y.start)
    at_step(8, home_d.start)
    at_step(12, home_c.start)
    for step in range(16):
        at_step(step, *acts_at("pull%d" % step))
    attend_pull(r, c, hooks)
    r.dq_out[...] = (r.dqt[half:D, :] * HEAD**-0.5).astype(BF)
    dq_c = net.send(r.dq_out, r.from_c.at[0:half], "c")
    r.dsum[rows16(c * half, half), :] = (r.dqt[0:half, :] * HEAD**-0.5).astype(BF)
    point("home")
    home_y.wait()
    home_d.wait()
    home_c.wait()

    def total(i, carry):
        for part in range(2):
            rows = rows16(part * half + i * 32, 32)
            mine = r.dkv[rows16(3 * both + part * half + i * 32, 32), :].astype(F32) + r.from_y[rows, :].astype(F32)
            r.dsum[rows16((1 + part) * D + c * half + i * 32, 32), :] = mine.astype(BF)
            other = r.from_c[rows16((1 + part) * half + i * 32, 32), :].astype(F32) + r.from_d[rows, :].astype(F32)
            r.dsum[rows16((1 + part) * D + (1 - c) * half + i * 32, 32), :] = other.astype(BF)
        return carry

    lax.fori_loop(0, half // 32, total, 0)

    def queries_came():
        dq_c.wait()
        r.dsum[rows16((1 - c) * half, half), :] = r.from_c[0:half, :]

    for part in (1, 2):
        stage_qkv_weights(r, part)
        ready("qkv%d" % part)
        point("qkvw%d" % part)
    stage_qkv_pull(r, queries_came)
    point("norm")
    stage_norm_pull(r)
    rim = [net.send(r.sg.at[0:16], r.slots.at[0, i], dim) for i, dim in enumerate(("c", "y"))]
    point("c2")
    for part in range(3):
        stage_conv2_weights(r, part)
        ready("c2%d" % part)
        point("c2w%d" % part)
    stage_qkv_weights(r, 0)
    ready("qkv0")
    point("qkvw0")

    def next_row():
        wait_all(rim)
        return pick_next(net, r.slots.at[0])

    stage_conv2_pull(r, next_row)
    point("first")
    stage_first_pull(r)
    rim = [net.send(r.fe.at[0:16], r.slots.at[1, i], dim) for i, dim in enumerate(("c", "y"))]
    rim += [net.send(r.fo.at[T - 16 : T], r.slots.at[2, i], dim) for i, dim in enumerate(("c", "y"))]
    point("c1")
    stage_conv1_weights(r)
    ready("c10", "vec0")
    point("c1w")
    wait_all(rim)
    stage_mel(r, pick_next(net, r.slots.at[1]), pick_prev(net, r.slots.at[2]))
    rows_of_yours = rows16((1 - sub) * T, T)
    mel_y = net.send(r.melg, r.melg_got, "y")
    point("mel")
    wait_all(enc)
    ends = [
        net.here(r.enc_got, r.enc_o.at[rows_of_yours]),
        net.here(r.melg, r.mel_o.at[rows_of_mine]),
    ]
    point("end")
    drain(*tracks.values())
    mel_y.wait()
    ends.append(net.here(r.melg_got, r.mel_o.at[rows_of_yours]))
    ends.append(net.here(r.small, r.small_o))
    wait_all(ends)
    for copies in leaving.values():
        wait_all(copies)


def run_layer(bits, near, far, outs, T, D, F2, lanes):
    half, H = D // 2, D // HEAD
    td, dt = (T, D), (D, T)
    buckets = dict(down=(D, 2, F2 // D), up=(D, 2, F2 // D), out=(half, 2, 1), qkv=(half, 2, 3), c2=(D, 1, 3), c1=(lanes, 1, 1))
    scratch = dict(
        melbuf=((128, 4 * T + 256), BF),
        mele=((T + 24, 128), F32),
        melo=((T + 24, 128), F32),
        xe=((T, 384), BF),
        xo=((T, 384), BF),
        w1p=((384, D), BF),
        w2=((3, D, D), BF),
        bg=(td, BF),
        wqkv=((2, 3, D, half), BF),
        wo=((D, D), BF),
        up=((2, D, F2), BF),
        down=((2 * F2, D), BF),
        vecs=((16, D), F32),
        vec_mine=((8, D), F32),
        vec_got=((8, D), F32),
        stream=(td, F32),
        he=(td, BF),
        ho=(td, BF),
        hp=(td, BF),
        dge=(td, F32),
        dgo=(td, F32),
        dg2=(td, F32),
        normed=(td, BF),
        kv=((15 * half, T), BF),
        mixt=(dt, F32),
        mixb=(dt, BF),
        normedt=(dt, BF),
        ntwot=(dt, BF),
        mix_got=((half, T), BF),
        dot=(dt, BF),
        dot_out=((half, T), BF),
        top=((H, 1, T), F32),
        total=((H, 1, T), F32),
        diag=((H, 1, T), F32),
        tmp=(td, F32),
        tmp2=(td, F32),
        shift=((T + 16, D), F32),
        wide=((T + 16, 128), F32),
        mid=(td, F32),
        ntwo=(td, BF),
        act=(td, BF),
        ing=(td, BF),
        ffo=(td, F32),
        ntg=(td, F32),
        attg=(td, BF),
        dqt=(dt, F32),
        dq_out=((half, T), BF),
        pb=((T, 2 * T), BF),
        ds=((T, 2 * T), BF),
        dkv=((8 * half, T), BF),
        from_y=((2 * half, T), BF),
        from_d=((2 * half, T), BF),
        from_c=((3 * half, T), BF),
        dsum=((3 * D, T), BF),
        enc_got=(td, BF),
        melg=((T, 256), BF),
        melg_got=((T, 256), BF),
        small=((16, D), F32),
        got_small=((sum(len(subsets(dims)) for dims in orders("vec", bits)[0]), 16, D), F32),
        slots=((3, 2, 16, D), BF),
    )
    alias = T == D
    for n, (rows, halves, parts) in buckets.items():
        if n not in ("qkv", "c2"):
            scratch["g_" + n] = ((rows * halves * parts, D), BF)
        for part in range(parts):
            need = sum_plan(rows, halves, orders(n, bits)[part])[1]
            scratch["got_%s%d" % (n, part)] = ((need, D), BF)
        scratch["done_" + n] = ((rows * parts, D), BF)
    if not alias:
        scratch.update({"tapt%d" % i: (dt, BF) for i in range(3)})
        scratch["turn"] = ((256, T), F32)
        scratch.update(g_qkv=((6 * half, D), BF), g_c2=((6 * half, D), BF))
    names = list(near) + list(far) + list(outs) + list(scratch) + ["send", "recv", "own"]

    def kernel(*refs):
        r = Box()
        for n, ref in zip(names, refs):
            setattr(r, n, ref)
        r.odd, r.smg, r.sg, r.fe, r.fo, r.enc = r.shift, r.mid, r.ntwo, r.act, r.ing, r.bg
        r.qrow, r.dorow = r.act, r.ing
        if alias:
            r.turn = r.tmp.at[0:256]
        r.tapt = (r.hp, r.he, r.ho) if alias else (r.tapt0, r.tapt1, r.tapt2)
        if alias:
            r.g_qkv, r.g_c2 = r.kv.at[0 : 6 * half], r.kv.at[6 * half : 12 * half]
        layer(r, bits)

    vmem, anywhere = pl.BlockSpec(memory_space=pltpu.VMEM), pl.BlockSpec(memory_space=pl.ANY)
    got = pl.pallas_call(
        kernel,
        name="layer",
        out_shape=[jax.ShapeDtypeStruct(*o) for o in outs.values()],
        in_specs=[vmem] * len(near) + [anywhere] * len(far),
        out_specs=[anywhere] * len(outs),
        scratch_shapes=[pltpu.VMEM(*s) for s in scratch.values()]
        + [pltpu.SemaphoreType.DMA((256,)), pltpu.SemaphoreType.DMA((256,)), pltpu.SemaphoreType.DMA((40,))],
        compiler_params=pltpu.CompilerParams(
            vmem_limit_bytes=VMEM_LIMIT, collective_id=1, has_side_effects=True
        ),
    )(*near.values(), *far.values())
    return dict(zip(outs, got))


def run_finish(got, mels, side):
    T2, D = got["enc_o"].shape
    half = D // 2
    ins = list(got)
    outs = dict(
        enc=((1, T2, D), BF),
        mel=((1, mels, 2 * T2), F32),
        c1=((3, mels, D), F32),
        c2=((3, D, D), F32),
        qkv=((3, D, half), F32),
        qkvb=((2, half), F32),
        out=((half, D), F32),
        up=((D, side * D), F32),
        upb=((side * D,), F32),
        down=((side * D, D), F32),
    )
    outs.update({n: ((D,), F32) for n in ROW_BIASES})

    big = ("mel", "c1", "c2", "qkv", "out", "up", "down")
    names = ins + list(outs) + ["in_" + n for n in ins] + ["out_" + n for n in big] + ["came", "went"]

    def kernel(*refs):
        r = Box()
        for n, ref in zip(names, refs):
            setattr(r, n, ref)
        m = lax.axis_index("mp")
        order = ["small_o", "enc_o", "down_o", "up_o", "qkv_o", "c2_o", "mel_o", "out_o", "c1_o"]
        loads = {}
        for k, n in enumerate(order):
            loads[n] = pltpu.make_async_copy(getattr(r, n), getattr(r, "in_" + n), r.came.at[k])
            loads[n].start()
        went = []

        def leave(n):
            copy = pltpu.make_async_copy(getattr(r, "out_" + n), getattr(r, n), r.went.at[len(went)])
            copy.start()
            went.append(copy)

        def cast(src, dst):
            def one(rows):
                dst[rows, :] = src[rows, :].astype(dst.dtype)

            rows_loop(src.shape[0], 256, one)

        loads["small_o"].wait()
        for k, n in enumerate(ROW_BIASES):
            getattr(r, n)[...] = r.in_small_o[k : k + 1, :].reshape(D)
        r.qkvb[...] = r.in_small_o[QB : QB + 2, pl.ds(pl.multiple_of(m * half, 128), half)]
        for k in range(side):
            r.upb[k * D : (k + 1) * D] = r.in_small_o[pl.ds(UPB + m * side + k, 1), :].reshape(D)
        loads["enc_o"].wait()
        copy = pltpu.make_async_copy(r.in_enc_o, r.enc.at[0], r.went.at[len(big)])
        copy.start()
        for n in ("down", "up"):
            loads[n + "_o"].wait()
            cast(getattr(r, "in_" + n + "_o"), getattr(r, "out_" + n))
            leave(n)
        loads["qkv_o"].wait()
        for o in range(3):
            cast(r.in_qkv_o.at[o], r.out_qkv.at[o])
        leave("qkv")
        loads["c2_o"].wait()
        for o in range(3):
            cast(r.in_c2_o.at[o * D : (o + 1) * D], r.out_c2.at[o])
        leave("c2")
        row = lax.broadcasted_iota(jnp.int32, (128, 256), 0)
        lane = lax.broadcasted_iota(jnp.int32, (128, 256), 1)
        even = jnp.where(lane == 2 * row, 1.0, 0.0).astype(BF)
        odd = jnp.where(lane == 2 * row + 1, 1.0, 0.0).astype(BF)
        loads["mel_o"].wait()
        for k in range(T2 // 128):
            rows = slice(k * 128, (k + 1) * 128)
            value = tn(r.in_mel_o[rows, 0:128], even) + tn(r.in_mel_o[rows, 128:256], odd)
            r.out_mel[0, :, k * 256 : (k + 1) * 256] = value[0:mels, :]
        leave("mel")
        loads["out_o"].wait()
        cast(r.in_out_o, r.out_out)
        leave("out")
        loads["c1_o"].wait()
        for o in range(3):
            r.out_c1[o] = r.in_c1_o[o * mels : (o + 1) * mels, :].astype(F32)
        leave("c1")
        copy.wait()
        wait_all(went)

    vmem, anywhere = pl.BlockSpec(memory_space=pltpu.VMEM), pl.BlockSpec(memory_space=pl.ANY)
    done = pl.pallas_call(
        kernel,
        name="finish",
        out_shape=[jax.ShapeDtypeStruct(*o) for o in outs.values()],
        in_specs=[anywhere] * len(ins),
        out_specs=[anywhere if n in big + ("enc",) else vmem for n in outs],
        scratch_shapes=[pltpu.VMEM(got[n].shape, got[n].dtype) for n in ins]
        + [pltpu.VMEM(*outs[n]) for n in big]
        + [pltpu.SemaphoreType.DMA((len(ins),)), pltpu.SemaphoreType.DMA((len(big) + 1,))],
        compiler_params=pltpu.CompilerParams(vmem_limit_bytes=VMEM_LIMIT),
    )(*got.values())
    return dict(zip(outs, done))


def sine_tables(frames, channels, fine):
    half_width = channels // 2
    rate = np.exp(-(math.log(10000.0) / (half_width - 1)) * np.arange(half_width))
    small = np.arange(fine)[:, None] * rate[None, :]
    large = np.arange(0, frames, fine)[:, None] * rate[None, :]
    table = dict(fine_s=np.sin(small), fine_c=np.cos(small), coarse_s=np.sin(large), coarse_c=np.cos(large))
    return {n: jnp.asarray(t, F32) for n, t in table.items()}


def on_device(
    mel_input,
    conv1_weight,
    conv1_bias,
    conv2_weight,
    conv2_bias,
    norm1_gain,
    norm1_bias,
    qkv_weight,
    qkv_bias,
    out_weight,
    out_bias,
    norm2_gain,
    norm2_bias,
    up_weight,
    up_bias,
    down_weight,
    down_bias,
    cotangent,
    speech_mask,
):
    mels = mel_input.shape[1]
    T, D = cotangent.shape[1] // 2, cotangent.shape[2]
    F2 = up_weight.shape[1]
    side, half = F2 // D, D // 2
    bits = (lax.axis_size("dp") - 1).bit_length()
    lanes = -(-3 * mels // 128) * 128
    near = dict(
        w1=conv1_weight,
        mask=speech_mask,
        qkvb=qkv_bias,
        upb=up_bias,
        c1b=conv1_bias,
        c2b=conv2_bias,
        n1g=norm1_gain,
        n1b=norm1_bias,
        oub=out_bias,
        n2g=norm2_gain,
        n2b=norm2_bias,
        dnb=down_bias,
    )
    near.update(sine_tables(4 * T, D, 32))
    got = run_layer(
        bits,
        near,
        dict(
            mel=mel_input,
            cot=cotangent,
            w2_l=conv2_weight,
            wqkv_l=qkv_weight,
            wo_l=out_weight,
            up_l=up_weight,
            down_l=down_weight,
        ),
        dict(
            enc_o=((2 * T, D), BF),
            mel_o=((2 * T, 256), BF),
            down_o=((F2, D), BF),
            up_o=((D, F2), BF),
            out_o=((half, D), BF),
            qkv_o=((3, D, half), BF),
            c2_o=((3 * D, D), BF),
            c1_o=((lanes, D), BF),
            small_o=((16, D), F32),
        ),
        T,
        D,
        F2,
        lanes,
    )
    done = run_finish(got, mels, side)
    names = ("enc", "mel", "c1", "c1b", "c2", "c2b", "n1g", "n1b", "qkv", "qkvb")
    names += ("out", "oub", "n2g", "n2b", "up", "upb", "down", "dnb")
    return tuple(done[n] for n in names)


def solution(mesh):
    placed = (
        P("dp", None, "seq"),
        P(),
        P(),
        P(),
        P(),
        P(),
        P(),
        P(None, None, "mp"),
        P(None, "mp"),
        P("mp", None),
        P(),
        P(),
        P(),
        P(None, "mp"),
        P("mp"),
        P("mp", None),
        P(),
        P("dp", "seq", None),
        P("dp", "seq"),
    )
    return jax.shard_map(
        on_device,
        mesh=mesh,
        in_specs=placed,
        out_specs=(
            P("dp", "seq", None),
            P("dp", None, "seq"),
            P(),
            P(),
            P(),
            P(),
            P(),
            P(),
            P(None, None, "mp"),
            P(None, "mp"),
            P("mp", None),
            P(),
            P(),
            P(),
            P(None, "mp"),
            P("mp"),
            P("mp", None),
            P(),
        ),
        check_vma=False,
    )
```

```python
import functools
import math

import jax
import jax.numpy as jnp
import numpy as np
from jax import lax
from jax.experimental import pallas as pl
from jax.experimental.pallas import tpu as pltpu
from jax.sharding import PartitionSpec as P

HEAD = 64
BF = jnp.bfloat16
F32 = jnp.float32
MESH = pl.DeviceIdType.MESH
VMEM_LIMIT = 62 * 1024 * 1024
C1B, C2B, N1G, N1B, OUB, N2G, N2B, DNB, QB, VB, UPB = range(11)


class Box:
    pass


def dot(a, b, ca, cb):
    return lax.dot_general(a, b, (((ca,), (cb,)), ((), ())), preferred_element_type=F32)


def nn(a, b):
    return dot(a, b, 1, 0)


def nt(a, b):
    return dot(a, b, 1, 1)


def tn(a, b):
    return dot(a, b, 0, 0)


def flip(value):
    return value.astype(F32).T.astype(BF)


def rows_loop(total, step, body, unroll=1):
    step = min(step, total)

    def one(i, carry):
        body(pl.ds(pl.multiple_of(i * step, step), step))
        return carry

    lax.fori_loop(0, total // step, one, 0, unroll=min(unroll, total // step))


def gelu_parts(v):
    t = 1.0 / (1.0 + (0.3275911 / math.sqrt(2.0)) * jnp.abs(v))
    e = jnp.exp(-0.5 * v * v)
    poly = 1.061405429 * t - 1.453152027
    poly = poly * t + 1.421413741
    poly = poly * t - 0.284496736
    poly = poly * t + 0.254829592
    tail = (0.5 * t) * poly * e
    return jnp.where(v >= 0, 1.0 - tail, tail), e * (1.0 / math.sqrt(2.0 * math.pi))


def gelu_both(v):
    cdf, pdf = gelu_parts(v)
    return v * cdf, cdf + v * pdf


def normal(x):
    center = x - jnp.mean(x, axis=-1, keepdims=True)
    spread = jnp.mean(center * center, axis=-1, keepdims=True)
    inv = lax.rsqrt(spread + 1e-05)
    return center * inv, inv


def normal_pull(gy, hat, inv):
    return inv * (
        gy
        - jnp.mean(gy, axis=-1, keepdims=True)
        - hat * jnp.mean(gy * hat, axis=-1, keepdims=True)
    )


def vec(r, i):
    return r.vecs[i : i + 1, :]


def add_small(r, i, value):
    r.small[i : i + 1, :] += value


def col(value):
    return jnp.sum(value, axis=0, keepdims=True)


def stage_mel_rows(r, sub, rim_came):
    T, D = r.stream.shape
    row = lax.broadcasted_iota(jnp.int32, (256, 256), 0)
    lane = lax.broadcasted_iota(jnp.int32, (256, 256), 1)
    pick = jnp.where(lane == 2 * (row % 128) + row // 128, 1.0, 0.0).astype(BF)
    base = sub * 2 * T

    def lanes(start, size):
        return r.melbuf[:, pl.ds(pl.multiple_of(base + start, 128), size)]

    row = lax.broadcasted_iota(jnp.int32, (16, 128), 0)
    lane = lax.broadcasted_iota(jnp.int32, (16, 128), 1)

    def select(at, to):
        return jnp.where(jnp.logical_and(row == to, lane == at), 1.0, 0.0).astype(BF)

    for k in range(T // 128):
        both = nt(pick, lanes(128 + 256 * k, 256))
        r.mele[8 + 128 * k : 136 + 128 * k, :] = both[0:128, :]
        r.melo[8 + 128 * k : 136 + 128 * k, :] = both[128:256, :]
    rim_came()
    before, after = lanes(0, 128), lanes(128 + 2 * T, 128)
    r.mele[0:8, :] = nt(select(126, 7), before)[0:8, :]
    r.melo[0:8, :] = nt(select(127, 7), before)[0:8, :]
    r.mele[T + 8 : T + 16, :] = nt(select(0, 0), after)[0:8, :]


def three(a, b, c):
    return jnp.concatenate([a, b, c], axis=1).astype(BF)


def stage_first(r, first):
    T, D = r.stream.shape
    for o in range(3):
        r.w1p[128 * o : 128 * o + r.w1.shape[1], :] = r.w1[o]
        r.w1p[128 * o + r.w1.shape[1] : 128 * (o + 1), :] = jnp.zeros((128 - r.w1.shape[1], D), BF)
    w1 = r.w1p[...]
    edge = nn(three(r.mele[0:16, :], r.melo[0:16, :], r.mele[1:17, :]), w1) + vec(r, C1B)
    edge = gelu_both(edge)[0] * jnp.where(first, 0.0, 1.0)
    r.odd[0:8, :] = edge[0:8, :]
    r.xe[...] = three(r.melo[7 : 7 + T, :], r.mele[8 : 8 + T, :], r.melo[8 : 8 + T, :])
    r.xo[...] = three(r.mele[8 : 8 + T, :], r.melo[8 : 8 + T, :], r.mele[9 : 9 + T, :])
    r.tmp[...] = nn(r.xe[...], w1)

    def even(rows):
        value, slope = gelu_both(r.tmp[rows, :] + vec(r, C1B))
        r.he[rows, :] = value.astype(BF)
        r.dge[rows, :] = slope

    rows_loop(T, 32, even)


def stage_odd(r):
    T, D = r.stream.shape
    r.tmp[...] = nn(r.xo[...], r.w1p[...])

    def odd(rows):
        value, slope = gelu_both(r.tmp[rows, :] + vec(r, C1B))
        r.ho[rows, :] = value.astype(BF)
        r.odd[pl.ds(pl.multiple_of(rows.start + 8, 8), rows.size), :] = value
        r.dgo[rows, :] = slope

    rows_loop(T, 32, odd)


def stage_second(r, place):
    T, D = r.stream.shape
    r.hp[...] = r.odd[7 : 7 + T, :].astype(BF)
    r.tmp[...] = nn(r.hp[...], r.w2[0]) + nn(r.he[...], r.w2[1]) + nn(r.ho[...], r.w2[2])
    fine = r.fine_s.shape[0]

    def second(rows):
        value, slope = gelu_both(r.tmp[rows, :] + vec(r, C2B))
        at = place * (T // fine) + rows.start // fine
        s0, c0 = r.coarse_s[pl.ds(at, 1), :], r.coarse_c[pl.ds(at, 1), :]
        s1, c1 = r.fine_s[...], r.fine_c[...]
        stream = value + jnp.concatenate([s0 * c1 + c0 * s1, c0 * c1 - s0 * s1], axis=1)
        r.dg2[rows, :] = slope
        r.stream[rows, :] = stream
        r.normed[rows, :] = (normal(stream)[0] * vec(r, N1G) + vec(r, N1B)).astype(BF)

    rows_loop(T, fine, second)


def stage_mask(r, sub):
    T, D = r.stream.shape
    row = r.mask[0:1, pl.ds(pl.multiple_of(sub * T, 128), T)].astype(F32)
    r.wide[0:T, :] = jnp.broadcast_to(row, (128, T)).T

    def one(rows):
        keep = r.wide[rows, :]
        keep = jnp.concatenate([keep] * (D // 128), axis=1)
        r.bg[rows, :] = (r.bg[rows, :].astype(F32) * keep).astype(BF)

    rows_loop(T, 32, one)


def stage_qkv(r, part, h):
    T, D = r.stream.shape
    half, qr = D // 2, D // 4
    bias, scale = ((QB, HEAD**-0.5), (None, 1.0), (VB, 1.0))[part]
    value = nn(r.normed[...], r.wqkv[h, part])
    if bias is not None:
        value = value + r.vecs[bias : bias + 1, pl.ds(pl.multiple_of(h * half, half), half)]
    value = (value.astype(BF).astype(F32) * scale).T.astype(BF)
    for k in range(2):
        r.kv[rows16((3 * (3 + k) + part) * half + h * qr, qr), :] = value[k * qr : (k + 1) * qr, :]


def at_head(start, h):
    return pl.ds(pl.multiple_of(start + h * HEAD, HEAD), HEAD)


def head_loop(steps, hooks, body):
    def one(step, carry):
        for at, todo in hooks.items():
            if not todo:
                continue

            @pl.when(step == at)
            def _(todo=todo):
                for act in todo:
                    act()

        body(step)
        return carry

    lax.fori_loop(0, steps, one, 0)


def attend(r, c, m, hooks):
    S, T = r.kv.shape[0] // 15, r.kv.shape[1]
    heads = S // HEAD
    r.top[...] = jnp.full(r.top.shape, -jnp.inf, F32)
    r.total[...] = jnp.zeros(r.total.shape, F32)
    r.mixt[...] = jnp.zeros(r.mixt.shape, F32)

    def body(step):
        quarter, u, pair = step // heads, step % heads, heads // 2
        g = 2 * (quarter // 2) + u // pair
        h = (m + (1 - 2 * m) * ((quarter + 1) // 2 % 2)) * pair + u % pair
        own = (3 - g) // 3
        slot = own * (3 + c) + (1 - own) * ((g + 1) % 3)
        k = r.kv[at_head((3 * slot + 1) * S, h), :]
        v = r.kv[at_head((3 * slot + 2) * S, h), :]
        for i, home in enumerate((3 + c, 2)):
            q = r.kv[at_head(3 * home * S, h), :]
            s = tn(k, q)
            before = r.top[i * heads + h]
            top = jnp.maximum(before, jnp.max(s, axis=0, keepdims=True))
            p = jnp.exp(s - top)
            keep = jnp.exp(before - top)
            rows = at_head(i * S, h)
            r.top[i * heads + h] = top
            r.total[i * heads + h] = keep * r.total[i * heads + h] + jnp.sum(p, axis=0, keepdims=True)
            r.mixt[rows, :] = keep * r.mixt[rows, :] + nn(v, p.astype(BF))

    head_loop(4 * heads, hooks, body)


def attend_end(r, i):
    S = r.kv.shape[0] // 15
    heads = S // HEAD

    def one(h, carry):
        rows = at_head(i * S, h)
        total = r.total[i * heads + h]
        value = r.mixt[rows, :] * (1.0 / total)
        r.mixt[rows, :] = value
        r.mixb[rows, :] = value.astype(BF)
        r.top[i * heads + h] = r.top[i * heads + h] + jnp.log(total)
        return carry

    lax.fori_loop(0, heads, one, 0)


def stage_mid(r, c, mix_came, weights_came):
    T, D = r.stream.shape
    half = D // 2
    weights_came()
    r.tmp[...] = tn(r.mixb[0:half, :], r.wo[rows16(c * half, half), :])
    mix_came()
    r.tmp[...] += tn(r.mix_got[...], r.wo[rows16((1 - c) * half, half), :])

    def one(rows):
        mid = r.stream[rows, :] + r.tmp[rows, :] + vec(r, OUB)
        r.mid[rows, :] = mid
        r.ntwo[rows, :] = (normal(mid)[0] * vec(r, N2G) + vec(r, N2B)).astype(BF)

    rows_loop(T, 32, one)


def stage_ff(r, hooks):
    T, D = r.stream.shape
    side = r.up.shape[2] // D
    parts, width = 2 * side, D

    def chunk(t):
        into, at = t % 2, t // 2
        j = into * side + at
        up = r.up[into, :, pl.ds(pl.multiple_of(at * D, D), D)]
        down = r.down[pl.ds(pl.multiple_of(j * D, D), D), :]
        r.tmp[...] = nn(r.ntwo[...], up)
        r.tmp2[...] = nt(r.bg[...], down)
        bias = r.vecs[pl.ds(UPB + j, 1), :]

        def one(i, acc):
            rows = pl.ds(pl.multiple_of(i * 32, 32), 32)
            value, slope = gelu_both(r.tmp[rows, :] + bias)
            r.act[rows, :] = value.astype(BF)
            grad = (r.tmp2[rows, :] * slope).astype(BF)
            r.ing[rows, :] = grad
            return acc + col(grad.astype(F32))

        r.small[pl.ds(UPB + j, 1), :] = lax.fori_loop(0, T // 32, one, jnp.zeros((1, width), F32))
        act = r.act[...]
        ing = r.ing[...]
        out = nn(act, down)
        back = nt(ing, up)

        r.ffo[...] += out
        r.ntg[...] += back
        rows = pl.ds(pl.multiple_of(t * D, D), D)
        r.g_down[rows, :] = tn(act, r.bg[...]).astype(BF)
        r.g_up[rows, :] = nn(r.ntwot[...], ing).astype(BF)

    r.ntwot[...] = flip(r.ntwo[...])
    r.ffo[...] = jnp.zeros_like(r.ffo)
    r.ntg[...] = jnp.zeros_like(r.ntg)
    head_loop(parts, hooks, chunk)


def stage_mid_pull(r):
    T, D = r.stream.shape

    def one(i, accs):
        rows = pl.ds(pl.multiple_of(i * 32, 32), 32)
        mid = r.mid[rows, :]
        enc = (mid + r.ffo[rows, :] + vec(r, DNB)).astype(BF)
        hat, inv = normal(mid)
        grad = r.ntg[rows, :]
        smg = r.bg[rows, :].astype(F32) + normal_pull(grad * vec(r, N2G), hat, inv)
        r.enc[rows, :] = enc
        r.smg[rows, :] = smg
        attg = smg.astype(BF)
        r.attg[rows, :] = attg
        return accs[0] + col(grad * hat), accs[1] + col(grad), accs[2] + col(attg.astype(F32))

    zero = jnp.zeros((1, D), F32)
    gain, bias, out_bias = lax.fori_loop(0, T // 32, one, (zero, zero, zero))
    add_small(r, N2G, gain)
    add_small(r, N2B, bias)
    add_small(r, OUB, out_bias)


def stage_do(r, c, own):
    half = r.attg.shape[1] // 2
    k = c if own else 1 - c
    value = nt(r.wo[rows16(k * half, half), :], r.attg[...]).astype(BF)
    if own:
        r.dot[0:half, :] = value
    else:
        r.dot_out[...] = value


def stage_out_weights(r, c):
    D = r.attg.shape[1]
    half, qr = D // 2, D // 4
    for k, mix in ((c, r.mixb[0:half, :]), (1 - c, r.mix_got[...])):
        value = nn(mix, r.attg[...]).astype(BF)
        for h in range(2):
            r.g_out[rows16(h * half + k * qr, qr), :] = value[h * qr : (h + 1) * qr, :]


def stage_diag(r, i):
    S = r.kv.shape[0] // 15
    heads = S // HEAD

    def one(h, carry):
        rows = at_head(i * S, h)
        value = r.dot[rows, :].astype(F32) * r.mixt[rows, :]
        r.diag[i * heads + h] = jnp.sum(value, axis=0, keepdims=True)
        return carry

    lax.fori_loop(0, heads, one, 0)


def attend_pull(r, c, hooks):
    S, T = r.kv.shape[0] // 15, r.kv.shape[1]
    heads = S // HEAD
    r.dqt[...] = jnp.zeros(r.dqt.shape, F32)

    def body(step):
        g, h = step // heads, step % heads
        slot = g + (g // 3) * c
        k = r.kv[at_head((3 * slot + 1) * S, h), :]
        v = r.kv[at_head((3 * slot + 2) * S, h), :]
        qs = [r.kv[at_head(3 * home * S, h), :] for home in (3 + c, 2)]
        dos = [r.dot[at_head(i * S, h), :] for i in range(2)]
        for i in range(2):
            top, diag = r.top[i * heads + h], r.diag[i * heads + h]
            for at in range(0, T, 128):
                rows, cols = slice(at, at + 128), slice(i * T, (i + 1) * T)
                p = jnp.exp(tn(k[:, rows], qs[i]) - top)
                r.pb[rows, cols] = p.astype(BF)
                r.ds[rows, cols] = (p * (tn(v[:, rows], dos[i]) - diag)).astype(BF)
        pair = [pl.ds(pl.multiple_of(i * S + h // 2 * 128, 128), 128) for i in range(2)]
        for part, left, right in ((0, r.ds, r.qrow), (1, r.pb, r.dorow)):
            r.turn[128 * part : 128 * (part + 1), :] = sum(
                nn(left[:, i * T : (i + 1) * T], right[:, pair[i]]) for i in range(2)
            ).T
            value = r.turn[pl.ds(pl.multiple_of(128 * part + h % 2 * HEAD, HEAD), HEAD), :]
            r.dkv[at_head((2 * g + part) * S, h), :] = value.astype(BF)
        dq = nn(k, r.ds[...])
        for i in range(2):
            r.dqt[at_head(i * S, h), :] += dq[:, i * T : (i + 1) * T]

    head_loop(4 * heads, hooks, body)


def piece_of(r, part, h):
    D, qr = r.attg.shape[1], r.attg.shape[1] // 4
    at = part * D + h * qr
    return jnp.concatenate([r.dsum[at : at + qr, :], r.dsum[at + 2 * qr : at + 3 * qr, :]], axis=0)


def stage_qkv_weights(r, part):
    T, D = r.stream.shape
    half = D // 2
    ones = jnp.ones((8, T), BF)
    for h in range(2):
        piece = piece_of(r, part, h)
        if part != 1:
            row = QB if part == 0 else VB
            r.small[row : row + 1, h * half : (h + 1) * half] = nt(ones, piece)[0:1, :]
        grad = nt(r.normedt[...], piece).astype(BF)
        at = (2 * part + h) * half
        r.g_qkv[at : at + half, 0:half] = grad[0:half, :]
        r.g_qkv[at : at + half, half:D] = grad[half:D, :]


def stage_qkv_pull(r, queries_came):
    T, D = r.stream.shape
    total = None
    for part in (1, 2, 0):
        if part == 0:
            queries_came()
        for h in range(2):
            back = nn(r.wqkv[h, part], piece_of(r, part, h))
            total = back if total is None else total + back
    r.tmp[...] = total.T


def stage_norm_pull(r):
    T, D = r.stream.shape

    def one(i, accs):
        rows = pl.ds(pl.multiple_of(i * 32, 32), 32)
        hat, inv = normal(r.stream[rows, :])
        grad = r.tmp[rows, :]
        back = r.smg[rows, :] + normal_pull(grad * vec(r, N1G), hat, inv)
        sg = (back * r.dg2[rows, :]).astype(BF)
        r.sg[rows, :] = sg
        return accs[0] + col(grad * hat), accs[1] + col(grad), accs[2] + col(sg.astype(F32))

    zero = jnp.zeros((1, D), F32)
    gain, bias, c2b = lax.fori_loop(0, T // 32, one, (zero, zero, zero))
    add_small(r, N1G, gain)
    add_small(r, N1B, bias)
    add_small(r, C2B, c2b)


def stage_conv2_pull(r, next_row):
    T, D = r.stream.shape
    sg = r.sg[...]
    r.shift[0:T, :] = nt(sg, r.w2[0])
    r.tmp[...] = nt(sg, r.w2[1])
    r.shift[T : T + 16, :] = nt(next_row(), r.w2[0])
    r.tmp2[...] = nt(sg, r.w2[2]) + r.shift[1 : T + 1, :]


def stage_first_pull(r):
    T, D = r.stream.shape

    def one(i, acc):
        rows = pl.ds(pl.multiple_of(i * 32, 32), 32)
        even = (r.tmp[rows, :] * r.dge[rows, :]).astype(BF)
        odd = (r.tmp2[rows, :] * r.dgo[rows, :]).astype(BF)
        r.fe[rows, :] = even
        r.fo[rows, :] = odd
        return acc + col(even.astype(F32)) + col(odd.astype(F32))

    add_small(r, C1B, lax.fori_loop(0, T // 32, one, jnp.zeros((1, D), F32)))


def stage_conv2_weights(r, i):
    D = r.stream.shape[1]
    r.g_c2[i * D : (i + 1) * D, :] = nn(r.tapt[i][...], r.sg[...]).astype(BF)


def stage_conv1_weights(r):
    value = (tn(r.xe[...], r.fe[...]) + tn(r.xo[...], r.fo[...])).astype(BF)
    mels = r.w1.shape[1]
    for o in range(3):
        r.g_c1[mels * o : mels * (o + 1), :] = value[128 * o : 128 * o + mels, :]
    r.g_c1[3 * mels :, :] = jnp.zeros((r.g_c1.shape[0] - 3 * mels, r.g_c1.shape[1]), BF)


def stage_mel(r, next_row, prev_row):
    T, D = r.stream.shape
    fe, fo = r.fe[...], r.fo[...]
    w = [r.w1p[128 * o : 128 * (o + 1), :] for o in range(3)]
    r.wide[16 : 16 + T, :] = nt(fo, w[2])
    r.wide[0:16, :] = nt(prev_row, w[2])
    r.melg[:, 0:128] = (nt(fe, w[1]) + nt(fo, w[0]) + r.wide[15 : 15 + T, :]).astype(BF)
    r.wide[0:T, :] = nt(fe, w[0])
    r.wide[T : T + 16, :] = nt(next_row, w[0])
    r.melg[:, 128:256] = (nt(fe, w[2]) + nt(fo, w[1]) + r.wide[1 : 1 + T, :]).astype(BF)


class Net:
    def __init__(self, r, bits):
        self.r, self.bits, self.used, self.used_here = r, bits, 0, 0
        self.d, self.c, self.m = (lax.axis_index(n) for n in ("dp", "seq", "mp"))

    def bit(self, dim):
        if dim == "c":
            return self.c
        if dim == "y":
            return self.m
        return (self.d // (1 << dim)) % 2

    def peer(self, dims):
        d = self.d
        for k in dims:
            if k not in ("c", "y"):
                d = d + (1 << k) - 2 * (1 << k) * self.bit(k)
        return (
            d,
            1 - self.c if "c" in dims else self.c,
            1 - self.m if "y" in dims else self.m,
        )

    def greet(self, partners):
        barrier = pltpu.get_barrier_semaphore()
        for dims in partners:
            pl.semaphore_signal(barrier, inc=1, device_id=self.peer(dims), device_id_type=MESH)
        pl.semaphore_wait(barrier, len(partners))

    def copy(self, src, dst, *dims):
        i = self.used
        self.used += 1
        return pltpu.make_async_remote_copy(
            src_ref=src,
            dst_ref=dst,
            send_sem=self.r.send.at[i],
            recv_sem=self.r.recv.at[i],
            device_id=self.peer(dims),
            device_id_type=MESH,
        )

    def send(self, src, dst, *dims):
        copy = self.copy(src, dst, *dims)
        copy.start()
        return copy

    def here_later(self, src, dst):
        i = self.used_here
        self.used_here += 1
        return pltpu.make_async_copy(src, dst, self.r.own.at[i])

    def here(self, src, dst):
        copy = self.here_later(src, dst)
        copy.start()
        return copy


def start_all(copies):
    for copy in copies:
        copy.start()


def wait_all(copies):
    for copy in copies:
        copy.wait()


def rows16(start, size):
    return pl.ds(pl.multiple_of(start, 16), size)


def subsets(dims):
    found = [()]
    for dim in dims:
        found += [one + (dim,) for one in found]
    return found[1:]


def sum_plan(rows, halves, order):
    steps, need = [], 0
    for dims in order:
        by_half = halves == 2 and "y" in dims
        cutting = [dim for dim in dims if not (by_half and dim == "y")]
        if rows % (16 << len(cutting)):
            cutting = []
        rows >>= len(cutting)
        if by_half:
            halves = 1
        steps.append((dims, cutting, rows, halves, by_half))
        need += rows * halves * len(subsets(dims))
    return steps, need


class Track:
    def __init__(self, acts):
        self.acts = list(acts)

    def take(self):
        return [self.acts.pop(0)] if self.acts else []

    def then(self, more):
        last = self.acts.pop()

        def act():
            last()
            more()

        self.acts.append(act)


def bucket_sum(net, g, got, done, halves, order):
    R = g.shape[0] // halves
    lo, rows, at, bases = 0, R, 0, [h * R for h in range(halves)]
    acts, back, end = [], [], None

    def start_after(end, copies):
        def act():
            if end is not None:
                end()
            for copy in copies:
                copy.start()

        return act

    def adder(copies, places, n):
        step = 64 if n % 64 == 0 else 32 if n % 32 == 0 else 16

        def end():
            wait_all(copies)
            for to, ofs in places:

                def add(k, carry, to=to, ofs=ofs):
                    mine = rows16(to + k * step, step)
                    value = g[mine, :].astype(F32)
                    for of in ofs:
                        value = value + got[rows16(of + k * step, step), :].astype(F32)
                    g[mine, :] = value.astype(BF)
                    return carry

                lax.fori_loop(0, n // step, add, 0)

        return end

    for dims, cutting, n, _, by_half in sum_plan(R, halves, order)[0]:

        def part_of(other):
            start = lo
            for i, dim in enumerate(reversed(cutting)):
                b = net.bit(dim)
                start = start + (1 - b if dim in other else b) * (n << i)
            return start

        keep = part_of(())
        if by_half:
            bases = [net.m * R]
        copies, ofs = [], [[] for _ in bases]
        for other in subsets(dims):
            sources = [(1 - net.m) * R] if by_half and "y" in other else bases
            for i, base in enumerate(sources):
                src = g.at[rows16(base + part_of(other), n)]
                copies.append(net.copy(src, got.at[rows16(at, n)], *other))
                ofs[i].append(at)
                at += n
        acts.append(start_after(end, copies))
        end = adder(copies, [(base + keep, of) for base, of in zip(bases, ofs)], n)
        if cutting:
            back.append((cutting, n, lo))
        lo, rows = keep, n

    def settle(end=end, lo=lo, base=bases[0], rows=rows):
        end()
        for k in range(rows // 16):
            done[rows16(lo + 16 * k, 16), :] = g[rows16(base + lo + 16 * k, 16), :]

    end = settle
    for cutting, n, before in reversed(back):
        part = rows16(lo, n)
        copies = [net.copy(done.at[part], done.at[part], *other) for other in subsets(cutting)]
        acts.append(start_after(end, copies))
        end = functools.partial(wait_all, copies)
        lo = before
    return Track(acts + [end])


def small_sum(net, value, slots, order):
    acts, end, at = [], None, 0
    for dims in order:
        copies = [net.copy(value, slots.at[at + i], *other) for i, other in enumerate(subsets(dims))]

        def act(end=end, copies=copies):
            if end is not None:
                end()
            start_all(copies)

        def end(copies=copies, at=at):
            wait_all(copies)
            total = value[...]
            for i in range(len(copies)):
                total = total + slots[at + i]
            value[...] = total

        at += len(copies)
        acts.append(act)
    return Track(acts + [end])


def ready(*names):
    pass


def advance(*sums):
    for one in sums:
        for act in one.take():
            act()


def drain(*sums):
    while any(one.acts for one in sums):
        advance(*sums)


def quarter(net):
    return 2 * net.c + net.c + net.m - 2 * net.c * net.m


def choose(slots, by_core, by_y):
    core = jnp.where(by_core, 1.0, 0.0)
    y = jnp.where(by_y, 1.0, 0.0)
    return (slots[0].astype(F32) * core + slots[1].astype(F32) * y).astype(BF)


def pick_next(net, slots):
    q = quarter(net)
    return choose(slots, q == 1, q % 2 == 0)


def pick_prev(net, slots):
    q = quarter(net)
    return choose(slots, q == 2, q % 2 == 1)


ROW_BIASES = ("c1b", "c2b", "n1g", "n1b", "oub", "n2g", "n2b", "dnb")


ORDERS = dict(
    down=("c-z-wy-x", "c-y-zx-w"),
    up=("c-xy-wz", "c-zx-wy"),
    out=("c-y-wx-z",),
    qkv=("c-w-yx-z", "c-zy-x-w", "x-c-z-y-w"),
    c2=("c-z-xy-w", "c-xy-z-w", "c-xy-w-z"),
    c1=("cy-xz-w",),
    vec=("c-y-w-z-x",),
)
TRACKS = (
    ("down", 0), ("down", 1), ("up", 0), ("up", 1), ("out", 0), ("qkv", 0), ("qkv", 1), ("qkv", 2),
    ("c2", 0), ("c2", 1), ("c2", 2), ("c1", 0), ("vec", 0),
)
SCHEDULE = dict(
    ff2=(0, 2),
    ffo=(0, 1, 2, 3),
    out=(1, 3, 4),
    pull1=(0, 4),
    pull2=(2,),
    pull3=(3,),
    pull6=(0, 2),
    pull7=(3, 4),
    pull8=(0, 1),
    pull9=(2,),
    pull10=(0, 3, 4),
    pull11=(1,),
    pull12=(2, 4),
    pull14=(0, 1, 2, 3, 4),
    home=(3,),
    qkvw1=(6,),
    qkvw2=(1, 4, 7),
    norm=(0,),
    c2=(4, 6),
    c2w0=(8,),
    c2w1=(9,),
    c2w2=(0, 10),
    qkvw0=(5,),
    first=(1, 8, 9),
    c1=(5, 6, 7, 10),
    c1w=(1, 11, 12),
    mel=(6, 7, 8, 9, 12),
    end=(
        5, 10, 11, 6, 7, 9, 8, 12, 5, 10, 11, 6, 9, 7, 8, 12, 6, 5, 10, 11, 9, 7, 8, 5, 12, 10,
        11, 7, 8, 9, 6, 5, 12, 10, 6, 7, 11, 7, 8, 5, 9, 10, 8, 5, 9, 7, 10,
    ),
)


def orders(name, bits):
    dims = dict(c=["c"], y=["y"], x=[0], z=list(range(1, min(2, bits))), w=list(range(2, min(3, bits))))
    found = []
    for spec in ORDERS[name]:
        groups = [tuple(dim for ch in group for dim in dims[ch]) for group in spec.split("-")]
        found.append([group for group in groups if group] + [(dim,) for dim in range(3, bits)])
    return found


def partners(bits):
    found = [("c",), ("y",), ("c", "y")] + [(dim,) for dim in range(bits)]
    for name in ORDERS:
        for order in orders(name, bits):
            for dims in order:
                found += [one for one in subsets(dims) if set(one) not in [set(x) for x in found]]
    return found


def layer(r, bits):
    T, D = r.stream.shape
    half, F2 = D // 2, r.down_l.shape[0]
    side = F2 // D
    mels, span = r.w1.shape[1], 4 * T
    net = Net(r, bits)
    c, m = net.c, net.m
    sub = c + m - 2 * c * m
    rows_of_mine = rows16(sub * T, T)

    r.melbuf[...] = jnp.zeros_like(r.melbuf)
    mel_own = net.here(r.mel.at[0], r.melbuf.at[0:mels, 128 : 128 + span])
    qkv_own = net.here(r.wqkv_l, r.wqkv.at[m])
    w2_own = net.here(r.w2_l, r.w2)
    own = [
        net.here(r.wo_l.at[0 : D // 4], r.wo.at[rows16(m * (D // 4), D // 4)]),
        net.here(r.wo_l.at[D // 4 : half], r.wo.at[rows16(half + m * (D // 4), D // 4)]),
        net.here(r.up_l, r.up.at[m]),
        net.here(r.down_l, r.down.at[rows16(m * F2, F2)]),
        net.here(r.cot.at[0, rows_of_mine], r.bg),
    ]
    r.vec_mine[...] = jnp.zeros_like(r.vec_mine)
    own_lanes = pl.ds(pl.multiple_of(m * half, 128), half)
    r.vec_mine[0:2, own_lanes] = r.qkvb[...].astype(F32)
    for k in range(side):
        r.vec_mine[pl.ds(2 + m * side + k, 1), :] = r.upb[k * D : (k + 1) * D].astype(F32).reshape(1, D)
    for k, n in enumerate(ROW_BIASES):
        r.vecs[k : k + 1, :] = getattr(r, n)[...].astype(F32).reshape(1, D)
    net.greet(partners(bits))
    vec_copy = net.send(r.vec_mine, r.vec_got, "y")
    mel_own.wait()
    src = pl.ds(pl.multiple_of(128 + (1 - c) * (span - 128), 128), 128)
    dst = pl.ds(pl.multiple_of(c * (span + 128), 128), 128)
    mel_rim = net.send(r.melbuf.at[0:mels, src], r.melbuf.at[0:mels, dst], "c")
    p = 4 * c + 2 * net.bit(0) + net.bit(1) if bits > 1 else 2 * c + net.bit(0)
    cuts = 8 if bits > 1 else 4

    def pass_on(of, at, count, dim):
        def cut(n, base):
            return rows16(base + at * (n // cuts), count * (n // cuts))

        wo = rows16(c * half + of * (D // 4) + (at - c * (cuts // 2)) * (half // cuts), count * (half // cuts))
        parts = [r.wo.at[wo], r.up.at[of, cut(D, 0)], r.down.at[cut(F2, of * F2)]]
        return [net.copy(x, x, dim) for x in parts]

    def pass_qkv(of, at, count, dim):
        rows = r.wqkv.at[of, :, rows16(at * (D // 4), count * (D // 4))]
        return net.copy(rows, rows, dim)

    two = 2 if bits > 1 else 1
    qkv_y = pass_qkv(m, 2 * c + net.bit(0), 1, "y")
    qkv_x = pass_qkv(1 - m, 2 * c + net.bit(0), 1, 0)
    qkv_c = pass_qkv(1 - m, 2 * c, 2, "c")
    ff_y = pass_on(m, p, 1, "y")
    ff_z = pass_on(1 - m, p, 1, 1) if bits > 1 else []
    ff_x = pass_on(1 - m, (p // two) * two, two, 0)
    ff_c = pass_on(1 - m, c * (cuts // 2), cuts // 2, "c")
    qkv_own.wait()
    qkv_y.start()
    wait_all(own)
    r.small[...] = jnp.zeros_like(r.small)
    stage_mel_rows(r, sub, mel_rim.wait)
    stage_first(r, jnp.logical_and(c == 0, m == 0))
    qkv_y.wait()
    qkv_x.start()
    start_all(ff_y)
    stage_odd(r)
    w2_own.wait()
    stage_second(r, quarter(net))
    vec_copy.wait()
    r.vecs[8:16, :] = r.vec_mine[...] + r.vec_got[...]
    qkv_x.wait()
    qkv_c.start()
    wait_all(ff_y)
    start_all(ff_z)

    def block(slot, part, h):
        return r.kv.at[rows16((3 * slot + part) * half + h * (half // 2), half // 2)]

    def project(h, at_once):
        far, near = [], []
        for part in (1, 2, 0):
            stage_qkv(r, part, h)
            if part:
                far.append(net.copy(block(3 + c, part, h), block(0, part, h), "y"))
                far.append(net.copy(block(4 - c, part, h), block(1, part, h), "c", "y"))
                if at_once:
                    start_all(far[-2:])
            near.append(net.send(block(4 - c, part, h), block(2, part, h), "c"))
        return far, near

    far_own, near_own = project(m, True)
    stage_mask(r, sub)
    add_small(r, DNB, col(r.bg[...].astype(F32)))
    r.normedt[...] = flip(r.normed[...])
    qkv_c.wait()
    far_other, near_other = project(1 - m, False)
    wait_all(near_own)
    heads = half // HEAD

    def flip_taps():
        for tap, to in zip((r.hp, r.he, r.ho), r.tapt):
            to[...] = flip(tap[...])

    hooks = {
        heads: [lambda: start_all(far_other), lambda: wait_all(near_other), lambda: wait_all(ff_z), lambda: start_all(ff_x)],
        2 * heads - 1: [flip_taps],
        2 * heads: [lambda: wait_all(far_own)],
        3 * heads: [lambda: wait_all(far_other), lambda: wait_all(ff_x), lambda: start_all(ff_c)],
    }
    attend(r, c, m, hooks)
    attend_end(r, 1)
    mix_c = net.send(r.mixb.at[half:D], r.mix_got, "c")
    attend_end(r, 0)
    stage_mid(r, c, mix_c.wait, lambda: wait_all(ff_c))

    def summed(n, part, rows, halves):
        views = [
            getattr(r, "g_" + n).at[part * rows * halves : (part + 1) * rows * halves],
            getattr(r, "got_%s%d" % (n, part)),
            getattr(r, "done_" + n).at[part * rows : (part + 1) * rows],
        ]
        return bucket_sum(net, *views, halves, orders(n, bits)[part])

    def leave(n, part):
        done = getattr(r, "done_" + n)
        size = half if n == "qkv" else D
        rows = done if n in ("out", "c1") else done.at[part * size : (part + 1) * size]
        if n == "qkv":
            pairs = [(rows.at[:, j * half : (j + 1) * half], r.qkv_o.at[part, j * half : (j + 1) * half]) for j in range(2)]
        elif n == "up":
            pairs = [(rows, r.up_o.at[:, part * D : (part + 1) * D])]
        elif n in ("down", "c2"):
            pairs = [(rows, getattr(r, n + "_o").at[part * D : (part + 1) * D])]
        else:
            pairs = [(done, getattr(r, n + "_o"))]
        return [net.here_later(src, dst) for src, dst in pairs]

    tracks, leaving = {}, {}
    for n, rows, halves, parts in (
        ("down", D, 2, side),
        ("up", D, 2, side),
        ("out", half, 2, 1),
        ("qkv", half, 2, 3),
        ("c2", D, 1, 3),
        ("c1", r.g_c1.shape[0], 1, 1),
    ):
        for part in range(parts):
            name = "%s%d" % (n, part)
            tracks[name] = summed(n, part, rows, halves)
            leaving[name] = leave(n, part)
            tracks[name].then(functools.partial(start_all, leaving[name]))
    tracks["vec0"] = small_sum(net, r.small, r.got_small, orders("vec", bits)[0])

    def acts_at(name):
        names = ["%s%d" % TRACKS[k] for k in SCHEDULE.get(name, ())]
        return [act for n in names if n in tracks for act in tracks[n].take()]

    def point(name):
        for act in acts_at(name):
            act()

    hooks = {}
    for step in range(2 * side):
        if step and step % 2 == 0:
            ready("down%d" % (step // 2 - 1), "up%d" % (step // 2 - 1))
        hooks[step] = acts_at("ff%d" % step)
    stage_ff(r, hooks)
    ready("down%d" % (side - 1), "up%d" % (side - 1))
    point("ffo")
    stage_mid_pull(r)
    enc = [
        net.copy(r.enc, r.enc_got, "y"),
        pltpu.make_async_copy(r.enc, r.enc_o.at[rows_of_mine], r.own.at[39]),
    ]
    start_all(enc)
    stage_do(r, c, False)
    do_c = net.send(r.dot_out, r.dot.at[half:D], "c")
    point("mid")
    stage_out_weights(r, c)
    ready("out0")
    point("out")
    stage_do(r, c, True)
    stage_diag(r, 0)
    for i, home in enumerate((3 + c, 2)):
        r.qrow[:, i * half : (i + 1) * half] = flip(r.kv[rows16(3 * home * half, half), :])
    r.dorow[:, 0:half] = flip(r.dot[0:half, :])
    do_c.wait()
    r.dorow[:, half:D] = flip(r.dot[half:D, :])
    stage_diag(r, 1)
    both = half * 2
    home_y = net.copy(r.dkv.at[0:both], r.from_y, "y")
    home_d = net.copy(r.dkv.at[both : 2 * both], r.from_d, "c", "y")
    home_c = net.copy(r.dkv.at[2 * both : 3 * both], r.from_c.at[half:], "c")
    hooks = {}

    def at_step(step, *acts):
        hooks.setdefault(step * heads // 4, []).extend(acts)

    at_step(4, home_y.start)
    at_step(8, home_d.start)
    at_step(12, home_c.start)
    for step in range(16):
        at_step(step, *acts_at("pull%d" % step))
    attend_pull(r, c, hooks)
    r.dq_out[...] = (r.dqt[half:D, :] * HEAD**-0.5).astype(BF)
    dq_c = net.send(r.dq_out, r.from_c.at[0:half], "c")
    r.dsum[rows16(c * half, half), :] = (r.dqt[0:half, :] * HEAD**-0.5).astype(BF)
    point("home")
    home_y.wait()
    home_d.wait()
    home_c.wait()

    def total(i, carry):
        for part in range(2):
            rows = rows16(part * half + i * 32, 32)
            mine = r.dkv[rows16(3 * both + part * half + i * 32, 32), :].astype(F32) + r.from_y[rows, :].astype(F32)
            r.dsum[rows16((1 + part) * D + c * half + i * 32, 32), :] = mine.astype(BF)
            other = r.from_c[rows16((1 + part) * half + i * 32, 32), :].astype(F32) + r.from_d[rows, :].astype(F32)
            r.dsum[rows16((1 + part) * D + (1 - c) * half + i * 32, 32), :] = other.astype(BF)
        return carry

    lax.fori_loop(0, half // 32, total, 0)

    def queries_came():
        dq_c.wait()
        r.dsum[rows16((1 - c) * half, half), :] = r.from_c[0:half, :]

    for part in (1, 2):
        stage_qkv_weights(r, part)
        ready("qkv%d" % part)
        point("qkvw%d" % part)
    stage_qkv_pull(r, queries_came)
    point("norm")
    stage_norm_pull(r)
    rim = [net.send(r.sg.at[0:16], r.slots.at[0, i], dim) for i, dim in enumerate(("c", "y"))]
    point("c2")
    for part in range(3):
        stage_conv2_weights(r, part)
        ready("c2%d" % part)
        point("c2w%d" % part)
    stage_qkv_weights(r, 0)
    ready("qkv0")
    point("qkvw0")

    def next_row():
        wait_all(rim)
        return pick_next(net, r.slots.at[0])

    stage_conv2_pull(r, next_row)
    point("first")
    stage_first_pull(r)
    rim = [net.send(r.fe.at[0:16], r.slots.at[1, i], dim) for i, dim in enumerate(("c", "y"))]
    rim += [net.send(r.fo.at[T - 16 : T], r.slots.at[2, i], dim) for i, dim in enumerate(("c", "y"))]
    point("c1")
    stage_conv1_weights(r)
    ready("c10", "vec0")
    point("c1w")
    wait_all(rim)
    stage_mel(r, pick_next(net, r.slots.at[1]), pick_prev(net, r.slots.at[2]))
    rows_of_yours = rows16((1 - sub) * T, T)
    mel_y = net.send(r.melg, r.melg_got, "y")
    point("mel")
    wait_all(enc)
    ends = [
        net.here(r.enc_got, r.enc_o.at[rows_of_yours]),
        net.here(r.melg, r.mel_o.at[rows_of_mine]),
    ]
    point("end")
    drain(*tracks.values())
    mel_y.wait()
    ends.append(net.here(r.melg_got, r.mel_o.at[rows_of_yours]))
    ends.append(net.here(r.small, r.small_o))
    wait_all(ends)
    for copies in leaving.values():
        wait_all(copies)


def run_layer(bits, near, far, outs, T, D, F2, lanes):
    half, H = D // 2, D // HEAD
    td, dt = (T, D), (D, T)
    buckets = dict(down=(D, 2, F2 // D), up=(D, 2, F2 // D), out=(half, 2, 1), qkv=(half, 2, 3), c2=(D, 1, 3), c1=(lanes, 1, 1))
    scratch = dict(
        melbuf=((128, 4 * T + 256), BF),
        mele=((T + 24, 128), F32),
        melo=((T + 24, 128), F32),
        xe=((T, 384), BF),
        xo=((T, 384), BF),
        w1p=((384, D), BF),
        w2=((3, D, D), BF),
        bg=(td, BF),
        wqkv=((2, 3, D, half), BF),
        wo=((D, D), BF),
        up=((2, D, F2), BF),
        down=((2 * F2, D), BF),
        vecs=((16, D), F32),
        vec_mine=((8, D), F32),
        vec_got=((8, D), F32),
        stream=(td, F32),
        he=(td, BF),
        ho=(td, BF),
        hp=(td, BF),
        dge=(td, F32),
        dgo=(td, F32),
        dg2=(td, F32),
        normed=(td, BF),
        kv=((15 * half, T), BF),
        mixt=(dt, F32),
        mixb=(dt, BF),
        normedt=(dt, BF),
        ntwot=(dt, BF),
        mix_got=((half, T), BF),
        dot=(dt, BF),
        dot_out=((half, T), BF),
        top=((H, 1, T), F32),
        total=((H, 1, T), F32),
        diag=((H, 1, T), F32),
        tmp=(td, F32),
        tmp2=(td, F32),
        shift=((T + 16, D), F32),
        wide=((T + 16, 128), F32),
        mid=(td, F32),
        ntwo=(td, BF),
        act=(td, BF),
        ing=(td, BF),
        ffo=(td, F32),
        ntg=(td, F32),
        attg=(td, BF),
        dqt=(dt, F32),
        dq_out=((half, T), BF),
        pb=((T, 2 * T), BF),
        ds=((T, 2 * T), BF),
        dkv=((8 * half, T), BF),
        from_y=((2 * half, T), BF),
        from_d=((2 * half, T), BF),
        from_c=((3 * half, T), BF),
        dsum=((3 * D, T), BF),
        enc_got=(td, BF),
        melg=((T, 256), BF),
        melg_got=((T, 256), BF),
        small=((16, D), F32),
        got_small=((sum(len(subsets(dims)) for dims in orders("vec", bits)[0]), 16, D), F32),
        slots=((3, 2, 16, D), BF),
    )
    alias = T == D
    for n, (rows, halves, parts) in buckets.items():
        if n not in ("qkv", "c2"):
            scratch["g_" + n] = ((rows * halves * parts, D), BF)
        for part in range(parts):
            need = sum_plan(rows, halves, orders(n, bits)[part])[1]
            scratch["got_%s%d" % (n, part)] = ((need, D), BF)
        scratch["done_" + n] = ((rows * parts, D), BF)
    if not alias:
        scratch.update({"tapt%d" % i: (dt, BF) for i in range(3)})
        scratch["turn"] = ((256, T), F32)
        scratch.update(g_qkv=((6 * half, D), BF), g_c2=((6 * half, D), BF))
    names = list(near) + list(far) + list(outs) + list(scratch) + ["send", "recv", "own"]

    def kernel(*refs):
        r = Box()
        for n, ref in zip(names, refs):
            setattr(r, n, ref)
        r.odd, r.smg, r.sg, r.fe, r.fo, r.enc = r.shift, r.mid, r.ntwo, r.act, r.ing, r.bg
        r.qrow, r.dorow = r.act, r.ing
        if alias:
            r.turn = r.tmp.at[0:256]
        r.tapt = (r.hp, r.he, r.ho) if alias else (r.tapt0, r.tapt1, r.tapt2)
        if alias:
            r.g_qkv, r.g_c2 = r.kv.at[0 : 6 * half], r.kv.at[6 * half : 12 * half]
        layer(r, bits)

    vmem, anywhere = pl.BlockSpec(memory_space=pltpu.VMEM), pl.BlockSpec(memory_space=pl.ANY)
    got = pl.pallas_call(
        kernel,
        name="layer",
        out_shape=[jax.ShapeDtypeStruct(*o) for o in outs.values()],
        in_specs=[vmem] * len(near) + [anywhere] * len(far),
        out_specs=[anywhere] * len(outs),
        scratch_shapes=[pltpu.VMEM(*s) for s in scratch.values()]
        + [pltpu.SemaphoreType.DMA((256,)), pltpu.SemaphoreType.DMA((256,)), pltpu.SemaphoreType.DMA((40,))],
        compiler_params=pltpu.CompilerParams(
            vmem_limit_bytes=VMEM_LIMIT, collective_id=1, has_side_effects=True
        ),
    )(*near.values(), *far.values())
    return dict(zip(outs, got))


def run_finish(got, mels, side):
    T2, D = got["enc_o"].shape
    half = D // 2
    ins = list(got)
    outs = dict(
        enc=((1, T2, D), BF),
        mel=((1, mels, 2 * T2), F32),
        c1=((3, mels, D), F32),
        c2=((3, D, D), F32),
        qkv=((3, D, half), F32),
        qkvb=((2, half), F32),
        out=((half, D), F32),
        up=((D, side * D), F32),
        upb=((side * D,), F32),
        down=((side * D, D), F32),
    )
    outs.update({n: ((D,), F32) for n in ROW_BIASES})

    big = ("mel", "c1", "c2", "qkv", "out", "up", "down")
    names = ins + list(outs) + ["in_" + n for n in ins] + ["out_" + n for n in big] + ["came", "went"]

    def kernel(*refs):
        r = Box()
        for n, ref in zip(names, refs):
            setattr(r, n, ref)
        m = lax.axis_index("mp")
        order = ["small_o", "enc_o", "down_o", "up_o", "qkv_o", "c2_o", "mel_o", "out_o", "c1_o"]
        loads = {}
        for k, n in enumerate(order):
            loads[n] = pltpu.make_async_copy(getattr(r, n), getattr(r, "in_" + n), r.came.at[k])
            loads[n].start()
        went = []

        def leave(n):
            copy = pltpu.make_async_copy(getattr(r, "out_" + n), getattr(r, n), r.went.at[len(went)])
            copy.start()
            went.append(copy)

        def cast(src, dst):
            def one(rows):
                dst[rows, :] = src[rows, :].astype(dst.dtype)

            rows_loop(src.shape[0], 256, one)

        loads["small_o"].wait()
        for k, n in enumerate(ROW_BIASES):
            getattr(r, n)[...] = r.in_small_o[k : k + 1, :].reshape(D)
        r.qkvb[...] = r.in_small_o[QB : QB + 2, pl.ds(pl.multiple_of(m * half, 128), half)]
        for k in range(side):
            r.upb[k * D : (k + 1) * D] = r.in_small_o[pl.ds(UPB + m * side + k, 1), :].reshape(D)
        loads["enc_o"].wait()
        copy = pltpu.make_async_copy(r.in_enc_o, r.enc.at[0], r.went.at[len(big)])
        copy.start()
        for n in ("down", "up"):
            loads[n + "_o"].wait()
            cast(getattr(r, "in_" + n + "_o"), getattr(r, "out_" + n))
            leave(n)
        loads["qkv_o"].wait()
        for o in range(3):
            cast(r.in_qkv_o.at[o], r.out_qkv.at[o])
        leave("qkv")
        loads["c2_o"].wait()
        for o in range(3):
            cast(r.in_c2_o.at[o * D : (o + 1) * D], r.out_c2.at[o])
        leave("c2")
        row = lax.broadcasted_iota(jnp.int32, (128, 256), 0)
        lane = lax.broadcasted_iota(jnp.int32, (128, 256), 1)
        even = jnp.where(lane == 2 * row, 1.0, 0.0).astype(BF)
        odd = jnp.where(lane == 2 * row + 1, 1.0, 0.0).astype(BF)
        loads["mel_o"].wait()
        for k in range(T2 // 128):
            rows = slice(k * 128, (k + 1) * 128)
            value = tn(r.in_mel_o[rows, 0:128], even) + tn(r.in_mel_o[rows, 128:256], odd)
            r.out_mel[0, :, k * 256 : (k + 1) * 256] = value[0:mels, :]
        leave("mel")
        loads["out_o"].wait()
        cast(r.in_out_o, r.out_out)
        leave("out")
        loads["c1_o"].wait()
        for o in range(3):
            r.out_c1[o] = r.in_c1_o[o * mels : (o + 1) * mels, :].astype(F32)
        leave("c1")
        copy.wait()
        wait_all(went)

    vmem, anywhere = pl.BlockSpec(memory_space=pltpu.VMEM), pl.BlockSpec(memory_space=pl.ANY)
    done = pl.pallas_call(
        kernel,
        name="finish",
        out_shape=[jax.ShapeDtypeStruct(*o) for o in outs.values()],
        in_specs=[anywhere] * len(ins),
        out_specs=[anywhere if n in big + ("enc",) else vmem for n in outs],
        scratch_shapes=[pltpu.VMEM(got[n].shape, got[n].dtype) for n in ins]
        + [pltpu.VMEM(*outs[n]) for n in big]
        + [pltpu.SemaphoreType.DMA((len(ins),)), pltpu.SemaphoreType.DMA((len(big) + 1,))],
        compiler_params=pltpu.CompilerParams(vmem_limit_bytes=VMEM_LIMIT),
    )(*got.values())
    return dict(zip(outs, done))


def sine_tables(frames, channels, fine):
    half_width = channels // 2
    rate = np.exp(-(math.log(10000.0) / (half_width - 1)) * np.arange(half_width))
    small = np.arange(fine)[:, None] * rate[None, :]
    large = np.arange(0, frames, fine)[:, None] * rate[None, :]
    table = dict(fine_s=np.sin(small), fine_c=np.cos(small), coarse_s=np.sin(large), coarse_c=np.cos(large))
    return {n: jnp.asarray(t, F32) for n, t in table.items()}


def on_device(
    mel_input,
    conv1_weight,
    conv1_bias,
    conv2_weight,
    conv2_bias,
    norm1_gain,
    norm1_bias,
    qkv_weight,
    qkv_bias,
    out_weight,
    out_bias,
    norm2_gain,
    norm2_bias,
    up_weight,
    up_bias,
    down_weight,
    down_bias,
    cotangent,
    speech_mask,
):
    mels = mel_input.shape[1]
    T, D = cotangent.shape[1] // 2, cotangent.shape[2]
    F2 = up_weight.shape[1]
    side, half = F2 // D, D // 2
    bits = (lax.axis_size("dp") - 1).bit_length()
    lanes = -(-3 * mels // 128) * 128
    near = dict(
        w1=conv1_weight,
        mask=speech_mask,
        qkvb=qkv_bias,
        upb=up_bias,
        c1b=conv1_bias,
        c2b=conv2_bias,
        n1g=norm1_gain,
        n1b=norm1_bias,
        oub=out_bias,
        n2g=norm2_gain,
        n2b=norm2_bias,
        dnb=down_bias,
    )
    near.update(sine_tables(4 * T, D, 32))
    got = run_layer(
        bits,
        near,
        dict(
            mel=mel_input,
            cot=cotangent,
            w2_l=conv2_weight,
            wqkv_l=qkv_weight,
            wo_l=out_weight,
            up_l=up_weight,
            down_l=down_weight,
        ),
        dict(
            enc_o=((2 * T, D), BF),
            mel_o=((2 * T, 256), BF),
            down_o=((F2, D), BF),
            up_o=((D, F2), BF),
            out_o=((half, D), BF),
            qkv_o=((3, D, half), BF),
            c2_o=((3 * D, D), BF),
            c1_o=((lanes, D), BF),
            small_o=((16, D), F32),
        ),
        T,
        D,
        F2,
        lanes,
    )
    done = run_finish(got, mels, side)
    names = ("enc", "mel", "c1", "c1b", "c2", "c2b", "n1g", "n1b", "qkv", "qkvb")
    names += ("out", "oub", "n2g", "n2b", "up", "upb", "down", "dnb")
    return tuple(done[n] for n in names)


def solution(mesh):
    placed = (
        P("dp", None, "seq"),
        P(),
        P(),
        P(),
        P(),
        P(),
        P(),
        P(None, None, "mp"),
        P(None, "mp"),
        P("mp", None),
        P(),
        P(),
        P(),
        P(None, "mp"),
        P("mp"),
        P("mp", None),
        P(),
        P("dp", "seq", None),
        P("dp", "seq"),
    )
    return jax.shard_map(
        on_device,
        mesh=mesh,
        in_specs=placed,
        out_specs=(
            P("dp", "seq", None),
            P("dp", None, "seq"),
            P(),
            P(),
            P(),
            P(),
            P(),
            P(),
            P(None, None, "mp"),
            P(None, "mp"),
            P("mp", None),
            P(),
            P(),
            P(),
            P(None, "mp"),
            P("mp"),
            P("mp", None),
            P(),
        ),
        check_vma=False,
    )
```
